32 devices in a mesh: dp: 8 (over z, y), group: 4 (over x, core).
Axes of the slice: x: 2, y: 2, z: 4, core: 2. Of those that a mesh axis runs over, the one named last changes fastest.
Arguments:
- tokens: bfloat16 [16384, 1024], P(('dp', 'group')), may hold values from -6 to 6
- cotangent: bfloat16 [16384, 1024], P(('dp', 'group')), may hold values from -6 to 6
- variate: int32 [16384], P('dp'), may hold values from 0 to 3
- seq_len: int32 [8, 3], P('dp'), may hold values from 1 to 1024, 2048 in all within a row
- seq_adapter: int32 [8, 3], P('dp'), may hold values from 0 to 7
- block_order: int32 [8, 16], P('dp'), may hold values from 0 to 15, each once within a row
- attn_gain: bfloat16 [1024], replicated, may hold values from 0.5 to 1.5
- ffn_gain: bfloat16 [1024], replicated, may hold values from 0.5 to 1.5
- q_gain: bfloat16 [64], replicated, may hold values from 0.25 to 1.75
- k_gain: bfloat16 [64], replicated, may hold values from 0.25 to 1.75
- attn_bias: float32 [2, 16], replicated, may hold values from -4 to 4
- query_weight: bfloat16 [1024, 1024], replicated, may hold values from -0.1875 to 0.1875
- key_weight: bfloat16 [1024, 1024], replicated, may hold values from -0.1875 to 0.1875
- value_weight: bfloat16 [1024, 1024], replicated, may hold values from -0.1875 to 0.1875
- output_weight: bfloat16 [1024, 1024], replicated, may hold values from -1.5 to 1.5
- gate_weight: bfloat16 [1024, 4096], replicated, may hold values from -0.1875 to 0.1875
- up_weight: bfloat16 [1024, 4096], replicated, may hold values from -0.1875 to 0.1875
- down_weight: bfloat16 [4096, 1024], replicated, may hold values from -0.09375 to 0.09375
- adapters: bfloat16 [3014656], replicated, may hold values from -0.1796875 to 0.1796875
- moment1: float32 [3014656], P(('dp', 'group')), may hold values from -6 to 6
- moment2: float32 [3014656], P(('dp', 'group')), may hold values from 0.01 to 100
Outputs:
- layer_out: bfloat16 [16384, 1024], P(('dp', 'group'))
- input_grad: bfloat16 [16384, 1024], P(('dp', 'group'))
- adapter_grad: float32 [3014656], P(('dp', 'group'))
- moment1_new: float32 [3014656], P(('dp', 'group'))
- moment2_new: float32 [3014656], P(('dp', 'group'))
- adapters_new: bfloat16 [3014656], replicated
The draws below stay inside these ranges and needn't reach their ends.
Inputs may be any that keep to these rules, and one draw needn't show every extreme that they name: `seq_len`: each row sums to 2048; the largest of each row is 1024. `block_order`: each row is a permutation.
All inputs are finite; a program needn't handle non-finite values.
Results may differ from the reference program's by a relative error of at most 0.015.
Values may be sent and summed in bfloat16 or wider, within the bound.
No kernel may reach another device: no remote copies, remote signals or barrier semaphores. Data moves between devices by JAX's collectives and lax.ppermute only.
A program may use at most 256 MiB of HBM per device.

```python
import math
import jax
import jax.numpy as jnp
import numpy as np
from jax import lax

D = 1024
HEADS = 16
HEAD_DIM = 64
FF = 4096
RANK = 16
ADAPTERS = 8
VARIATES = 4
SEQ_GRP = 3
GROUP_TOK = 2048
TOKENS = 16384
NB = 16
MAXLEN = 1024
ADP = 3014656
N_DP = 8


def plant(result, key, smallest, largest):
    longest = result.shape.index(max(result.shape))
    spots = []
    for shift in (0, 1):
        where = [jax.random.randint(jax.random.fold_in(key, axis), (), 0, length) for axis, length in enumerate(result.shape)]
        where[longest] = (where[longest] + shift) % result.shape[longest]
        spots.append(tuple(where))
    return result.at[spots[0]].set(smallest).at[spots[1]].set(largest)


def steps_of(own_key, dims, shards, smallest, top_value):
    loudness = 1.0
    for axis_at, blocks in shards:
        draws = jax.random.uniform(jax.random.fold_in(jax.random.fold_in(own_key, 6), axis_at), (blocks,), jnp.float32, smallest / len(shards), top_value / len(shards))
        loudness = loudness * jnp.repeat(jnp.exp(draws), dims[axis_at] // blocks).reshape((-1,) + (1,) * (len(dims) - 1 - axis_at))
    return loudness


def length_profile(number_of, total, reach, slope):
    portions = [(1 << 20) // math.isqrt(grade ** slope) + 1 for grade in range(2, number_of + 1)]
    spare, counts = total - reach - (number_of - 1), [1] * (number_of - 1)
    while spare > 0:
        free = [i for i in range(number_of - 1) if counts[i] < reach]
        mass, left = sum([portions[i] for i in free]), spare
        for i in free:
            extra = min(reach - counts[i], max(1, left * portions[i] // mass), spare)
            counts[i] = counts[i] + extra
            spare = spare - extra
    return np.array([reach] + counts)


def ragged(key, count, total, limit, slope):
    if count == 2:
        one = jax.random.randint(key, (), max(1, total - limit), min(limit, total - 1) + 1)
        return jnp.stack([one, total - one])
    tallies = jnp.asarray(length_profile(count, total, limit, slope), jnp.int32)
    twos = (count - 1) // 2
    source_of, taker = tallies[1:1 + 2 * twos:2], tallies[2:2 + 2 * twos:2]
    margin = jnp.minimum(source_of - 1, limit - taker)
    moved = jax.random.randint(jax.random.fold_in(key, 1), (twos,), 0, 1 << 20) % (margin + 1)
    tallies = tallies.at[1:1 + 2 * twos:2].set(source_of - moved).at[2:2 + 2 * twos:2].set(taker + moved)
    return tallies[jax.random.permutation(jax.random.fold_in(key, 2), count)]


def normal_values(stream_key, extent, width, bound, shards=(), kind=jnp.bfloat16):
    result = jax.random.normal(stream_key, extent, jnp.float32) * width
    if len(shards) > 0:
        result = steps_of(stream_key, extent, shards, -0.22, 0.18) * result
    return jnp.clip(result, min=-bound, max=bound).astype(kind)


def setup_inputs(seed: int = 0) -> dict:
    splits = jax.random.split(jax.random.key(seed), 22)
    tokens = normal_values(splits[0], (TOKENS, D), 1.0, 6.0, ((0, 32),))
    cotangent = normal_values(splits[1], (TOKENS, D), 1.0, 6.0, ((0, 32),))
    variate = plant(jax.random.randint(splits[2], (TOKENS,), 0, VARIATES), jax.random.fold_in(splits[2], 1), 0, VARIATES - 1).astype(jnp.int32)
    seq_len = jax.vmap(lambda own: ragged(own, SEQ_GRP, GROUP_TOK, MAXLEN, 1))(jax.random.split(splits[3], N_DP)).reshape((N_DP, SEQ_GRP)).astype(jnp.int32)
    seq_adapter = plant(jax.random.randint(splits[4], (N_DP, SEQ_GRP), 0, ADAPTERS), jax.random.fold_in(splits[4], 1), 0, ADAPTERS - 1).astype(jnp.int32)
    block_order = jax.vmap(lambda own: jax.random.permutation(own, NB))(jax.random.split(splits[5], N_DP)).reshape((N_DP, NB)).astype(jnp.int32)
    attn_gain = jnp.clip(1.0 + 0.1 * jax.random.normal(splits[6], (D,), jnp.float32), 0.5, 1.5).astype(jnp.bfloat16)
    ffn_gain = jnp.clip(1.0 + 0.1 * jax.random.normal(splits[7], (D,), jnp.float32), 0.5, 1.5).astype(jnp.bfloat16)
    q_gain = jnp.clip(1.0 + 0.15 * jax.random.normal(splits[8], (HEAD_DIM,), jnp.float32), 0.25, 1.75).astype(jnp.bfloat16)
    k_gain = jnp.clip(1.0 + 0.15 * jax.random.normal(splits[9], (HEAD_DIM,), jnp.float32), 0.25, 1.75).astype(jnp.bfloat16)
    attn_bias = normal_values(splits[10], (2, HEADS), 1.0, 4.0, (), jnp.float32)
    query_weight = normal_values(splits[11], (D, D), D ** -0.5, 0.1875)
    key_weight = normal_values(splits[12], (D, D), D ** -0.5, 0.1875)
    value_weight = normal_values(splits[13], (D, D), D ** -0.5, 0.1875)
    output_weight = normal_values(splits[14], (D, D), (max(1, D // 64)) ** -0.5, 1.5)
    gate_weight = normal_values(splits[15], (D, FF), D ** -0.5, 0.1875)
    up_weight = normal_values(splits[16], (D, FF), D ** -0.5, 0.1875)
    down_weight = normal_values(splits[17], (FF, D), FF ** -0.5, 0.09375)
    adapters = normal_values(splits[18], (ADP,), 0.03, 0.1796875)
    moment1 = normal_values(splits[19], (ADP,), 1.0, 6.0, ((0, 32),), jnp.float32)
    moment2 = jnp.clip(jnp.exp(math.log(100.0) - 9.2103404 * jax.random.uniform(splits[20], (ADP,), jnp.float32) ** steps_of(splits[20], (ADP,), ((0, 32),), -0.2, 0.2)), 0.01, 100.0)
    return dict(tokens=tokens, cotangent=cotangent, variate=variate, seq_len=seq_len, seq_adapter=seq_adapter, block_order=block_order, attn_gain=attn_gain, ffn_gain=ffn_gain, q_gain=q_gain, k_gain=k_gain, attn_bias=attn_bias, query_weight=query_weight, key_weight=key_weight, value_weight=value_weight, output_weight=output_weight, gate_weight=gate_weight, up_weight=up_weight, down_weight=down_weight, adapters=adapters, moment1=moment1, moment2=moment2)


@jax.custom_vjp
def lowrank_product(v):
    return lax.optimization_barrier(v.astype(jnp.bfloat16)).astype(jnp.float32)

@jax.custom_vjp
def lowrank_backward(v):
    return v

def low_keep(v):
    return (lowrank_product(v), None)

def low_pass(kept, grad):
    return (grad,)

def back_keep(v):
    return (v, None)

def back_low(kept, grad):
    return (lowrank_product(grad),)
lowrank_product.defvjp(low_keep, low_pass)
lowrank_backward.defvjp(back_keep, back_low)
NORM_EPS = 1e-06
ADAPTER_SCALE = 2.0
ROPE_BASE = 10000.0
MASKED = -1e+30
LEARN_RATE = 0.01
BETA_ONE = 0.9
BETA_TWO = 0.999
ADAM_EPS = 1e-08
WEIGHT_DECAY = 0.01
update_count = 10.0

def matrix_multiply(left, right):
    return jnp.dot(left, right, precision=lax.Precision.HIGHEST, preferred_element_type=jnp.float32)

def rms_norm(values, norm_gain):
    scaled = values * lax.rsqrt(lax.optimization_barrier(jnp.mean(values * values, axis=-1, keepdims=True)) + NORM_EPS)
    return scaled * norm_gain.astype(jnp.float32)

def rope_tables(position, head_width):
    half_width = head_width // 2
    freq_index = jnp.arange(half_width, dtype=jnp.float32)
    frequency = ROPE_BASE ** (-2.0 * freq_index / head_width)
    angles = position.astype(jnp.float32)[:, None] * frequency[None, :]
    return (jnp.cos(angles), jnp.sin(angles))

def shape_heads(values, norm_gain, cos_table, sin_table, head_width):
    row_count = values.shape[0]
    per_head = values.reshape(row_count, -1, head_width)
    normalized_input = rms_norm(per_head, norm_gain)
    half_width = head_width // 2
    first_half = normalized_input[..., :half_width]
    second_half = normalized_input[..., half_width:]
    cos_part = cos_table[:, None, :]
    sin_part = sin_table[:, None, :]
    turned = jnp.concatenate([first_half * cos_part - second_half * sin_part, first_half * sin_part + second_half * cos_part], axis=-1)
    return turned.reshape(row_count, -1)

def unpack(flat_params, shapes, columns):
    partial_pieces = []
    offset = 0
    for fan_in, fan_out in shapes:
        down_size = fan_in * columns
        a_matrix = lax.slice_in_dim(flat_params, offset, offset + down_size).reshape(fan_in, columns)
        offset = offset + down_size
        up_size = columns * fan_out
        b_matrix = lax.slice_in_dim(flat_params, offset, offset + up_size).reshape(columns, fan_out)
        offset = offset + up_size
        partial_pieces.append((a_matrix, b_matrix))
    return partial_pieces

def pack_layer(tokens, flat_params, variate, lengths, adapter_ids, block_list, gains, weights, attn_bias):
    attn_gain, ffn_gain, q_gain, k_gain = gains
    query_weight, key_weight, value_weight, output_weight, gate_weight, up_weight, down_weight = weights
    blocks = block_list.shape[0]
    block_rows = GROUP_TOK // blocks
    work_rows = tokens.reshape(blocks, block_rows, D)[block_list].reshape(GROUP_TOK, D)
    variate_work = variate.reshape(blocks, block_rows)[block_list].reshape(GROUP_TOK)
    seq_ends = jnp.cumsum(lengths)
    seq_starts = seq_ends - lengths
    row_index = jnp.arange(GROUP_TOK, dtype=jnp.int32)
    segment = lax.optimization_barrier(jnp.sum((row_index[:, None] >= seq_ends[None, :]).astype(jnp.int32), axis=1))
    picked = (segment[:, None] == jnp.arange(SEQ_GRP, dtype=jnp.int32)[None, :]).astype(jnp.int32)
    position = row_index - lax.optimization_barrier(jnp.sum(picked * seq_starts[None, :], axis=1))
    row_adapter = lax.optimization_barrier(jnp.sum(picked * adapter_ids[None, :], axis=1))
    columns = ADAPTERS * RANK
    adapter_selector_mask = (row_adapter[:, None] == (jnp.arange(columns, dtype=jnp.int32) // RANK)[None, :]).astype(jnp.float32)
    same_seq = segment[:, None] == segment[None, :]
    same_var = variate_work[:, None] == variate_work[None, :]
    cos_table, sin_table = rope_tables(position, HEAD_DIM)
    shapes = [(D, D), (D, D), (D, D), (D, D), (D, FF), (D, FF), (FF, D)]
    partial_pieces = unpack(flat_params, shapes, columns)

    def lowrank_adapter(layer_inputs, weight_matrix, partial_piece):
        lowrank_inner = lowrank_product(lowrank_backward(matrix_multiply(layer_inputs, partial_piece[0]) * adapter_selector_mask))
        return matrix_multiply(layer_inputs, weight_matrix) + ADAPTER_SCALE * matrix_multiply(lowrank_inner, partial_piece[1])
    normalized_input = lowrank_product(rms_norm(work_rows, attn_gain))
    query_preactivation = lowrank_backward(lowrank_adapter(normalized_input, query_weight, partial_pieces[0]))
    key_preactivation = lowrank_backward(lowrank_adapter(normalized_input, key_weight, partial_pieces[1]))
    value_lowrank = lowrank_product(lowrank_backward(lowrank_adapter(normalized_input, value_weight, partial_pieces[2])))
    query_low = lowrank_product(shape_heads(query_preactivation, q_gain, cos_table, sin_table, HEAD_DIM))
    key_low = lowrank_product(shape_heads(key_preactivation, k_gain, cos_table, sin_table, HEAD_DIM))

    def head_split(values):
        return jnp.transpose(values.reshape(GROUP_TOK, HEADS, HEAD_DIM), (1, 0, 2))

    def one_head(head_items):
        query_head, key_head, value_head, bias_pair = head_items
        scores = matrix_multiply(query_head, key_head.T) * HEAD_DIM ** (-0.5) + jnp.where(same_var, bias_pair[0], bias_pair[1])
        scores = jnp.where(same_seq, lowrank_backward(scores), MASKED)
        exp_score = jnp.exp(scores - lax.optimization_barrier(jnp.max(scores, axis=1, keepdims=True)))
        softmax_prob = exp_score / lax.optimization_barrier(jnp.sum(exp_score, axis=1, keepdims=True))
        return matrix_multiply(lowrank_product(softmax_prob), value_head)
    attended_tokens = lax.map(jax.checkpoint(one_head), (head_split(query_low), head_split(key_low), head_split(value_lowrank), jnp.transpose(attn_bias)))
    attended_tokens = jnp.transpose(attended_tokens, (1, 0, 2)).reshape(GROUP_TOK, D)
    attended_tokens = lowrank_product(lowrank_backward(attended_tokens))
    attention_output = lowrank_backward(lowrank_adapter(attended_tokens, output_weight, partial_pieces[3]))
    residual_stream = work_rows + attention_output
    hidden_lowrank = lowrank_product(rms_norm(residual_stream, ffn_gain))
    gate_preactivation = lowrank_backward(lowrank_adapter(hidden_lowrank, gate_weight, partial_pieces[4]))
    up_preactivation = lowrank_backward(lowrank_adapter(hidden_lowrank, up_weight, partial_pieces[5]))
    activated_hidden = lowrank_product(jax.nn.silu(gate_preactivation) * up_preactivation)
    final_result = residual_stream + lowrank_adapter(activated_hidden, down_weight, partial_pieces[6])
    placed = jnp.zeros((blocks, block_rows, D), jnp.float32).at[block_list].set(final_result.reshape(blocks, block_rows, D))
    return placed.reshape(GROUP_TOK, D)

def reference(tokens, cotangent, variate, seq_len, seq_adapter, block_order, attn_gain, ffn_gain, q_gain, k_gain, attn_bias, query_weight, key_weight, value_weight, output_weight, gate_weight, up_weight, down_weight, adapters, moment1, moment2):
    gains = tuple((g.astype(jnp.float32) for g in (attn_gain, ffn_gain, q_gain, k_gain)))
    weights = tuple((w.astype(jnp.float32) for w in (query_weight, key_weight, value_weight, output_weight, gate_weight, up_weight, down_weight)))
    flat_params = adapters.astype(jnp.float32)
    packed_x = tokens.astype(jnp.float32).reshape(N_DP, GROUP_TOK, D)
    packed_dy = cotangent.astype(jnp.float32).reshape(N_DP, GROUP_TOK, D)
    packed_var = variate.reshape(N_DP, GROUP_TOK)

    def one_pack(grad_sum, pack_items):
        pack_x, pack_dy, pack_var, pack_len, pack_adapter, pack_order = pack_items

        def layer_fn(x_values, param_values):
            return pack_layer(x_values, param_values, pack_var, pack_len, pack_adapter, pack_order, gains, weights, attn_bias)
        final_result, backward = jax.vjp(layer_fn, pack_x, flat_params)
        grad_x, grad_params = backward(pack_dy)
        return (grad_sum + grad_params, (final_result.astype(jnp.bfloat16), grad_x.astype(jnp.bfloat16)))
    grad_sum, (outputs, grads) = lax.scan(one_pack, jnp.zeros((ADP,), jnp.float32), (packed_x, packed_dy, packed_var, seq_len, seq_adapter, block_order))
    first_moment = BETA_ONE * moment1 + (1.0 - BETA_ONE) * grad_sum
    second_moment = BETA_TWO * moment2 + (1.0 - BETA_TWO) * grad_sum * grad_sum
    first_fix = first_moment / (1.0 - BETA_ONE ** update_count)
    second_fix = second_moment / (1.0 - BETA_TWO ** update_count)
    updated = flat_params - LEARN_RATE * (first_fix / (jnp.sqrt(second_fix) + ADAM_EPS) + WEIGHT_DECAY * flat_params)
    return (outputs.reshape(TOKENS, D), grads.reshape(TOKENS, D), grad_sum, first_moment, second_moment, updated.astype(jnp.bfloat16))
```

```python
import functools

import jax
import jax.numpy as jnp
from jax import lax
from jax.experimental import pallas as pl
from jax.experimental.pallas import tpu as pltpu
from jax.sharding import PartitionSpec as P

RANK = 16
ADAPTERS = 8


NORM_EPS = 1e-06
ADAPTER_SCALE = 2.0
ROPE_BASE = 10000.0
MASKED = -1e30
LEARN_RATE = 0.01
BETA_ONE = 0.9
BETA_TWO = 0.999
ADAM_EPS = 1e-08
WEIGHT_DECAY = 0.01
update_count = 10.0


def rms_norm(values, norm_gain):
    scaled = values * lax.rsqrt(jnp.mean(values * values, axis=-1, keepdims=True) + NORM_EPS)
    return scaled * norm_gain.astype(jnp.float32)


def rope_tables(position, head_width):
    half_width = head_width // 2
    freq_index = jnp.arange(half_width, dtype=jnp.float32)
    frequency = ROPE_BASE ** (-2.0 * freq_index / head_width)
    angles = position.astype(jnp.float32)[:, None] * frequency[None, :]
    return (jnp.cos(angles), jnp.sin(angles))


def shape_heads(values, norm_gain, cos_table, sin_table, head_width):
    row_count = values.shape[0]
    per_head = values.reshape(row_count, -1, head_width)
    normalized_input = rms_norm(per_head, norm_gain)
    half_width = head_width // 2
    first_half = normalized_input[..., :half_width]
    second_half = normalized_input[..., half_width:]
    cos_part = cos_table[:, None, :]
    sin_part = sin_table[:, None, :]
    turned = jnp.concatenate(
        [
            first_half * cos_part - second_half * sin_part,
            first_half * sin_part + second_half * cos_part,
        ],
        axis=-1,
    )
    return turned.reshape(row_count, -1)


def unpack(flat_params, shapes, columns):
    partial_pieces = []
    offset = 0
    for fan_in, fan_out in shapes:
        down_size = fan_in * columns
        a_matrix = lax.slice_in_dim(flat_params, offset, offset + down_size).reshape(
            fan_in, columns
        )
        offset = offset + down_size
        up_size = columns * fan_out
        b_matrix = lax.slice_in_dim(flat_params, offset, offset + up_size).reshape(columns, fan_out)
        offset = offset + up_size
        partial_pieces.append((a_matrix, b_matrix))
    return partial_pieces


def contract_leading_rows(left, right):
    return lax.dot_general(
        left, right, (((0,), (0,)), ((), ())), preferred_element_type=jnp.float32
    )


def contract_columns(left, right):
    return lax.dot_general(
        left, right, (((1,), (1,)), ((), ())), preferred_element_type=jnp.float32
    )


def project(low_in, weight_matrix, partial_piece, adapter_selector_mask):
    base_product = jnp.dot(low_in, weight_matrix, preferred_element_type=jnp.float32)
    lowrank_inner = (
        jnp.dot(low_in, partial_piece[0], preferred_element_type=jnp.float32)
        * adapter_selector_mask
    ).astype(jnp.bfloat16)
    return (
        base_product
        + ADAPTER_SCALE
        * jnp.dot(lowrank_inner, partial_piece[1], preferred_element_type=jnp.float32),
        lowrank_inner,
    )


def project_back(
    gradient_lowrank, low_in, lowrank_inner, weight_matrix, partial_piece, adapter_selector_mask
):
    grad_in = contract_columns(gradient_lowrank, weight_matrix)
    gradient_inner = (
        ADAPTER_SCALE * contract_columns(gradient_lowrank, partial_piece[1]) * adapter_selector_mask
    ).astype(jnp.bfloat16)
    grad_in = grad_in + contract_columns(gradient_inner, partial_piece[0])
    grad_a = contract_leading_rows(low_in, gradient_inner)
    grad_up_factor = ADAPTER_SCALE * contract_leading_rows(lowrank_inner, gradient_lowrank)
    return (grad_in, grad_a, grad_up_factor)


VARIATES = 4
VMEM_LIMIT = 56 * 1024 * 1024
EXACT_PARTS = 3


def contract_last(left, right):
    return lax.dot_general(
        left, right, (((1,), (1,)), ((), ())), preferred_element_type=jnp.float32
    )


def exact_parts(values):
    parts = []
    for _ in range(EXACT_PARTS):
        part = values.astype(jnp.bfloat16).astype(jnp.float32)
        parts.append(part)
        values = values - part
    return parts


def spread_parts(column, parts, first):
    result = jnp.zeros(column.shape, jnp.float32)
    for index, part in enumerate(parts):
        result = jnp.where(column == first + index, part, result)
    return result


def query_extension(bias_ref, head, query_var, query_seg, column, segments):
    same = exact_parts(jnp.full((1, column.shape[1]), bias_ref[0, head], jnp.float32))
    other = exact_parts(jnp.full((1, column.shape[1]), bias_ref[1, head], jnp.float32))
    is_same = (column % VARIATES) == query_var
    result = jnp.zeros(column.shape, jnp.float32)
    for index in range(EXACT_PARTS):
        here = (column // VARIATES) == index
        result = jnp.where(here, jnp.where(is_same, same[index], other[index]), result)
    seg_column = column - EXACT_PARTS * VARIATES
    apart = (seg_column >= 0) & (seg_column < segments) & (seg_column != query_seg)
    return jnp.where(apart, MASKED, result)


def key_extension(key_var, key_seg, column, segments):
    seg_column = column - EXACT_PARTS * VARIATES
    one = (column < EXACT_PARTS * VARIATES) & ((column % VARIATES) == key_var)
    one = one | ((seg_column >= 0) & (seg_column < segments) & (seg_column == key_seg))
    one = one | ((seg_column >= segments) & (seg_column < segments + EXACT_PARTS))
    return jnp.where(one, 1.0, 0.0)


def attend_kernel(key_blocks, segments, width, bias_ref, query_ref, qmeta_ref, *refs):
    key_refs, value_refs, kmeta_refs = (
        refs[:key_blocks],
        refs[key_blocks : 2 * key_blocks],
        refs[2 * key_blocks : 3 * key_blocks],
    )
    out_ref, total_ref = refs[3 * key_blocks :]
    pair = pl.program_id(0)
    rows, lanes = query_ref.shape
    lane = lax.broadcasted_iota(jnp.int32, (rows, lanes), 1)
    column = lane % width
    scaled = query_ref[...].astype(jnp.float32) * width ** (-0.5)
    results = []
    for head in range(lanes // width):
        inside = (lane // width) == head
        extension = query_extension(
            bias_ref,
            pair * (lanes // width) + head,
            qmeta_ref[:, 0:1],
            qmeta_ref[:, 1:2],
            column,
            segments,
        )
        left = jnp.where(inside, scaled, extension).astype(jnp.bfloat16)
        total = jnp.zeros((rows, lanes), jnp.float32)
        for block in range(key_blocks):
            key_side = key_extension(
                kmeta_refs[block][:, 0:1], kmeta_refs[block][:, 1:2], column, segments
            )
            right = jnp.where(inside, key_refs[block][...].astype(jnp.float32), key_side)
            scores = contract_last(left, right.astype(jnp.bfloat16))
            weights = jnp.exp(scores).astype(jnp.bfloat16)
            values = jnp.where(inside, value_refs[block][...].astype(jnp.float32), 1.0)
            total = total + jnp.dot(
                weights, values.astype(jnp.bfloat16), preferred_element_type=jnp.float32
            )
        results.append(total)
    first = (lane // width) == 0
    numerator = jnp.where(first, results[0], results[1])
    crossed = jnp.where(first, results[1], results[0])
    out_ref[...] = (numerator / pltpu.roll(crossed, width, 1)).astype(jnp.bfloat16)
    total_ref[...] = jnp.log(crossed)


def lane_block(rows, lanes):
    return pl.BlockSpec((rows, lanes), lambda pair: (0, pair))


def whole_block(shape):
    return pl.BlockSpec(shape, lambda pair: (0,) * len(shape))


def attend(attn_bias, query_low, query_meta, keys, values, key_metas, segments, width):
    rows, features = query_low.shape
    lanes = 2 * width
    count = len(keys)
    flops = 4 * rows * rows * count * features
    return pl.pallas_call(
        functools.partial(attend_kernel, count, segments, width),
        grid=(features // lanes,),
        in_specs=[
            pl.BlockSpec(memory_space=pltpu.SMEM),
            lane_block(rows, lanes),
            whole_block(query_meta.shape),
        ]
        + [lane_block(rows, lanes)] * (2 * count)
        + [whole_block(query_meta.shape)] * count,
        out_specs=[lane_block(rows, lanes)] * 2,
        out_shape=[
            jax.ShapeDtypeStruct((rows, features), jnp.bfloat16),
            jax.ShapeDtypeStruct((rows, features), jnp.float32),
        ],
        compiler_params=pltpu.CompilerParams(vmem_limit_bytes=VMEM_LIMIT),
        cost_estimate=pl.CostEstimate(
            flops=flops, bytes_accessed=12 * rows * features, transcendentals=0
        ),
        name="attend",
    )(attn_bias, query_low, query_meta, *keys, *values, *key_metas)


def attend_back_kernel(
    key_blocks,
    segments,
    width,
    bias_ref,
    query_ref,
    qmeta_ref,
    total_ref,
    attended_ref,
    grad_ref,
    *refs,
):
    key_refs, value_refs, kmeta_refs = (
        refs[:key_blocks],
        refs[key_blocks : 2 * key_blocks],
        refs[2 * key_blocks : 3 * key_blocks],
    )
    grad_query_ref = refs[3 * key_blocks]
    grad_key_refs = refs[3 * key_blocks + 1 : 4 * key_blocks + 1]
    grad_value_refs = refs[4 * key_blocks + 1 :]
    pair = pl.program_id(0)
    rows, lanes = query_ref.shape
    lane = lax.broadcasted_iota(jnp.int32, (rows, lanes), 1)
    column = lane % width
    ones_at = EXACT_PARTS * VARIATES + segments
    scaled = query_ref[...].astype(jnp.float32) * width ** (-0.5)
    scaled_low = scaled.astype(jnp.bfloat16)
    grad_low = grad_ref[...]
    grad = grad_low.astype(jnp.float32)
    overlap = grad * attended_ref[...].astype(jnp.float32)
    total_parts = exact_parts(-total_ref[...])
    grad_query_parts = []
    grad_keys = [[] for _ in range(key_blocks)]
    grad_values = [[] for _ in range(key_blocks)]
    for head in range(lanes // width):
        inside = (lane // width) == head
        extension = query_extension(
            bias_ref,
            pair * (lanes // width) + head,
            qmeta_ref[:, 0:1],
            qmeta_ref[:, 1:2],
            column,
            segments,
        ) + spread_parts(column, total_parts, ones_at)
        right = jnp.where(inside, scaled, extension).astype(jnp.bfloat16)
        prob_dot = jnp.sum(jnp.where(inside, overlap, 0.0), axis=1, keepdims=True)
        dot_side = spread_parts(column, exact_parts(-prob_dot), ones_at)
        grad_right = jnp.where(inside, grad, dot_side).astype(jnp.bfloat16)
        turned = jnp.zeros((width, rows), jnp.float32)
        for block in range(key_blocks):
            key_side = key_extension(
                kmeta_refs[block][:, 0:1], kmeta_refs[block][:, 1:2], column, segments
            )
            key = key_refs[block][...]
            left = jnp.where(inside, key.astype(jnp.float32), key_side).astype(jnp.bfloat16)
            prob = jnp.exp(contract_last(left, right))
            value = value_refs[block][...].astype(jnp.float32)
            value_left = jnp.where(inside, value, key_side).astype(jnp.bfloat16)
            grad_score = prob * contract_last(value_left, grad_right)
            grad_score = grad_score.astype(jnp.bfloat16)
            grad_values[block].append(
                jnp.dot(prob.astype(jnp.bfloat16), grad_low, preferred_element_type=jnp.float32)
            )
            grad_keys[block].append(
                jnp.dot(grad_score, scaled_low, preferred_element_type=jnp.float32)
            )
            key_turned = jnp.transpose(key)[head * width : (head + 1) * width]
            turned = turned + jnp.dot(key_turned, grad_score, preferred_element_type=jnp.float32)
        grad_query_parts.append(turned)
    first = (lane // width) == 0
    stacked = jnp.concatenate(grad_query_parts, axis=0) * width ** (-0.5)
    grad_query_ref[...] = jnp.transpose(stacked)
    for block in range(key_blocks):
        grad_key_refs[block][...] = jnp.where(first, *grad_keys[block]).astype(
            grad_key_refs[block].dtype
        )
        grad_value_refs[block][...] = jnp.where(first, *grad_values[block]).astype(
            grad_value_refs[block].dtype
        )


def attend_back(
    attn_bias,
    query_low,
    query_meta,
    log_total,
    attended_low,
    grad_attended,
    keys,
    values,
    key_metas,
    segments,
    width,
):
    rows, features = query_low.shape
    lanes = 2 * width
    count = len(keys)
    flops = 10 * rows * rows * count * features
    full = jax.ShapeDtypeStruct((rows, features), jnp.float32)
    low = jax.ShapeDtypeStruct((rows, features), jnp.bfloat16)
    results = pl.pallas_call(
        functools.partial(attend_back_kernel, count, segments, width),
        grid=(features // lanes,),
        in_specs=[
            pl.BlockSpec(memory_space=pltpu.SMEM),
            lane_block(rows, lanes),
            whole_block(query_meta.shape),
        ]
        + [lane_block(rows, lanes)] * (3 + 2 * count)
        + [whole_block(query_meta.shape)] * count,
        out_specs=[lane_block(rows, lanes)] * (1 + 2 * count),
        out_shape=[full] + ([full] + [low] * (count - 1)) * 2,
        compiler_params=pltpu.CompilerParams(vmem_limit_bytes=VMEM_LIMIT),
        cost_estimate=pl.CostEstimate(
            flops=flops, bytes_accessed=24 * rows * features, transcendentals=0
        ),
        name="attend_back",
    )(
        attn_bias,
        query_low,
        query_meta,
        log_total,
        attended_low,
        grad_attended,
        *keys,
        *values,
        *key_metas,
    )
    return results[0], results[1 : 1 + count], results[1 + count :]


def pick_rows(wanted, held, rows):
    chosen = (wanted[:, None] == held[None, :]).astype(jnp.bfloat16)
    return jnp.dot(chosen, rows, preferred_element_type=jnp.float32).astype(jnp.bfloat16)


def within_half(array, shift, groups):
    half = groups // 2
    pairs = [
        (base + (place + shift) % half, base + place)
        for base in (0, half)
        for place in range(half)
    ]
    return lax.ppermute(array, "group", pairs)


def gather_half(array, groups):
    return [array] + [within_half(array, shift, groups) for shift in range(1, groups // 2)]


def to_other_half(array, groups):
    half = groups // 2
    return lax.ppermute(array, "group", [(i, (i + half) % groups) for i in range(groups)])


def scatter_sum(array, axis_sizes):
    for name, size in reversed(axis_sizes):
        outer = array.shape[0] // size
        array = array.reshape((outer, size) + array.shape[1:])
        bit = 1
        while bit < size:
            index = lax.axis_index(name)
            own = (index // bit) % 2
            spread = array.reshape((outer, size // (2 * bit), 2) + array.shape[2:])
            keep = lax.dynamic_index_in_dim(spread, own, 2, keepdims=False)
            send = lax.dynamic_index_in_dim(spread, 1 - own, 2, keepdims=False)
            got = lax.ppermute(send, name, [(i, i ^ bit) for i in range(size)])
            array = (keep.astype(jnp.float32) + got.astype(jnp.float32)).astype(jnp.bfloat16)
            bit *= 2
        array = array.reshape((outer,) + array.shape[2:])
    return array


def per_device(
    tokens,
    cotangent,
    variate,
    seq_len,
    seq_adapter,
    block_order,
    attn_gain,
    ffn_gain,
    q_gain,
    k_gain,
    attn_bias,
    query_weight,
    key_weight,
    value_weight,
    output_weight,
    gate_weight,
    up_weight,
    down_weight,
    adapters,
    moment1,
    moment2,
):
    groups = lax.axis_size("group")
    member = lax.axis_index("group")
    row_count, feature_width = tokens.shape
    hidden_width = gate_weight.shape[1]
    head_width = q_gain.shape[0]
    half_devices = groups // 2
    half_rows = half_devices * row_count
    pack_rows = groups * row_count
    swap_rows = row_count // 2
    my_half, my_place = member // half_devices, member % half_devices

    block_list = block_order[0]
    blocks = block_list.shape[0]
    block_rows = pack_rows // blocks
    lengths = seq_len[0]
    segments = lengths.shape[0]
    seq_ends = jnp.cumsum(lengths)
    seq_starts = seq_ends - lengths
    block_index = jnp.arange(blocks, dtype=jnp.int32)
    work_block = jnp.sum(
        jnp.where(block_list[None, :] == block_index[:, None], block_index[None, :], 0), axis=1
    )
    work_row = (
        work_block[:, None] * block_rows + jnp.arange(block_rows, dtype=jnp.int32)[None, :]
    ).reshape(2, half_rows)
    long_start = jnp.sum(jnp.where(lengths == half_rows, seq_starts, 0))
    is_long = (work_row >= long_start) & (work_row < long_start + half_rows)
    long_half = (2 * jnp.sum(is_long[0].astype(jnp.int32)) < half_rows).astype(jnp.int32)
    side = jnp.arange(2, dtype=jnp.int32)[:, None]
    target = jnp.where(is_long, long_half, 1 - long_half)
    foreign = (target != side).astype(jnp.int32)
    foreign_rank = jnp.cumsum(foreign, axis=1) - foreign
    kept_rank = jnp.arange(half_rows, dtype=jnp.int32)[None, :] - foreign_rank
    moved = jnp.sum(foreign[0])
    place = jnp.zeros_like(kept_rank)
    offset = jnp.zeros_like(kept_rank)
    for index in range(1, half_devices):
        start = index * row_count - jnp.minimum(moved, index * swap_rows)
        place = place + (kept_rank >= start)
        offset = jnp.where(kept_rank >= start, start, offset)
    kept_slot = side * half_rows + place * row_count + kept_rank - offset
    foreign_place = foreign_rank // swap_rows
    received = jnp.clip(moved - foreign_place * swap_rows, 0, swap_rows)
    foreign_slot = (
        (1 - side) * half_rows
        + foreign_place * row_count
        + row_count
        - received
        + foreign_rank % swap_rows
    )
    slot = jnp.where(foreign == 1, foreign_slot, kept_slot)
    row_range = jnp.arange(row_count, dtype=jnp.int32)
    order = [(my_place + shift) % half_devices for shift in range(half_devices)]
    half_ids = jnp.concatenate(
        [my_half * half_rows + place_of * row_count + row_range for place_of in order]
    )
    my_slots = half_ids[:row_count]
    away_ids = jnp.concatenate(
        [
            (1 - my_half) * half_rows + place_of * row_count + row_range[swap_rows:]
            for place_of in order
        ]
    )
    slot_mine = lax.dynamic_index_in_dim(slot, my_half, 0, keepdims=False).reshape(
        half_devices, row_count
    )
    held_slots = jnp.concatenate(
        [lax.dynamic_index_in_dim(slot_mine, place_of, 0, keepdims=False) for place_of in order]
    )
    slot_here = held_slots[:row_count]
    wanted = jnp.concatenate([my_slots, away_ids[:swap_rows]])

    def bring(rows):
        picked = pick_rows(wanted, held_slots, jnp.concatenate(gather_half(rows, groups)))
        arrived = to_other_half(picked[row_count:], groups)
        return jnp.concatenate(
            [picked[:swap_rows], picked[swap_rows:row_count] + arrived]
        )

    returned_ids = jnp.concatenate([half_ids, away_ids])

    def send_back(rows):
        back = to_other_half(rows[swap_rows:], groups)
        held = gather_half(rows, groups) + gather_half(back, groups)
        return pick_rows(slot_here, returned_ids, jnp.concatenate(held))

    facts = jnp.stack(
        [
            work_row.reshape(-1) // block_rows,
            work_row.reshape(-1) % block_rows,
            variate,
        ],
        axis=1,
    ).astype(jnp.bfloat16)
    chosen = (half_ids[:, None] == slot.reshape(-1)[None, :]).astype(jnp.bfloat16)
    facts = jnp.dot(chosen, facts, preferred_element_type=jnp.float32).astype(jnp.int32)
    half_row = facts[:, 0] * block_rows + facts[:, 1]
    segment = jnp.sum((half_row[:, None] >= seq_ends[None, :]).astype(jnp.int32), axis=1)
    picked = (segment[:, None] == jnp.arange(segments, dtype=jnp.int32)[None, :]).astype(jnp.int32)
    position = half_row - jnp.sum(picked * seq_starts[None, :], axis=1)
    row_adapter = jnp.sum(picked * seq_adapter[0][None, :], axis=1)
    meta = jnp.stack([facts[:, 2], segment], axis=1)
    key_metas = [meta[i * row_count : (i + 1) * row_count] for i in range(half_devices)]
    columns = ADAPTERS * RANK
    adapter_selector_mask = (
        row_adapter[:row_count, None] == (jnp.arange(columns, dtype=jnp.int32) // RANK)[None, :]
    ).astype(jnp.float32)
    cos_table, sin_table = rope_tables(position[:row_count], head_width)

    my_tokens = bring(tokens).astype(jnp.float32)
    my_grads = bring(cotangent)
    shapes = [(feature_width, feature_width)] * 4 + [
        (feature_width, hidden_width),
        (feature_width, hidden_width),
        (hidden_width, feature_width),
    ]
    partial_pieces = unpack(adapters, shapes, columns)
    normalized_input = rms_norm(my_tokens, attn_gain).astype(jnp.bfloat16)
    query_preactivation, query_inner = project(
        normalized_input, query_weight, partial_pieces[0], adapter_selector_mask
    )
    key_preactivation, key_inner = project(
        normalized_input, key_weight, partial_pieces[1], adapter_selector_mask
    )
    value_raw, value_inner = project(
        normalized_input, value_weight, partial_pieces[2], adapter_selector_mask
    )
    value_lowrank = value_raw.astype(jnp.bfloat16)
    query_low = shape_heads(query_preactivation, q_gain, cos_table, sin_table, head_width).astype(
        jnp.bfloat16
    )
    key_low = shape_heads(key_preactivation, k_gain, cos_table, sin_table, head_width).astype(
        jnp.bfloat16
    )
    keys = gather_half(key_low, groups)
    values = gather_half(value_lowrank, groups)
    attended_low, log_total = attend(
        attn_bias, query_low, key_metas[0], keys, values, key_metas, segments, head_width
    )
    attention_output, out_inner = project(
        attended_low, output_weight, partial_pieces[3], adapter_selector_mask
    )
    residual_stream = my_tokens + attention_output
    hidden_lowrank = rms_norm(residual_stream, ffn_gain).astype(jnp.bfloat16)
    gate_preactivation, gate_inner = project(
        hidden_lowrank, gate_weight, partial_pieces[4], adapter_selector_mask
    )
    up_preactivation, up_inner = project(
        hidden_lowrank, up_weight, partial_pieces[5], adapter_selector_mask
    )
    activated_hidden = (jax.nn.silu(gate_preactivation) * up_preactivation).astype(jnp.bfloat16)
    ffn_out, down_inner = project(
        activated_hidden, down_weight, partial_pieces[6], adapter_selector_mask
    )
    final_result = residual_stream + ffn_out
    layer_out = send_back(final_result.astype(jnp.bfloat16))
    grad_act, down_a, down_b = project_back(
        my_grads,
        activated_hidden,
        down_inner,
        down_weight,
        partial_pieces[6],
        adapter_selector_mask,
    )
    _, act_back = jax.vjp(
        lambda gate_values, up_values: jax.nn.silu(gate_values) * up_values,
        gate_preactivation,
        up_preactivation,
    )
    grad_gate, grad_up = act_back(grad_act)
    grad_hidden_gate, gate_a, gate_b = project_back(
        grad_gate.astype(jnp.bfloat16),
        hidden_lowrank,
        gate_inner,
        gate_weight,
        partial_pieces[4],
        adapter_selector_mask,
    )
    grad_hidden_up, up_a, up_b = project_back(
        grad_up.astype(jnp.bfloat16),
        hidden_lowrank,
        up_inner,
        up_weight,
        partial_pieces[5],
        adapter_selector_mask,
    )
    _, ffn_norm_back = jax.vjp(lambda values: rms_norm(values, ffn_gain), residual_stream)
    grad_residual = (
        my_grads.astype(jnp.float32) + ffn_norm_back(grad_hidden_gate + grad_hidden_up)[0]
    )
    grad_attended, out_a, out_b = project_back(
        grad_residual.astype(jnp.bfloat16),
        attended_low,
        out_inner,
        output_weight,
        partial_pieces[3],
        adapter_selector_mask,
    )
    grad_attended_low = grad_attended.astype(jnp.bfloat16)
    grad_query, grad_keys, grad_values = attend_back(
        attn_bias,
        query_low,
        key_metas[0],
        log_total,
        attended_low,
        grad_attended_low,
        keys,
        values,
        key_metas,
        segments,
        head_width,
    )
    grad_key, grad_value = grad_keys[0], grad_values[0]
    for shift in range(1, half_devices):
        back_shift = half_devices - shift
        grad_key = grad_key + within_half(grad_keys[shift], back_shift, groups).astype(jnp.float32)
        grad_value = grad_value + within_half(grad_values[shift], back_shift, groups).astype(
            jnp.float32
        )
    _, query_head_back = jax.vjp(
        lambda values: shape_heads(values, q_gain, cos_table, sin_table, head_width),
        query_preactivation,
    )
    _, key_head_back = jax.vjp(
        lambda values: shape_heads(values, k_gain, cos_table, sin_table, head_width),
        key_preactivation,
    )
    grad_query_raw = query_head_back(grad_query)[0].astype(jnp.bfloat16)
    grad_key_raw = key_head_back(grad_key)[0].astype(jnp.bfloat16)
    grad_norm_q, query_a, query_b = project_back(
        grad_query_raw,
        normalized_input,
        query_inner,
        query_weight,
        partial_pieces[0],
        adapter_selector_mask,
    )
    grad_norm_k, key_a, key_b = project_back(
        grad_key_raw,
        normalized_input,
        key_inner,
        key_weight,
        partial_pieces[1],
        adapter_selector_mask,
    )
    grad_norm_v, value_a, value_b = project_back(
        grad_value.astype(jnp.bfloat16),
        normalized_input,
        value_inner,
        value_weight,
        partial_pieces[2],
        adapter_selector_mask,
    )
    _, attn_norm_back = jax.vjp(lambda values: rms_norm(values, attn_gain), my_tokens)
    grad_tokens = grad_residual + attn_norm_back(grad_norm_q + grad_norm_k + grad_norm_v)[0]
    input_grad = send_back(grad_tokens.astype(jnp.bfloat16))
    pairs = [
        (query_a, query_b),
        (key_a, key_b),
        (value_a, value_b),
        (out_a, out_b),
        (gate_a, gate_b),
        (up_a, up_b),
        (down_a, down_b),
    ]
    flat_grads = jnp.concatenate(
        [partial_piece.reshape(-1) for pair_grads in pairs for partial_piece in pair_grads]
    )
    axis_sizes = [("dp", lax.axis_size("dp")), ("group", groups)]
    shards = axis_sizes[0][1] * groups
    grad_shard = scatter_sum(flat_grads.astype(jnp.bfloat16).reshape(shards, -1), axis_sizes)
    grad_shard = grad_shard.reshape(-1).astype(jnp.float32)
    shard_count = grad_shard.shape[0]
    shard_start = lax.axis_index(("dp", "group")) * shard_count
    current = lax.dynamic_slice_in_dim(adapters, shard_start, shard_count).astype(jnp.float32)
    first_moment = BETA_ONE * moment1 + (1.0 - BETA_ONE) * grad_shard
    second_moment = BETA_TWO * moment2 + (1.0 - BETA_TWO) * grad_shard * grad_shard
    first_fix = first_moment / (1.0 - BETA_ONE**update_count)
    second_fix = second_moment / (1.0 - BETA_TWO**update_count)
    updated = current - LEARN_RATE * (
        first_fix / (jnp.sqrt(second_fix) + ADAM_EPS) + WEIGHT_DECAY * current
    )
    adapters_new = lax.all_gather(updated.astype(jnp.bfloat16), ("dp", "group"), axis=0, tiled=True)
    return (layer_out, input_grad, grad_shard, first_moment, second_moment, adapters_new)


def solution(mesh):
    in_specs = (
        P(("dp", "group"), None),
        P(("dp", "group"), None),
        P("dp"),
        P("dp", None),
        P("dp", None),
        P("dp", None),
        P(),
        P(),
        P(),
        P(),
        P(),
        P(),
        P(),
        P(),
        P(),
        P(),
        P(),
        P(),
        P(),
        P(("dp", "group")),
        P(("dp", "group")),
    )
    out_specs = (
        P(("dp", "group"), None),
        P(("dp", "group"), None),
        P(("dp", "group")),
        P(("dp", "group")),
        P(("dp", "group")),
        P(),
    )
    return jax.shard_map(
        per_device, mesh=mesh, in_specs=in_specs, out_specs=out_specs, check_vma=False
    )
```

```python
import functools

import jax
import jax.numpy as jnp
from jax import lax
from jax.experimental import pallas as pl
from jax.experimental.pallas import tpu as pltpu
from jax.sharding import PartitionSpec as P

RANK = 16
ADAPTERS = 8
NORM_EPS = 1e-06
ADAPTER_SCALE = 2.0
ROPE_BASE = 10000.0
MASKED = -1e30
LEARN_RATE = 0.01
BETA_ONE = 0.9
BETA_TWO = 0.999
ADAM_EPS = 1e-08
WEIGHT_DECAY = 0.01
update_count = 10.0
VARIATES = 4
VMEM_LIMIT = 56 * 1024 * 1024
EXACT_PARTS = 3


def contract_last(left, right):
    return lax.dot_general(
        left, right, (((1,), (1,)), ((), ())), preferred_element_type=jnp.float32
    )


def exact_parts(values):
    parts = []
    for _ in range(EXACT_PARTS):
        part = values.astype(jnp.bfloat16).astype(jnp.float32)
        parts.append(part)
        values = values - part
    return parts


def spread_parts(column, parts, first):
    result = jnp.zeros(column.shape, jnp.float32)
    for index, part in enumerate(parts):
        result = jnp.where(column == first + index, part, result)
    return result


def query_extension(bias_ref, head, query_var, query_seg, column, segments):
    same = exact_parts(jnp.full((1, column.shape[1]), bias_ref[0, head], jnp.float32))
    other = exact_parts(jnp.full((1, column.shape[1]), bias_ref[1, head], jnp.float32))
    is_same = (column % VARIATES) == query_var
    result = jnp.zeros(column.shape, jnp.float32)
    for index in range(EXACT_PARTS):
        here = (column // VARIATES) == index
        result = jnp.where(here, jnp.where(is_same, same[index], other[index]), result)
    seg_column = column - EXACT_PARTS * VARIATES
    apart = (seg_column >= 0) & (seg_column < segments) & (seg_column != query_seg)
    return jnp.where(apart, MASKED, result)


def key_extension(key_var, key_seg, column, segments):
    seg_column = column - EXACT_PARTS * VARIATES
    one = (column < EXACT_PARTS * VARIATES) & ((column % VARIATES) == key_var)
    one = one | ((seg_column >= 0) & (seg_column < segments) & (seg_column == key_seg))
    one = one | ((seg_column >= segments) & (seg_column < segments + EXACT_PARTS))
    return jnp.where(one, 1.0, 0.0)


def attend_kernel(key_blocks, segments, width, bias_ref, query_ref, qmeta_ref, *refs):
    key_refs, value_refs, kmeta_refs = (
        refs[:key_blocks],
        refs[key_blocks : 2 * key_blocks],
        refs[2 * key_blocks : 3 * key_blocks],
    )
    out_ref, total_ref = refs[3 * key_blocks :]
    pair = pl.program_id(0)
    rows, lanes = query_ref.shape
    lane = lax.broadcasted_iota(jnp.int32, (rows, lanes), 1)
    column = lane % width
    scaled = query_ref[...].astype(jnp.float32) * width ** (-0.5)
    results = []
    for head in range(lanes // width):
        inside = (lane // width) == head
        extension = query_extension(
            bias_ref,
            pair * (lanes // width) + head,
            qmeta_ref[:, 0:1],
            qmeta_ref[:, 1:2],
            column,
            segments,
        )
        left = jnp.where(inside, scaled, extension).astype(jnp.bfloat16)
        total = jnp.zeros((rows, lanes), jnp.float32)
        for block in range(key_blocks):
            key_side = key_extension(
                kmeta_refs[block][:, 0:1], kmeta_refs[block][:, 1:2], column, segments
            )
            right = jnp.where(inside, key_refs[block][...].astype(jnp.float32), key_side)
            scores = contract_last(left, right.astype(jnp.bfloat16))
            weights = jnp.exp(scores).astype(jnp.bfloat16)
            values = jnp.where(inside, value_refs[block][...].astype(jnp.float32), 1.0)
            total = total + jnp.dot(
                weights, values.astype(jnp.bfloat16), preferred_element_type=jnp.float32
            )
        results.append(total)
    first = (lane // width) == 0
    numerator = jnp.where(first, results[0], results[1])
    crossed = jnp.where(first, results[1], results[0])
    out_ref[...] = (numerator / pltpu.roll(crossed, width, 1)).astype(jnp.bfloat16)
    total_ref[...] = jnp.log(crossed)


def lane_block(rows, lanes):
    return pl.BlockSpec((rows, lanes), lambda pair: (0, pair))


def whole_block(shape):
    return pl.BlockSpec(shape, lambda pair: (0,) * len(shape))


def attend(attn_bias, query_low, query_meta, keys, values, key_metas, segments, width):
    rows, features = query_low.shape
    lanes = 2 * width
    count = len(keys)
    flops = 4 * rows * rows * count * features
    return pl.pallas_call(
        functools.partial(attend_kernel, count, segments, width),
        grid=(features // lanes,),
        in_specs=[
            pl.BlockSpec(memory_space=pltpu.SMEM),
            lane_block(rows, lanes),
            whole_block(query_meta.shape),
        ]
        + [lane_block(rows, lanes)] * (2 * count)
        + [whole_block(query_meta.shape)] * count,
        out_specs=[lane_block(rows, lanes)] * 2,
        out_shape=[
            jax.ShapeDtypeStruct((rows, features), jnp.bfloat16),
            jax.ShapeDtypeStruct((rows, features), jnp.float32),
        ],
        compiler_params=pltpu.CompilerParams(vmem_limit_bytes=VMEM_LIMIT),
        cost_estimate=pl.CostEstimate(
            flops=flops, bytes_accessed=12 * rows * features, transcendentals=0
        ),
        name="attend",
    )(attn_bias, query_low, query_meta, *keys, *values, *key_metas)


def attend_back_kernel(
    key_blocks,
    segments,
    width,
    bias_ref,
    query_ref,
    qmeta_ref,
    total_ref,
    attended_ref,
    grad_ref,
    *refs,
):
    key_refs, value_refs, kmeta_refs = (
        refs[:key_blocks],
        refs[key_blocks : 2 * key_blocks],
        refs[2 * key_blocks : 3 * key_blocks],
    )
    grad_query_ref = refs[3 * key_blocks]
    grad_key_refs = refs[3 * key_blocks + 1 : 4 * key_blocks + 1]
    grad_value_refs = refs[4 * key_blocks + 1 :]
    pair = pl.program_id(0)
    rows, lanes = query_ref.shape
    lane = lax.broadcasted_iota(jnp.int32, (rows, lanes), 1)
    column = lane % width
    ones_at = EXACT_PARTS * VARIATES + segments
    scaled = query_ref[...].astype(jnp.float32) * width ** (-0.5)
    scaled_low = scaled.astype(jnp.bfloat16)
    grad_low = grad_ref[...]
    grad = grad_low.astype(jnp.float32)
    overlap = grad * attended_ref[...].astype(jnp.float32)
    total_parts = exact_parts(-total_ref[...])
    grad_query_parts = []
    grad_keys = [[] for _ in range(key_blocks)]
    grad_values = [[] for _ in range(key_blocks)]
    for head in range(lanes // width):
        inside = (lane // width) == head
        extension = query_extension(
            bias_ref,
            pair * (lanes // width) + head,
            qmeta_ref[:, 0:1],
            qmeta_ref[:, 1:2],
            column,
            segments,
        ) + spread_parts(column, total_parts, ones_at)
        right = jnp.where(inside, scaled, extension).astype(jnp.bfloat16)
        prob_dot = jnp.sum(jnp.where(inside, overlap, 0.0), axis=1, keepdims=True)
        dot_side = spread_parts(column, exact_parts(-prob_dot), ones_at)
        grad_right = jnp.where(inside, grad, dot_side).astype(jnp.bfloat16)
        turned = jnp.zeros((width, rows), jnp.float32)
        for block in range(key_blocks):
            key_side = key_extension(
                kmeta_refs[block][:, 0:1], kmeta_refs[block][:, 1:2], column, segments
            )
            key = key_refs[block][...]
            left = jnp.where(inside, key.astype(jnp.float32), key_side).astype(jnp.bfloat16)
            prob = jnp.exp(contract_last(left, right))
            value = value_refs[block][...].astype(jnp.float32)
            value_left = jnp.where(inside, value, key_side).astype(jnp.bfloat16)
            grad_score = prob * contract_last(value_left, grad_right)
            grad_score = grad_score.astype(jnp.bfloat16)
            grad_values[block].append(
                jnp.dot(prob.astype(jnp.bfloat16), grad_low, preferred_element_type=jnp.float32)
            )
            grad_keys[block].append(
                jnp.dot(grad_score, scaled_low, preferred_element_type=jnp.float32)
            )
            key_turned = jnp.transpose(key)[head * width : (head + 1) * width]
            turned = turned + jnp.dot(key_turned, grad_score, preferred_element_type=jnp.float32)
        grad_query_parts.append(turned)
    first = (lane // width) == 0
    stacked = jnp.concatenate(grad_query_parts, axis=0) * width ** (-0.5)
    grad_query_ref[...] = jnp.transpose(stacked)
    for block in range(key_blocks):
        grad_key_refs[block][...] = jnp.where(first, *grad_keys[block]).astype(
            grad_key_refs[block].dtype
        )
        grad_value_refs[block][...] = jnp.where(first, *grad_values[block]).astype(
            grad_value_refs[block].dtype
        )


def attend_back(
    attn_bias,
    query_low,
    query_meta,
    log_total,
    attended_low,
    grad_attended,
    keys,
    values,
    key_metas,
    segments,
    width,
):
    rows, features = query_low.shape
    lanes = 2 * width
    count = len(keys)
    flops = 10 * rows * rows * count * features
    full = jax.ShapeDtypeStruct((rows, features), jnp.float32)
    low = jax.ShapeDtypeStruct((rows, features), jnp.bfloat16)
    results = pl.pallas_call(
        functools.partial(attend_back_kernel, count, segments, width),
        grid=(features // lanes,),
        in_specs=[
            pl.BlockSpec(memory_space=pltpu.SMEM),
            lane_block(rows, lanes),
            whole_block(query_meta.shape),
        ]
        + [lane_block(rows, lanes)] * (3 + 2 * count)
        + [whole_block(query_meta.shape)] * count,
        out_specs=[lane_block(rows, lanes)] * (1 + 2 * count),
        out_shape=[full] + ([full] + [low] * (count - 1)) * 2,
        compiler_params=pltpu.CompilerParams(vmem_limit_bytes=VMEM_LIMIT),
        cost_estimate=pl.CostEstimate(
            flops=flops, bytes_accessed=24 * rows * features, transcendentals=0
        ),
        name="attend_back",
    )(
        attn_bias,
        query_low,
        query_meta,
        log_total,
        attended_low,
        grad_attended,
        *keys,
        *values,
        *key_metas,
    )
    return results[0], results[1 : 1 + count], results[1 + count :]


def pick_rows(wanted, held, rows):
    chosen = (wanted[:, None] == held[None, :]).astype(jnp.bfloat16)
    return jnp.dot(chosen, rows, preferred_element_type=jnp.float32).astype(jnp.bfloat16)


def within_half(array, shift, groups):
    half = groups // 2
    pairs = [
        (base + (place + shift) % half, base + place)
        for base in (0, half)
        for place in range(half)
    ]
    return lax.ppermute(array, "group", pairs)


def gather_half(array, groups):
    return [array] + [within_half(array, shift, groups) for shift in range(1, groups // 2)]


def to_other_half(array, groups):
    half = groups // 2
    return lax.ppermute(array, "group", [(i, (i + half) % groups) for i in range(groups)])


def scatter_sum(array, axis_sizes):
    for name, size in reversed(axis_sizes):
        outer = array.shape[0] // size
        array = array.reshape((outer, size) + array.shape[1:])
        bit = 1
        while bit < size:
            index = lax.axis_index(name)
            own = (index // bit) % 2
            spread = array.reshape((outer, size // (2 * bit), 2) + array.shape[2:])
            keep = lax.dynamic_index_in_dim(spread, own, 2, keepdims=False)
            send = lax.dynamic_index_in_dim(spread, 1 - own, 2, keepdims=False)
            got = lax.ppermute(send, name, [(i, i ^ bit) for i in range(size)])
            array = (keep.astype(jnp.float32) + got.astype(jnp.float32)).astype(jnp.bfloat16)
            bit *= 2
        array = array.reshape((outer,) + array.shape[2:])
    return array


LANES = 128


def adam(current, first_old, second_old, grad):
    first_moment = BETA_ONE * first_old + (1.0 - BETA_ONE) * grad
    second_moment = BETA_TWO * second_old + (1.0 - BETA_TWO) * grad * grad
    first_fix = first_moment / (1.0 - BETA_ONE**update_count)
    second_fix = second_moment / (1.0 - BETA_TWO**update_count)
    updated = current - LEARN_RATE * (
        first_fix / (jnp.sqrt(second_fix) + ADAM_EPS) + WEIGHT_DECAY * current
    )
    return first_moment, second_moment, updated.astype(jnp.bfloat16)


def settle_shards(grads, few_choice, adapters, moment1, moment2, groups):
    a_qkv, b_qkv, a_guo, a_down, b_gu, b_do = grads
    features, few = a_qkv.shape[0], few_choice.shape[1]
    quarters = a_down.shape[1] // few
    down = jnp.concatenate([a_down[:, i * few : (i + 1) * few] for i in range(quarters)])
    wide = [a_qkv[:, i * few : (i + 1) * few] for i in range(3)]
    wide += [a_guo[:, i * few : (i + 1) * few] for i in (2, 0, 1)] + [down]
    tall = [b_qkv[i * few : (i + 1) * few] for i in range(3)]
    tall += [b_do[2 * few : 3 * few], b_gu[:few], b_gu[few : 2 * few], b_do[:few]]
    pieces = []
    for grad_a, grad_b in zip(wide, tall):
        pieces.append(lax.dot_general(grad_a, few_choice, (((1,), (1,)), ((), ()))).reshape(-1))
        pieces.append(jnp.dot(few_choice, grad_b).reshape(-1))
    axis_sizes = [("dp", lax.axis_size("dp")), ("group", groups)]
    shards = axis_sizes[0][1] * groups
    flat_grads = jnp.concatenate(pieces).astype(jnp.bfloat16).reshape(shards, -1)
    grad_shard = scatter_sum(flat_grads, axis_sizes).reshape(-1).astype(jnp.float32)
    shard_count = grad_shard.shape[0]
    shard_start = lax.axis_index(("dp", "group")) * shard_count
    current = lax.dynamic_slice_in_dim(adapters, shard_start, shard_count).astype(jnp.float32)
    first_moment, second_moment, updated = adam(current, moment1, moment2, grad_shard)
    adapters_new = lax.all_gather(updated, ("dp", "group"), axis=0, tiled=True)
    return grad_shard, first_moment, second_moment, adapters_new


def spreads_evenly(devices, features, hidden, total, turns):
    rows = total // LANES
    chunks = features // LANES
    return (
        turns == 2
        and ADAPTERS * RANK == LANES
        and devices * chunks == 256
        and chunks == 8
        and hidden == devices * LANES
        and hidden == 4 * features
        and rows % (devices * devices) == 0
        and devices & (devices - 1) == 0
    )


def spread_wide(grads, devices):
    rows = grads.shape[0] // devices
    return jnp.transpose(grads.reshape(rows, devices, LANES), (1, 0, 2))


def spread_tall(grad, devices):
    return jnp.transpose(grad.reshape(grad.shape[0], devices, LANES), (1, 0, 2))


def spread_square(grad, devices):
    chunks = grad.shape[1] // LANES
    classes = devices // chunks
    parts = grad.reshape(2, RANK // classes, classes, chunks, LANES)
    return jnp.transpose(parts, (2, 3, 0, 1, 4)).reshape(devices, 2 * RANK // classes, LANES)


def one_hot(condition):
    return jnp.where(condition, 1.0, 0.0).astype(jnp.bfloat16)


def sum_wide(table_ref, arrived_ref, first, width):
    sources = arrived_ref.shape[0]
    rows = lax.broadcasted_iota(jnp.int32, (LANES, width * LANES), 0)
    columns = lax.broadcasted_iota(jnp.int32, (LANES, width * LANES), 1)
    fits = (rows // (2 * RANK) == columns // LANES) & (rows % RANK == columns % RANK)
    second = (rows // RANK) % 2 == 1
    adapter = jnp.where(fits, (columns % LANES) // RANK, -1)
    total = jnp.zeros((32, width * LANES), jnp.float32)
    for source in range(sources):
        chosen = jnp.where(second, table_ref[source, 1], table_ref[source, 0])
        total = total + jnp.dot(
            arrived_ref[source, first : first + 32, :],
            one_hot(adapter == chosen),
            preferred_element_type=jnp.float32,
        )
    return total


def sum_tall(adapter_row, arrived_ref, first):
    sources = arrived_ref.shape[0]
    depth = sources * 2 * RANK
    rows = lax.broadcasted_iota(jnp.int32, (LANES, depth), 0)
    columns = lax.broadcasted_iota(jnp.int32, (LANES, depth), 1)
    choice = one_hot((rows // RANK == adapter_row) & (rows % RANK == columns % RANK))
    held = arrived_ref[:, first : first + 2 * RANK, :].reshape(depth, LANES)
    return jnp.dot(choice, held, preferred_element_type=jnp.float32)


def sum_square(adapter_row, arrived_ref, first):
    sources = arrived_ref.shape[0]
    depth = sources * 16
    rows = lax.broadcasted_iota(jnp.int32, (64, depth), 0)
    columns = lax.broadcasted_iota(jnp.int32, (64, depth), 1)
    choice = one_hot(
        ((rows % 32) // 4 == adapter_row)
        & (rows % 4 == columns % 4)
        & (rows // 32 == (columns % 16) // 8)
    )
    held = arrived_ref[:, first : first + 16, :].reshape(depth, LANES)
    return jnp.dot(choice, held, preferred_element_type=jnp.float32)


def settle_kernel(
    early, table_ref, tall_ref, square_ref, arrived_ref, param_ref, m1_ref, m2_ref, grad_ref, new_ref
):
    if early:
        wide = sum_wide(table_ref, arrived_ref, 0, 3)
        last = sum_wide(table_ref, arrived_ref, 32, 4)
        square = sum_square(square_ref[...], arrived_ref, 128)
        parts = [
            wide[:, 2 * LANES :],
            square[32:],
            wide[:, :LANES],
            sum_tall(tall_ref[...], arrived_ref, 64),
            wide[:, LANES : 2 * LANES],
            sum_tall(tall_ref[...], arrived_ref, 96),
        ]
        parts += [last[:, i * LANES : (i + 1) * LANES] for i in range(4)]
        parts.append(square[:32])
    else:
        wide = sum_wide(table_ref, arrived_ref, 0, 3)
        square = [sum_square(square_ref[...], arrived_ref, first) for first in (32, 48)]
        parts = []
        for index in range(3):
            parts.append(wide[:, index * LANES : (index + 1) * LANES])
            parts.append(square[index // 2][(index % 2) * 32 : (index % 2) * 32 + 32])
    row = 0
    for part in parts:
        here = slice(row, row + part.shape[0])
        row += part.shape[0]
        low = part.astype(jnp.bfloat16)
        grad_ref[here, :] = low
        new_ref[here, :] = adam(
            param_ref[here, :].astype(jnp.float32),
            m1_ref[here, :],
            m2_ref[here, :],
            low.astype(jnp.float32),
        )[2]


def settle(early, table, arrived, params, first_old, second_old):
    sources = table.shape[0]
    tall_row = jnp.repeat(table.reshape(-1), RANK)[None, :]
    square_row = jnp.repeat(jnp.tile(table, (1, 2)).reshape(-1), 4)[None, :]
    shape = jax.ShapeDtypeStruct(params.shape, jnp.bfloat16)
    return pl.pallas_call(
        functools.partial(settle_kernel, early),
        in_specs=[pl.BlockSpec(memory_space=pltpu.SMEM)]
        + [pl.BlockSpec(memory_space=pltpu.VMEM)] * 6,
        out_specs=[pl.BlockSpec(memory_space=pltpu.VMEM)] * 2,
        out_shape=[shape, shape],
        compiler_params=pltpu.CompilerParams(vmem_limit_bytes=VMEM_LIMIT),
        cost_estimate=pl.CostEstimate(
            flops=sources * 2**24, bytes_accessed=4 * arrived.size, transcendentals=0
        ),
        name="settle_early" if early else "settle_late",
    )(table, tall_row, square_row, arrived, params, first_old, second_old)


def gather_everywhere(rows, devices, groups):
    pieces = [rows[None]]
    bit = devices // 2
    while bit:
        send = jnp.concatenate(pieces) if len(pieces) > 1 else pieces[0]
        if bit >= groups:
            step = bit // groups
            pairs = [(i, i ^ step) for i in range(devices // groups)]
            pieces.append(lax.ppermute(send, "dp", pairs))
        else:
            pieces.append(lax.ppermute(send, "group", [(i, i ^ bit) for i in range(groups)]))
        bit //= 2
    return pieces


def assemble_kernel(count, order_ref, *refs):
    piece_refs, out_ref = refs[:count], refs[-1]
    block = piece_refs[0].shape[1]
    devices = 2 * piece_refs[-1].shape[0]
    for start in range(0, block, 16):
        held = jnp.concatenate([ref[:, start : start + 16, :] for ref in piece_refs], axis=0)
        out_ref[start * devices : (start + 16) * devices, :] = jnp.dot(
            order_ref[...],
            held.reshape(16 * devices, LANES),
            preferred_element_type=jnp.float32,
        ).astype(jnp.bfloat16)


def assemble(order, pieces, total_rows, first, block, before):
    devices = 2 * pieces[-1].shape[0]
    steps = pieces[0].shape[1] // block
    in_specs = [pl.BlockSpec(order.shape, lambda step: (0, 0))]
    in_specs += [
        pl.BlockSpec((piece.shape[0], block, LANES), lambda step: (0, step, 0)) for piece in pieces
    ]
    operands = [order, *pieces]
    aliases = {}
    if before is not None:
        aliases = {len(operands): 0}
        in_specs.append(pl.BlockSpec(memory_space=pl.ANY))
        operands.append(before)
    skip = first // block
    return pl.pallas_call(
        functools.partial(assemble_kernel, len(pieces)),
        grid=(steps,),
        in_specs=in_specs,
        out_specs=pl.BlockSpec((block * devices, LANES), lambda step: (step + skip, 0)),
        out_shape=jax.ShapeDtypeStruct((total_rows, LANES), jnp.bfloat16),
        input_output_aliases=aliases,
        compiler_params=pltpu.CompilerParams(vmem_limit_bytes=VMEM_LIMIT),
        cost_estimate=pl.CostEstimate(
            flops=steps * block * devices * 2**17,
            bytes_accessed=steps * block * devices * 512,
            transcendentals=0,
        ),
        name="assemble",
    )(*operands)


def rope_tables(position, head_width):
    lane = jnp.arange(LANES, dtype=jnp.int32)
    freq_index = (lane % (head_width // 2)).astype(jnp.float32)
    frequency = ROPE_BASE ** (-2.0 * freq_index / head_width)
    angles = position.astype(jnp.float32)[:, None] * frequency[None, :]
    sign = jnp.where(lane % head_width < head_width // 2, -1.0, 1.0)
    return jnp.cos(angles), jnp.sin(angles) * sign[None, :]


def head_gain(gain):
    return jnp.tile(gain.astype(jnp.float32), LANES // gain.shape[0])[None, :]


def select_kernel(features, hidden, turn_ref, flat_ref, *out_refs):
    a_qkv_ref, a_guo_ref, a_down_ref, b_qkv_ref, b_gu_ref, b_do_ref = out_refs
    few = 2 * RANK
    rows = lax.broadcasted_iota(jnp.int32, (LANES, LANES), 0)
    columns = lax.broadcasted_iota(jnp.int32, (LANES, LANES), 1)
    chosen = jnp.where((columns // RANK) % 2 == 1, turn_ref[1], turn_ref[0])
    fits = (rows // RANK == chosen) & (rows % RANK == columns % RANK)
    start = {}
    row = 0
    for name, rows_in, rows_out in (
        ("q", features, features),
        ("k", features, features),
        ("v", features, features),
        ("o", features, features),
        ("g", features, hidden),
        ("u", features, hidden),
        ("d", hidden, features),
    ):
        start[name] = (row, row + rows_in)
        row += rows_in + rows_out

    def wide(names, length):
        total = jnp.zeros((length, LANES), jnp.float32)
        for place, name in enumerate(names):
            first = start[name][0]
            total = total + jnp.dot(
                flat_ref[first : first + length, :],
                one_hot(fits & (columns // few == place)),
                preferred_element_type=jnp.float32,
            )
        return total.astype(jnp.bfloat16)

    a_qkv_ref[...] = wide("qkv", features)
    a_guo_ref[...] = wide("guo", features)
    for first in range(0, hidden, features):
        a_down_ref[first : first + features, :] = jnp.dot(
            flat_ref[start["d"][0] + first : start["d"][0] + first + features, :],
            one_hot(fits & (columns // few == 0)),
            preferred_element_type=jnp.float32,
        ).astype(jnp.bfloat16)

    def tall(name, length, out_ref, place):
        chunks = length // LANES
        size = RANK * chunks
        to_row = lax.broadcasted_iota(jnp.int32, (size, size), 0)
        from_row = lax.broadcasted_iota(jnp.int32, (size, size), 1)
        turned = one_hot(
            (to_row // RANK == from_row % chunks) & (to_row % RANK == from_row // chunks)
        )
        for turn in range(2):
            first = start[name][1] + pl.multiple_of(turn_ref[turn] * size, LANES)
            block = jnp.dot(
                turned, flat_ref[pl.ds(first, size), :], preferred_element_type=jnp.float32
            ).astype(jnp.bfloat16)
            here = place * few + turn * RANK
            for chunk in range(chunks):
                out_ref[here : here + RANK, chunk * LANES : (chunk + 1) * LANES] = block[
                    chunk * RANK : (chunk + 1) * RANK
                ]

    for out_ref, names in ((b_qkv_ref, "qkv"), (b_gu_ref, "gu"), (b_do_ref, "d.o")):
        out_ref[...] = jnp.zeros(out_ref.shape, out_ref.dtype)
        for place, name in enumerate(names):
            if name != ".":
                tall(name, out_ref.shape[1], out_ref, place)


def select(turn_adapter, adapters, features, hidden):
    shapes = [(features, LANES), (features, LANES), (hidden, LANES)]
    shapes += [(LANES, features), (LANES, hidden), (LANES, features)]
    return pl.pallas_call(
        functools.partial(select_kernel, features, hidden),
        in_specs=[
            pl.BlockSpec(memory_space=pltpu.SMEM),
            pl.BlockSpec(memory_space=pltpu.VMEM),
        ],
        out_specs=[pl.BlockSpec(memory_space=pltpu.VMEM)] * 6,
        out_shape=[jax.ShapeDtypeStruct(shape, jnp.bfloat16) for shape in shapes],
        compiler_params=pltpu.CompilerParams(vmem_limit_bytes=VMEM_LIMIT),
        cost_estimate=pl.CostEstimate(
            flops=2**31, bytes_accessed=4 * adapters.shape[0], transcendentals=0
        ),
        name="select",
    )(turn_adapter, adapters.reshape(-1, LANES))


def dot(left, right):
    return jnp.dot(left, right, preferred_element_type=jnp.float32)


def turn_mask(meta_ref):
    rows = meta_ref.shape[0]
    lane = lax.broadcasted_iota(jnp.int32, (rows, LANES), 1)
    mask = jnp.where((lane // RANK) % 2 == meta_ref[:, 2:3], 1.0, 0.0)
    return mask, lane // (2 * RANK)


def row_norm(values):
    return lax.rsqrt(jnp.mean(values * values, axis=1, keepdims=True) + NORM_EPS)


def row_norm_back(values, gain, grad):
    scale = row_norm(values)
    unit = values * scale
    grad = grad * gain
    return scale * (grad - unit * jnp.mean(grad * unit, axis=1, keepdims=True))


def head_mean(values, width):
    lanes = values.shape[1]
    rows = lax.broadcasted_iota(jnp.int32, (lanes, lanes), 0)
    columns = lax.broadcasted_iota(jnp.int32, (lanes, lanes), 1)
    ones = one_hot(rows // width == columns // width)
    high = values.astype(jnp.bfloat16)
    low = (values - high.astype(jnp.float32)).astype(jnp.bfloat16)
    return (dot(high, ones) + dot(low, ones)) * (1.0 / width)


def swap_halves(values, width):
    lanes = values.shape[1]
    lane = lax.broadcasted_iota(jnp.int32, values.shape, 1)
    ahead = pltpu.roll(values, lanes - width // 2, 1)
    behind = pltpu.roll(values, width // 2, 1)
    return jnp.where(lane % width < width // 2, ahead, behind)


def widen(table, lanes):
    return jnp.concatenate([table] * (lanes // table.shape[1]), axis=1)


def project_heads_kernel(
    width,
    x_ref,
    gain_ref,
    wq_ref,
    wk_ref,
    wv_ref,
    a_ref,
    b_ref,
    meta_ref,
    cos_ref,
    sin_ref,
    q_gain_ref,
    k_gain_ref,
    normed_ref,
    inner_ref,
    q_raw_ref,
    k_raw_ref,
    q_ref,
    k_ref,
    v_ref,
):
    mask, place = turn_mask(meta_ref)

    @pl.when(pl.program_id(0) == 0)
    def _():
        values = x_ref[...].astype(jnp.float32)
        normed = (values * row_norm(values) * gain_ref[...].astype(jnp.float32)).astype(
            jnp.bfloat16
        )
        normed_ref[...] = normed
        inner_ref[...] = (dot(normed, a_ref[...]) * mask).astype(jnp.bfloat16)

    normed = normed_ref[...]
    inner = inner_ref[...].astype(jnp.float32)
    lanes = wq_ref.shape[1]

    def lora(weight_ref, index):
        own = jnp.where(place == index, inner, 0.0).astype(jnp.bfloat16)
        return dot(normed, weight_ref[...]) + ADAPTER_SCALE * dot(own, b_ref[...])

    cosine, sine = widen(cos_ref[...], lanes), widen(sin_ref[...], lanes)

    def turned(raw, head_gain_ref):
        unit = raw * lax.rsqrt(head_mean(raw * raw, width) + NORM_EPS)
        unit = unit * widen(head_gain_ref[...], lanes)
        return (unit * cosine + swap_halves(unit, width) * sine).astype(jnp.bfloat16)

    query = lora(wq_ref, 0)
    q_raw_ref[...] = query
    q_ref[...] = turned(query, q_gain_ref)
    key = lora(wk_ref, 1)
    k_raw_ref[...] = key
    k_ref[...] = turned(key, k_gain_ref)
    v_ref[...] = lora(wv_ref, 2).astype(jnp.bfloat16)


def project_heads(
    rows_in, gain, weights, a_qkv, b_qkv, meta, cos_table, sin_table, q_gain, k_gain, width
):
    rows, features = rows_in.shape
    tile = 256
    grid = (features // tile,)

    def tiled(height):
        return pl.BlockSpec((height, tile), lambda step: (0, step))

    def shape(dtype):
        return jax.ShapeDtypeStruct((rows, features), dtype)

    return pl.pallas_call(
        functools.partial(project_heads_kernel, width),
        grid=grid,
        in_specs=[whole_block((rows, features)), whole_block((1, features))]
        + [tiled(features)] * 3
        + [whole_block((features, LANES)), tiled(LANES), whole_block(meta.shape)]
        + [whole_block((rows, LANES))] * 2
        + [whole_block((1, LANES))] * 2,
        out_specs=[whole_block((rows, features)), whole_block((rows, LANES))] + [tiled(rows)] * 5,
        out_shape=[
            shape(jnp.bfloat16),
            jax.ShapeDtypeStruct((rows, LANES), jnp.bfloat16),
            shape(jnp.float32),
            shape(jnp.float32),
            shape(jnp.bfloat16),
            shape(jnp.bfloat16),
            shape(jnp.bfloat16),
        ],
        compiler_params=pltpu.CompilerParams(vmem_limit_bytes=VMEM_LIMIT),
        cost_estimate=pl.CostEstimate(
            flops=8 * rows * features * features,
            bytes_accessed=6 * features * features + 20 * rows * features,
            transcendentals=0,
        ),
        name="project_heads",
    )(
        rows_in,
        gain[None, :],
        *weights,
        a_qkv,
        b_qkv,
        meta,
        cos_table,
        sin_table,
        q_gain,
        k_gain,
    )


def project_heads_back_kernel(
    count,
    width,
    gq_ref,
    *refs,
):
    gk_refs, gv_refs, refs = refs[:count], refs[count : 2 * count], refs[2 * count :]
    (
        q_raw_ref,
        k_raw_ref,
        normed_ref,
        inner_ref,
        x_ref,
        residual_ref,
        gain_ref,
        wq_ref,
        wk_ref,
        wv_ref,
        a_ref,
        b_ref,
        meta_ref,
        cos_ref,
        sin_ref,
        q_gain_ref,
        k_gain_ref,
        out_ref,
        grad_a_ref,
        grad_b_ref,
        total_ref,
        few_ref,
    ) = refs
    step = pl.program_id(0)
    lanes = wq_ref.shape[1]
    mask, place = turn_mask(meta_ref)
    cosine, sine = widen(cos_ref[...], lanes), widen(sin_ref[...], lanes)

    def turned_back(grad, raw, head_gain_ref):
        grad = grad * cosine - swap_halves(grad, width) * sine
        scale = lax.rsqrt(head_mean(raw * raw, width) + NORM_EPS)
        unit = raw * scale
        grad = grad * widen(head_gain_ref[...], lanes)
        return (scale * (grad - unit * head_mean(grad * unit, width))).astype(jnp.bfloat16)

    def summed(term_refs):
        total = term_refs[0][...].astype(jnp.float32)
        for ref in term_refs[1:]:
            total = total + ref[...].astype(jnp.float32)
        return total

    @pl.when(step == 0)
    def _():
        total_ref[...] = jnp.zeros(total_ref.shape, jnp.float32)
        few_ref[...] = jnp.zeros(few_ref.shape, jnp.float32)

    inner_turned = jnp.transpose(inner_ref[...].astype(jnp.float32) * ADAPTER_SCALE).astype(
        jnp.bfloat16
    )
    errors = [
        turned_back(gq_ref[...], q_raw_ref[...], q_gain_ref),
        turned_back(summed(gk_refs), k_raw_ref[...], k_gain_ref),
        summed(gv_refs).astype(jnp.bfloat16),
    ]
    total = total_ref[...]
    few = few_ref[...]
    wide = 2 * RANK
    for index, (error, weight_ref) in enumerate(zip(errors, (wq_ref, wk_ref, wv_ref))):
        total = total + contract_last(error, weight_ref[...])
        few = few + jnp.where(place == index, contract_last(error, b_ref[...]), 0.0)
        here = slice(index * wide, (index + 1) * wide)
        grad_b_ref[here, :] = dot(inner_turned[here], error).astype(jnp.bfloat16)
    grad_b_ref[3 * wide :, :] = jnp.zeros((LANES - 3 * wide, lanes), jnp.bfloat16)
    total_ref[...] = total
    few_ref[...] = few

    @pl.when(step == pl.num_programs(0) - 1)
    def _():
        low = (ADAPTER_SCALE * few_ref[...] * mask).astype(jnp.bfloat16)
        low_turned = jnp.transpose(low.astype(jnp.float32)).astype(jnp.bfloat16)
        grad_a_ref[...] = jnp.transpose(dot(low_turned, normed_ref[...])).astype(jnp.bfloat16)
        grad = total_ref[...] + contract_last(low, a_ref[...])
        out_ref[...] = (
            residual_ref[...]
            + row_norm_back(
                x_ref[...].astype(jnp.float32), gain_ref[...].astype(jnp.float32), grad
            )
        ).astype(jnp.bfloat16)


def project_heads_back(
    grad_query,
    key_terms,
    value_terms,
    query_raw,
    key_raw,
    normed,
    inner,
    rows_in,
    grad_residual,
    gain,
    weights,
    a_qkv,
    b_qkv,
    meta,
    cos_table,
    sin_table,
    q_gain,
    k_gain,
    width,
):
    rows, features = rows_in.shape
    count = len(key_terms)
    tile = 256

    def tiled(height):
        return pl.BlockSpec((height, tile), lambda step: (0, step))

    full = whole_block((rows, features))
    return pl.pallas_call(
        functools.partial(project_heads_back_kernel, count, width),
        grid=(features // tile,),
        in_specs=[tiled(rows)] * (3 + 2 * count)
        + [full, whole_block((rows, LANES)), full, full, whole_block((1, features))]
        + [tiled(features)] * 3
        + [whole_block((features, LANES)), tiled(LANES), whole_block(meta.shape)]
        + [whole_block((rows, LANES))] * 2
        + [whole_block((1, LANES))] * 2,
        out_specs=[full, whole_block((features, LANES)), tiled(LANES)],
        out_shape=[
            jax.ShapeDtypeStruct((rows, features), jnp.bfloat16),
            jax.ShapeDtypeStruct((features, LANES), jnp.bfloat16),
            jax.ShapeDtypeStruct((LANES, features), jnp.bfloat16),
        ],
        scratch_shapes=[
            pltpu.VMEM((rows, features), jnp.float32),
            pltpu.VMEM((rows, LANES), jnp.float32),
        ],
        compiler_params=pltpu.CompilerParams(vmem_limit_bytes=VMEM_LIMIT),
        cost_estimate=pl.CostEstimate(
            flops=8 * rows * features * features,
            bytes_accessed=6 * features * features + 30 * rows * features,
            transcendentals=0,
        ),
        name="project_heads_back",
    )(
        grad_query,
        *key_terms,
        *value_terms,
        query_raw,
        key_raw,
        normed,
        inner,
        rows_in,
        grad_residual,
        gain[None, :],
        *weights,
        a_qkv,
        b_qkv,
        meta,
        cos_table,
        sin_table,
        q_gain,
        k_gain,
    )


def feed_forward_kernel(
    att_ref,
    x_ref,
    e_ref,
    gain_ref,
    wo_ref,
    wg_ref,
    wu_ref,
    wd_ref,
    a_guo_ref,
    a_down_ref,
    b_gu_ref,
    b_do_ref,
    meta_ref,
    out_ref,
    grad_res_ref,
    grad_att_ref,
    grad_a_ref,
    grad_ad_ref,
    grad_bgu_ref,
    grad_bdo_ref,
    res_ref,
    hidden_ref,
    inner_ref,
    inner_turned_ref,
    sum_ref,
    grad_hidden_ref,
    inner_down_ref,
    few_ref,
    few_down_ref,
    few_down_turned_ref,
    down_ref,
):
    step = pl.program_id(0)
    mask, place = turn_mask(meta_ref)
    tile = wg_ref.shape[1]
    features = wo_ref.shape[0]
    wide = 2 * RANK

    def only(values, index):
        return jnp.where(place == index, values, 0.0).astype(jnp.bfloat16)

    def turn(values):
        return jnp.transpose(values.astype(jnp.float32)).astype(jnp.bfloat16)

    @pl.when(step == 0)
    def _():
        att = att_ref[...]
        inner_out = dot(att, a_guo_ref[...]) * mask
        res = (
            x_ref[...].astype(jnp.float32)
            + dot(att, wo_ref[...])
            + ADAPTER_SCALE * dot(only(inner_out, 2), b_do_ref[...])
        )
        res_ref[...] = res
        hidden = (res * row_norm(res) * gain_ref[...].astype(jnp.float32)).astype(jnp.bfloat16)
        hidden_ref[...] = hidden
        inner = dot(hidden, a_guo_ref[...]) * mask
        inner = jnp.where(place == 2, inner_out, inner).astype(jnp.bfloat16)
        inner_ref[...] = inner
        inner_turned_ref[...] = turn(inner.astype(jnp.float32) * ADAPTER_SCALE)
        few_down = only(ADAPTER_SCALE * contract_last(e_ref[...], b_do_ref[...]) * mask, 0)
        few_down_ref[...] = few_down
        few_down_turned_ref[...] = turn(few_down)[:wide]
        sum_ref[...] = jnp.zeros(sum_ref.shape, jnp.float32)
        grad_hidden_ref[...] = jnp.zeros(grad_hidden_ref.shape, jnp.float32)
        inner_down_ref[...] = jnp.zeros(inner_down_ref.shape, jnp.float32)
        few_ref[...] = jnp.zeros(few_ref.shape, jnp.float32)

    hidden = hidden_ref[...]
    inner = inner_ref[...].astype(jnp.float32)
    gate_weight, up_weight, down_weight = wg_ref[...], wu_ref[...], wd_ref[...]
    b_tile = b_gu_ref[...]
    gate = dot(hidden, gate_weight) + ADAPTER_SCALE * dot(only(inner, 0), b_tile)
    up = dot(hidden, up_weight) + ADAPTER_SCALE * dot(only(inner, 1), b_tile)
    grad_act = contract_last(e_ref[...], down_weight) + contract_last(
        few_down_ref[...], a_down_ref[...]
    )
    sigmoid = 1.0 / (1.0 + jnp.exp(-gate))
    silu = gate * sigmoid
    act = (silu * up).astype(jnp.bfloat16)
    grad_up = (grad_act * silu).astype(jnp.bfloat16)
    grad_gate = (grad_act * up * (sigmoid * (1.0 + gate * (1.0 - sigmoid)))).astype(jnp.bfloat16)
    sum_ref[...] += dot(act, down_weight)
    inner_down_ref[...] += dot(act, a_down_ref[...])
    grad_hidden_ref[...] += contract_last(grad_gate, gate_weight) + contract_last(
        grad_up, up_weight
    )
    few_ref[...] += jnp.where(
        place == 0, contract_last(grad_gate, b_tile), contract_last(grad_up, b_tile)
    )
    grad_bgu_ref[:wide, :] = dot(inner_turned_ref[:wide, :], grad_gate).astype(jnp.bfloat16)
    grad_bgu_ref[wide:, :] = dot(inner_turned_ref[wide : 2 * wide, :], grad_up).astype(
        jnp.bfloat16
    )
    per_quarter = features // tile
    down_ref[
        pl.ds(pl.multiple_of((step // per_quarter) * wide, wide), wide),
        pl.ds(pl.multiple_of((step % per_quarter) * tile, tile), tile),
    ] = dot(few_down_turned_ref[...], act)

    @pl.when(step == pl.num_programs(0) - 1)
    def _():
        grads_out = e_ref[...]
        inner_down = only(inner_down_ref[...] * mask, 0)
        res = res_ref[...]
        out_ref[...] = (
            res + sum_ref[...] + ADAPTER_SCALE * dot(inner_down, b_do_ref[...])
        ).astype(jnp.bfloat16)
        few = jnp.where(place < 2, ADAPTER_SCALE * few_ref[...] * mask, 0.0).astype(jnp.bfloat16)
        grad_hidden = grad_hidden_ref[...] + contract_last(few, a_guo_ref[...])
        grad_res = grads_out.astype(jnp.float32) + row_norm_back(
            res, gain_ref[...].astype(jnp.float32), grad_hidden
        )
        grad_res_ref[...] = grad_res
        low = grad_res.astype(jnp.bfloat16)
        few_out = only(ADAPTER_SCALE * contract_last(low, b_do_ref[...]) * mask, 2)
        grad_att_ref[...] = (
            contract_last(low, wo_ref[...]) + contract_last(few_out, a_guo_ref[...])
        ).astype(jnp.bfloat16)
        grad_a = dot(turn(few), hidden_ref[...]) + dot(turn(few_out), att_ref[...])
        grad_a_ref[...] = jnp.transpose(grad_a).astype(jnp.bfloat16)
        grad_ad_ref[...] = jnp.transpose(down_ref[...]).astype(jnp.bfloat16)
        inner_out = only(inner_ref[...].astype(jnp.float32), 2)
        grad_bdo_ref[...] = (
            ADAPTER_SCALE * (dot(turn(inner_down), grads_out) + dot(turn(inner_out), low))
        ).astype(jnp.bfloat16)


def feed_forward(attended, rows_in, grads_out, gain, weights, selected, meta):
    rows, features = rows_in.shape
    hidden = weights[1].shape[1]
    tile = 512
    full = whole_block((rows, features))
    square = whole_block((features, features))
    column = pl.BlockSpec((features, tile), lambda step: (0, step))

    def shape(height, length, dtype):
        return jax.ShapeDtypeStruct((height, length), dtype)

    return pl.pallas_call(
        feed_forward_kernel,
        grid=(hidden // tile,),
        in_specs=[
            full,
            full,
            full,
            whole_block((1, features)),
            square,
            column,
            column,
            pl.BlockSpec((tile, features), lambda step: (step, 0)),
            whole_block((features, LANES)),
            pl.BlockSpec((tile, LANES), lambda step: (step, 0)),
            pl.BlockSpec((LANES, tile), lambda step: (0, step)),
            whole_block((LANES, features)),
            whole_block(meta.shape),
        ],
        out_specs=[
            full,
            full,
            full,
            whole_block((features, LANES)),
            whole_block((features, LANES)),
            pl.BlockSpec((4 * RANK, tile), lambda step: (0, step)),
            whole_block((LANES, features)),
        ],
        out_shape=[
            shape(rows, features, jnp.bfloat16),
            shape(rows, features, jnp.float32),
            shape(rows, features, jnp.bfloat16),
            shape(features, LANES, jnp.bfloat16),
            shape(features, LANES, jnp.bfloat16),
            shape(4 * RANK, hidden, jnp.bfloat16),
            shape(LANES, features, jnp.bfloat16),
        ],
        scratch_shapes=[
            pltpu.VMEM((rows, features), jnp.float32),
            pltpu.VMEM((rows, features), jnp.bfloat16),
            pltpu.VMEM((rows, LANES), jnp.bfloat16),
            pltpu.VMEM((LANES, rows), jnp.bfloat16),
            pltpu.VMEM((rows, features), jnp.float32),
            pltpu.VMEM((rows, features), jnp.float32),
            pltpu.VMEM((rows, LANES), jnp.float32),
            pltpu.VMEM((rows, LANES), jnp.float32),
            pltpu.VMEM((rows, LANES), jnp.bfloat16),
            pltpu.VMEM((2 * RANK, rows), jnp.bfloat16),
            pltpu.VMEM((LANES, features), jnp.float32),
        ],
        compiler_params=pltpu.CompilerParams(vmem_limit_bytes=VMEM_LIMIT),
        cost_estimate=pl.CostEstimate(
            flops=14 * rows * features * hidden,
            bytes_accessed=8 * features * hidden + 16 * rows * features,
            transcendentals=0,
        ),
        name="feed_forward",
    )(attended, rows_in, grads_out, gain[None, :], *weights, *selected, meta)


def settle_spread(grads, turn_adapter, adapters, moment1, moment2, devices):
    a_qkv, b_qkv, a_guo, a_down, b_gu, b_do = grads
    axes = ("dp", "group")
    groups = lax.axis_size("group")
    me = lax.axis_index(axes)
    total_rows = adapters.shape[0] // LANES
    spread_rows = total_rows // devices
    own_rows = spread_rows // devices
    features = a_qkv.shape[0]
    late_rows = 6 * features // devices
    few = 2 * RANK

    moments = jnp.concatenate(
        [
            jnp.transpose(flat.reshape(own_rows, devices, LANES), (1, 0, 2))
            for flat in (moment1, moment2)
        ],
        axis=1,
    )
    moments, a_guo = lax.optimization_barrier((moments, a_guo))
    moments = lax.all_to_all(moments, axes, 0, 0, tiled=True)
    first_old = moments[:, :own_rows].reshape(spread_rows, LANES)
    second_old = moments[:, own_rows:].reshape(spread_rows, LANES)
    params = lax.dynamic_index_in_dim(
        adapters.reshape(spread_rows, devices, LANES), me, 1, keepdims=False
    )
    told = jnp.where(
        jnp.arange(LANES, dtype=jnp.int32) == 3 * few,
        turn_adapter[0],
        jnp.where(jnp.arange(LANES, dtype=jnp.int32) == 3 * few + 1, turn_adapter[1], 0),
    ).astype(jnp.bfloat16)
    early = jnp.concatenate(
        [
            spread_wide(a_guo + told[None, :], devices),
            spread_wide(a_down, devices),
            spread_tall(b_gu[:few], devices),
            spread_tall(b_gu[few : 2 * few], devices),
            spread_square(b_do[:few], devices),
            spread_square(b_do[2 * few : 3 * few], devices),
        ],
        axis=1,
    )
    early = lax.all_to_all(early, axes, 0, 0, tiled=True)
    table = early[:, 0, 3 * few : 3 * few + 2].astype(jnp.int32)
    early_grad, early_new = settle(
        True, table, early, params[late_rows:], first_old[late_rows:], second_old[late_rows:]
    )
    piece_range = jnp.arange(devices, dtype=jnp.int32)
    reversed_bits = jnp.zeros_like(piece_range)
    bit = 1
    while bit < devices:
        reversed_bits = reversed_bits * 2 + (piece_range // bit) % 2
        bit *= 2
    unit = jnp.arange(16, dtype=jnp.int32)
    order = (
        (unit[:, None, None, None] == unit[None, None, None, :])
        & (piece_range[None, :, None, None] == (me ^ reversed_bits)[None, None, :, None])
    ).astype(jnp.bfloat16)
    order = order.reshape(16 * devices, 16 * devices)
    early_pieces = gather_everywhere(early_new, devices, groups)
    adapters_new = assemble(order, early_pieces, total_rows, late_rows, 32, None)
    late = jnp.concatenate(
        [spread_wide(a_qkv, devices)]
        + [spread_square(b_qkv[i * few : (i + 1) * few], devices) for i in range(4)],
        axis=1,
    )
    late = lax.all_to_all(late, axes, 0, 0, tiled=True)
    late_grad, late_new = settle(
        False, table, late, params[:late_rows], first_old[:late_rows], second_old[:late_rows]
    )
    late_pieces = gather_everywhere(late_new, devices, groups)
    adapters_new = assemble(order, late_pieces, total_rows, 0, 64, adapters_new)
    grads = jnp.concatenate([late_grad, early_grad]).reshape(devices, own_rows, LANES)
    grads = lax.all_to_all(grads, axes, 0, 0, tiled=True)
    grad_shard = jnp.transpose(grads, (1, 0, 2)).reshape(-1).astype(jnp.float32)
    current = jnp.zeros((), jnp.float32)
    first_moment, second_moment, _ = adam(current, moment1, moment2, grad_shard)
    return grad_shard, first_moment, second_moment, adapters_new.reshape(-1)


def per_device(
    tokens,
    cotangent,
    variate,
    seq_len,
    seq_adapter,
    block_order,
    attn_gain,
    ffn_gain,
    q_gain,
    k_gain,
    attn_bias,
    query_weight,
    key_weight,
    value_weight,
    output_weight,
    gate_weight,
    up_weight,
    down_weight,
    adapters,
    moment1,
    moment2,
):
    groups = lax.axis_size("group")
    member = lax.axis_index("group")
    row_count, feature_width = tokens.shape
    hidden_width = gate_weight.shape[1]
    head_width = q_gain.shape[0]
    half_devices = groups // 2
    half_rows = half_devices * row_count
    pack_rows = groups * row_count
    swap_rows = row_count // 2
    my_half, my_place = member // half_devices, member % half_devices

    block_list = block_order[0]
    blocks = block_list.shape[0]
    block_rows = pack_rows // blocks
    lengths = seq_len[0]
    segments = lengths.shape[0]
    seq_ends = jnp.cumsum(lengths)
    seq_starts = seq_ends - lengths
    block_index = jnp.arange(blocks, dtype=jnp.int32)
    work_block = jnp.sum(
        jnp.where(block_list[None, :] == block_index[:, None], block_index[None, :], 0), axis=1
    )
    work_row = (
        work_block[:, None] * block_rows + jnp.arange(block_rows, dtype=jnp.int32)[None, :]
    ).reshape(2, half_rows)
    long_start = jnp.sum(jnp.where(lengths == half_rows, seq_starts, 0))
    is_long = (work_row >= long_start) & (work_row < long_start + half_rows)
    long_half = (2 * jnp.sum(is_long[0].astype(jnp.int32)) < half_rows).astype(jnp.int32)
    side = jnp.arange(2, dtype=jnp.int32)[:, None]
    target = jnp.where(is_long, long_half, 1 - long_half)
    foreign = (target != side).astype(jnp.int32)
    foreign_rank = jnp.cumsum(foreign, axis=1) - foreign
    kept_rank = jnp.arange(half_rows, dtype=jnp.int32)[None, :] - foreign_rank
    moved = jnp.sum(foreign[0])
    place = jnp.zeros_like(kept_rank)
    offset = jnp.zeros_like(kept_rank)
    for index in range(1, half_devices):
        start = index * row_count - jnp.minimum(moved, index * swap_rows)
        place = place + (kept_rank >= start)
        offset = jnp.where(kept_rank >= start, start, offset)
    kept_slot = side * half_rows + place * row_count + kept_rank - offset
    foreign_place = foreign_rank // swap_rows
    received = jnp.clip(moved - foreign_place * swap_rows, 0, swap_rows)
    foreign_slot = (
        (1 - side) * half_rows
        + foreign_place * row_count
        + row_count
        - received
        + foreign_rank % swap_rows
    )
    slot = jnp.where(foreign == 1, foreign_slot, kept_slot)
    row_range = jnp.arange(row_count, dtype=jnp.int32)
    order = [(my_place + shift) % half_devices for shift in range(half_devices)]
    half_ids = jnp.concatenate(
        [my_half * half_rows + place_of * row_count + row_range for place_of in order]
    )
    my_slots = half_ids[:row_count]
    away_ids = jnp.concatenate(
        [
            (1 - my_half) * half_rows + place_of * row_count + row_range[swap_rows:]
            for place_of in order
        ]
    )
    slot_mine = lax.dynamic_index_in_dim(slot, my_half, 0, keepdims=False).reshape(
        half_devices, row_count
    )
    held_slots = jnp.concatenate(
        [lax.dynamic_index_in_dim(slot_mine, place_of, 0, keepdims=False) for place_of in order]
    )
    slot_here = held_slots[:row_count]
    wanted = jnp.concatenate([my_slots, away_ids[:swap_rows]])

    def bring(rows):
        picked = pick_rows(wanted, held_slots, jnp.concatenate(gather_half(rows, groups)))
        arrived = to_other_half(picked[row_count:], groups)
        return jnp.concatenate(
            [picked[:swap_rows], picked[swap_rows:row_count] + arrived]
        )

    returned_ids = jnp.concatenate([half_ids, away_ids])

    def send_back(rows):
        back = to_other_half(rows[swap_rows:], groups)
        held = gather_half(rows, groups) + gather_half(back, groups)
        return pick_rows(slot_here, returned_ids, jnp.concatenate(held))

    facts = jnp.stack(
        [
            work_row.reshape(-1) // block_rows,
            work_row.reshape(-1) % block_rows,
            variate,
        ],
        axis=1,
    ).astype(jnp.bfloat16)
    chosen = (half_ids[:, None] == slot.reshape(-1)[None, :]).astype(jnp.bfloat16)
    facts = jnp.dot(chosen, facts, preferred_element_type=jnp.float32).astype(jnp.int32)
    half_row = facts[:, 0] * block_rows + facts[:, 1]
    segment = jnp.sum((half_row[:, None] >= seq_ends[None, :]).astype(jnp.int32), axis=1)
    picked = (segment[:, None] == jnp.arange(segments, dtype=jnp.int32)[None, :]).astype(jnp.int32)
    position = half_row - jnp.sum(picked * seq_starts[None, :], axis=1)
    turns = max(1, segments - 1)
    long_index = jnp.sum(jnp.where(lengths == half_rows, jnp.arange(segments, dtype=jnp.int32), 0))
    on_long = my_half == long_half
    turn_range = jnp.arange(turns, dtype=jnp.int32)
    turn_segment = jnp.where(
        on_long, long_index, turn_range + (turn_range >= long_index).astype(jnp.int32)
    )
    turn_adapter = jnp.sum(
        jnp.where(
            turn_segment[:, None] == jnp.arange(segments, dtype=jnp.int32)[None, :],
            seq_adapter[0][None, :],
            0,
        ),
        axis=1,
    )
    row_turn = jnp.where(on_long, 0, segment - (segment > long_index).astype(jnp.int32))
    meta = jnp.stack([facts[:, 2], segment, row_turn], axis=1)
    key_metas = [meta[i * row_count : (i + 1) * row_count] for i in range(half_devices)]
    meta = key_metas[0]
    columns = ADAPTERS * RANK
    few = turns * RANK
    few_range = jnp.arange(few, dtype=jnp.int32)
    few_column = jnp.repeat(turn_adapter, RANK) * RANK + few_range % RANK
    few_choice = (jnp.arange(columns, dtype=jnp.int32)[:, None] == few_column[None, :]).astype(
        jnp.bfloat16
    )
    cos_table, sin_table = rope_tables(position[:row_count], head_width)
    selected = select(turn_adapter, adapters, feature_width, hidden_width)
    a_qkv, a_guo, a_down, b_qkv, b_gu, b_do = selected
    q_gain_row = head_gain(q_gain)
    k_gain_row = head_gain(k_gain)

    my_tokens = bring(tokens)
    my_grads = bring(cotangent)
    normed, inner, query_raw, key_raw, query_low, key_low, value_low = project_heads(
        my_tokens,
        attn_gain,
        (query_weight, key_weight, value_weight),
        a_qkv,
        b_qkv,
        meta,
        cos_table,
        sin_table,
        q_gain_row,
        k_gain_row,
        head_width,
    )
    keys = gather_half(key_low, groups)
    values = gather_half(value_low, groups)
    attended_low, log_total = attend(
        attn_bias, query_low, meta, keys, values, key_metas, segments, head_width
    )
    layer_rows, grad_residual, grad_attended, grad_a_guo, grad_a_down, grad_b_gu, grad_b_do = (
        feed_forward(
            attended_low,
            my_tokens,
            my_grads,
            ffn_gain,
            (output_weight, gate_weight, up_weight, down_weight),
            (a_guo, a_down, b_gu, b_do),
            meta,
        )
    )
    layer_out = send_back(layer_rows)
    grad_query, grad_keys, grad_values = attend_back(
        attn_bias,
        query_low,
        meta,
        log_total,
        attended_low,
        grad_attended,
        keys,
        values,
        key_metas,
        segments,
        head_width,
    )
    key_terms, value_terms = [grad_keys[0]], [grad_values[0]]
    for shift in range(1, half_devices):
        back_shift = half_devices - shift
        key_terms.append(within_half(grad_keys[shift], back_shift, groups))
        value_terms.append(within_half(grad_values[shift], back_shift, groups))
    grad_rows, grad_a_qkv, grad_b_qkv = project_heads_back(
        grad_query,
        key_terms,
        value_terms,
        query_raw,
        key_raw,
        normed,
        inner,
        my_tokens,
        grad_residual,
        attn_gain,
        (query_weight, key_weight, value_weight),
        a_qkv,
        b_qkv,
        meta,
        cos_table,
        sin_table,
        q_gain_row,
        k_gain_row,
        head_width,
    )
    input_grad = send_back(grad_rows)
    grads = (grad_a_qkv, grad_b_qkv, grad_a_guo, grad_a_down, grad_b_gu, grad_b_do)
    devices = lax.axis_size("dp") * groups
    if spreads_evenly(devices, feature_width, hidden_width, adapters.shape[0], turns):
        settled = settle_spread(grads, turn_adapter, adapters, moment1, moment2, devices)
    else:
        settled = settle_shards(grads, few_choice, adapters, moment1, moment2, groups)
    return (layer_out, input_grad) + settled


def solution(mesh):
    in_specs = (
        P(("dp", "group"), None),
        P(("dp", "group"), None),
        P("dp"),
        P("dp", None),
        P("dp", None),
        P("dp", None),
        P(),
        P(),
        P(),
        P(),
        P(),
        P(),
        P(),
        P(),
        P(),
        P(),
        P(),
        P(),
        P(),
        P(("dp", "group")),
        P(("dp", "group")),
    )
    out_specs = (
        P(("dp", "group"), None),
        P(("dp", "group"), None),
        P(("dp", "group")),
        P(("dp", "group")),
        P(("dp", "group")),
        P(),
    )
    return jax.shard_map(
        per_device, mesh=mesh, in_specs=in_specs, out_specs=out_specs, check_vma=False
    )
```

```python
import functools

import jax
import jax.numpy as jnp
from jax import lax
from jax.experimental import pallas as pl
from jax.experimental.pallas import tpu as pltpu
from jax.sharding import PartitionSpec as P

RANK = 16
ADAPTERS = 8
NORM_EPS = 1e-06
ADAPTER_SCALE = 2.0
ROPE_BASE = 10000.0
MASKED = -1e30
LEARN_RATE = 0.01
BETA_ONE = 0.9
BETA_TWO = 0.999
ADAM_EPS = 1e-08
WEIGHT_DECAY = 0.01
update_count = 10.0
VARIATES = 4
VMEM_LIMIT = 56 * 1024 * 1024
EXACT_PARTS = 3


def contract_last(left, right):
    return lax.dot_general(
        left, right, (((1,), (1,)), ((), ())), preferred_element_type=jnp.float32
    )


def exact_parts(values):
    parts = []
    for _ in range(EXACT_PARTS):
        part = values.astype(jnp.bfloat16).astype(jnp.float32)
        parts.append(part)
        values = values - part
    return parts


def spread_parts(column, parts, first):
    result = jnp.zeros(column.shape, jnp.float32)
    for index, part in enumerate(parts):
        result = jnp.where(column == first + index, part, result)
    return result


def query_extension(bias_ref, head, query_var, query_seg, column, segments):
    same = exact_parts(jnp.full((1, column.shape[1]), bias_ref[0, head], jnp.float32))
    other = exact_parts(jnp.full((1, column.shape[1]), bias_ref[1, head], jnp.float32))
    is_same = (column % VARIATES) == query_var
    result = jnp.zeros(column.shape, jnp.float32)
    for index in range(EXACT_PARTS):
        here = (column // VARIATES) == index
        result = jnp.where(here, jnp.where(is_same, same[index], other[index]), result)
    seg_column = column - EXACT_PARTS * VARIATES
    apart = (seg_column >= 0) & (seg_column < segments) & (seg_column != query_seg)
    return jnp.where(apart, MASKED, result)


def key_extension(key_var, key_seg, column, segments):
    seg_column = column - EXACT_PARTS * VARIATES
    one = (column < EXACT_PARTS * VARIATES) & ((column % VARIATES) == key_var)
    one = one | ((seg_column >= 0) & (seg_column < segments) & (seg_column == key_seg))
    one = one | ((seg_column >= segments) & (seg_column < segments + EXACT_PARTS))
    return jnp.where(one, 1.0, 0.0)


def attend_kernel(key_blocks, segments, width, bias_ref, query_ref, qmeta_ref, *refs):
    key_refs, value_refs, kmeta_refs = (
        refs[:key_blocks],
        refs[key_blocks : 2 * key_blocks],
        refs[2 * key_blocks : 3 * key_blocks],
    )
    out_ref, total_ref = refs[3 * key_blocks :]
    pair = pl.program_id(0)
    rows, lanes = query_ref.shape
    lane = lax.broadcasted_iota(jnp.int32, (rows, lanes), 1)
    column = lane % width
    scaled = query_ref[...].astype(jnp.float32) * width ** (-0.5)
    results = []
    for head in range(lanes // width):
        inside = (lane // width) == head
        extension = query_extension(
            bias_ref,
            pair * (lanes // width) + head,
            qmeta_ref[:, 0:1],
            qmeta_ref[:, 1:2],
            column,
            segments,
        )
        left = jnp.where(inside, scaled, extension).astype(jnp.bfloat16)
        total = jnp.zeros((rows, lanes), jnp.float32)
        for block in range(key_blocks):
            key_side = key_extension(
                kmeta_refs[block][:, 0:1], kmeta_refs[block][:, 1:2], column, segments
            )
            right = jnp.where(inside, key_refs[block][...].astype(jnp.float32), key_side)
            scores = contract_last(left, right.astype(jnp.bfloat16))
            weights = jnp.exp(scores).astype(jnp.bfloat16)
            values = jnp.where(inside, value_refs[block][...].astype(jnp.float32), 1.0)
            total = total + jnp.dot(
                weights, values.astype(jnp.bfloat16), preferred_element_type=jnp.float32
            )
        results.append(total)
    first = (lane // width) == 0
    numerator = jnp.where(first, results[0], results[1])
    crossed = jnp.where(first, results[1], results[0])
    out_ref[...] = (numerator / pltpu.roll(crossed, width, 1)).astype(jnp.bfloat16)
    total_ref[...] = jnp.log(crossed)


def lane_block(rows, lanes, first=0):
    return pl.BlockSpec((rows, lanes), lambda pair: (0, pair + first))


def whole_block(shape):
    return pl.BlockSpec(shape, lambda pair: (0,) * len(shape))


def attend(attn_bias, query_low, query_meta, keys, values, key_metas, segments, width):
    rows, features = query_low.shape
    lanes = 2 * width
    count = len(keys)
    flops = 4 * rows * rows * count * features
    return pl.pallas_call(
        functools.partial(attend_kernel, count, segments, width),
        grid=(features // lanes,),
        in_specs=[
            pl.BlockSpec(memory_space=pltpu.SMEM),
            lane_block(rows, lanes),
            whole_block(query_meta.shape),
        ]
        + [lane_block(rows, lanes)] * (2 * count)
        + [whole_block(query_meta.shape)] * count,
        out_specs=[lane_block(rows, lanes)] * 2,
        out_shape=[
            jax.ShapeDtypeStruct((rows, features), jnp.bfloat16),
            jax.ShapeDtypeStruct((rows, features), jnp.float32),
        ],
        compiler_params=pltpu.CompilerParams(vmem_limit_bytes=VMEM_LIMIT),
        cost_estimate=pl.CostEstimate(
            flops=flops, bytes_accessed=12 * rows * features, transcendentals=0
        ),
        name="attend",
    )(attn_bias, query_low, query_meta, *keys, *values, *key_metas)


def attend_back_kernel(
    first_pair,
    key_blocks,
    segments,
    width,
    bias_ref,
    query_ref,
    qmeta_ref,
    total_ref,
    attended_ref,
    grad_ref,
    *refs,
):
    key_refs, value_refs, kmeta_refs = (
        refs[:key_blocks],
        refs[key_blocks : 2 * key_blocks],
        refs[2 * key_blocks : 3 * key_blocks],
    )
    results = refs[len(refs) - 1 - 2 * key_blocks :]
    grad_query_ref = results[0]
    grad_key_refs = results[1 : key_blocks + 1]
    grad_value_refs = results[key_blocks + 1 :]
    pair = pl.program_id(0) + first_pair
    rows, lanes = query_ref.shape
    lane = lax.broadcasted_iota(jnp.int32, (rows, lanes), 1)
    column = lane % width
    ones_at = EXACT_PARTS * VARIATES + segments
    scaled = query_ref[...].astype(jnp.float32) * width ** (-0.5)
    scaled_low = scaled.astype(jnp.bfloat16)
    grad_low = grad_ref[...]
    grad = grad_low.astype(jnp.float32)
    overlap = grad * attended_ref[...].astype(jnp.float32)
    total_parts = exact_parts(-total_ref[...])
    grad_query_parts = []
    grad_keys = [[] for _ in range(key_blocks)]
    grad_values = [[] for _ in range(key_blocks)]
    for head in range(lanes // width):
        inside = (lane // width) == head
        extension = query_extension(
            bias_ref,
            pair * (lanes // width) + head,
            qmeta_ref[:, 0:1],
            qmeta_ref[:, 1:2],
            column,
            segments,
        ) + spread_parts(column, total_parts, ones_at)
        right = jnp.where(inside, scaled, extension).astype(jnp.bfloat16)
        prob_dot = jnp.sum(jnp.where(inside, overlap, 0.0), axis=1, keepdims=True)
        dot_side = spread_parts(column, exact_parts(-prob_dot), ones_at)
        grad_right = jnp.where(inside, grad, dot_side).astype(jnp.bfloat16)
        turned = jnp.zeros((width, rows), jnp.float32)
        for block in range(key_blocks):
            key_side = key_extension(
                kmeta_refs[block][:, 0:1], kmeta_refs[block][:, 1:2], column, segments
            )
            key = key_refs[block][...]
            left = jnp.where(inside, key.astype(jnp.float32), key_side).astype(jnp.bfloat16)
            prob = jnp.exp(contract_last(left, right))
            value = value_refs[block][...].astype(jnp.float32)
            value_left = jnp.where(inside, value, key_side).astype(jnp.bfloat16)
            grad_score = prob * contract_last(value_left, grad_right)
            grad_score = grad_score.astype(jnp.bfloat16)
            grad_values[block].append(
                jnp.dot(prob.astype(jnp.bfloat16), grad_low, preferred_element_type=jnp.float32)
            )
            grad_keys[block].append(
                jnp.dot(grad_score, scaled_low, preferred_element_type=jnp.float32)
            )
            key_turned = jnp.transpose(key)[head * width : (head + 1) * width]
            turned = turned + jnp.dot(key_turned, grad_score, preferred_element_type=jnp.float32)
        grad_query_parts.append(turned)
    first = (lane // width) == 0
    stacked = jnp.concatenate(grad_query_parts, axis=0) * width ** (-0.5)
    grad_query_ref[...] = jnp.transpose(stacked)
    for block in range(key_blocks):
        grad_key_refs[block][...] = jnp.where(first, *grad_keys[block]).astype(
            grad_key_refs[block].dtype
        )
        grad_value_refs[block][...] = jnp.where(first, *grad_values[block]).astype(
            grad_value_refs[block].dtype
        )


def attend_back(
    attn_bias,
    query_low,
    query_meta,
    log_total,
    attended_low,
    grad_attended,
    keys,
    values,
    key_metas,
    segments,
    width,
    pairs,
    before,
    after,
):
    rows, features = query_low.shape
    lanes = 2 * width
    count = len(keys)
    first, last = pairs
    here = lane_block(rows, lanes, first)
    anywhere = pl.BlockSpec(memory_space=pl.ANY)
    operands = 6 + 3 * count
    aliases = {operands + index: index for index in range(len(before))}
    flops = 10 * rows * rows * count * lanes * (last - first)
    full = jax.ShapeDtypeStruct((rows, features), jnp.float32)
    low = jax.ShapeDtypeStruct((rows, features), jnp.bfloat16)
    results = pl.pallas_call(
        functools.partial(attend_back_kernel, first, count, segments, width),
        grid=(last - first,),
        in_specs=[
            pl.BlockSpec(memory_space=pltpu.SMEM),
            here,
            whole_block(query_meta.shape),
        ]
        + [here] * (3 + 2 * count)
        + [whole_block(query_meta.shape)] * count
        + [anywhere] * (len(before) + len(after)),
        out_specs=[here] * (1 + 2 * count),
        input_output_aliases=aliases,
        out_shape=[full] + ([full] + [low] * (count - 1)) * 2,
        compiler_params=pltpu.CompilerParams(vmem_limit_bytes=VMEM_LIMIT),
        cost_estimate=pl.CostEstimate(
            flops=flops,
            bytes_accessed=24 * rows * lanes * (last - first),
            transcendentals=0,
        ),
        name="attend_back",
    )(
        attn_bias,
        query_low,
        query_meta,
        log_total,
        attended_low,
        grad_attended,
        *keys,
        *values,
        *key_metas,
        *before,
        *after,
    )
    return results


def plan_kernel(
    groups,
    rows,
    member_ref,
    length_ref,
    adapter_ref,
    order_ref,
    variate_ref,
    chosen_ref,
    back_ref,
    turn_ref,
    *refs,
):
    meta_refs, slot_ref = refs[:-1], refs[-1]
    blocks = variate_ref.shape[0]
    half_devices = groups // 2
    half_blocks = blocks // 2
    half_rows = half_blocks * LANES
    swap_rows = rows // 2
    member = member_ref[0]
    my_half, my_place = member // half_devices, member % half_devices
    places = [lax.rem(my_place + shift, half_devices) for shift in range(half_devices)]
    segments = length_ref.shape[1]
    starts = [jnp.int32(0)]
    for segment in range(segments):
        starts.append(starts[-1] + length_ref[0, segment])
    long_start, long_index = jnp.int32(0), jnp.int32(0)
    for segment in range(segments):
        is_half = length_ref[0, segment] == half_rows
        long_start = jnp.where(is_half, starts[segment], long_start)
        long_index = jnp.where(is_half, segment, long_index)

    block = lax.broadcasted_iota(jnp.int32, (blocks, LANES), 0)
    lane = lax.broadcasted_iota(jnp.int32, (blocks, LANES), 1)
    work_block = jnp.zeros((blocks, LANES), jnp.int32)
    for index in range(blocks):
        work_block = jnp.where(block == order_ref[0, index], index, work_block)
    work_row = work_block * LANES + lane
    is_long = (work_row >= long_start) & (work_row < long_start + half_rows)
    in_first = block < half_blocks
    long_count = jnp.sum(jnp.where(is_long & in_first, 1.0, 0.0)).astype(jnp.int32)
    long_half = jnp.where(2 * long_count < half_rows, 1, 0)
    side = jnp.where(in_first, 0, 1)
    target = jnp.where(is_long, long_half, 1 - long_half)
    foreign = target != side
    flags = jnp.where(foreign, 1.0, 0.0)
    moved = jnp.sum(jnp.where(in_first, flags, 0.0)).astype(jnp.int32)
    square_row = lax.broadcasted_iota(jnp.int32, (LANES, LANES), 0)
    square_column = lax.broadcasted_iota(jnp.int32, (LANES, LANES), 1)
    within = dot(flags.astype(jnp.bfloat16), one_hot(square_row < square_column))
    block_sum = jnp.broadcast_to(jnp.sum(flags, axis=1, keepdims=True), (blocks, LANES))
    from_block = lax.broadcasted_iota(jnp.int32, (blocks, blocks), 1)
    to_block = lax.broadcasted_iota(jnp.int32, (blocks, blocks), 0)
    earlier = (from_block < to_block) & ((from_block < half_blocks) == (to_block < half_blocks))
    before = dot(one_hot(earlier), block_sum.astype(jnp.bfloat16))
    foreign_rank = (within + before).astype(jnp.int32)
    kept_rank = (block - side * half_blocks) * LANES + lane - foreign_rank
    kept_slot = side * half_rows + kept_rank
    foreign_slot = (1 - side) * half_rows + rows + foreign_rank
    foreign_slot = foreign_slot - jnp.clip(moved, 0, swap_rows)
    for index in range(1, half_devices):
        start = index * rows - jnp.minimum(moved, index * swap_rows)
        last = (index - 1) * rows - jnp.minimum(moved, (index - 1) * swap_rows)
        kept_slot = jnp.where(kept_rank >= start, kept_slot + rows - (start - last), kept_slot)
        received = jnp.clip(moved - index * swap_rows, 0, swap_rows)
        previous = jnp.clip(moved - (index - 1) * swap_rows, 0, swap_rows)
        foreign_slot = jnp.where(
            foreign_rank >= index * swap_rows,
            foreign_slot + rows - swap_rows + previous - received,
            foreign_slot,
        )
    slot = jnp.where(foreign, foreign_slot, kept_slot)
    slot_ref[...] = slot

    per_device = rows // LANES
    wanted = lax.broadcasted_iota(jnp.int32, (rows + swap_rows, 1), 0)
    wanted = jnp.where(
        wanted < rows,
        my_half * half_rows + my_place * rows + wanted,
        (1 - my_half) * half_rows + my_place * rows + wanted - swap_rows,
    )
    for shift in range(half_devices):
        for index in range(per_device):
            held = my_half * half_blocks + places[shift] * per_device + index
            column = (shift * per_device + index) * LANES
            chosen_ref[:, column : column + LANES] = one_hot(
                wanted == slot_ref[pl.ds(held, 1), :]
            )

    slot_turned = jnp.transpose(slot.astype(jnp.float32))
    turned_lane = lax.broadcasted_iota(jnp.int32, (LANES, blocks), 1)
    first_lane = lax.broadcasted_iota(jnp.int32, (1, LANES), 1)
    for index in range(per_device):
        held = my_half * half_blocks + my_place * per_device + index
        mine = jnp.sum(
            jnp.where(turned_lane == held, slot_turned, 0.0), axis=1, keepdims=True
        ).astype(jnp.int32)
        here = slice(index * LANES, (index + 1) * LANES)
        column = 0
        for first, half, length in ((0, my_half, rows), (swap_rows, 1 - my_half, swap_rows)):
            for shift in range(half_devices):
                for chunk in range(0, length, LANES):
                    number = half * half_rows + places[shift] * rows + first + chunk
                    back_ref[here, column : column + LANES] = one_hot(mine == number + first_lane)
                    column += LANES

    on_long = my_half == long_half
    for turn in range(2):
        chosen_segment = jnp.where(
            on_long, long_index, jnp.where(long_index <= turn, turn + 1, turn)
        )
        adapter = adapter_ref[0, 0]
        for segment in range(1, segments):
            adapter = jnp.where(chosen_segment == segment, adapter_ref[0, segment], adapter)
        turn_ref[turn] = adapter

    variate_turned = jnp.transpose(variate_ref[...].astype(jnp.float32))
    known = []
    for index in range(blocks):
        values = jnp.where(
            square_column == 0,
            work_block[index : index + 1, :].astype(jnp.float32),
            jnp.where(
                square_column == 1,
                square_row.astype(jnp.float32),
                variate_turned[:, index : index + 1],
            ),
        )
        known.append(jnp.where(square_column < 3, values, 0.0).astype(jnp.bfloat16))
    number = lax.broadcasted_iota(jnp.int32, (rows, 1), 0)
    wide_lane = lax.broadcasted_iota(jnp.int32, (rows, LANES), 1)
    for shift in range(half_devices):
        slots = my_half * half_rows + places[shift] * rows + number
        facts = jnp.zeros((rows, LANES), jnp.float32)
        for index in range(blocks):
            facts = facts + dot(one_hot(slots == slot[index : index + 1, :]), known[index])
        facts = facts.astype(jnp.int32)
        row = facts[:, 0:1] * LANES + facts[:, 1:2]
        segment = jnp.zeros((rows, 1), jnp.int32)
        first_row = jnp.zeros((rows, 1), jnp.int32)
        for index in range(1, segments):
            segment = jnp.where(row >= starts[index], index, segment)
            first_row = jnp.where(row >= starts[index], starts[index], first_row)
        turn = jnp.where(segment > long_index, segment - 1, segment)
        turn = jnp.where(on_long, 0, turn)
        meta_refs[shift][...] = jnp.where(
            wide_lane == 0,
            facts[:, 2:3],
            jnp.where(
                wide_lane == 1, segment, jnp.where(wide_lane == 2, turn, row - first_row)
            ),
        )


def plan(groups, rows, member, seq_len, seq_adapter, block_order, variate):
    half_devices = groups // 2
    half_rows = half_devices * rows
    blocks = block_order.shape[1]
    smem = pl.BlockSpec(memory_space=pltpu.SMEM)
    vmem = pl.BlockSpec(memory_space=pltpu.VMEM)
    results = pl.pallas_call(
        functools.partial(plan_kernel, groups, rows),
        in_specs=[smem, smem, smem, smem, vmem],
        out_specs=[vmem, vmem, smem] + [vmem] * half_devices,
        out_shape=[
            jax.ShapeDtypeStruct((rows + rows // 2, half_rows), jnp.bfloat16),
            jax.ShapeDtypeStruct((rows, half_rows + half_rows // 2), jnp.bfloat16),
            jax.ShapeDtypeStruct((2,), jnp.int32),
        ]
        + [jax.ShapeDtypeStruct((rows, LANES), jnp.int32)] * half_devices,
        scratch_shapes=[pltpu.VMEM((blocks, LANES), jnp.int32)],
        compiler_params=pltpu.CompilerParams(vmem_limit_bytes=VMEM_LIMIT),
        cost_estimate=pl.CostEstimate(
            flops=2**31, bytes_accessed=4 * rows * half_rows, transcendentals=0
        ),
        name="plan",
    )(member, seq_len, seq_adapter, block_order, variate.reshape(blocks, LANES))
    return results[0], results[1], results[2], results[3:]


def pick_kernel(chosen_ref, *refs):
    held_refs, out_ref = refs[:-1], refs[-1]
    total = jnp.zeros(out_ref.shape, jnp.float32)
    column = 0
    for ref in held_refs:
        rows = ref.shape[0]
        total = total + dot(chosen_ref[:, column : column + rows], ref[...])
        column += rows
    out_ref[...] = total.astype(out_ref.dtype)


def pick(chosen, first, count, held):
    features = held[0].shape[1]
    tile = features // 2
    return pl.pallas_call(
        pick_kernel,
        grid=(features // tile,),
        in_specs=[pl.BlockSpec((count, chosen.shape[1]), lambda step: (first // count, 0))]
        + [pl.BlockSpec((part.shape[0], tile), lambda step: (0, step)) for part in held],
        out_specs=pl.BlockSpec((count, tile), lambda step: (0, step)),
        out_shape=jax.ShapeDtypeStruct((count, features), jnp.bfloat16),
        compiler_params=pltpu.CompilerParams(vmem_limit_bytes=VMEM_LIMIT),
        cost_estimate=pl.CostEstimate(
            flops=2 * count * chosen.shape[1] * features,
            bytes_accessed=8 * count * features,
            transcendentals=0,
        ),
        name="pick",
    )(chosen, *held)


def within_half(array, shift, groups):
    half = groups // 2
    pairs = [
        (base + (place + shift) % half, base + place)
        for base in (0, half)
        for place in range(half)
    ]
    return lax.ppermute(array, "group", pairs)


def gather_half(array, groups):
    return [array] + [within_half(array, shift, groups) for shift in range(1, groups // 2)]


def to_other_half(array, groups):
    half = groups // 2
    return lax.ppermute(array, "group", [(i, (i + half) % groups) for i in range(groups)])


def scatter_sum(array, axis_sizes):
    for name, size in reversed(axis_sizes):
        outer = array.shape[0] // size
        array = array.reshape((outer, size) + array.shape[1:])
        bit = 1
        while bit < size:
            index = lax.axis_index(name)
            own = (index // bit) % 2
            spread = array.reshape((outer, size // (2 * bit), 2) + array.shape[2:])
            keep = lax.dynamic_index_in_dim(spread, own, 2, keepdims=False)
            send = lax.dynamic_index_in_dim(spread, 1 - own, 2, keepdims=False)
            got = lax.ppermute(send, name, [(i, i ^ bit) for i in range(size)])
            array = (keep.astype(jnp.float32) + got.astype(jnp.float32)).astype(jnp.bfloat16)
            bit *= 2
        array = array.reshape((outer,) + array.shape[2:])
    return array


LANES = 128


def adam(current, first_old, second_old, grad):
    first_moment = BETA_ONE * first_old + (1.0 - BETA_ONE) * grad
    second_moment = BETA_TWO * second_old + (1.0 - BETA_TWO) * grad * grad
    first_fix = first_moment / (1.0 - BETA_ONE**update_count)
    second_fix = second_moment / (1.0 - BETA_TWO**update_count)
    updated = current - LEARN_RATE * (
        first_fix / (jnp.sqrt(second_fix) + ADAM_EPS) + WEIGHT_DECAY * current
    )
    return first_moment, second_moment, updated.astype(jnp.bfloat16)


def settle_shards(grads, few_choice, adapters, moment1, moment2, groups):
    a_qkv, b_qkv, a_guo, a_down, b_gu, b_do = grads
    features, few = a_qkv.shape[0], few_choice.shape[1]
    quarters = a_down.shape[1] // few
    down = jnp.concatenate([a_down[:, i * few : (i + 1) * few] for i in range(quarters)])
    wide = [a_qkv[:, i * few : (i + 1) * few] for i in range(3)]
    wide += [a_guo[:, i * few : (i + 1) * few] for i in (2, 0, 1)] + [down]
    tall = [b_qkv[i * few : (i + 1) * few] for i in range(3)]
    tall += [b_do[2 * few : 3 * few], b_gu[:few], b_gu[few : 2 * few], b_do[:few]]
    pieces = []
    for grad_a, grad_b in zip(wide, tall):
        pieces.append(lax.dot_general(grad_a, few_choice, (((1,), (1,)), ((), ()))).reshape(-1))
        pieces.append(jnp.dot(few_choice, grad_b).reshape(-1))
    axis_sizes = [("dp", lax.axis_size("dp")), ("group", groups)]
    shards = axis_sizes[0][1] * groups
    flat_grads = jnp.concatenate(pieces).astype(jnp.bfloat16).reshape(shards, -1)
    grad_shard = scatter_sum(flat_grads, axis_sizes).reshape(-1).astype(jnp.float32)
    shard_count = grad_shard.shape[0]
    shard_start = lax.axis_index(("dp", "group")) * shard_count
    current = lax.dynamic_slice_in_dim(adapters, shard_start, shard_count).astype(jnp.float32)
    first_moment, second_moment, updated = adam(current, moment1, moment2, grad_shard)
    adapters_new = lax.all_gather(updated, ("dp", "group"), axis=0, tiled=True)
    return grad_shard, first_moment, second_moment, adapters_new


def spreads_evenly(devices, features, hidden, total):
    rows = total // LANES
    chunks = features // LANES
    return (
        ADAPTERS * RANK == LANES
        and devices * chunks == 256
        and chunks == 8
        and hidden == devices * LANES
        and hidden == 4 * features
        and rows % (devices * devices) == 0
        and devices & (devices - 1) == 0
    )


def one_hot(condition):
    return jnp.where(condition, 1.0, 0.0).astype(jnp.bfloat16)


def sum_wide(table_ref, arrived_ref, first, width):
    sources = arrived_ref.shape[0]
    rows = lax.broadcasted_iota(jnp.int32, (LANES, width * LANES), 0)
    columns = lax.broadcasted_iota(jnp.int32, (LANES, width * LANES), 1)
    fits = (rows // (2 * RANK) == columns // LANES) & (rows % RANK == columns % RANK)
    second = (rows // RANK) % 2 == 1
    adapter = jnp.where(fits, (columns % LANES) // RANK, -1)
    total = jnp.zeros((32, width * LANES), jnp.float32)
    for source in range(sources):
        chosen = jnp.where(second, table_ref[source, 1], table_ref[source, 0])
        total = total + jnp.dot(
            arrived_ref[source, first : first + 32, :],
            one_hot(adapter == chosen),
            preferred_element_type=jnp.float32,
        )
    return total


def sum_tall(adapter_row, arrived_ref, first):
    sources = arrived_ref.shape[0]
    depth = sources * 2 * RANK
    rows = lax.broadcasted_iota(jnp.int32, (LANES, depth), 0)
    columns = lax.broadcasted_iota(jnp.int32, (LANES, depth), 1)
    choice = one_hot((rows // RANK == adapter_row) & (rows % RANK == columns % RANK))
    held = arrived_ref[:, first : first + 2 * RANK, :].reshape(depth, LANES)
    return jnp.dot(choice, held, preferred_element_type=jnp.float32)


def sum_square(adapter_row, arrived_ref, first):
    sources = arrived_ref.shape[0]
    depth = sources * 16
    rows = lax.broadcasted_iota(jnp.int32, (64, depth), 0)
    columns = lax.broadcasted_iota(jnp.int32, (64, depth), 1)
    choice = one_hot(
        ((rows % 32) // 4 == adapter_row)
        & (rows % 4 == columns % 4)
        & (rows // 32 == (columns % 16) // 8)
    )
    held = arrived_ref[:, first : first + 16, :].reshape(depth, LANES)
    return jnp.dot(choice, held, preferred_element_type=jnp.float32)


def settle_kernel(
    early, table_ref, tall_ref, square_ref, arrived_ref, param_ref, m1_ref, m2_ref, *refs
):
    grad_ref, new_ref = refs[-2:]
    if early:
        wide = sum_wide(table_ref, arrived_ref, 0, 3)
        last = sum_wide(table_ref, arrived_ref, 32, 4)
        square = sum_square(square_ref[...], arrived_ref, 128)
        parts = [
            wide[:, 2 * LANES :],
            square[32:],
            wide[:, :LANES],
            sum_tall(tall_ref[...], arrived_ref, 64),
            wide[:, LANES : 2 * LANES],
            sum_tall(tall_ref[...], arrived_ref, 96),
        ]
        parts += [last[:, i * LANES : (i + 1) * LANES] for i in range(4)]
        parts.append(square[:32])
    else:
        wide = sum_wide(table_ref, arrived_ref, 0, 3)
        square = [sum_square(square_ref[...], arrived_ref, first) for first in (32, 48)]
        parts = []
        for index in range(3):
            parts.append(wide[:, index * LANES : (index + 1) * LANES])
            parts.append(square[index // 2][(index % 2) * 32 : (index % 2) * 32 + 32])
    row = 0
    skip = param_ref.shape[0] - grad_ref.shape[0] if early else 0
    for part in parts:
        here = slice(row, row + part.shape[0])
        there = slice(skip + row, skip + row + part.shape[0])
        row += part.shape[0]
        low = part.astype(jnp.bfloat16)
        grad_ref[here, :] = low
        new = adam(
            param_ref[there, :].astype(jnp.float32),
            m1_ref[there, :],
            m2_ref[there, :],
            low.astype(jnp.float32),
        )[2]
        for copy in range(new_ref.shape[0]):
            new_ref[copy, here, :] = new


def settle(early, rows, table, arrived, params, first_old, second_old, after):
    sources = table.shape[0]
    tall_row = jnp.repeat(table.reshape(-1), RANK)[None, :]
    square_row = jnp.repeat(jnp.tile(table, (1, 2)).reshape(-1), 4)[None, :]
    return pl.pallas_call(
        functools.partial(settle_kernel, early),
        in_specs=[pl.BlockSpec(memory_space=pltpu.SMEM)]
        + [pl.BlockSpec(memory_space=pltpu.VMEM)] * 6
        + [pl.BlockSpec(memory_space=pl.ANY)] * len(after),
        out_specs=[pl.BlockSpec(memory_space=pltpu.VMEM)] * 2,
        out_shape=[
            jax.ShapeDtypeStruct((rows, LANES), jnp.bfloat16),
            jax.ShapeDtypeStruct((lax.axis_size("dp"), rows, LANES), jnp.bfloat16),
        ],
        compiler_params=pltpu.CompilerParams(vmem_limit_bytes=VMEM_LIMIT),
        cost_estimate=pl.CostEstimate(
            flops=sources * 2**24, bytes_accessed=4 * arrived.size, transcendentals=0
        ),
        name="settle_early" if early else "settle_late",
    )(table, tall_row, square_row, arrived, params, first_old, second_old, *after)


def gather_inner(piece, groups):
    pieces = [piece]
    bit = groups // 2
    while bit:
        pairs = [(i, i ^ bit) for i in range(groups)]
        pieces = pieces + [lax.ppermute(piece, "group", pairs) for piece in pieces]
        bit //= 2
    return pieces


def placing_order(groups, devices, unit):
    member = lax.axis_index("group")
    piece = jnp.arange(groups, dtype=jnp.int32)
    mask = jnp.zeros_like(piece)
    bit = 1
    while bit < groups:
        mask = mask * 2 + (piece // bit) % 2
        bit *= 2
    outer = jnp.arange(devices // groups, dtype=jnp.int32)
    device = (outer[None, :] * groups + (member ^ mask)[:, None]).reshape(-1)
    size = unit * devices
    to_row = lax.broadcasted_iota(jnp.int32, (size, size), 0)
    from_row = jnp.arange(size, dtype=jnp.int32)
    source = (from_row % unit) * devices + jnp.repeat(device, unit)
    return (to_row == source[None, :]).astype(jnp.bfloat16)


def assemble_kernel(count, block, order_ref, *refs):
    piece_refs, out_ref = refs[:count], refs[-1]
    outer = piece_refs[0].shape[0]
    devices = count * outer
    unit = order_ref.shape[0] // devices
    first = pl.program_id(0) * block
    for start in range(0, block, 2 * unit):
        sides = []
        for side in (start, start + unit):
            here = pl.ds(pl.multiple_of(first + side, unit), unit)
            held = jnp.concatenate([ref[:, here, :] for ref in piece_refs], axis=0)
            sides.append(held.reshape(unit * devices, LANES))
        placed = dot(order_ref[...], jnp.concatenate(sides, axis=1)).astype(jnp.bfloat16)
        for index, side in enumerate((start, start + unit)):
            out_ref[side * devices : (side + unit) * devices, :] = placed[
                :, index * LANES : (index + 1) * LANES
            ]


def assemble(order, pieces, total_rows, first, block, before):
    devices = len(pieces) * pieces[0].shape[0]
    rows = pieces[0].shape[1]
    in_specs = [whole_block(order.shape)] + [whole_block(piece.shape) for piece in pieces]
    operands = [order, *pieces]
    aliases = {}
    if before is not None:
        aliases = {len(operands): 0}
        in_specs.append(pl.BlockSpec(memory_space=pl.ANY))
        operands.append(before)
    skip = first // block
    return pl.pallas_call(
        functools.partial(assemble_kernel, len(pieces), block),
        grid=(rows // block,),
        in_specs=in_specs,
        out_specs=pl.BlockSpec((block * devices, LANES), lambda step: (step + skip, 0)),
        out_shape=jax.ShapeDtypeStruct((total_rows, LANES), jnp.bfloat16),
        input_output_aliases=aliases,
        compiler_params=pltpu.CompilerParams(vmem_limit_bytes=VMEM_LIMIT),
        cost_estimate=pl.CostEstimate(
            flops=rows * devices * 2**17, bytes_accessed=rows * devices * 512, transcendentals=0
        ),
        name="assemble",
    )(*operands)


def rope_tables(position, head_width):
    lane = jnp.arange(LANES, dtype=jnp.int32)
    freq_index = (lane % (head_width // 2)).astype(jnp.float32)
    frequency = ROPE_BASE ** (-2.0 * freq_index / head_width)
    angles = position.astype(jnp.float32)[:, None] * frequency[None, :]
    sign = jnp.where(lane % head_width < head_width // 2, -1.0, 1.0)
    return jnp.cos(angles), jnp.sin(angles) * sign[None, :]


def head_gain(gain):
    return jnp.tile(gain.astype(jnp.float32), LANES // gain.shape[0])[None, :]


def select_kernel(features, hidden, turn_ref, flat_ref, *out_refs):
    a_qkv_ref, a_guo_ref, a_down_ref, b_qkv_ref, b_gu_ref, b_do_ref = out_refs
    few = 2 * RANK
    rows = lax.broadcasted_iota(jnp.int32, (LANES, LANES), 0)
    columns = lax.broadcasted_iota(jnp.int32, (LANES, LANES), 1)
    chosen = jnp.where((columns // RANK) % 2 == 1, turn_ref[1], turn_ref[0])
    fits = (rows // RANK == chosen) & (rows % RANK == columns % RANK)
    start = {}
    row = 0
    for name, rows_in, rows_out in (
        ("q", features, features),
        ("k", features, features),
        ("v", features, features),
        ("o", features, features),
        ("g", features, hidden),
        ("u", features, hidden),
        ("d", hidden, features),
    ):
        start[name] = (row, row + rows_in)
        row += rows_in + rows_out

    def wide(names, length):
        total = jnp.zeros((length, LANES), jnp.float32)
        for place, name in enumerate(names):
            first = start[name][0]
            total = total + jnp.dot(
                flat_ref[first : first + length, :],
                one_hot(fits & (columns // few == place)),
                preferred_element_type=jnp.float32,
            )
        return total.astype(jnp.bfloat16)

    a_qkv_ref[...] = wide("qkv", features)
    a_guo_ref[...] = wide("guo", features)
    for first in range(0, hidden, features):
        a_down_ref[first : first + features, :] = jnp.dot(
            flat_ref[start["d"][0] + first : start["d"][0] + first + features, :],
            one_hot(fits & (columns // few == 0)),
            preferred_element_type=jnp.float32,
        ).astype(jnp.bfloat16)

    def tall(name, length, out_ref, place):
        chunks = length // LANES
        size = RANK * chunks
        to_row = lax.broadcasted_iota(jnp.int32, (size, size), 0)
        from_row = lax.broadcasted_iota(jnp.int32, (size, size), 1)
        turned = one_hot(
            (to_row // RANK == from_row % chunks) & (to_row % RANK == from_row // chunks)
        )
        for turn in range(2):
            first = start[name][1] + pl.multiple_of(turn_ref[turn] * size, LANES)
            block = jnp.dot(
                turned, flat_ref[pl.ds(first, size), :], preferred_element_type=jnp.float32
            ).astype(jnp.bfloat16)
            here = place * few + turn * RANK
            for chunk in range(chunks):
                out_ref[here : here + RANK, chunk * LANES : (chunk + 1) * LANES] = block[
                    chunk * RANK : (chunk + 1) * RANK
                ]

    for out_ref, names in ((b_qkv_ref, "qkv"), (b_gu_ref, "gu"), (b_do_ref, "d.o")):
        out_ref[...] = jnp.zeros(out_ref.shape, out_ref.dtype)
        for place, name in enumerate(names):
            if name != ".":
                tall(name, out_ref.shape[1], out_ref, place)


def select(turn_adapter, adapters, features, hidden):
    shapes = [(features, LANES), (features, LANES), (hidden, LANES)]
    shapes += [(LANES, features), (LANES, hidden), (LANES, features)]
    return pl.pallas_call(
        functools.partial(select_kernel, features, hidden),
        in_specs=[
            pl.BlockSpec(memory_space=pltpu.SMEM),
            pl.BlockSpec(memory_space=pltpu.VMEM),
        ],
        out_specs=[pl.BlockSpec(memory_space=pltpu.VMEM)] * 6,
        out_shape=[jax.ShapeDtypeStruct(shape, jnp.bfloat16) for shape in shapes],
        compiler_params=pltpu.CompilerParams(vmem_limit_bytes=VMEM_LIMIT),
        cost_estimate=pl.CostEstimate(
            flops=2**31, bytes_accessed=4 * adapters.shape[0], transcendentals=0
        ),
        name="select",
    )(turn_adapter, adapters.reshape(-1, LANES))


def dot(left, right):
    return jnp.dot(left, right, preferred_element_type=jnp.float32)


def turn_mask(meta_ref):
    rows = meta_ref.shape[0]
    lane = lax.broadcasted_iota(jnp.int32, (rows, LANES), 1)
    mask = jnp.where((lane // RANK) % 2 == meta_ref[:, 2:3], 1.0, 0.0)
    return mask, lane // (2 * RANK)


def row_norm(values):
    return lax.rsqrt(jnp.mean(values * values, axis=1, keepdims=True) + NORM_EPS)


def row_norm_back(values, gain, grad):
    scale = row_norm(values)
    unit = values * scale
    grad = grad * gain
    return scale * (grad - unit * jnp.mean(grad * unit, axis=1, keepdims=True))


def head_mean(values, width):
    lanes = values.shape[1]
    rows = lax.broadcasted_iota(jnp.int32, (lanes, lanes), 0)
    columns = lax.broadcasted_iota(jnp.int32, (lanes, lanes), 1)
    ones = one_hot(rows // width == columns // width)
    high = values.astype(jnp.bfloat16)
    low = (values - high.astype(jnp.float32)).astype(jnp.bfloat16)
    return (dot(high, ones) + dot(low, ones)) * (1.0 / width)


def swap_halves(values, width):
    lanes = values.shape[1]
    lane = lax.broadcasted_iota(jnp.int32, values.shape, 1)
    ahead = pltpu.roll(values, lanes - width // 2, 1)
    behind = pltpu.roll(values, width // 2, 1)
    return jnp.where(lane % width < width // 2, ahead, behind)


def widen(table, lanes):
    return jnp.concatenate([table] * (lanes // table.shape[1]), axis=1)


def joined(kept_ref, arrived_ref):
    first = kept_ref.shape[0] - arrived_ref.shape[0]
    kept = kept_ref[...]
    return jnp.concatenate([kept[:first], kept[first:] + arrived_ref[...]], axis=0)


def turned_heads(raw, gain_ref, cosine, sine, width):
    unit = raw * lax.rsqrt(head_mean(raw * raw, width) + NORM_EPS)
    unit = unit * widen(gain_ref[...], raw.shape[1])
    return (unit * cosine + swap_halves(unit, width) * sine).astype(jnp.bfloat16)


def project_own(normed, inner, place, index, weight_ref, b_ref):
    own = jnp.where(place == index, inner, 0.0).astype(jnp.bfloat16)
    return dot(normed, weight_ref[...]) + ADAPTER_SCALE * dot(own, b_ref[...])


def project_key_value_kernel(
    width,
    kept_ref,
    arrived_ref,
    gain_ref,
    wk_ref,
    wv_ref,
    a_ref,
    b_ref,
    meta_ref,
    cos_ref,
    sin_ref,
    k_gain_ref,
    x_ref,
    normed_ref,
    inner_ref,
    raw_ref,
    k_ref,
    v_ref,
):
    mask, place = turn_mask(meta_ref)

    @pl.when(pl.program_id(0) == 0)
    def _():
        rows = joined(kept_ref, arrived_ref)
        x_ref[...] = rows
        values = rows.astype(jnp.float32)
        normed = (values * row_norm(values) * gain_ref[...].astype(jnp.float32)).astype(
            jnp.bfloat16
        )
        normed_ref[...] = normed
        inner_ref[...] = (dot(normed, a_ref[...]) * mask).astype(jnp.bfloat16)

    normed = normed_ref[...]
    inner = inner_ref[...].astype(jnp.float32)
    lanes = wk_ref.shape[1]
    cosine, sine = widen(cos_ref[...], lanes), widen(sin_ref[...], lanes)
    key = project_own(normed, inner, place, 1, wk_ref, b_ref)
    raw_ref[...] = key
    k_ref[...] = turned_heads(key, k_gain_ref, cosine, sine, width)
    v_ref[...] = project_own(normed, inner, place, 2, wv_ref, b_ref).astype(jnp.bfloat16)


def project_query_kernel(
    width, normed_ref, inner_ref, wq_ref, b_ref, cos_ref, sin_ref, q_gain_ref, raw_ref, q_ref
):
    lanes = wq_ref.shape[1]
    place = lax.broadcasted_iota(jnp.int32, inner_ref.shape, 1) // (2 * RANK)
    cosine, sine = widen(cos_ref[...], lanes), widen(sin_ref[...], lanes)
    inner = inner_ref[...].astype(jnp.float32)
    query = project_own(normed_ref[...], inner, place, 0, wq_ref, b_ref)
    raw_ref[...] = query
    q_ref[...] = turned_heads(query, q_gain_ref, cosine, sine, width)


def project_heads(
    kept, arrived, gain, weights, a_qkv, b_qkv, meta, cos_table, sin_table, q_gain, k_gain, width
):
    rows, features = kept.shape
    tile = 256
    grid = (features // tile,)

    def tiled(height):
        return pl.BlockSpec((height, tile), lambda step: (0, step))

    def shape(dtype):
        return jax.ShapeDtypeStruct((rows, features), dtype)

    full, few = whole_block((rows, features)), whole_block((rows, LANES))
    low, high = shape(jnp.bfloat16), shape(jnp.float32)
    x, normed, inner, key_raw, key, value = pl.pallas_call(
        functools.partial(project_key_value_kernel, width),
        grid=grid,
        in_specs=[full, whole_block(arrived.shape), whole_block((1, features))]
        + [tiled(features)] * 2
        + [whole_block((features, LANES)), tiled(LANES), few, few, few]
        + [whole_block((1, LANES))],
        out_specs=[full, full, few] + [tiled(rows)] * 3,
        out_shape=[
            low,
            low,
            jax.ShapeDtypeStruct((rows, LANES), jnp.bfloat16),
            high,
            low,
            low,
        ],
        compiler_params=pltpu.CompilerParams(vmem_limit_bytes=VMEM_LIMIT),
        cost_estimate=pl.CostEstimate(
            flops=6 * rows * features * features,
            bytes_accessed=4 * features * features + 14 * rows * features,
            transcendentals=0,
        ),
        name="project_key_value",
    )(
        kept,
        arrived,
        gain[None, :],
        *weights[1:],
        a_qkv,
        b_qkv,
        meta,
        cos_table,
        sin_table,
        k_gain,
    )
    query_raw, query = pl.pallas_call(
        functools.partial(project_query_kernel, width),
        grid=grid,
        in_specs=[full, few, tiled(features), tiled(LANES), few, few, whole_block((1, LANES))],
        out_specs=[tiled(rows)] * 2,
        out_shape=[high, low],
        compiler_params=pltpu.CompilerParams(vmem_limit_bytes=VMEM_LIMIT),
        cost_estimate=pl.CostEstimate(
            flops=3 * rows * features * features,
            bytes_accessed=2 * features * features + 8 * rows * features,
            transcendentals=0,
        ),
        name="project_query",
    )(normed, inner, weights[0], b_qkv, cos_table, sin_table, q_gain)
    return x, normed, inner, query_raw, key_raw, query, key, value


def project_heads_back_kernel(
    count,
    width,
    devices,
    gq_ref,
    *refs,
):
    gk_refs, gv_refs, refs = refs[:count], refs[count : 2 * count], refs[2 * count :]
    (
        q_raw_ref,
        k_raw_ref,
        normed_ref,
        inner_ref,
        x_ref,
        residual_ref,
        gain_ref,
        wq_ref,
        wk_ref,
        wv_ref,
        a_ref,
        b_ref,
        meta_ref,
        cos_ref,
        sin_ref,
        q_gain_ref,
        k_gain_ref,
    ) = refs[:17]
    if devices:
        _, out_ref, spread_ref, total_ref, few_ref, tall_ref, square_ref = refs[17:]
    else:
        out_ref, grad_a_ref, grad_b_ref, total_ref, few_ref, tall_ref, square_ref = refs[17:]
    step = pl.program_id(0)
    lanes = wq_ref.shape[1]
    mask, place = turn_mask(meta_ref)
    cosine, sine = widen(cos_ref[...], lanes), widen(sin_ref[...], lanes)

    def turned_back(grad, raw, head_gain_ref):
        grad = grad * cosine - swap_halves(grad, width) * sine
        scale = lax.rsqrt(head_mean(raw * raw, width) + NORM_EPS)
        unit = raw * scale
        grad = grad * widen(head_gain_ref[...], lanes)
        return (scale * (grad - unit * head_mean(grad * unit, width))).astype(jnp.bfloat16)

    def summed(term_refs):
        total = term_refs[0][...].astype(jnp.float32)
        for ref in term_refs[1:]:
            total = total + ref[...].astype(jnp.float32)
        return total

    @pl.when(step == 0)
    def _():
        total_ref[...] = jnp.zeros(total_ref.shape, jnp.float32)
        few_ref[...] = jnp.zeros(few_ref.shape, jnp.float32)

    inner_turned = jnp.transpose(inner_ref[...].astype(jnp.float32) * ADAPTER_SCALE).astype(
        jnp.bfloat16
    )
    errors = [
        turned_back(gq_ref[...], q_raw_ref[...], q_gain_ref),
        turned_back(summed(gk_refs), k_raw_ref[...], k_gain_ref),
        summed(gv_refs).astype(jnp.bfloat16),
    ]
    total = total_ref[...]
    few = few_ref[...]
    wide = 2 * RANK
    for index, (error, weight_ref) in enumerate(zip(errors, (wq_ref, wk_ref, wv_ref))):
        total = total + contract_last(error, weight_ref[...])
        few = few + jnp.where(place == index, contract_last(error, b_ref[...]), 0.0)
        here = slice(index * wide, (index + 1) * wide)
        grad_b = dot(inner_turned[here], error)
        for part in range(lanes // LANES):
            square_ref[part, here, :] = grad_b[:, part * LANES : (part + 1) * LANES]
    square_ref[:, 3 * wide :, :] = jnp.zeros(
        (lanes // LANES, LANES - 3 * wide, LANES), jnp.float32
    )
    if devices:
        chunks = normed_ref.shape[1] // LANES
        for index in range(lanes // LANES):
            for first, starts in ((wide, (0, wide)), (wide + RANK, (2 * wide, 3 * wide))):
                spread_square_to(
                    spread_ref,
                    first,
                    square_ref,
                    starts,
                    step * (lanes // LANES) + index,
                    chunks,
                    index,
                )
    else:
        for part in range(lanes // LANES):
            grad_b_ref[:, part * LANES : (part + 1) * LANES] = square_ref[part].astype(
                jnp.bfloat16
            )
    total_ref[...] = total
    few_ref[...] = few

    @pl.when(step == pl.num_programs(0) - 1)
    def _():
        low = (ADAPTER_SCALE * few_ref[...] * mask).astype(jnp.bfloat16)
        low_turned = jnp.transpose(low.astype(jnp.float32)).astype(jnp.bfloat16)
        tall_ref[...] = jnp.transpose(dot(low_turned, normed_ref[...]))
        if devices:
            spread_wide_to(spread_ref, 0, tall_ref)
        else:
            grad_a_ref[...] = tall_ref[...].astype(jnp.bfloat16)
        grad = total_ref[...] + contract_last(low, a_ref[...])
        out_ref[...] = (
            residual_ref[...]
            + row_norm_back(
                x_ref[...].astype(jnp.float32), gain_ref[...].astype(jnp.float32), grad
            )
        ).astype(jnp.bfloat16)


def project_heads_back(
    devices,
    after,
    grad_query,
    key_terms,
    value_terms,
    query_raw,
    key_raw,
    normed,
    inner,
    rows_in,
    grad_residual,
    gain,
    weights,
    a_qkv,
    b_qkv,
    meta,
    cos_table,
    sin_table,
    q_gain,
    k_gain,
    width,
):
    rows, features = rows_in.shape
    count = len(key_terms)
    tile = 256

    def tiled(height):
        return pl.BlockSpec((height, tile), lambda step: (0, step))

    full = whole_block((rows, features))
    if devices:
        spread = (devices, 4 * RANK, LANES)
        grad_specs = [whole_block(spread)]
        grad_shapes = [jax.ShapeDtypeStruct(spread, jnp.bfloat16)]
    else:
        grad_specs = [whole_block((features, LANES)), tiled(LANES)]
        grad_shapes = [
            jax.ShapeDtypeStruct((features, LANES), jnp.bfloat16),
            jax.ShapeDtypeStruct((LANES, features), jnp.bfloat16),
        ]
    return pl.pallas_call(
        functools.partial(project_heads_back_kernel, count, width, devices),
        grid=(features // tile,),
        in_specs=[tiled(rows)] * (3 + 2 * count)
        + [full, whole_block((rows, LANES)), full, full, whole_block((1, features))]
        + [tiled(features)] * 3
        + [whole_block((features, LANES)), tiled(LANES), whole_block(meta.shape)]
        + [whole_block((rows, LANES))] * 2
        + [whole_block((1, LANES))] * 2
        + [pl.BlockSpec(memory_space=pl.ANY)] * len(after),
        out_specs=[full, *grad_specs],
        out_shape=[jax.ShapeDtypeStruct((rows, features), jnp.bfloat16), *grad_shapes],
        scratch_shapes=[
            pltpu.VMEM((rows, features), jnp.float32),
            pltpu.VMEM((rows, LANES), jnp.float32),
            pltpu.VMEM((features, LANES), jnp.float32),
            pltpu.VMEM((tile // LANES, LANES, LANES), jnp.float32),
        ],
        compiler_params=pltpu.CompilerParams(vmem_limit_bytes=VMEM_LIMIT),
        cost_estimate=pl.CostEstimate(
            flops=8 * rows * features * features,
            bytes_accessed=6 * features * features + 30 * rows * features,
            transcendentals=0,
        ),
        name="project_heads_back",
    )(
        grad_query,
        *key_terms,
        *value_terms,
        query_raw,
        key_raw,
        normed,
        inner,
        rows_in,
        grad_residual,
        gain[None, :],
        *weights,
        a_qkv,
        b_qkv,
        meta,
        cos_table,
        sin_table,
        q_gain,
        k_gain,
        *after,
    )


def spread_wide_to(spread_ref, first, held_ref):
    devices = spread_ref.shape[0]
    count = held_ref.shape[0] // devices
    for device in range(devices):
        spread_ref[device, first : first + count, :] = held_ref[
            pl.ds(device, count, stride=devices), :
        ].astype(jnp.bfloat16)


def spread_square_to(spread_ref, first, held_ref, starts, chunk, chunks, index):
    classes = spread_ref.shape[0] // chunks
    count = 2 * RANK // classes
    for part in range(classes):
        rows = [
            held_ref[index, pl.ds(start + part, count, stride=classes), :]
            for start in starts
        ]
        spread_ref[part * chunks + chunk, first : first + 2 * count, :] = jnp.concatenate(
            rows, axis=0
        ).astype(jnp.bfloat16)


def feed_forward_kernel(
    devices,
    turn_ref,
    att_ref,
    x_ref,
    kept_ref,
    arrived_ref,
    gain_ref,
    wo_ref,
    wg_ref,
    wu_ref,
    wd_ref,
    a_guo_ref,
    a_down_ref,
    b_gu_ref,
    b_do_ref,
    meta_ref,
    out_ref,
    grad_res_ref,
    grad_att_ref,
    *refs,
):
    if devices:
        spread_ref, refs = refs[0], refs[1:]
    else:
        (grad_a_ref, grad_ad_ref, grad_bgu_ref, grad_bdo_ref), refs = refs[:4], refs[4:]
    (
        res_ref,
        hidden_ref,
        inner_ref,
        inner_turned_ref,
        sum_ref,
        grad_hidden_ref,
        inner_down_ref,
        few_ref,
        few_down_ref,
        few_down_turned_ref,
        down_ref,
        tall_ref,
        square_ref,
        e_ref,
    ) = refs
    step = pl.program_id(0)
    mask, place = turn_mask(meta_ref)
    tile = wg_ref.shape[1]
    features = wo_ref.shape[0]
    wide = 2 * RANK

    def only(values, index):
        return jnp.where(place == index, values, 0.0).astype(jnp.bfloat16)

    def turn(values):
        return jnp.transpose(values.astype(jnp.float32)).astype(jnp.bfloat16)

    @pl.when(step == 0)
    def _():
        e_ref[...] = joined(kept_ref, arrived_ref)
        att = att_ref[...]
        inner_out = dot(att, a_guo_ref[...]) * mask
        res = (
            x_ref[...].astype(jnp.float32)
            + dot(att, wo_ref[...])
            + ADAPTER_SCALE * dot(only(inner_out, 2), b_do_ref[...])
        )
        res_ref[...] = res
        hidden = (res * row_norm(res) * gain_ref[...].astype(jnp.float32)).astype(jnp.bfloat16)
        hidden_ref[...] = hidden
        inner = dot(hidden, a_guo_ref[...]) * mask
        inner = jnp.where(place == 2, inner_out, inner).astype(jnp.bfloat16)
        inner_ref[...] = inner
        inner_turned_ref[...] = turn(inner.astype(jnp.float32) * ADAPTER_SCALE)
        few_down = only(ADAPTER_SCALE * contract_last(e_ref[...], b_do_ref[...]) * mask, 0)
        few_down_ref[...] = few_down
        few_down_turned_ref[...] = turn(few_down)[:wide]
        sum_ref[...] = jnp.zeros(sum_ref.shape, jnp.float32)
        grad_hidden_ref[...] = jnp.zeros(grad_hidden_ref.shape, jnp.float32)
        inner_down_ref[...] = jnp.zeros(inner_down_ref.shape, jnp.float32)
        few_ref[...] = jnp.zeros(few_ref.shape, jnp.float32)

    hidden = hidden_ref[...]
    inner = inner_ref[...].astype(jnp.float32)
    gate_weight, up_weight, down_weight = wg_ref[...], wu_ref[...], wd_ref[...]
    b_tile = b_gu_ref[...]
    gate = dot(hidden, gate_weight) + ADAPTER_SCALE * dot(only(inner, 0), b_tile)
    up = dot(hidden, up_weight) + ADAPTER_SCALE * dot(only(inner, 1), b_tile)
    grad_act = contract_last(e_ref[...], down_weight) + contract_last(
        few_down_ref[...], a_down_ref[...]
    )
    sigmoid = 1.0 / (1.0 + jnp.exp(-gate))
    silu = gate * sigmoid
    act = (silu * up).astype(jnp.bfloat16)
    grad_up = (grad_act * silu).astype(jnp.bfloat16)
    grad_gate = (grad_act * up * (sigmoid * (1.0 + gate * (1.0 - sigmoid)))).astype(jnp.bfloat16)
    sum_ref[...] += dot(act, down_weight)
    inner_down_ref[...] += dot(act, a_down_ref[...])
    grad_hidden_ref[...] += contract_last(grad_gate, gate_weight) + contract_last(
        grad_up, up_weight
    )
    few_ref[...] += jnp.where(
        place == 0, contract_last(grad_gate, b_tile), contract_last(grad_up, b_tile)
    )
    grad_b_gate = dot(inner_turned_ref[:wide, :], grad_gate).astype(jnp.bfloat16)
    grad_b_up = dot(inner_turned_ref[wide : 2 * wide, :], grad_up).astype(jnp.bfloat16)
    if devices:
        for index in range(tile // LANES):
            device = step * (tile // LANES) + index
            chunk = slice(index * LANES, (index + 1) * LANES)
            spread_ref[device, 2 * wide : 3 * wide, :] = grad_b_gate[:, chunk]
            spread_ref[device, 3 * wide : 4 * wide, :] = grad_b_up[:, chunk]
    else:
        grad_bgu_ref[:wide, :] = grad_b_gate
        grad_bgu_ref[wide:, :] = grad_b_up
    per_quarter = features // tile
    down_ref[
        pl.ds(pl.multiple_of((step // per_quarter) * wide, wide), wide),
        pl.ds(pl.multiple_of((step % per_quarter) * tile, tile), tile),
    ] = dot(few_down_turned_ref[...], act)

    @pl.when(step == pl.num_programs(0) - 1)
    def _():
        grads_out = e_ref[...]
        inner_down = only(inner_down_ref[...] * mask, 0)
        res = res_ref[...]
        out_ref[...] = (
            res + sum_ref[...] + ADAPTER_SCALE * dot(inner_down, b_do_ref[...])
        ).astype(jnp.bfloat16)
        few = jnp.where(place < 2, ADAPTER_SCALE * few_ref[...] * mask, 0.0).astype(jnp.bfloat16)
        grad_hidden = grad_hidden_ref[...] + contract_last(few, a_guo_ref[...])
        grad_res = grads_out.astype(jnp.float32) + row_norm_back(
            res, gain_ref[...].astype(jnp.float32), grad_hidden
        )
        grad_res_ref[...] = grad_res
        low = grad_res.astype(jnp.bfloat16)
        few_out = only(ADAPTER_SCALE * contract_last(low, b_do_ref[...]) * mask, 2)
        grad_att_ref[...] = (
            contract_last(low, wo_ref[...]) + contract_last(few_out, a_guo_ref[...])
        ).astype(jnp.bfloat16)
        grad_a = dot(turn(few), hidden_ref[...]) + dot(turn(few_out), att_ref[...])
        inner_out = only(inner_ref[...].astype(jnp.float32), 2)
        grad_b = ADAPTER_SCALE * (
            dot(turn(inner_down), grads_out) + dot(turn(inner_out), low)
        )
        if devices:
            lane = lax.broadcasted_iota(jnp.int32, (features, LANES), 1)
            told = jnp.where(
                lane == 3 * wide, turn_ref[0], jnp.where(lane == 3 * wide + 1, turn_ref[1], 0)
            )
            tall_ref[...] = jnp.transpose(grad_a) + told.astype(jnp.float32)
            spread_wide_to(spread_ref, 0, tall_ref)
            tall_ref[...] = jnp.transpose(down_ref[...])
            spread_wide_to(spread_ref, wide, tall_ref)
            chunks = features // LANES
            for chunk in range(chunks):
                square_ref[chunk] = grad_b[:, chunk * LANES : (chunk + 1) * LANES]
                spread_square_to(
                    spread_ref, 4 * wide, square_ref, (0, 2 * wide), chunk, chunks, chunk
                )
        else:
            grad_a_ref[...] = jnp.transpose(grad_a).astype(jnp.bfloat16)
            grad_ad_ref[...] = jnp.transpose(down_ref[...]).astype(jnp.bfloat16)
            grad_bdo_ref[...] = grad_b.astype(jnp.bfloat16)


def feed_forward(
    devices, turn_adapter, attended, rows_in, kept, arrived, gain, weights, selected, meta
):
    rows, features = rows_in.shape
    hidden = weights[1].shape[1]
    tile = 512
    full = whole_block((rows, features))
    square = whole_block((features, features))
    column = pl.BlockSpec((features, tile), lambda step: (0, step))

    def shape(height, length, dtype):
        return jax.ShapeDtypeStruct((height, length), dtype)

    if devices:
        spread = (devices, 9 * RANK, LANES)
        grad_specs = [whole_block(spread)]
        grad_shapes = [jax.ShapeDtypeStruct(spread, jnp.bfloat16)]
    else:
        grad_specs = [
            whole_block((features, LANES)),
            whole_block((features, LANES)),
            pl.BlockSpec((4 * RANK, tile), lambda step: (0, step)),
            whole_block((LANES, features)),
        ]
        grad_shapes = [
            shape(features, LANES, jnp.bfloat16),
            shape(features, LANES, jnp.bfloat16),
            shape(4 * RANK, hidden, jnp.bfloat16),
            shape(LANES, features, jnp.bfloat16),
        ]
    return pl.pallas_call(
        functools.partial(feed_forward_kernel, devices),
        grid=(hidden // tile,),
        in_specs=[
            pl.BlockSpec(memory_space=pltpu.SMEM),
            full,
            full,
            full,
            whole_block(arrived.shape),
            whole_block((1, features)),
            square,
            column,
            column,
            pl.BlockSpec((tile, features), lambda step: (step, 0)),
            whole_block((features, LANES)),
            pl.BlockSpec((tile, LANES), lambda step: (step, 0)),
            pl.BlockSpec((LANES, tile), lambda step: (0, step)),
            whole_block((LANES, features)),
            whole_block(meta.shape),
        ],
        out_specs=[
            full,
            full,
            full,
            *grad_specs,
        ],
        out_shape=[
            shape(rows, features, jnp.bfloat16),
            shape(rows, features, jnp.float32),
            shape(rows, features, jnp.bfloat16),
            *grad_shapes,
        ],
        scratch_shapes=[
            pltpu.VMEM((rows, features), jnp.float32),
            pltpu.VMEM((rows, features), jnp.bfloat16),
            pltpu.VMEM((rows, LANES), jnp.bfloat16),
            pltpu.VMEM((LANES, rows), jnp.bfloat16),
            pltpu.VMEM((rows, features), jnp.float32),
            pltpu.VMEM((rows, features), jnp.float32),
            pltpu.VMEM((rows, LANES), jnp.float32),
            pltpu.VMEM((rows, LANES), jnp.float32),
            pltpu.VMEM((rows, LANES), jnp.bfloat16),
            pltpu.VMEM((2 * RANK, rows), jnp.bfloat16),
            pltpu.VMEM((LANES, features), jnp.float32),
            pltpu.VMEM((features, LANES), jnp.float32),
            pltpu.VMEM((features // LANES, LANES, LANES), jnp.float32),
            pltpu.VMEM((rows, features), jnp.bfloat16),
        ],
        compiler_params=pltpu.CompilerParams(vmem_limit_bytes=VMEM_LIMIT),
        cost_estimate=pl.CostEstimate(
            flops=14 * rows * features * hidden,
            bytes_accessed=8 * features * hidden + 16 * rows * features,
            transcendentals=0,
        ),
        name="feed_forward",
    )(
        turn_adapter, attended, rows_in, kept, arrived, gain[None, :], *weights, *selected, meta
    )


def spread_state(adapters, moment1, moment2, devices):
    axes = ("dp", "group")
    total_rows = adapters.shape[0] // LANES
    spread_rows = total_rows // devices
    own_rows = spread_rows // devices
    moments = jnp.concatenate(
        [
            jnp.transpose(flat.reshape(own_rows, devices, LANES), (1, 0, 2))
            for flat in (moment1, moment2)
        ],
        axis=1,
    )
    moments = lax.all_to_all(moments, axes, 0, 0, tiled=True)
    first_old = moments[:, :own_rows].reshape(spread_rows, LANES)
    second_old = moments[:, own_rows:].reshape(spread_rows, LANES)
    params = lax.dynamic_index_in_dim(
        adapters.reshape(spread_rows, devices, LANES), lax.axis_index(axes), 1, keepdims=False
    )
    return params, first_old, second_old


def settle_owned(late_grad, early_grad, moment1, moment2, devices):
    grads = jnp.concatenate([late_grad, early_grad])
    grads = grads.reshape(devices, grads.shape[0] // devices, LANES)
    grads = lax.all_to_all(grads, ("dp", "group"), 0, 0, tiled=True)
    grad_shard = jnp.transpose(grads, (1, 0, 2)).reshape(-1).astype(jnp.float32)
    current = jnp.zeros((), jnp.float32)
    first_moment, second_moment, _ = adam(current, moment1, moment2, grad_shard)
    return grad_shard, first_moment, second_moment


def per_device(
    tokens,
    cotangent,
    variate,
    seq_len,
    seq_adapter,
    block_order,
    attn_gain,
    ffn_gain,
    q_gain,
    k_gain,
    attn_bias,
    query_weight,
    key_weight,
    value_weight,
    output_weight,
    gate_weight,
    up_weight,
    down_weight,
    adapters,
    moment1,
    moment2,
):
    groups = lax.axis_size("group")
    member = lax.axis_index("group")
    row_count, feature_width = tokens.shape
    hidden_width = gate_weight.shape[1]
    head_width = q_gain.shape[0]
    half_devices = groups // 2
    segments = seq_len.shape[1]
    chosen, back, turn_adapter, key_metas = plan(
        groups, row_count, member[None], seq_len, seq_adapter, block_order, variate
    )
    meta = key_metas[0]
    cos_table, sin_table = rope_tables(meta[:, 3], head_width)
    selected = select(turn_adapter, adapters, feature_width, hidden_width)
    a_qkv, a_guo, a_down, b_qkv, b_gu, b_do = selected
    q_gain_row = head_gain(q_gain)
    k_gain_row = head_gain(k_gain)

    def bring(rows):
        held = gather_half(rows, groups)
        sent = pick(chosen, row_count, row_count // 2, held)
        arrived = to_other_half(sent, groups)
        return pick(chosen, 0, row_count, held), arrived

    def send_back(rows):
        returned = to_other_half(rows[row_count // 2 :], groups)
        held = gather_half(rows, groups) + gather_half(returned, groups)
        return pick(back, 0, row_count, held)

    kept_tokens, arrived_tokens = bring(tokens)
    kept_grads, arrived_grads = bring(cotangent)
    my_tokens, normed, inner, query_raw, key_raw, query_low, key_low, value_low = project_heads(
        kept_tokens,
        arrived_tokens,
        attn_gain,
        (query_weight, key_weight, value_weight),
        a_qkv,
        b_qkv,
        meta,
        cos_table,
        sin_table,
        q_gain_row,
        k_gain_row,
        head_width,
    )
    keys = gather_half(key_low, groups)
    values = gather_half(value_low, groups)
    attended_low, log_total = attend(
        attn_bias, query_low, meta, keys, values, key_metas, segments, head_width
    )
    devices = lax.axis_size("dp") * groups
    even = spreads_evenly(devices, feature_width, hidden_width, adapters.shape[0])
    spread = devices if even else 0
    layer_rows, grad_residual, grad_attended, *forward_grads = feed_forward(
        spread,
        turn_adapter,
        attended_low,
        my_tokens,
        kept_grads,
        arrived_grads,
        ffn_gain,
        (output_weight, gate_weight, up_weight, down_weight),
        (a_guo, a_down, b_gu, b_do),
        meta,
    )
    layer_out = send_back(layer_rows)

    def back_part(pairs, before, after):
        return attend_back(
            attn_bias,
            query_low,
            meta,
            log_total,
            attended_low,
            grad_attended,
            keys,
            values,
            key_metas,
            segments,
            head_width,
            pairs,
            before,
            after,
        )

    axes = ("dp", "group")
    pair_count = feature_width // (2 * head_width)
    first_pairs = 3 * pair_count // 4
    after = []
    if even:
        total_rows = adapters.shape[0] // LANES
        late_rows = 6 * feature_width // devices
        params, first_old, second_old = spread_state(adapters, moment1, moment2, devices)
        order = placing_order(groups, devices, 16)
        early = lax.all_to_all(forward_grads[0], axes, 0, 0, tiled=True)
        after = [first_old]
    results = back_part((0, first_pairs), [], after)
    if even:
        told = 6 * RANK
        table = early[:, 0, told : told + 2].astype(jnp.int32)
        early_rows = params.shape[0] - late_rows
        state = (params, first_old, second_old)
        early_grad, early_new = settle(True, early_rows, table, early, *state, results[:1])
        after = [early_new]
        early_outer = lax.all_to_all(early_new, "dp", 0, 0, tiled=True)
    results = back_part((first_pairs, pair_count), results, after)
    grad_query = results[0]
    grad_keys = results[1 : 1 + half_devices]
    grad_values = results[1 + half_devices :]
    key_terms, value_terms = [grad_keys[0]], [grad_values[0]]
    for shift in range(1, half_devices):
        back_shift = half_devices - shift
        key_terms.append(within_half(grad_keys[shift], back_shift, groups))
        value_terms.append(within_half(grad_values[shift], back_shift, groups))
    grad_rows, *back_grads = project_heads_back(
        spread,
        [early_outer] if even else [],
        grad_query,
        key_terms,
        value_terms,
        query_raw,
        key_raw,
        normed,
        inner,
        my_tokens,
        grad_residual,
        attn_gain,
        (query_weight, key_weight, value_weight),
        a_qkv,
        b_qkv,
        meta,
        cos_table,
        sin_table,
        q_gain_row,
        k_gain_row,
        head_width,
    )
    input_grad = send_back(grad_rows)
    if not even:
        grads = (*back_grads, *forward_grads)
        column = jnp.arange(2 * RANK, dtype=jnp.int32)
        few_choice = one_hot(
            jnp.arange(LANES, dtype=jnp.int32)[:, None]
            == (jnp.repeat(turn_adapter, RANK) * RANK + column % RANK)[None, :]
        )
        settled = settle_shards(grads, few_choice, adapters, moment1, moment2, groups)
        return (layer_out, input_grad) + settled
    late = lax.all_to_all(back_grads[0], axes, 0, 0, tiled=True)
    early_pieces = gather_inner(early_outer, groups)
    late_grad, late_new = settle(False, late_rows, table, late, *state, early_pieces[1:2])
    late_pieces = gather_inner(lax.all_to_all(late_new, "dp", 0, 0, tiled=True), groups)
    adapters_new = assemble(order, early_pieces, total_rows, late_rows, 32, None)
    adapters_new = assemble(order, late_pieces, total_rows, 0, 64, adapters_new)
    owned = settle_owned(late_grad, early_grad, moment1, moment2, devices)
    return (layer_out, input_grad, *owned, adapters_new.reshape(-1))


def solution(mesh):
    in_specs = (
        P(("dp", "group"), None),
        P(("dp", "group"), None),
        P("dp"),
        P("dp", None),
        P("dp", None),
        P("dp", None),
        P(),
        P(),
        P(),
        P(),
        P(),
        P(),
        P(),
        P(),
        P(),
        P(),
        P(),
        P(),
        P(),
        P(("dp", "group")),
        P(("dp", "group")),
    )
    out_specs = (
        P(("dp", "group"), None),
        P(("dp", "group"), None),
        P(("dp", "group")),
        P(("dp", "group")),
        P(("dp", "group")),
        P(),
    )
    return jax.shard_map(
        per_device, mesh=mesh, in_specs=in_specs, out_specs=out_specs, check_vma=False
    )
```

```python
import functools

import jax
import jax.numpy as jnp
from jax import lax
from jax.experimental import pallas as pl
from jax.experimental.pallas import tpu as pltpu
from jax.sharding import PartitionSpec as P

RANK = 16
ADAPTERS = 8
NORM_EPS = 1e-06
ADAPTER_SCALE = 2.0
ROPE_BASE = 10000.0
MASKED = -1e30
LEARN_RATE = 0.01
BETA_ONE = 0.9
BETA_TWO = 0.999
ADAM_EPS = 1e-08
WEIGHT_DECAY = 0.01
update_count = 10.0
VARIATES = 4
VMEM_LIMIT = 56 * 1024 * 1024
EXACT_PARTS = 3


def contract_last(left, right):
    return lax.dot_general(
        left, right, (((1,), (1,)), ((), ())), preferred_element_type=jnp.float32
    )


def exact_parts(values):
    parts = []
    for _ in range(EXACT_PARTS):
        part = values.astype(jnp.bfloat16).astype(jnp.float32)
        parts.append(part)
        values = values - part
    return parts


def parts_in_lanes(values, first, column):
    result = jnp.zeros(values.shape, jnp.float32)
    for index, part in enumerate(exact_parts(values)):
        result = jnp.where(column == first + index, part, result)
    return result


def note_keys(side_ref, kmeta_refs, column, lane, width, segments):
    seg_column = column - EXACT_PARTS * VARIATES
    ones = (seg_column >= segments) & (seg_column < segments + EXACT_PARTS)
    for block, kmeta_ref in enumerate(kmeta_refs):
        one = (column < EXACT_PARTS * VARIATES) & ((column % VARIATES) == kmeta_ref[:, 0:1])
        in_seg = (seg_column >= 0) & (seg_column < segments) & (seg_column == kmeta_ref[:, 1:2])
        for head in range(2):
            outside = (lane // width) != head
            side_ref[head, block] = one_hot((one | in_seg | ones) & outside)


def note_queries(match_ref, apart_ref, qmeta_ref, column, segments):
    same = (column < EXACT_PARTS * VARIATES) & ((column % VARIATES) == qmeta_ref[:, 0:1])
    match_ref[...] = jnp.where(same, 1.0, 0.0)
    seg_column = column - EXACT_PARTS * VARIATES
    apart = (seg_column >= 0) & (seg_column < segments) & (seg_column != qmeta_ref[:, 1:2])
    apart_ref[...] = jnp.where(apart, MASKED, 0.0)


def bias_rows(bias_ref, head, column):
    rows = []
    for which in range(2):
        row = jnp.zeros(column.shape, jnp.float32)
        value = jnp.full(column.shape, bias_ref[which, head], jnp.float32)
        for index, part in enumerate(exact_parts(value)):
            row = jnp.where(column // VARIATES == index, part, row)
        rows.append(row)
    return rows


def query_side(match_ref, apart_ref, bias_ref, head, column):
    same, other = bias_rows(bias_ref, head, column[:1])
    return jnp.where(match_ref[...] > 0.0, same, other) + apart_ref[...]


def head_lanes(head, width, lanes):
    lane = lax.broadcasted_iota(jnp.int32, (1, lanes), 1)
    return jnp.where(lane // width == head, 1.0, 0.0).astype(jnp.bfloat16)


def attend_kernel(key_blocks, segments, width, bias_ref, query_ref, qmeta_ref, *refs):
    key_refs, value_refs, kmeta_refs = (
        refs[:key_blocks],
        refs[key_blocks : 2 * key_blocks],
        refs[2 * key_blocks : 3 * key_blocks],
    )
    out_ref, total_ref, side_ref, match_ref, apart_ref = refs[3 * key_blocks :]
    pair = pl.program_id(0)
    rows, lanes = query_ref.shape
    lane = lax.broadcasted_iota(jnp.int32, (rows, lanes), 1)
    column = lane % width

    @pl.when(pair == 0)
    def _():
        note_keys(side_ref, kmeta_refs, column, lane, width, segments)
        note_queries(match_ref, apart_ref, qmeta_ref, column, segments)

    scaled = query_ref[...].astype(jnp.float32) * width ** (-0.5)
    results = []
    for head in range(lanes // width):
        extension = query_side(
            match_ref, apart_ref, bias_ref, pair * (lanes // width) + head, column
        )
        left = jnp.where((lane // width) == head, scaled, extension).astype(jnp.bfloat16)
        inside = head_lanes(head, width, lanes)
        outside = head_lanes(1 - head, width, lanes)
        total = jnp.zeros((rows, lanes), jnp.float32)
        for block in range(key_blocks):
            right = key_refs[block][...] * inside + side_ref[head, block]
            weights = jnp.exp(contract_last(left, right)).astype(jnp.bfloat16)
            total = total + dot(weights, value_refs[block][...] * inside + outside)
        results.append(total)
    first = (lane // width) == 0
    numerator = jnp.where(first, results[0], results[1])
    crossed = jnp.where(first, results[1], results[0])
    out_ref[...] = (numerator / pltpu.roll(crossed, width, 1)).astype(jnp.bfloat16)
    total_ref[...] = jnp.log(crossed)


def lane_block(rows, lanes):
    return pl.BlockSpec((rows, lanes), lambda pair: (0, pair))


def whole_block(shape):
    return pl.BlockSpec(shape, lambda pair: (0,) * len(shape))


def attend(attn_bias, query_low, query_meta, keys, values, key_metas, segments, width):
    rows, features = query_low.shape
    lanes = 2 * width
    count = len(keys)
    flops = 4 * rows * rows * count * features
    return pl.pallas_call(
        functools.partial(attend_kernel, count, segments, width),
        grid=(features // lanes,),
        in_specs=[
            pl.BlockSpec(memory_space=pltpu.SMEM),
            lane_block(rows, lanes),
            whole_block(query_meta.shape),
        ]
        + [lane_block(rows, lanes)] * (2 * count)
        + [whole_block(query_meta.shape)] * count,
        out_specs=[lane_block(rows, lanes)] * 2,
        out_shape=[
            jax.ShapeDtypeStruct((rows, features), jnp.bfloat16),
            jax.ShapeDtypeStruct((rows, features), jnp.float32),
        ],
        scratch_shapes=[
            pltpu.VMEM((2, count, rows, lanes), jnp.bfloat16),
            pltpu.VMEM((rows, lanes), jnp.float32),
            pltpu.VMEM((rows, lanes), jnp.float32),
        ],
        compiler_params=pltpu.CompilerParams(vmem_limit_bytes=VMEM_LIMIT),
        cost_estimate=pl.CostEstimate(
            flops=flops, bytes_accessed=12 * rows * features, transcendentals=0
        ),
        name="attend",
    )(attn_bias, query_low, query_meta, *keys, *values, *key_metas)


def attend_back_kernel(
    key_blocks,
    segments,
    width,
    bias_ref,
    query_ref,
    qmeta_ref,
    total_ref,
    attended_ref,
    grad_ref,
    *refs,
):
    key_refs, value_refs, kmeta_refs = (
        refs[:key_blocks],
        refs[key_blocks : 2 * key_blocks],
        refs[2 * key_blocks : 3 * key_blocks],
    )
    results = refs[len(refs) - 4 - 2 * key_blocks :]
    grad_query_ref = results[0]
    grad_key_refs = results[1 : key_blocks + 1]
    grad_value_refs = results[key_blocks + 1 : 2 * key_blocks + 1]
    side_ref, match_ref, apart_ref = results[2 * key_blocks + 1 :]
    pair = pl.program_id(0)
    rows, lanes = query_ref.shape
    lane = lax.broadcasted_iota(jnp.int32, (rows, lanes), 1)
    column = lane % width
    ones_at = EXACT_PARTS * VARIATES + segments

    @pl.when(pair == 0)
    def _():
        note_keys(side_ref, kmeta_refs, column, lane, width, segments)
        note_queries(match_ref, apart_ref, qmeta_ref, column, segments)

    scaled = query_ref[...].astype(jnp.float32) * width ** (-0.5)
    scaled_low = scaled.astype(jnp.bfloat16)
    grad_low = grad_ref[...]
    grad = grad_low.astype(jnp.float32)
    overlap = grad * attended_ref[...].astype(jnp.float32)
    square_row = lax.broadcasted_iota(jnp.int32, (lanes, lanes), 0)
    square_column = lax.broadcasted_iota(jnp.int32, (lanes, lanes), 1)
    across = one_hot(square_row // width != square_column // width)
    high = overlap.astype(jnp.bfloat16)
    rest = (overlap - high.astype(jnp.float32)).astype(jnp.bfloat16)
    dot_side = parts_in_lanes(-(dot(high, across) + dot(rest, across)), ones_at, column)
    total_side = parts_in_lanes(-total_ref[...], ones_at, column)
    grad_query_parts = []
    grad_keys = [[] for _ in range(key_blocks)]
    grad_values = [[] for _ in range(key_blocks)]
    for head in range(lanes // width):
        inside = (lane // width) == head
        extension = total_side + query_side(
            match_ref, apart_ref, bias_ref, pair * (lanes // width) + head, column
        )
        right = jnp.where(inside, scaled, extension).astype(jnp.bfloat16)
        grad_right = jnp.where(inside, grad, dot_side).astype(jnp.bfloat16)
        own_lanes = head_lanes(head, width, lanes)
        turned = jnp.zeros((width, rows), jnp.float32)
        for block in range(key_blocks):
            key = key_refs[block][...]
            side = side_ref[head, block]
            prob = jnp.exp(contract_last(key * own_lanes + side, right))
            value_left = value_refs[block][...] * own_lanes + side
            grad_score = (prob * contract_last(value_left, grad_right)).astype(jnp.bfloat16)
            grad_values[block].append(dot(prob.astype(jnp.bfloat16), grad_low))
            grad_keys[block].append(dot(grad_score, scaled_low))
            key_turned = jnp.transpose(key)[head * width : (head + 1) * width]
            turned = turned + dot(key_turned, grad_score)
        grad_query_parts.append(turned)
    first = (lane // width) == 0
    stacked = jnp.concatenate(grad_query_parts, axis=0) * width ** (-0.5)
    grad_query_ref[...] = jnp.transpose(stacked).astype(jnp.bfloat16)
    for block in range(key_blocks):
        grad_key_refs[block][...] = jnp.where(first, *grad_keys[block]).astype(
            grad_key_refs[block].dtype
        )
        grad_value_refs[block][...] = jnp.where(first, *grad_values[block]).astype(
            grad_value_refs[block].dtype
        )


def attend_back(
    attn_bias,
    query_low,
    query_meta,
    log_total,
    attended_low,
    grad_attended,
    keys,
    values,
    key_metas,
    segments,
    width,
):
    rows, features = query_low.shape
    lanes = 2 * width
    count = len(keys)
    here = lane_block(rows, lanes)
    flops = 10 * rows * rows * count * features
    low = jax.ShapeDtypeStruct((rows, features), jnp.bfloat16)
    results = pl.pallas_call(
        functools.partial(attend_back_kernel, count, segments, width),
        grid=(features // lanes,),
        in_specs=[
            pl.BlockSpec(memory_space=pltpu.SMEM),
            here,
            whole_block(query_meta.shape),
        ]
        + [here] * (3 + 2 * count)
        + [whole_block(query_meta.shape)] * count,
        out_specs=[here] * (1 + 2 * count),
        out_shape=[low] * (1 + 2 * count),
        scratch_shapes=[
            pltpu.VMEM((2, count, rows, lanes), jnp.bfloat16),
            pltpu.VMEM((rows, lanes), jnp.float32),
            pltpu.VMEM((rows, lanes), jnp.float32),
        ],
        compiler_params=pltpu.CompilerParams(vmem_limit_bytes=VMEM_LIMIT),
        cost_estimate=pl.CostEstimate(
            flops=flops, bytes_accessed=20 * rows * features, transcendentals=0
        ),
        name="attend_back",
    )(
        attn_bias,
        query_low,
        query_meta,
        log_total,
        attended_low,
        grad_attended,
        *keys,
        *values,
        *key_metas,
    )
    return results


def plan_kernel(
    groups,
    rows,
    member_ref,
    length_ref,
    adapter_ref,
    order_ref,
    variate_ref,
    chosen_ref,
    back_ref,
    turn_ref,
    *refs,
):
    meta_refs, slot_ref = refs[:-1], refs[-1]
    blocks = variate_ref.shape[0]
    half_devices = groups // 2
    half_blocks = blocks // 2
    half_rows = half_blocks * LANES
    swap_rows = rows // 2
    member = member_ref[0]
    my_half, my_place = member // half_devices, member % half_devices
    places = [lax.rem(my_place + shift, half_devices) for shift in range(half_devices)]
    segments = length_ref.shape[1]
    starts = [jnp.int32(0)]
    for segment in range(segments):
        starts.append(starts[-1] + length_ref[0, segment])
    long_start, long_index = jnp.int32(0), jnp.int32(0)
    for segment in range(segments):
        is_half = length_ref[0, segment] == half_rows
        long_start = jnp.where(is_half, starts[segment], long_start)
        long_index = jnp.where(is_half, segment, long_index)

    block = lax.broadcasted_iota(jnp.int32, (blocks, LANES), 0)
    lane = lax.broadcasted_iota(jnp.int32, (blocks, LANES), 1)
    work_block = jnp.zeros((blocks, LANES), jnp.int32)
    for index in range(blocks):
        work_block = jnp.where(block == order_ref[0, index], index, work_block)
    work_row = work_block * LANES + lane
    is_long = (work_row >= long_start) & (work_row < long_start + half_rows)
    in_first = block < half_blocks
    long_count = jnp.sum(jnp.where(is_long & in_first, 1.0, 0.0)).astype(jnp.int32)
    long_half = jnp.where(2 * long_count < half_rows, 1, 0)
    side = jnp.where(in_first, 0, 1)
    target = jnp.where(is_long, long_half, 1 - long_half)
    foreign = target != side
    flags = jnp.where(foreign, 1.0, 0.0)
    moved = jnp.sum(jnp.where(in_first, flags, 0.0)).astype(jnp.int32)
    square_row = lax.broadcasted_iota(jnp.int32, (LANES, LANES), 0)
    square_column = lax.broadcasted_iota(jnp.int32, (LANES, LANES), 1)
    within = dot(flags.astype(jnp.bfloat16), one_hot(square_row < square_column))
    block_sum = jnp.broadcast_to(jnp.sum(flags, axis=1, keepdims=True), (blocks, LANES))
    from_block = lax.broadcasted_iota(jnp.int32, (blocks, blocks), 1)
    to_block = lax.broadcasted_iota(jnp.int32, (blocks, blocks), 0)
    earlier = (from_block < to_block) & ((from_block < half_blocks) == (to_block < half_blocks))
    before = dot(one_hot(earlier), block_sum.astype(jnp.bfloat16))
    foreign_rank = (within + before).astype(jnp.int32)
    kept_rank = (block - side * half_blocks) * LANES + lane - foreign_rank
    kept_slot = side * half_rows + kept_rank
    foreign_slot = (1 - side) * half_rows + rows + foreign_rank
    foreign_slot = foreign_slot - jnp.clip(moved, 0, swap_rows)
    for index in range(1, half_devices):
        start = index * rows - jnp.minimum(moved, index * swap_rows)
        last = (index - 1) * rows - jnp.minimum(moved, (index - 1) * swap_rows)
        kept_slot = jnp.where(kept_rank >= start, kept_slot + rows - (start - last), kept_slot)
        received = jnp.clip(moved - index * swap_rows, 0, swap_rows)
        previous = jnp.clip(moved - (index - 1) * swap_rows, 0, swap_rows)
        foreign_slot = jnp.where(
            foreign_rank >= index * swap_rows,
            foreign_slot + rows - swap_rows + previous - received,
            foreign_slot,
        )
    slot = jnp.where(foreign, foreign_slot, kept_slot)
    slot_ref[...] = slot

    per_device = rows // LANES
    wanted = lax.broadcasted_iota(jnp.int32, (rows + swap_rows, 1), 0)
    wanted = jnp.where(
        wanted < rows,
        my_half * half_rows + my_place * rows + wanted,
        (1 - my_half) * half_rows + my_place * rows + wanted - swap_rows,
    )
    for shift in range(half_devices):
        for index in range(per_device):
            held = my_half * half_blocks + places[shift] * per_device + index
            column = (shift * per_device + index) * LANES
            chosen_ref[:, column : column + LANES] = one_hot(
                wanted == slot_ref[pl.ds(held, 1), :]
            )

    slot_turned = jnp.transpose(slot.astype(jnp.float32))
    turned_lane = lax.broadcasted_iota(jnp.int32, (LANES, blocks), 1)
    first_lane = lax.broadcasted_iota(jnp.int32, (1, LANES), 1)
    for index in range(per_device):
        held = my_half * half_blocks + my_place * per_device + index
        mine = jnp.sum(
            jnp.where(turned_lane == held, slot_turned, 0.0), axis=1, keepdims=True
        ).astype(jnp.int32)
        here = slice(index * LANES, (index + 1) * LANES)
        column = 0
        for first, half, length in ((0, my_half, rows), (swap_rows, 1 - my_half, swap_rows)):
            for shift in range(half_devices):
                for chunk in range(0, length, LANES):
                    number = half * half_rows + places[shift] * rows + first + chunk
                    back_ref[here, column : column + LANES] = one_hot(mine == number + first_lane)
                    column += LANES

    on_long = my_half == long_half
    for turn in range(2):
        chosen_segment = jnp.where(
            on_long, long_index, jnp.where(long_index <= turn, turn + 1, turn)
        )
        adapter = adapter_ref[0, 0]
        for segment in range(1, segments):
            adapter = jnp.where(chosen_segment == segment, adapter_ref[0, segment], adapter)
        turn_ref[turn] = adapter

    variate_turned = jnp.transpose(variate_ref[...].astype(jnp.float32))
    known = []
    for index in range(blocks):
        values = jnp.where(
            square_column == 0,
            work_block[index : index + 1, :].astype(jnp.float32),
            jnp.where(
                square_column == 1,
                square_row.astype(jnp.float32),
                variate_turned[:, index : index + 1],
            ),
        )
        known.append(jnp.where(square_column < 3, values, 0.0).astype(jnp.bfloat16))
    number = lax.broadcasted_iota(jnp.int32, (rows, 1), 0)
    wide_lane = lax.broadcasted_iota(jnp.int32, (rows, LANES), 1)
    for shift in range(half_devices):
        slots = my_half * half_rows + places[shift] * rows + number
        facts = jnp.zeros((rows, LANES), jnp.float32)
        for index in range(blocks):
            facts = facts + dot(one_hot(slots == slot[index : index + 1, :]), known[index])
        facts = facts.astype(jnp.int32)
        row = facts[:, 0:1] * LANES + facts[:, 1:2]
        segment = jnp.zeros((rows, 1), jnp.int32)
        first_row = jnp.zeros((rows, 1), jnp.int32)
        for index in range(1, segments):
            segment = jnp.where(row >= starts[index], index, segment)
            first_row = jnp.where(row >= starts[index], starts[index], first_row)
        turn = jnp.where(segment > long_index, segment - 1, segment)
        turn = jnp.where(on_long, 0, turn)
        meta_refs[shift][...] = jnp.where(
            wide_lane == 0,
            facts[:, 2:3],
            jnp.where(
                wide_lane == 1, segment, jnp.where(wide_lane == 2, turn, row - first_row)
            ),
        )


def plan(groups, rows, member, seq_len, seq_adapter, block_order, variate):
    half_devices = groups // 2
    half_rows = half_devices * rows
    blocks = block_order.shape[1]
    smem = pl.BlockSpec(memory_space=pltpu.SMEM)
    vmem = pl.BlockSpec(memory_space=pltpu.VMEM)
    results = pl.pallas_call(
        functools.partial(plan_kernel, groups, rows),
        in_specs=[smem, smem, smem, smem, vmem],
        out_specs=[vmem, vmem, smem] + [vmem] * half_devices,
        out_shape=[
            jax.ShapeDtypeStruct((rows + rows // 2, half_rows), jnp.bfloat16),
            jax.ShapeDtypeStruct((rows, half_rows + half_rows // 2), jnp.bfloat16),
            jax.ShapeDtypeStruct((2,), jnp.int32),
        ]
        + [jax.ShapeDtypeStruct((rows, LANES), jnp.int32)] * half_devices,
        scratch_shapes=[pltpu.VMEM((blocks, LANES), jnp.int32)],
        compiler_params=pltpu.CompilerParams(vmem_limit_bytes=VMEM_LIMIT),
        cost_estimate=pl.CostEstimate(
            flops=2**31, bytes_accessed=4 * rows * half_rows, transcendentals=0
        ),
        name="plan",
    )(member, seq_len, seq_adapter, block_order, variate.reshape(blocks, LANES))
    return results[0], results[1], results[2], results[3:]


def pick_kernel(counts, later_count, chosen_ref, *refs):
    outs = refs[sum(counts) + later_count : sum(counts) + later_count + len(counts)]
    refs = iter(refs[: sum(counts)])
    for count, out_ref in zip(counts, outs):
        total = jnp.zeros(out_ref.shape, jnp.float32)
        column = 0
        for _ in range(count):
            ref = next(refs)
            rows = ref.shape[0]
            total = total + dot(chosen_ref[:, column : column + rows], ref[...])
            column += rows
        out_ref[...] = total.astype(out_ref.dtype)


def pick(chosen, first, count, *helds, later=()):
    features = helds[0][0].shape[1]
    tile = features // 2
    parts = [part for held in helds for part in held]
    return pl.pallas_call(
        functools.partial(pick_kernel, [len(held) for held in helds], len(later)),
        grid=(features // tile,),
        in_specs=[pl.BlockSpec((count, chosen.shape[1]), lambda step: (first // count, 0))]
        + [pl.BlockSpec((part.shape[0], tile), lambda step: (0, step)) for part in parts]
        + [pl.BlockSpec(memory_space=pl.ANY)] * len(later),
        out_specs=[pl.BlockSpec((count, tile), lambda step: (0, step))] * len(helds)
        + [pl.BlockSpec(memory_space=pl.ANY)] * len(later),
        out_shape=[jax.ShapeDtypeStruct((count, features), jnp.bfloat16)] * len(helds)
        + [jax.ShapeDtypeStruct(array.shape, array.dtype) for array in later],
        input_output_aliases={1 + len(parts) + i: len(helds) + i for i in range(len(later))},
        compiler_params=pltpu.CompilerParams(vmem_limit_bytes=VMEM_LIMIT),
        cost_estimate=pl.CostEstimate(
            flops=2 * count * chosen.shape[1] * features * len(helds),
            bytes_accessed=8 * count * features * len(helds),
            transcendentals=0,
        ),
        name="pick",
    )(chosen, *parts, *later)


def axis_count(names):
    count = 1
    for name in names:
        count *= lax.axis_size(name)
    return count


def within_half(array, shift, groups):
    half = groups // 2
    pairs = [
        (base + (place + shift) % half, base + place)
        for base in (0, half)
        for place in range(half)
    ]
    return lax.ppermute(array, GROUP, pairs)


def gather_half(array, groups):
    return [array] + [within_half(array, shift, groups) for shift in range(1, groups // 2)]


def to_other_half(array, groups):
    half = groups // 2
    return lax.ppermute(array, GROUP, [(i, (i + half) % groups) for i in range(groups)])


def scatter_sum(array, axis_sizes):
    for name, size in reversed(axis_sizes):
        outer = array.shape[0] // size
        array = array.reshape((outer, size) + array.shape[1:])
        bit = 1
        while bit < size:
            index = lax.axis_index(name)
            own = (index // bit) % 2
            spread = array.reshape((outer, size // (2 * bit), 2) + array.shape[2:])
            keep = lax.dynamic_index_in_dim(spread, own, 2, keepdims=False)
            send = lax.dynamic_index_in_dim(spread, 1 - own, 2, keepdims=False)
            got = lax.ppermute(send, name, [(i, i ^ bit) for i in range(size)])
            array = (keep.astype(jnp.float32) + got.astype(jnp.float32)).astype(jnp.bfloat16)
            bit *= 2
        array = array.reshape((outer,) + array.shape[2:])
    return array


LANES = 128
MOMENT_ROWS = 24
PACKS = ("far", "near")
GROUP = ("half", "core")
ALL = PACKS + GROUP


def adam(current, first_old, second_old, grad):
    first_moment = BETA_ONE * first_old + (1.0 - BETA_ONE) * grad
    second_moment = BETA_TWO * second_old + (1.0 - BETA_TWO) * grad * grad
    first_fix = first_moment / (1.0 - BETA_ONE**update_count)
    second_fix = second_moment / (1.0 - BETA_TWO**update_count)
    updated = current - LEARN_RATE * (
        first_fix / (jnp.sqrt(second_fix) + ADAM_EPS) + WEIGHT_DECAY * current
    )
    return first_moment, second_moment, updated.astype(jnp.bfloat16)


def settle_shards(grads, few_choice, adapters, moment1, moment2, groups):
    a_qkv, b_qkv, a_guo, a_down, b_gu, b_do = grads
    features, few = a_qkv.shape[0], few_choice.shape[1]
    quarters = a_down.shape[1] // few
    down = jnp.concatenate([a_down[:, i * few : (i + 1) * few] for i in range(quarters)])
    wide = [a_qkv[:, i * few : (i + 1) * few] for i in range(3)]
    wide += [a_guo[:, i * few : (i + 1) * few] for i in (2, 0, 1)] + [down]
    tall = [b_qkv[i * few : (i + 1) * few] for i in range(3)]
    tall += [b_do[2 * few : 3 * few], b_gu[:few], b_gu[few : 2 * few], b_do[:few]]
    pieces = []
    for grad_a, grad_b in zip(wide, tall):
        pieces.append(lax.dot_general(grad_a, few_choice, (((1,), (1,)), ((), ()))).reshape(-1))
        pieces.append(jnp.dot(few_choice, grad_b).reshape(-1))
    axis_sizes = [(PACKS, axis_count(PACKS)), (GROUP, groups)]
    shards = axis_sizes[0][1] * groups
    flat_grads = jnp.concatenate(pieces).astype(jnp.bfloat16).reshape(shards, -1)
    grad_shard = scatter_sum(flat_grads, axis_sizes).reshape(-1).astype(jnp.float32)
    shard_count = grad_shard.shape[0]
    shard_start = lax.axis_index(ALL) * shard_count
    current = lax.dynamic_slice_in_dim(adapters, shard_start, shard_count).astype(jnp.float32)
    first_moment, second_moment, updated = adam(current, moment1, moment2, grad_shard)
    adapters_new = lax.all_gather(updated, ALL, axis=0, tiled=True)
    return grad_shard, first_moment, second_moment, adapters_new


def spreads_evenly(devices, groups, features, hidden, total):
    rows = total // LANES
    chunks = features // LANES
    return (
        groups == 4
        and ADAPTERS * RANK == LANES
        and devices * chunks == 256
        and chunks == 8
        and hidden == devices * LANES
        and hidden == 4 * features
        and rows % (devices * devices) == 0
        and devices & (devices - 1) == 0
    )


def one_hot(condition):
    return jnp.where(condition, 1.0, 0.0).astype(jnp.bfloat16)


def sum_wide(adapter_row, arrived_ref, first, width):
    sources = arrived_ref.shape[0]
    rows = lax.broadcasted_iota(jnp.int32, (LANES, width * LANES), 0)
    columns = lax.broadcasted_iota(jnp.int32, (LANES, width * LANES), 1)
    fits = (rows // (2 * RANK) == columns // LANES) & (rows % RANK == columns % RANK)
    second = (rows // RANK) % 2 == 1
    adapter = jnp.where(fits, (columns % LANES) // RANK, -1)
    total = jnp.zeros((32, width * LANES), jnp.float32)
    for source in range(sources):
        at = source * 2 * RANK
        chosen = jnp.where(
            second, adapter_row[:, at + RANK : at + RANK + 1], adapter_row[:, at : at + 1]
        )
        total = total + dot(
            arrived_ref[source, first : first + 32, :], one_hot(adapter == chosen)
        )
    return total


def sum_tall(adapter_row, arrived_ref, first):
    sources = arrived_ref.shape[0]
    depth = sources * 2 * RANK
    rows = lax.broadcasted_iota(jnp.int32, (LANES, depth), 0)
    columns = lax.broadcasted_iota(jnp.int32, (LANES, depth), 1)
    choice = one_hot((rows // RANK == adapter_row) & (rows % RANK == columns % RANK))
    held = arrived_ref[:, first : first + 2 * RANK, :].reshape(depth, LANES)
    return jnp.dot(choice, held, preferred_element_type=jnp.float32)


def sum_square(adapter_row, arrived_ref, first):
    sources = arrived_ref.shape[0]
    depth = sources * 16
    rows = lax.broadcasted_iota(jnp.int32, (64, depth), 0)
    columns = lax.broadcasted_iota(jnp.int32, (64, depth), 1)
    choice = one_hot(
        ((rows % 32) // 4 == adapter_row)
        & (rows % 4 == columns % 4)
        & (rows // 32 == (columns % 16) // 8)
    )
    held = arrived_ref[:, first : first + 16, :].reshape(depth, LANES)
    return jnp.dot(choice, held, preferred_element_type=jnp.float32)


def settle_rows(parts, skip, param_ref, m1_ref, m2_ref, m_skip, grad_ref, new_refs):
    row = 0
    for part in parts:
        here = slice(row, row + part.shape[0])
        there = slice(skip + row, skip + row + part.shape[0])
        at = slice(m_skip + row, m_skip + row + part.shape[0])
        row += part.shape[0]
        low = part.astype(jnp.bfloat16)
        grad_ref[here, :] = low
        new = adam(
            param_ref[there, :].astype(jnp.float32),
            m1_ref[at, :],
            m2_ref[at, :],
            low.astype(jnp.float32),
        )[2]
        for new_ref in new_refs:
            new_ref[here, :] = new


def settle_early_kernel(own_rows, arrived_ref, moments_ref, param_ref, *refs):
    grad_ref, new_ref, late_m1_ref, late_m2_ref, tall_ref, square_ref, m1_ref, m2_ref = refs[-8:]
    sources = arrived_ref.shape[0]
    told = 6 * RANK
    tall_column = lax.broadcasted_iota(jnp.int32, tall_ref.shape, 1)
    square_column = lax.broadcasted_iota(jnp.int32, square_ref.shape, 1)
    tall = jnp.zeros(tall_ref.shape, jnp.float32)
    square = jnp.zeros(square_ref.shape, jnp.float32)
    for source in range(sources):
        row = arrived_ref[source, 0:16, :].astype(jnp.float32)
        first, second = row[0:1, told : told + 1], row[0:1, told + 1 : told + 2]
        tall = jnp.where(
            tall_column // (2 * RANK) == source,
            jnp.where((tall_column // RANK) % 2 == 1, second, first),
            tall,
        )
        square = jnp.where(
            square_column // RANK == source,
            jnp.where((square_column // 4) % 2 == 1, second, first),
            square,
        )
        held = moments_ref[source].astype(jnp.float32)
        here = slice(source * own_rows, (source + 1) * own_rows)
        m1_ref[here, :] = held[:own_rows]
        m2_ref[here, :] = held[MOMENT_ROWS : MOMENT_ROWS + own_rows]
    tall = tall.astype(jnp.int32)
    square = square.astype(jnp.int32)
    tall_ref[...] = tall
    square_ref[...] = square
    late = late_m1_ref.shape[0]
    late_m1_ref[...] = m1_ref[:late, :]
    late_m2_ref[...] = m2_ref[:late, :]
    wide = sum_wide(tall, arrived_ref, 0, 3)
    last = sum_wide(tall, arrived_ref, 32, 4)
    pair = sum_square(square, arrived_ref, 128)
    parts = [
        wide[:, 2 * LANES :],
        pair[32:],
        wide[:, :LANES],
        sum_tall(tall, arrived_ref, 64),
        wide[:, LANES : 2 * LANES],
        sum_tall(tall, arrived_ref, 96),
    ]
    parts += [last[:, i * LANES : (i + 1) * LANES] for i in range(4)]
    parts.append(pair[:32])
    copies = [new_ref.at[copy] for copy in range(new_ref.shape[0])]
    settle_rows(parts, late, param_ref, m1_ref, m2_ref, late, grad_ref, copies)


def settle_early(arrived, moments, params, late_rows, after):
    sources = arrived.shape[0]
    rows = params.shape[0] - late_rows
    vmem = pl.BlockSpec(memory_space=pltpu.VMEM)
    low = jax.ShapeDtypeStruct((rows, LANES), jnp.bfloat16)
    late = jax.ShapeDtypeStruct((late_rows, LANES), jnp.float32)
    return pl.pallas_call(
        functools.partial(settle_early_kernel, params.shape[0] // sources),
        in_specs=[vmem, vmem, vmem] + [pl.BlockSpec(memory_space=pl.ANY)] * len(after),
        out_specs=[vmem] * 6,
        out_shape=[
            low,
            jax.ShapeDtypeStruct((lax.axis_size("far"), rows, LANES), jnp.bfloat16),
            late,
            late,
            jax.ShapeDtypeStruct((1, sources * 2 * RANK), jnp.int32),
            jax.ShapeDtypeStruct((1, sources * RANK), jnp.int32),
        ],
        scratch_shapes=[pltpu.VMEM(params.shape, jnp.float32)] * 2,
        compiler_params=pltpu.CompilerParams(vmem_limit_bytes=VMEM_LIMIT),
        cost_estimate=pl.CostEstimate(
            flops=sources * 2**24, bytes_accessed=4 * arrived.size, transcendentals=0
        ),
        name="settle_early",
    )(arrived, moments, params, *after)


def settle_late_kernel(
    tall_ref, square_ref, arrived_ref, param_ref, m1_ref, m2_ref, *refs
):
    early_grad_ref = refs[0]
    own_ref, new_ref, _, grad_ref = refs[-4:]
    wide = sum_wide(tall_ref[...], arrived_ref, 0, 3)
    pairs = [sum_square(square_ref[...], arrived_ref, first) for first in (32, 48)]
    parts = []
    for index in range(3):
        parts.append(wide[:, index * LANES : (index + 1) * LANES])
        parts.append(pairs[index // 2][(index % 2) * 32 : (index % 2) * 32 + 32])
    copies = [new_ref.at[copy] for copy in range(new_ref.shape[0])]
    settle_rows(parts, 0, param_ref, m1_ref, m2_ref, 0, grad_ref, copies)
    low = jnp.concatenate(
        [ref[...].astype(jnp.float32) for ref in (grad_ref, early_grad_ref)], axis=0
    )
    each = low.shape[0] // own_ref.shape[0]
    zeros = jnp.zeros((own_ref.shape[1] - each, LANES), jnp.float32)
    for owner in range(own_ref.shape[0]):
        own_ref[owner] = jnp.concatenate(
            [low[owner * each : (owner + 1) * each], zeros], axis=0
        ).astype(jnp.bfloat16)


def settle_late(tall, square, arrived, params, late_m1, late_m2, early_grad, later, after):
    rows = late_m1.shape[0]
    anywhere = pl.BlockSpec(memory_space=pl.ANY)
    vmem = pl.BlockSpec(memory_space=pltpu.VMEM)
    return pl.pallas_call(
        settle_late_kernel,
        in_specs=[vmem] * 7 + [anywhere] * (1 + len(after)),
        out_specs=[vmem, vmem, anywhere],
        scratch_shapes=[pltpu.VMEM((rows, LANES), jnp.bfloat16)],
        input_output_aliases={7: 2},
        out_shape=[
            jax.ShapeDtypeStruct((arrived.shape[0], MOMENT_ROWS, LANES), jnp.bfloat16),
            jax.ShapeDtypeStruct((axis_count(PACKS), rows, LANES), jnp.bfloat16),
            jax.ShapeDtypeStruct(later.shape, later.dtype),
        ],
        compiler_params=pltpu.CompilerParams(vmem_limit_bytes=VMEM_LIMIT),
        cost_estimate=pl.CostEstimate(
            flops=arrived.shape[0] * 2**24, bytes_accessed=4 * arrived.size, transcendentals=0
        ),
        name="settle_late",
    )(tall, square, arrived, params, late_m1, late_m2, early_grad, later, *after)


def gather_inner(piece, groups):
    pieces = [piece]
    bit = groups // 2
    while bit:
        pairs = [(i, i ^ bit) for i in range(groups)]
        pieces = pieces + [lax.ppermute(piece, GROUP, pairs) for piece in pieces]
        bit //= 2
    return pieces


def placing_order(device, unit):
    size = unit * device.shape[0]
    to_row = lax.broadcasted_iota(jnp.int32, (size, size), 0)
    from_row = jnp.arange(size, dtype=jnp.int32)
    source = (from_row % unit) * device.shape[0] + jnp.repeat(device, unit)
    return (to_row == source[None, :]).astype(jnp.bfloat16)


def piece_devices(groups, devices):
    member = lax.axis_index(GROUP)
    piece = jnp.arange(groups, dtype=jnp.int32)
    mask = jnp.zeros_like(piece)
    bit = 1
    while bit < groups:
        mask = mask * 2 + (piece // bit) % 2
        bit *= 2
    outer = jnp.arange(devices // groups, dtype=jnp.int32)
    return (outer[None, :] * groups + (member ^ mask)[:, None]).reshape(-1)


def assemble_kernel(counts, devices, chunks, first, order_ref, *refs):
    piece_refs = []
    for count in counts:
        piece_refs.append(refs[:count])
        refs = refs[count:]
    out_any, placed_ref, sems = refs[-3:]

    def held_rows(part_refs, start, stop):
        before = 0
        for ref in part_refs:
            if start < before + ref.shape[1]:
                return ref[:, start - before : stop - before, :]
            before += ref.shape[1]

    unit = order_ref.shape[0] // devices
    copies = []
    for index, (begin, end) in enumerate(chunks):
        for start in range(begin, end, 2 * unit):
            sides = []
            for side in (start, start + unit):
                held = jnp.concatenate(
                    [held_rows(part_refs, side, side + unit) for part_refs in piece_refs], axis=0
                )
                sides.append(held.reshape(unit * devices, LANES))
            placed = dot(order_ref[...], jnp.concatenate(sides, axis=1)).astype(jnp.bfloat16)
            for half, side in enumerate((start, start + unit)):
                placed_ref[side * devices : (side + unit) * devices, :] = placed[
                    :, half * LANES : (half + 1) * LANES
                ]
        here = slice(begin * devices, end * devices)
        there = slice((first + begin) * devices, (first + end) * devices)
        copies.append(
            pltpu.make_async_copy(placed_ref.at[here, :], out_any.at[there, :], sems.at[index])
        )
        copies[-1].start()
    for copy in copies:
        copy.wait()


def assemble(order, pieces, total_rows, first, before, after):
    devices = len(pieces) * pieces[0][0].shape[0]
    rows = pieces[0][0].shape[1]
    parts = [part for piece in pieces for part in piece]
    step = 32 * max(1, rows // 128)
    chunks = [(begin, min(begin + step, rows)) for begin in range(0, rows, step)]
    vmem, anywhere = pl.BlockSpec(memory_space=pltpu.VMEM), pl.BlockSpec(memory_space=pl.ANY)
    in_specs = [vmem] * (1 + len(parts)) + [anywhere] * len(after)
    operands = [order, *parts, *after]
    aliases = {}
    if before is not None:
        aliases = {len(operands): 0}
        in_specs.append(anywhere)
        operands.append(before)
    return pl.pallas_call(
        functools.partial(assemble_kernel, [len(piece) for piece in pieces], devices, chunks, first),
        in_specs=in_specs,
        out_specs=anywhere,
        out_shape=jax.ShapeDtypeStruct((total_rows, LANES), jnp.bfloat16),
        scratch_shapes=[
            pltpu.VMEM((rows * devices, LANES), jnp.bfloat16),
            pltpu.SemaphoreType.DMA((len(chunks),)),
        ],
        input_output_aliases=aliases,
        compiler_params=pltpu.CompilerParams(vmem_limit_bytes=VMEM_LIMIT),
        cost_estimate=pl.CostEstimate(
            flops=rows * devices * 2**17, bytes_accessed=rows * devices * 512, transcendentals=0
        ),
        name="assemble",
    )(*operands)


def rope_tables(position, head_width):
    lane = jnp.arange(LANES, dtype=jnp.int32)
    freq_index = (lane % (head_width // 2)).astype(jnp.float32)
    frequency = ROPE_BASE ** (-2.0 * freq_index / head_width)
    angles = position.astype(jnp.float32)[:, None] * frequency[None, :]
    sign = jnp.where(lane % head_width < head_width // 2, -1.0, 1.0)
    return jnp.cos(angles), jnp.sin(angles) * sign[None, :]


def head_gain(gain):
    return jnp.tile(gain.astype(jnp.float32), LANES // gain.shape[0])[None, :]


def select_kernel(features, hidden, devices, turn_ref, me_ref, flat_ref, *refs):
    m1_ref, m2_ref = refs[:2]
    out_refs = refs[3:]
    a_qkv_ref, a_guo_ref, a_down_ref, b_qkv_ref, b_gu_ref, b_do_ref = out_refs[:6]
    if devices:
        own_ref, moments_ref, wide_ref = out_refs[6:]
        count = m1_ref.shape[0] // devices
        for device in range(devices):
            rows = []
            for ref in (m1_ref, m2_ref):
                rows.append(ref[pl.ds(device, count, stride=devices), :])
                rows.append(jnp.zeros((MOMENT_ROWS - count, LANES), jnp.float32))
            moments_ref[device] = jnp.concatenate(rows, axis=0).astype(jnp.bfloat16)
        size = wide_ref.shape[0]
        each = size // devices
        for chunk in range(flat_ref.shape[0] // size):
            wide_ref[...] = flat_ref[chunk * size : (chunk + 1) * size, :].astype(jnp.float32)
            own_ref[chunk * each : (chunk + 1) * each, :] = wide_ref[
                pl.ds(me_ref[0], each, stride=devices), :
            ].astype(jnp.bfloat16)
    few = 2 * RANK
    rows = lax.broadcasted_iota(jnp.int32, (LANES, LANES), 0)
    columns = lax.broadcasted_iota(jnp.int32, (LANES, LANES), 1)
    chosen = jnp.where((columns // RANK) % 2 == 1, turn_ref[1], turn_ref[0])
    fits = (rows // RANK == chosen) & (rows % RANK == columns % RANK)
    start = {}
    row = 0
    for name, rows_in, rows_out in (
        ("q", features, features),
        ("k", features, features),
        ("v", features, features),
        ("o", features, features),
        ("g", features, hidden),
        ("u", features, hidden),
        ("d", hidden, features),
    ):
        start[name] = (row, row + rows_in)
        row += rows_in + rows_out

    def wide(names, length):
        total = jnp.zeros((length, LANES), jnp.float32)
        for place, name in enumerate(names):
            first = start[name][0]
            total = total + jnp.dot(
                flat_ref[first : first + length, :],
                one_hot(fits & (columns // few == place)),
                preferred_element_type=jnp.float32,
            )
        return total.astype(jnp.bfloat16)

    a_qkv_ref[...] = wide("qkv", features)
    a_guo_ref[...] = wide("guo", features)
    for first in range(0, hidden, features):
        a_down_ref[first : first + features, :] = jnp.dot(
            flat_ref[start["d"][0] + first : start["d"][0] + first + features, :],
            one_hot(fits & (columns // few == 0)),
            preferred_element_type=jnp.float32,
        ).astype(jnp.bfloat16)

    def tall(name, length, out_ref, place):
        chunks = length // LANES
        size = RANK * chunks
        to_row = lax.broadcasted_iota(jnp.int32, (size, size), 0)
        from_row = lax.broadcasted_iota(jnp.int32, (size, size), 1)
        turned = one_hot(
            (to_row // RANK == from_row % chunks) & (to_row % RANK == from_row // chunks)
        )
        for turn in range(2):
            first = start[name][1] + pl.multiple_of(turn_ref[turn] * size, LANES)
            block = jnp.dot(
                turned, flat_ref[pl.ds(first, size), :], preferred_element_type=jnp.float32
            ).astype(jnp.bfloat16)
            here = place * few + turn * RANK
            for chunk in range(chunks):
                out_ref[here : here + RANK, chunk * LANES : (chunk + 1) * LANES] = block[
                    chunk * RANK : (chunk + 1) * RANK
                ]

    for out_ref, names in ((b_qkv_ref, "qkv"), (b_gu_ref, "gu"), (b_do_ref, "d.o")):
        out_ref[...] = jnp.zeros(out_ref.shape, out_ref.dtype)
        for place, name in enumerate(names):
            if name != ".":
                tall(name, out_ref.shape[1], out_ref, place)


def select(devices, turn_adapter, me, adapters, moments, features, hidden, after):
    shapes = [(features, LANES), (features, LANES), (hidden, LANES)]
    shapes += [(LANES, features), (LANES, hidden), (LANES, features)]
    scratch = []
    if devices:
        shapes.append((adapters.shape[0] // (LANES * devices), LANES))
        shapes.append((devices, 2 * MOMENT_ROWS, LANES))
        scratch.append(pltpu.VMEM((1024, LANES), jnp.float32))
    return pl.pallas_call(
        functools.partial(select_kernel, features, hidden, devices),
        in_specs=[
            pl.BlockSpec(memory_space=pltpu.SMEM),
            pl.BlockSpec(memory_space=pltpu.SMEM),
            pl.BlockSpec(memory_space=pltpu.VMEM),
            pl.BlockSpec(memory_space=pltpu.VMEM),
            pl.BlockSpec(memory_space=pltpu.VMEM),
            pl.BlockSpec(memory_space=pl.ANY),
        ],
        out_specs=[pl.BlockSpec(memory_space=pltpu.VMEM)] * len(shapes),
        out_shape=[jax.ShapeDtypeStruct(shape, jnp.bfloat16) for shape in shapes],
        scratch_shapes=scratch,
        compiler_params=pltpu.CompilerParams(vmem_limit_bytes=VMEM_LIMIT),
        cost_estimate=pl.CostEstimate(
            flops=2**31, bytes_accessed=4 * adapters.shape[0], transcendentals=0
        ),
        name="select",
    )(turn_adapter, me, adapters.reshape(-1, LANES), *moments, after)


def dot(left, right):
    return jnp.dot(left, right, preferred_element_type=jnp.float32)


def turn_mask(meta_ref):
    rows = meta_ref.shape[0]
    lane = lax.broadcasted_iota(jnp.int32, (rows, LANES), 1)
    mask = jnp.where((lane // RANK) % 2 == meta_ref[:, 2:3], 1.0, 0.0)
    return mask, lane // (2 * RANK)


def row_norm(values):
    return lax.rsqrt(jnp.mean(values * values, axis=1, keepdims=True) + NORM_EPS)


def row_norm_back(values, gain, grad):
    scale = row_norm(values)
    unit = values * scale
    grad = grad * gain
    return scale * (grad - unit * jnp.mean(grad * unit, axis=1, keepdims=True))


def head_mean(values, width):
    lanes = values.shape[1]
    rows = lax.broadcasted_iota(jnp.int32, (lanes, lanes), 0)
    columns = lax.broadcasted_iota(jnp.int32, (lanes, lanes), 1)
    ones = one_hot(rows // width == columns // width)
    high = values.astype(jnp.bfloat16)
    low = (values - high.astype(jnp.float32)).astype(jnp.bfloat16)
    return (dot(high, ones) + dot(low, ones)) * (1.0 / width)


def swap_halves(values, width):
    lanes = values.shape[1]
    lane = lax.broadcasted_iota(jnp.int32, values.shape, 1)
    ahead = pltpu.roll(values, lanes - width // 2, 1)
    behind = pltpu.roll(values, width // 2, 1)
    return jnp.where(lane % width < width // 2, ahead, behind)


def widen(table, lanes):
    return jnp.concatenate([table] * (lanes // table.shape[1]), axis=1)


def joined(kept_ref, arrived_ref):
    first = kept_ref.shape[0] - arrived_ref.shape[0]
    kept = kept_ref[...]
    return jnp.concatenate([kept[:first], kept[first:] + arrived_ref[...]], axis=0)


def turned_heads(raw, gain_ref, cosine, sine, width):
    unit = raw * lax.rsqrt(head_mean(raw * raw, width) + NORM_EPS)
    unit = unit * widen(gain_ref[...], raw.shape[1])
    return (unit * cosine + swap_halves(unit, width) * sine).astype(jnp.bfloat16)


def project_own(normed, inner, place, index, weight_ref, b_ref):
    own = jnp.where(place == index, inner, 0.0).astype(jnp.bfloat16)
    return dot(normed, weight_ref[...]) + ADAPTER_SCALE * dot(own, b_ref[...])


def project_key_value_kernel(
    width,
    kept_ref,
    arrived_ref,
    gain_ref,
    wk_ref,
    wv_ref,
    a_ref,
    b_ref,
    meta_ref,
    cos_ref,
    sin_ref,
    k_gain_ref,
    _,
    x_ref,
    normed_ref,
    inner_ref,
    raw_ref,
    k_ref,
    v_ref,
    __,
):
    mask, place = turn_mask(meta_ref)

    @pl.when(pl.program_id(0) == 0)
    def _():
        rows = joined(kept_ref, arrived_ref)
        x_ref[...] = rows
        values = rows.astype(jnp.float32)
        normed = (values * row_norm(values) * gain_ref[...].astype(jnp.float32)).astype(
            jnp.bfloat16
        )
        normed_ref[...] = normed
        inner_ref[...] = (dot(normed, a_ref[...]) * mask).astype(jnp.bfloat16)

    normed = normed_ref[...]
    inner = inner_ref[...].astype(jnp.float32)
    lanes = wk_ref.shape[1]
    cosine, sine = widen(cos_ref[...], lanes), widen(sin_ref[...], lanes)
    key = project_own(normed, inner, place, 1, wk_ref, b_ref)
    raw_ref[...] = key.astype(jnp.bfloat16)
    k_ref[...] = turned_heads(key, k_gain_ref, cosine, sine, width)
    v_ref[...] = project_own(normed, inner, place, 2, wv_ref, b_ref).astype(jnp.bfloat16)


def project_query_kernel(
    width, normed_ref, inner_ref, wq_ref, b_ref, cos_ref, sin_ref, q_gain_ref, raw_ref, q_ref
):
    lanes = wq_ref.shape[1]
    place = lax.broadcasted_iota(jnp.int32, inner_ref.shape, 1) // (2 * RANK)
    cosine, sine = widen(cos_ref[...], lanes), widen(sin_ref[...], lanes)
    inner = inner_ref[...].astype(jnp.float32)
    query = project_own(normed_ref[...], inner, place, 0, wq_ref, b_ref)
    raw_ref[...] = query.astype(jnp.bfloat16)
    q_ref[...] = turned_heads(query, q_gain_ref, cosine, sine, width)


def project_heads(
    kept,
    arrived,
    later,
    gain,
    weights,
    a_qkv,
    b_qkv,
    meta,
    cos_table,
    sin_table,
    q_gain,
    k_gain,
    width,
):
    rows, features = kept.shape
    tile = 256
    grid = (features // tile,)

    def tiled(height):
        return pl.BlockSpec((height, tile), lambda step: (0, step))

    def shape(dtype):
        return jax.ShapeDtypeStruct((rows, features), dtype)

    full, few = whole_block((rows, features)), whole_block((rows, LANES))
    low = shape(jnp.bfloat16)
    anywhere = pl.BlockSpec(memory_space=pl.ANY)
    x, normed, inner, key_raw, key, value, later = pl.pallas_call(
        functools.partial(project_key_value_kernel, width),
        grid=grid,
        in_specs=[full, whole_block(arrived.shape), whole_block((1, features))]
        + [tiled(features)] * 2
        + [whole_block((features, LANES)), tiled(LANES), few, few, few]
        + [whole_block((1, LANES)), anywhere],
        out_specs=[full, full, few] + [tiled(rows)] * 3 + [anywhere],
        input_output_aliases={11: 6},
        out_shape=[
            low,
            low,
            jax.ShapeDtypeStruct((rows, LANES), jnp.bfloat16),
            low,
            low,
            low,
            jax.ShapeDtypeStruct(later.shape, later.dtype),
        ],
        compiler_params=pltpu.CompilerParams(vmem_limit_bytes=VMEM_LIMIT),
        cost_estimate=pl.CostEstimate(
            flops=6 * rows * features * features,
            bytes_accessed=4 * features * features + 14 * rows * features,
            transcendentals=0,
        ),
        name="project_key_value",
    )(
        kept,
        arrived,
        gain[None, :],
        *weights[1:],
        a_qkv,
        b_qkv,
        meta,
        cos_table,
        sin_table,
        k_gain,
        later,
    )
    query_raw, query = pl.pallas_call(
        functools.partial(project_query_kernel, width),
        grid=grid,
        in_specs=[full, few, tiled(features), tiled(LANES), few, few, whole_block((1, LANES))],
        out_specs=[tiled(rows)] * 2,
        out_shape=[low, low],
        compiler_params=pltpu.CompilerParams(vmem_limit_bytes=VMEM_LIMIT),
        cost_estimate=pl.CostEstimate(
            flops=3 * rows * features * features,
            bytes_accessed=2 * features * features + 8 * rows * features,
            transcendentals=0,
        ),
        name="project_query",
    )(normed, inner, weights[0], b_qkv, cos_table, sin_table, q_gain)
    return x, normed, inner, query_raw, key_raw, query, key, value, later


def project_heads_back_kernel(
    count,
    width,
    devices,
    gq_ref,
    *refs,
):
    gk_refs, gv_refs, refs = refs[:count], refs[count : 2 * count], refs[2 * count :]
    (
        q_raw_ref,
        k_raw_ref,
        normed_any,
        inner_ref,
        x_any,
        residual_any,
        gain_ref,
        wq_ref,
        wk_ref,
        wv_ref,
        a_ref,
        b_ref,
        meta_ref,
        cos_ref,
        sin_ref,
        q_gain_ref,
        k_gain_ref,
    ) = refs[:17]
    if devices:
        out_ref, tail_ref, spread_ref = refs[-9:-6]
    else:
        out_ref, tail_ref, grad_a_ref, grad_b_ref = refs[-10:-6]
    total_ref, few_ref, tall_ref, square_ref, held_ref, sems = refs[-6:]
    step = pl.program_id(0)
    lanes = wq_ref.shape[1]
    mask, place = turn_mask(meta_ref)
    cosine, sine = widen(cos_ref[...], lanes), widen(sin_ref[...], lanes)

    def turned_back(grad, raw, head_gain_ref):
        raw = raw.astype(jnp.float32)
        grad = grad * cosine - swap_halves(grad, width) * sine
        scale = lax.rsqrt(head_mean(raw * raw, width) + NORM_EPS)
        unit = raw * scale
        grad = grad * widen(head_gain_ref[...], lanes)
        return (scale * (grad - unit * head_mean(grad * unit, width))).astype(jnp.bfloat16)

    def summed(term_refs):
        total = term_refs[0][...].astype(jnp.float32)
        for ref in term_refs[1:]:
            total = total + ref[...].astype(jnp.float32)
        return total

    copies = [
        pltpu.make_async_copy(source, held_ref.at[index], sems.at[index])
        for index, source in enumerate((normed_any, x_any, residual_any))
    ]

    @pl.when(step == 0)
    def _():
        for copy in copies:
            copy.start()
        total_ref[...] = jnp.zeros(total_ref.shape, jnp.float32)
        few_ref[...] = jnp.zeros(few_ref.shape, jnp.float32)

    inner_turned = jnp.transpose(inner_ref[...].astype(jnp.float32) * ADAPTER_SCALE).astype(
        jnp.bfloat16
    )
    errors = [
        turned_back(gq_ref[...].astype(jnp.float32), q_raw_ref[...], q_gain_ref),
        turned_back(summed(gk_refs), k_raw_ref[...], k_gain_ref),
        summed(gv_refs).astype(jnp.bfloat16),
    ]
    total = total_ref[...]
    few = few_ref[...]
    wide = 2 * RANK
    for index, (error, weight_ref) in enumerate(zip(errors, (wq_ref, wk_ref, wv_ref))):
        total = total + contract_last(error, weight_ref[...])
        few = few + jnp.where(place == index, contract_last(error, b_ref[...]), 0.0)
        here = slice(index * wide, (index + 1) * wide)
        grad_b = dot(inner_turned[here], error)
        for part in range(lanes // LANES):
            square_ref[part, here, :] = grad_b[:, part * LANES : (part + 1) * LANES]
    square_ref[:, 3 * wide :, :] = jnp.zeros(
        (lanes // LANES, LANES - 3 * wide, LANES), jnp.float32
    )
    if devices:
        chunks = held_ref.shape[2] // LANES
        for index in range(lanes // LANES):
            for first, starts in ((wide, (0, wide)), (wide + RANK, (2 * wide, 3 * wide))):
                spread_square_to(
                    spread_ref,
                    first,
                    square_ref,
                    starts,
                    step * (lanes // LANES) + index,
                    chunks,
                    index,
                )
    else:
        for part in range(lanes // LANES):
            grad_b_ref[:, part * LANES : (part + 1) * LANES] = square_ref[part].astype(
                jnp.bfloat16
            )
    total_ref[...] = total
    few_ref[...] = few

    @pl.when(step == pl.num_programs(0) - 1)
    def _():
        low = (ADAPTER_SCALE * few_ref[...] * mask).astype(jnp.bfloat16)
        low_turned = jnp.transpose(low.astype(jnp.float32)).astype(jnp.bfloat16)
        for copy in copies:
            copy.wait()
        tall_ref[...] = jnp.transpose(dot(low_turned, held_ref[0]))
        if devices:
            spread_wide_to(spread_ref, 0, tall_ref)
        else:
            grad_a_ref[...] = tall_ref[...].astype(jnp.bfloat16)
        grad = total_ref[...] + contract_last(low, a_ref[...])
        out = held_ref[2].astype(jnp.float32) + row_norm_back(
            held_ref[1].astype(jnp.float32), gain_ref[...].astype(jnp.float32), grad
        )
        out_ref[...] = out.astype(jnp.bfloat16)
        tail_ref[...] = out[out.shape[0] - tail_ref.shape[0] :].astype(jnp.bfloat16)


def project_heads_back(
    devices,
    after,
    grad_query,
    key_terms,
    value_terms,
    query_raw,
    key_raw,
    normed,
    inner,
    rows_in,
    grad_residual,
    gain,
    weights,
    a_qkv,
    b_qkv,
    meta,
    cos_table,
    sin_table,
    q_gain,
    k_gain,
    width,
):
    rows, features = rows_in.shape
    count = len(key_terms)
    tile = 256

    def tiled(height):
        return pl.BlockSpec((height, tile), lambda step: (0, step))

    full = whole_block((rows, features))
    anywhere = pl.BlockSpec(memory_space=pl.ANY)
    if devices:
        spread = (devices, 4 * RANK, LANES)
        grad_specs = [whole_block(spread)]
        grad_shapes = [jax.ShapeDtypeStruct(spread, jnp.bfloat16)]
    else:
        grad_specs = [whole_block((features, LANES)), tiled(LANES)]
        grad_shapes = [
            jax.ShapeDtypeStruct((features, LANES), jnp.bfloat16),
            jax.ShapeDtypeStruct((LANES, features), jnp.bfloat16),
        ]
    return pl.pallas_call(
        functools.partial(project_heads_back_kernel, count, width, devices),
        grid=(features // tile,),
        in_specs=[tiled(rows)] * (3 + 2 * count)
        + [anywhere, whole_block((rows, LANES)), anywhere, anywhere, whole_block((1, features))]
        + [tiled(features)] * 3
        + [whole_block((features, LANES)), tiled(LANES), whole_block(meta.shape)]
        + [whole_block((rows, LANES))] * 2
        + [whole_block((1, LANES))] * 2
        + [anywhere] * len(after),
        out_specs=[full, whole_block((rows // 2, features)), *grad_specs],
        out_shape=[
            jax.ShapeDtypeStruct((rows, features), jnp.bfloat16),
            jax.ShapeDtypeStruct((rows // 2, features), jnp.bfloat16),
            *grad_shapes,
        ],
        scratch_shapes=[
            pltpu.VMEM((rows, features), jnp.float32),
            pltpu.VMEM((rows, LANES), jnp.float32),
            pltpu.VMEM((features, LANES), jnp.float32),
            pltpu.VMEM((tile // LANES, LANES, LANES), jnp.float32),
            pltpu.VMEM((3, rows, features), jnp.bfloat16),
            pltpu.SemaphoreType.DMA((3,)),
        ],
        compiler_params=pltpu.CompilerParams(vmem_limit_bytes=VMEM_LIMIT),
        cost_estimate=pl.CostEstimate(
            flops=8 * rows * features * features,
            bytes_accessed=6 * features * features + 30 * rows * features,
            transcendentals=0,
        ),
        name="project_heads_back",
    )(
        grad_query,
        *key_terms,
        *value_terms,
        query_raw,
        key_raw,
        normed,
        inner,
        rows_in,
        grad_residual,
        gain[None, :],
        *weights,
        a_qkv,
        b_qkv,
        meta,
        cos_table,
        sin_table,
        q_gain,
        k_gain,
        *after,
    )


def spread_wide_to(spread_ref, first, held_ref):
    devices = spread_ref.shape[0]
    count = held_ref.shape[0] // devices
    for device in range(devices):
        spread_ref[device, first : first + count, :] = held_ref[
            pl.ds(device, count, stride=devices), :
        ].astype(jnp.bfloat16)


def spread_square_to(spread_ref, first, held_ref, starts, chunk, chunks, index):
    classes = spread_ref.shape[0] // chunks
    count = 2 * RANK // classes
    for part in range(classes):
        rows = [
            held_ref[index, pl.ds(start + part, count, stride=classes), :]
            for start in starts
        ]
        spread_ref[part * chunks + chunk, first : first + 2 * count, :] = jnp.concatenate(
            rows, axis=0
        ).astype(jnp.bfloat16)


def feed_forward_kernel(
    devices,
    turn_ref,
    att_ref,
    x_ref,
    kept_ref,
    arrived_ref,
    gain_ref,
    wo_ref,
    wg_ref,
    wu_ref,
    wd_ref,
    a_guo_ref,
    a_down_ref,
    b_gu_ref,
    b_do_ref,
    meta_ref,
    out_ref,
    tail_ref,
    grad_res_ref,
    grad_att_ref,
    *refs,
):
    if devices:
        spread_ref, refs = refs[0], refs[1:]
    else:
        (grad_a_ref, grad_ad_ref, grad_bgu_ref, grad_bdo_ref), refs = refs[:4], refs[4:]
    (
        res_ref,
        hidden_ref,
        inner_ref,
        inner_turned_ref,
        sum_ref,
        grad_hidden_ref,
        inner_down_ref,
        few_ref,
        few_down_ref,
        few_down_turned_ref,
        down_ref,
        tall_ref,
        square_ref,
        e_ref,
    ) = refs
    step = pl.program_id(0)
    mask, place = turn_mask(meta_ref)
    tile = wg_ref.shape[1]
    features = wo_ref.shape[0]
    wide = 2 * RANK

    def only(values, index):
        return jnp.where(place == index, values, 0.0).astype(jnp.bfloat16)

    def turn(values):
        return jnp.transpose(values.astype(jnp.float32)).astype(jnp.bfloat16)

    @pl.when(step == 0)
    def _():
        e_ref[...] = joined(kept_ref, arrived_ref)
        att = att_ref[...]
        inner_out = dot(att, a_guo_ref[...]) * mask
        res = (
            x_ref[...].astype(jnp.float32)
            + dot(att, wo_ref[...])
            + ADAPTER_SCALE * dot(only(inner_out, 2), b_do_ref[...])
        )
        res_ref[...] = res
        hidden = (res * row_norm(res) * gain_ref[...].astype(jnp.float32)).astype(jnp.bfloat16)
        hidden_ref[...] = hidden
        inner = dot(hidden, a_guo_ref[...]) * mask
        inner = jnp.where(place == 2, inner_out, inner).astype(jnp.bfloat16)
        inner_ref[...] = inner
        inner_turned_ref[...] = turn(inner.astype(jnp.float32) * ADAPTER_SCALE)
        few_down = only(ADAPTER_SCALE * contract_last(e_ref[...], b_do_ref[...]) * mask, 0)
        few_down_ref[...] = few_down
        few_down_turned_ref[...] = turn(few_down)[:wide]
        sum_ref[...] = jnp.zeros(sum_ref.shape, jnp.float32)
        grad_hidden_ref[...] = jnp.zeros(grad_hidden_ref.shape, jnp.float32)
        inner_down_ref[...] = jnp.zeros(inner_down_ref.shape, jnp.float32)
        few_ref[...] = jnp.zeros(few_ref.shape, jnp.float32)

    hidden = hidden_ref[...]
    inner = inner_ref[...].astype(jnp.float32)
    gate_weight, up_weight, down_weight = wg_ref[...], wu_ref[...], wd_ref[...]
    b_tile = b_gu_ref[...]
    gate = dot(hidden, gate_weight) + ADAPTER_SCALE * dot(only(inner, 0), b_tile)
    up = dot(hidden, up_weight) + ADAPTER_SCALE * dot(only(inner, 1), b_tile)
    grad_act = contract_last(e_ref[...], down_weight) + contract_last(
        few_down_ref[...], a_down_ref[...]
    )
    sigmoid = 1.0 / (1.0 + jnp.exp(-gate))
    silu = gate * sigmoid
    act = (silu * up).astype(jnp.bfloat16)
    grad_up = (grad_act * silu).astype(jnp.bfloat16)
    grad_gate = (grad_act * up * (sigmoid * (1.0 + gate * (1.0 - sigmoid)))).astype(jnp.bfloat16)
    sum_ref[...] += dot(act, down_weight)
    inner_down_ref[...] += dot(act, a_down_ref[...])
    grad_hidden_ref[...] += contract_last(grad_gate, gate_weight) + contract_last(
        grad_up, up_weight
    )
    few_ref[...] += jnp.where(
        place == 0, contract_last(grad_gate, b_tile), contract_last(grad_up, b_tile)
    )
    grad_b_gate = dot(inner_turned_ref[:wide, :], grad_gate).astype(jnp.bfloat16)
    grad_b_up = dot(inner_turned_ref[wide : 2 * wide, :], grad_up).astype(jnp.bfloat16)
    if devices:
        for index in range(tile // LANES):
            device = step * (tile // LANES) + index
            chunk = slice(index * LANES, (index + 1) * LANES)
            spread_ref[device, 2 * wide : 3 * wide, :] = grad_b_gate[:, chunk]
            spread_ref[device, 3 * wide : 4 * wide, :] = grad_b_up[:, chunk]
    else:
        grad_bgu_ref[:wide, :] = grad_b_gate
        grad_bgu_ref[wide:, :] = grad_b_up
    per_quarter = features // tile
    down_ref[
        pl.ds(pl.multiple_of((step // per_quarter) * wide, wide), wide),
        pl.ds(pl.multiple_of((step % per_quarter) * tile, tile), tile),
    ] = dot(few_down_turned_ref[...], act)

    @pl.when(step == pl.num_programs(0) - 1)
    def _():
        grads_out = e_ref[...]
        inner_down = only(inner_down_ref[...] * mask, 0)
        res = res_ref[...]
        out = (res + sum_ref[...] + ADAPTER_SCALE * dot(inner_down, b_do_ref[...])).astype(
            jnp.bfloat16
        )
        out_ref[...] = out
        tail_ref[...] = out[out.shape[0] - tail_ref.shape[0] :]
        few = jnp.where(place < 2, ADAPTER_SCALE * few_ref[...] * mask, 0.0).astype(jnp.bfloat16)
        grad_hidden = grad_hidden_ref[...] + contract_last(few, a_guo_ref[...])
        grad_res = grads_out.astype(jnp.float32) + row_norm_back(
            res, gain_ref[...].astype(jnp.float32), grad_hidden
        )
        low = grad_res.astype(jnp.bfloat16)
        grad_res_ref[...] = low
        few_out = only(ADAPTER_SCALE * contract_last(low, b_do_ref[...]) * mask, 2)
        grad_att_ref[...] = (
            contract_last(low, wo_ref[...]) + contract_last(few_out, a_guo_ref[...])
        ).astype(jnp.bfloat16)
        grad_a = dot(turn(few), hidden_ref[...]) + dot(turn(few_out), att_ref[...])
        inner_out = only(inner_ref[...].astype(jnp.float32), 2)
        grad_b = ADAPTER_SCALE * (
            dot(turn(inner_down), grads_out) + dot(turn(inner_out), low)
        )
        if devices:
            lane = lax.broadcasted_iota(jnp.int32, (features, LANES), 1)
            told = jnp.where(
                lane == 3 * wide, turn_ref[0], jnp.where(lane == 3 * wide + 1, turn_ref[1], 0)
            )
            tall_ref[...] = jnp.transpose(grad_a) + told.astype(jnp.float32)
            spread_wide_to(spread_ref, 0, tall_ref)
            tall_ref[...] = jnp.transpose(down_ref[...])
            spread_wide_to(spread_ref, wide, tall_ref)
            chunks = features // LANES
            for chunk in range(chunks):
                square_ref[chunk] = grad_b[:, chunk * LANES : (chunk + 1) * LANES]
                spread_square_to(
                    spread_ref, 4 * wide, square_ref, (0, 2 * wide), chunk, chunks, chunk
                )
        else:
            grad_a_ref[...] = jnp.transpose(grad_a).astype(jnp.bfloat16)
            grad_ad_ref[...] = jnp.transpose(down_ref[...]).astype(jnp.bfloat16)
            grad_bdo_ref[...] = grad_b.astype(jnp.bfloat16)


def feed_forward(
    devices,
    turn_adapter,
    attended,
    rows_in,
    kept,
    arrived,
    gain,
    weights,
    selected,
    meta,
):
    rows, features = rows_in.shape
    hidden = weights[1].shape[1]
    tile = 512
    full = whole_block((rows, features))
    square = whole_block((features, features))
    column = pl.BlockSpec((features, tile), lambda step: (0, step))

    def shape(height, length, dtype):
        return jax.ShapeDtypeStruct((height, length), dtype)

    if devices:
        spread = (devices, 9 * RANK, LANES)
        grad_specs = [whole_block(spread)]
        grad_shapes = [jax.ShapeDtypeStruct(spread, jnp.bfloat16)]
    else:
        grad_specs = [
            whole_block((features, LANES)),
            whole_block((features, LANES)),
            pl.BlockSpec((4 * RANK, tile), lambda step: (0, step)),
            whole_block((LANES, features)),
        ]
        grad_shapes = [
            shape(features, LANES, jnp.bfloat16),
            shape(features, LANES, jnp.bfloat16),
            shape(4 * RANK, hidden, jnp.bfloat16),
            shape(LANES, features, jnp.bfloat16),
        ]
    return pl.pallas_call(
        functools.partial(feed_forward_kernel, devices),
        grid=(hidden // tile,),
        in_specs=[
            pl.BlockSpec(memory_space=pltpu.SMEM),
            full,
            full,
            full,
            whole_block(arrived.shape),
            whole_block((1, features)),
            square,
            column,
            column,
            pl.BlockSpec((tile, features), lambda step: (step, 0)),
            whole_block((features, LANES)),
            pl.BlockSpec((tile, LANES), lambda step: (step, 0)),
            pl.BlockSpec((LANES, tile), lambda step: (0, step)),
            whole_block((LANES, features)),
            whole_block(meta.shape),
        ],
        out_specs=[
            full,
            whole_block(arrived.shape),
            full,
            full,
            *grad_specs,
        ],
        out_shape=[
            shape(rows, features, jnp.bfloat16),
            shape(*arrived.shape, jnp.bfloat16),
            shape(rows, features, jnp.bfloat16),
            shape(rows, features, jnp.bfloat16),
            *grad_shapes,
        ],
        scratch_shapes=[
            pltpu.VMEM((rows, features), jnp.float32),
            pltpu.VMEM((rows, features), jnp.bfloat16),
            pltpu.VMEM((rows, LANES), jnp.bfloat16),
            pltpu.VMEM((LANES, rows), jnp.bfloat16),
            pltpu.VMEM((rows, features), jnp.float32),
            pltpu.VMEM((rows, features), jnp.float32),
            pltpu.VMEM((rows, LANES), jnp.float32),
            pltpu.VMEM((rows, LANES), jnp.float32),
            pltpu.VMEM((rows, LANES), jnp.bfloat16),
            pltpu.VMEM((2 * RANK, rows), jnp.bfloat16),
            pltpu.VMEM((LANES, features), jnp.float32),
            pltpu.VMEM((features, LANES), jnp.float32),
            pltpu.VMEM((features // LANES, LANES, LANES), jnp.float32),
            pltpu.VMEM((rows, features), jnp.bfloat16),
        ],
        compiler_params=pltpu.CompilerParams(vmem_limit_bytes=VMEM_LIMIT),
        cost_estimate=pl.CostEstimate(
            flops=14 * rows * features * hidden,
            bytes_accessed=8 * features * hidden + 16 * rows * features,
            transcendentals=0,
        ),
        name="feed_forward",
    )(
        turn_adapter,
        attended,
        rows_in,
        kept,
        arrived,
        gain[None, :],
        *weights,
        *selected,
        meta,
    )


def settle_owned(grads, moment1, moment2, devices):
    grads = lax.all_to_all(grads, ALL, 0, 0, tiled=True)
    grads = grads[:, : moment1.shape[0] // (LANES * devices)]
    grad_shard = jnp.transpose(grads, (1, 0, 2)).reshape(-1).astype(jnp.float32)
    current = jnp.zeros((), jnp.float32)
    first_moment, second_moment, _ = adam(current, moment1, moment2, grad_shard)
    return grad_shard, first_moment, second_moment


def per_device(
    tokens,
    cotangent,
    variate,
    seq_len,
    seq_adapter,
    block_order,
    attn_gain,
    ffn_gain,
    q_gain,
    k_gain,
    attn_bias,
    query_weight,
    key_weight,
    value_weight,
    output_weight,
    gate_weight,
    up_weight,
    down_weight,
    adapters,
    moment1,
    moment2,
):
    groups = axis_count(GROUP)
    member = lax.axis_index(GROUP)
    row_count, feature_width = tokens.shape
    hidden_width = gate_weight.shape[1]
    head_width = q_gain.shape[0]
    half_devices = groups // 2
    segments = seq_len.shape[1]
    chosen, back, turn_adapter, key_metas = plan(
        groups, row_count, member[None], seq_len, seq_adapter, block_order, variate
    )
    meta = key_metas[0]
    cos_table, sin_table = rope_tables(meta[:, 3], head_width)
    axes = ALL
    devices = axis_count(PACKS) * groups
    even = spreads_evenly(devices, groups, feature_width, hidden_width, adapters.shape[0])
    spread = devices if even else 0
    q_gain_row = head_gain(q_gain)
    k_gain_row = head_gain(k_gain)


    held = (gather_half(tokens, groups), gather_half(cotangent, groups))
    sent_tokens, sent_grads = pick(chosen, row_count, row_count // 2, *held)
    arrived_tokens = to_other_half(sent_tokens, groups)
    a_qkv, a_guo, a_down, b_qkv, b_gu, b_do, *spread_state = select(
        spread,
        turn_adapter,
        lax.axis_index(axes)[None],
        adapters,
        (moment1.reshape(-1, LANES), moment2.reshape(-1, LANES)),
        feature_width,
        hidden_width,
        sent_tokens,
    )
    if even:
        params, moments = spread_state
        moments = lax.all_to_all(moments, axes, 0, 0, tiled=True)
    kept_tokens, kept_grads = pick(chosen, 0, row_count, *held)
    (
        my_tokens,
        normed,
        inner,
        query_raw,
        key_raw,
        query_low,
        key_low,
        value_low,
        sent_grads,
    ) = project_heads(
        kept_tokens,
        arrived_tokens,
        sent_grads,
        attn_gain,
        (query_weight, key_weight, value_weight),
        a_qkv,
        b_qkv,
        meta,
        cos_table,
        sin_table,
        q_gain_row,
        k_gain_row,
        head_width,
    )
    arrived_grads = to_other_half(sent_grads, groups)
    keys = gather_half(key_low, groups)
    values = gather_half(value_low, groups)
    attended_low, log_total = attend(
        attn_bias, query_low, meta, keys, values, key_metas, segments, head_width
    )
    layer_rows, layer_tail, grad_residual, grad_attended, *forward_grads = feed_forward(
        spread,
        turn_adapter,
        attended_low,
        my_tokens,
        kept_grads,
        arrived_grads,
        ffn_gain,
        (output_weight, gate_weight, up_weight, down_weight),
        (a_guo, a_down, b_gu, b_do),
        meta,
    )
    layer_back = to_other_half(layer_tail, groups)
    layer_held = gather_half(layer_rows, groups) + gather_half(layer_back, groups)

    results = attend_back(
        attn_bias,
        query_low,
        meta,
        log_total,
        attended_low,
        grad_attended,
        keys,
        values,
        key_metas,
        segments,
        head_width,
    )
    after = []
    if even:
        total_rows = adapters.shape[0] // LANES
        late_rows = 6 * feature_width // devices
        early = lax.all_to_all(forward_grads[0], axes, 0, 0, tiled=True)
        early_grad, early_new, late_m1, late_m2, tall, square = settle_early(
            early, moments, params, late_rows, [results[0]]
        )
        early_outer = lax.all_to_all(early_new, "far", 0, 0, tiled=True)
        swap = [(0, 1), (1, 0)]
        early_near = lax.ppermute(early_outer, "near", swap)
        early_half = lax.ppermute(early_outer, "half", swap)
        after = [early_new, layer_back]
    grad_query = results[0]
    grad_keys = results[1 : 1 + half_devices]
    grad_values = results[1 + half_devices :]
    key_terms, value_terms = [grad_keys[0]], [grad_values[0]]
    for shift in range(1, half_devices):
        back_shift = half_devices - shift
        key_terms.append(within_half(grad_keys[shift], back_shift, groups))
        value_terms.append(within_half(grad_values[shift], back_shift, groups))
    grad_rows, grad_tail, *back_grads = project_heads_back(
        spread,
        after,
        grad_query,
        key_terms,
        value_terms,
        query_raw,
        key_raw,
        normed,
        inner,
        my_tokens,
        grad_residual,
        attn_gain,
        (query_weight, key_weight, value_weight),
        a_qkv,
        b_qkv,
        meta,
        cos_table,
        sin_table,
        q_gain_row,
        k_gain_row,
        head_width,
    )
    def bring_back(tail):
        return gather_half(grad_rows, groups) + gather_half(to_other_half(tail, groups), groups)

    if not even:
        grads = (*back_grads, *forward_grads)
        column = jnp.arange(2 * RANK, dtype=jnp.int32)
        few_choice = one_hot(
            jnp.arange(LANES, dtype=jnp.int32)[:, None]
            == (jnp.repeat(turn_adapter, RANK) * RANK + column % RANK)[None, :]
        )
        settled = settle_shards(grads, few_choice, adapters, moment1, moment2, groups)
        layer_out = pick(back, 0, row_count, layer_held)[0]
        input_grad = pick(back, 0, row_count, bring_back(grad_tail))[0]
        return (layer_out, input_grad) + settled
    late = lax.all_to_all(back_grads[0], axes, 0, 0, tiled=True)
    layer_out = pick(back, 0, row_count, layer_held)[0]
    own_grads, late_new, grad_tail = settle_late(
        tall, square, late, params, late_m1, late_m2, early_grad, grad_tail, [layer_out, early_near, early_half]
    )
    late_outer = lax.all_to_all(late_new, PACKS, 0, 0, tiled=True)
    late_pieces = gather_inner(late_outer, groups)
    input_grad, own_grads = pick(
        back, 0, row_count, bring_back(grad_tail), later=[own_grads]
    )
    cut_rows = early_outer.shape[1] // 2
    early_far = [
        lax.ppermute(early_near[:, :cut_rows], "half", swap),
        lax.ppermute(early_half[:, cut_rows:], "near", swap),
    ]
    early_pieces = [[early_outer], [early_near], [early_half], early_far]
    early_pieces += [
        [lax.ppermute(part, "core", swap) for part in piece] for piece in early_pieces
    ]
    far = jnp.arange(lax.axis_size("far"), dtype=jnp.int32)
    near, half, core = [lax.axis_index(name) for name in ALL[1:]]
    early_device = jnp.concatenate(
        [
            ((far * 2 + (near ^ flip_near)) * 2 + (half ^ flip_half)) * 2 + (core ^ flip_core)
            for flip_core in (0, 1)
            for flip_near, flip_half in ((0, 0), (1, 0), (0, 1), (1, 1))
        ]
    )
    late_pieces = [[piece] for piece in late_pieces]
    order = placing_order(piece_devices(groups, devices), 16)
    adapters_new = assemble(
        placing_order(early_device, 16),
        early_pieces,
        total_rows,
        late_rows,
        None,
        [input_grad, late_pieces[1][0]],
    )
    adapters_new = assemble(order, late_pieces, total_rows, 0, adapters_new, [])
    owned = settle_owned(own_grads, moment1, moment2, devices)
    return (layer_out, input_grad, *owned, adapters_new.reshape(-1))


def solution(mesh):
    packs, groups = mesh.shape["dp"], mesh.shape["group"]
    cut = jax.sharding.Mesh(mesh.devices.reshape(packs // 2, 2, groups // 2, 2), ALL)
    in_specs = (
        P(ALL, None),
        P(ALL, None),
        P(PACKS),
        P(PACKS, None),
        P(PACKS, None),
        P(PACKS, None),
        P(),
        P(),
        P(),
        P(),
        P(),
        P(),
        P(),
        P(),
        P(),
        P(),
        P(),
        P(),
        P(),
        P(ALL),
        P(ALL),
    )
    out_specs = (
        P(ALL, None),
        P(ALL, None),
        P(ALL),
        P(ALL),
        P(ALL),
        P(),
    )
    return jax.shard_map(
        per_device, mesh=cut, in_specs=in_specs, out_specs=out_specs, check_vma=False
    )
```

```python
import functools

import jax
import jax.numpy as jnp
import numpy as np
from jax import lax
from jax.experimental import pallas as pl
from jax.experimental.pallas import tpu as pltpu
from jax.sharding import PartitionSpec as P

RANK = 16
ADAPTERS = 8
NORM_EPS = 1e-06
ADAPTER_SCALE = 2.0
ROPE_BASE = 10000.0
MASKED = -1e30
LEARN_RATE = 0.01
BETA_ONE = 0.9
BETA_TWO = 0.999
ADAM_EPS = 1e-08
WEIGHT_DECAY = 0.01
update_count = 10.0
VARIATES = 4
VMEM_LIMIT = 56 * 1024 * 1024
EXACT_PARTS = 3


def contract_last(left, right):
    return lax.dot_general(
        left, right, (((1,), (1,)), ((), ())), preferred_element_type=jnp.float32
    )


def exact_parts(values):
    parts = []
    for _ in range(EXACT_PARTS):
        part = values.astype(jnp.bfloat16).astype(jnp.float32)
        parts.append(part)
        values = values - part
    return parts


def parts_in_lanes(values, first, column):
    result = jnp.zeros(values.shape, jnp.float32)
    for index, part in enumerate(exact_parts(values)):
        result = jnp.where(column == first + index, part, result)
    return result


def note_keys(side_ref, kmeta_refs, column, lane, width, segments):
    seg_column = column - EXACT_PARTS * VARIATES
    ones = (seg_column >= segments) & (seg_column < segments + EXACT_PARTS)
    for block, kmeta_ref in enumerate(kmeta_refs):
        one = (column < EXACT_PARTS * VARIATES) & ((column % VARIATES) == kmeta_ref[:, 0:1])
        in_seg = (seg_column >= 0) & (seg_column < segments) & (seg_column == kmeta_ref[:, 1:2])
        for head in range(2):
            outside = (lane // width) != head
            side_ref[head, block] = one_hot((one | in_seg | ones) & outside)


def note_queries(match_ref, apart_ref, qmeta_ref, column, segments):
    same = (column < EXACT_PARTS * VARIATES) & ((column % VARIATES) == qmeta_ref[:, 0:1])
    match_ref[...] = jnp.where(same, 1.0, 0.0)
    seg_column = column - EXACT_PARTS * VARIATES
    apart = (seg_column >= 0) & (seg_column < segments) & (seg_column != qmeta_ref[:, 1:2])
    apart_ref[...] = jnp.where(apart, MASKED, 0.0)


def bias_rows(bias_ref, head, column):
    rows = []
    for which in range(2):
        row = jnp.zeros(column.shape, jnp.float32)
        value = jnp.full(column.shape, bias_ref[which, head], jnp.float32)
        for index, part in enumerate(exact_parts(value)):
            row = jnp.where(column // VARIATES == index, part, row)
        rows.append(row)
    return rows


def query_side(match_ref, apart_ref, bias_ref, head, column):
    same, other = bias_rows(bias_ref, head, column[:1])
    return jnp.where(match_ref[...] > 0.0, same, other) + apart_ref[...]


def head_lanes(head, width, lanes):
    lane = lax.broadcasted_iota(jnp.int32, (1, lanes), 1)
    return jnp.where(lane // width == head, 1.0, 0.0).astype(jnp.bfloat16)


def attend_kernel(key_blocks, segments, width, bias_ref, query_ref, qmeta_ref, *refs):
    key_refs, value_refs, kmeta_refs = (
        refs[:key_blocks],
        refs[key_blocks : 2 * key_blocks],
        refs[2 * key_blocks : 3 * key_blocks],
    )
    out_ref, total_ref, side_ref, match_ref, apart_ref = refs[3 * key_blocks :]
    pair = pl.program_id(0)
    rows, lanes = query_ref.shape
    lane = lax.broadcasted_iota(jnp.int32, (rows, lanes), 1)
    column = lane % width

    @pl.when(pair == 0)
    def _():
        note_keys(side_ref, kmeta_refs, column, lane, width, segments)
        note_queries(match_ref, apart_ref, qmeta_ref, column, segments)

    scaled = query_ref[...].astype(jnp.float32) * width ** (-0.5)
    results = []
    for head in range(lanes // width):
        extension = query_side(
            match_ref, apart_ref, bias_ref, pair * (lanes // width) + head, column
        )
        left = jnp.where((lane // width) == head, scaled, extension).astype(jnp.bfloat16)
        inside = head_lanes(head, width, lanes)
        outside = head_lanes(1 - head, width, lanes)
        total = jnp.zeros((rows, lanes), jnp.float32)
        for block in range(key_blocks):
            right = key_refs[block][...] * inside + side_ref[head, block]
            weights = jnp.exp(contract_last(left, right)).astype(jnp.bfloat16)
            total = total + dot(weights, value_refs[block][...] * inside + outside)
        results.append(total)
    first = (lane // width) == 0
    numerator = jnp.where(first, results[0], results[1])
    crossed = jnp.where(first, results[1], results[0])
    out_ref[...] = (numerator / pltpu.roll(crossed, width, 1)).astype(jnp.bfloat16)
    total_ref[...] = jnp.log(crossed)


def lane_block(rows, lanes):
    return pl.BlockSpec((rows, lanes), lambda pair: (0, pair))


def whole_block(shape):
    return pl.BlockSpec(shape, lambda pair: (0,) * len(shape))


def attend(attn_bias, query_low, query_meta, keys, values, key_metas, segments, width):
    rows, features = query_low.shape
    lanes = 2 * width
    count = len(keys)
    flops = 4 * rows * rows * count * features
    return pl.pallas_call(
        functools.partial(attend_kernel, count, segments, width),
        grid=(features // lanes,),
        in_specs=[
            pl.BlockSpec(memory_space=pltpu.SMEM),
            lane_block(rows, lanes),
            whole_block(query_meta.shape),
        ]
        + [lane_block(rows, lanes)] * (2 * count)
        + [whole_block(query_meta.shape)] * count,
        out_specs=[lane_block(rows, lanes)] * 2,
        out_shape=[
            jax.ShapeDtypeStruct((rows, features), jnp.bfloat16),
            jax.ShapeDtypeStruct((rows, features), jnp.float32),
        ],
        scratch_shapes=[
            pltpu.VMEM((2, count, rows, lanes), jnp.bfloat16),
            pltpu.VMEM((rows, lanes), jnp.float32),
            pltpu.VMEM((rows, lanes), jnp.float32),
        ],
        compiler_params=pltpu.CompilerParams(vmem_limit_bytes=VMEM_LIMIT),
        cost_estimate=pl.CostEstimate(
            flops=flops, bytes_accessed=12 * rows * features, transcendentals=0
        ),
        name="attend",
    )(attn_bias, query_low, query_meta, *keys, *values, *key_metas)


def attend_back_kernel(
    key_blocks,
    segments,
    width,
    bias_ref,
    query_ref,
    qmeta_ref,
    total_ref,
    attended_ref,
    grad_ref,
    *refs,
):
    key_refs, value_refs, kmeta_refs = (
        refs[:key_blocks],
        refs[key_blocks : 2 * key_blocks],
        refs[2 * key_blocks : 3 * key_blocks],
    )
    results = refs[len(refs) - 4 - 2 * key_blocks :]
    grad_query_ref = results[0]
    grad_key_refs = results[1 : key_blocks + 1]
    grad_value_refs = results[key_blocks + 1 : 2 * key_blocks + 1]
    side_ref, match_ref, apart_ref = results[2 * key_blocks + 1 :]
    pair = pl.program_id(0)
    rows, lanes = query_ref.shape
    lane = lax.broadcasted_iota(jnp.int32, (rows, lanes), 1)
    column = lane % width
    ones_at = EXACT_PARTS * VARIATES + segments

    @pl.when(pair == 0)
    def _():
        note_keys(side_ref, kmeta_refs, column, lane, width, segments)
        note_queries(match_ref, apart_ref, qmeta_ref, column, segments)

    scaled = query_ref[...].astype(jnp.float32) * width ** (-0.5)
    scaled_low = scaled.astype(jnp.bfloat16)
    grad_low = grad_ref[...]
    grad = grad_low.astype(jnp.float32)
    overlap = grad * attended_ref[...].astype(jnp.float32)
    square_row = lax.broadcasted_iota(jnp.int32, (lanes, lanes), 0)
    square_column = lax.broadcasted_iota(jnp.int32, (lanes, lanes), 1)
    across = one_hot(square_row // width != square_column // width)
    high = overlap.astype(jnp.bfloat16)
    rest = (overlap - high.astype(jnp.float32)).astype(jnp.bfloat16)
    dot_side = parts_in_lanes(-(dot(high, across) + dot(rest, across)), ones_at, column)
    total_side = parts_in_lanes(-total_ref[...], ones_at, column)
    grad_query_parts = []
    grad_keys = [[] for _ in range(key_blocks)]
    grad_values = [[] for _ in range(key_blocks)]
    for head in range(lanes // width):
        inside = (lane // width) == head
        extension = total_side + query_side(
            match_ref, apart_ref, bias_ref, pair * (lanes // width) + head, column
        )
        right = jnp.where(inside, scaled, extension).astype(jnp.bfloat16)
        grad_right = jnp.where(inside, grad, dot_side).astype(jnp.bfloat16)
        own_lanes = head_lanes(head, width, lanes)
        turned = jnp.zeros((width, rows), jnp.float32)
        for block in range(key_blocks):
            key = key_refs[block][...]
            side = side_ref[head, block]
            prob = jnp.exp(contract_last(key * own_lanes + side, right))
            value_left = value_refs[block][...] * own_lanes + side
            grad_score = (prob * contract_last(value_left, grad_right)).astype(jnp.bfloat16)
            grad_values[block].append(dot(prob.astype(jnp.bfloat16), grad_low))
            grad_keys[block].append(dot(grad_score, scaled_low))
            key_turned = jnp.transpose(key)[head * width : (head + 1) * width]
            turned = turned + dot(key_turned, grad_score)
        grad_query_parts.append(turned)
    first = (lane // width) == 0
    stacked = jnp.concatenate(grad_query_parts, axis=0) * width ** (-0.5)
    grad_query_ref[...] = jnp.transpose(stacked).astype(jnp.bfloat16)
    for block in range(key_blocks):
        grad_key_refs[block][...] = jnp.where(first, *grad_keys[block]).astype(
            grad_key_refs[block].dtype
        )
        grad_value_refs[block][...] = jnp.where(first, *grad_values[block]).astype(
            grad_value_refs[block].dtype
        )


def attend_back(
    attn_bias,
    query_low,
    query_meta,
    log_total,
    attended_low,
    grad_attended,
    keys,
    values,
    key_metas,
    segments,
    width,
):
    rows, features = query_low.shape
    lanes = 2 * width
    count = len(keys)
    here = lane_block(rows, lanes)
    flops = 10 * rows * rows * count * features
    low = jax.ShapeDtypeStruct((rows, features), jnp.bfloat16)
    results = pl.pallas_call(
        functools.partial(attend_back_kernel, count, segments, width),
        grid=(features // lanes,),
        in_specs=[
            pl.BlockSpec(memory_space=pltpu.SMEM),
            here,
            whole_block(query_meta.shape),
        ]
        + [here] * (3 + 2 * count)
        + [whole_block(query_meta.shape)] * count,
        out_specs=[here] * (1 + 2 * count),
        out_shape=[low] * (1 + 2 * count),
        scratch_shapes=[
            pltpu.VMEM((2, count, rows, lanes), jnp.bfloat16),
            pltpu.VMEM((rows, lanes), jnp.float32),
            pltpu.VMEM((rows, lanes), jnp.float32),
        ],
        compiler_params=pltpu.CompilerParams(vmem_limit_bytes=VMEM_LIMIT),
        cost_estimate=pl.CostEstimate(
            flops=flops, bytes_accessed=20 * rows * features, transcendentals=0
        ),
        name="attend_back",
    )(
        attn_bias,
        query_low,
        query_meta,
        log_total,
        attended_low,
        grad_attended,
        *keys,
        *values,
        *key_metas,
    )
    return results


def plan_kernel(
    groups,
    rows,
    width,
    member_ref,
    length_ref,
    adapter_ref,
    order_ref,
    variate_ref,
    frequency_ref,
    chosen_ref,
    back_ref,
    turn_ref,
    cos_ref,
    sin_ref,
    *refs,
):
    meta_refs, slot_ref = refs[:-1], refs[-1]
    blocks = variate_ref.shape[0]
    half_devices = groups // 2
    half_blocks = blocks // 2
    half_rows = half_blocks * LANES
    swap_rows = rows // 2
    member = member_ref[0]
    my_half, my_place = member // half_devices, member % half_devices
    places = [lax.rem(my_place + shift, half_devices) for shift in range(half_devices)]
    segments = length_ref.shape[1]
    starts = [jnp.int32(0)]
    for segment in range(segments):
        starts.append(starts[-1] + length_ref[0, segment])
    long_start, long_index = jnp.int32(0), jnp.int32(0)
    for segment in range(segments):
        is_half = length_ref[0, segment] == half_rows
        long_start = jnp.where(is_half, starts[segment], long_start)
        long_index = jnp.where(is_half, segment, long_index)

    block = lax.broadcasted_iota(jnp.int32, (blocks, LANES), 0)
    lane = lax.broadcasted_iota(jnp.int32, (blocks, LANES), 1)
    work_block = jnp.zeros((blocks, LANES), jnp.int32)
    for index in range(blocks):
        work_block = jnp.where(block == order_ref[0, index], index, work_block)
    work_row = work_block * LANES + lane
    is_long = (work_row >= long_start) & (work_row < long_start + half_rows)
    in_first = block < half_blocks
    long_count = jnp.sum(jnp.where(is_long & in_first, 1.0, 0.0)).astype(jnp.int32)
    long_half = jnp.where(2 * long_count < half_rows, 1, 0)
    side = jnp.where(in_first, 0, 1)
    target = jnp.where(is_long, long_half, 1 - long_half)
    foreign = target != side
    flags = jnp.where(foreign, 1.0, 0.0)
    moved = jnp.sum(jnp.where(in_first, flags, 0.0)).astype(jnp.int32)
    square_row = lax.broadcasted_iota(jnp.int32, (LANES, LANES), 0)
    square_column = lax.broadcasted_iota(jnp.int32, (LANES, LANES), 1)
    within = dot(flags.astype(jnp.bfloat16), one_hot(square_row < square_column))
    block_sum = jnp.broadcast_to(jnp.sum(flags, axis=1, keepdims=True), (blocks, LANES))
    from_block = lax.broadcasted_iota(jnp.int32, (blocks, blocks), 1)
    to_block = lax.broadcasted_iota(jnp.int32, (blocks, blocks), 0)
    earlier = (from_block < to_block) & ((from_block < half_blocks) == (to_block < half_blocks))
    before = dot(one_hot(earlier), block_sum.astype(jnp.bfloat16))
    foreign_rank = (within + before).astype(jnp.int32)
    kept_rank = (block - side * half_blocks) * LANES + lane - foreign_rank
    kept_slot = side * half_rows + kept_rank
    foreign_slot = (1 - side) * half_rows + rows + foreign_rank
    foreign_slot = foreign_slot - jnp.clip(moved, 0, swap_rows)
    for index in range(1, half_devices):
        start = index * rows - jnp.minimum(moved, index * swap_rows)
        last = (index - 1) * rows - jnp.minimum(moved, (index - 1) * swap_rows)
        kept_slot = jnp.where(kept_rank >= start, kept_slot + rows - (start - last), kept_slot)
        received = jnp.clip(moved - index * swap_rows, 0, swap_rows)
        previous = jnp.clip(moved - (index - 1) * swap_rows, 0, swap_rows)
        foreign_slot = jnp.where(
            foreign_rank >= index * swap_rows,
            foreign_slot + rows - swap_rows + previous - received,
            foreign_slot,
        )
    slot = jnp.where(foreign, foreign_slot, kept_slot)
    slot_ref[...] = slot

    per_device = rows // LANES
    wanted = lax.broadcasted_iota(jnp.int32, (rows + swap_rows, 1), 0)
    wanted = jnp.where(
        wanted < rows,
        my_half * half_rows + my_place * rows + wanted,
        (1 - my_half) * half_rows + my_place * rows + wanted - swap_rows,
    )
    for shift in range(half_devices):
        for index in range(per_device):
            held = my_half * half_blocks + places[shift] * per_device + index
            column = (shift * per_device + index) * LANES
            chosen_ref[:, column : column + LANES] = one_hot(
                wanted == slot_ref[pl.ds(held, 1), :]
            )

    slot_turned = jnp.transpose(slot.astype(jnp.float32))
    turned_lane = lax.broadcasted_iota(jnp.int32, (LANES, blocks), 1)
    first_lane = lax.broadcasted_iota(jnp.int32, (1, LANES), 1)
    for index in range(per_device):
        held = my_half * half_blocks + my_place * per_device + index
        mine = jnp.sum(
            jnp.where(turned_lane == held, slot_turned, 0.0), axis=1, keepdims=True
        ).astype(jnp.int32)
        here = slice(index * LANES, (index + 1) * LANES)
        column = 0
        for first, half, length in ((0, my_half, rows), (swap_rows, 1 - my_half, swap_rows)):
            for shift in range(half_devices):
                for chunk in range(0, length, LANES):
                    number = half * half_rows + places[shift] * rows + first + chunk
                    back_ref[here, column : column + LANES] = one_hot(mine == number + first_lane)
                    column += LANES

    on_long = my_half == long_half
    for turn in range(2):
        chosen_segment = jnp.where(
            on_long, long_index, jnp.where(long_index <= turn, turn + 1, turn)
        )
        adapter = adapter_ref[0, 0]
        for segment in range(1, segments):
            adapter = jnp.where(chosen_segment == segment, adapter_ref[0, segment], adapter)
        turn_ref[turn] = adapter

    variate_turned = jnp.transpose(variate_ref[...].astype(jnp.float32))
    known = []
    for index in range(blocks):
        values = jnp.where(
            square_column == 0,
            work_block[index : index + 1, :].astype(jnp.float32),
            jnp.where(
                square_column == 1,
                square_row.astype(jnp.float32),
                variate_turned[:, index : index + 1],
            ),
        )
        known.append(jnp.where(square_column < 3, values, 0.0).astype(jnp.bfloat16))
    number = lax.broadcasted_iota(jnp.int32, (rows, 1), 0)
    wide_lane = lax.broadcasted_iota(jnp.int32, (rows, LANES), 1)
    for shift in range(half_devices):
        slots = my_half * half_rows + places[shift] * rows + number
        facts = jnp.zeros((rows, LANES), jnp.float32)
        for index in range(blocks):
            facts = facts + dot(one_hot(slots == slot[index : index + 1, :]), known[index])
        facts = facts.astype(jnp.int32)
        row = facts[:, 0:1] * LANES + facts[:, 1:2]
        segment = jnp.zeros((rows, 1), jnp.int32)
        first_row = jnp.zeros((rows, 1), jnp.int32)
        for index in range(1, segments):
            segment = jnp.where(row >= starts[index], index, segment)
            first_row = jnp.where(row >= starts[index], starts[index], first_row)
        turn = jnp.where(segment > long_index, segment - 1, segment)
        turn = jnp.where(on_long, 0, turn)
        meta_refs[shift][...] = jnp.where(
            wide_lane == 0, facts[:, 2:3], jnp.where(wide_lane == 1, segment, turn)
        )
        if shift == 0:
            angles = (row - first_row).astype(jnp.float32) * frequency_ref[...]
            sign = jnp.where(wide_lane % width < width // 2, -1.0, 1.0)
            cos_ref[...] = jnp.cos(angles)
            sin_ref[...] = jnp.sin(angles) * sign


def plan(groups, rows, width, member, seq_len, seq_adapter, block_order, variate):
    half_devices = groups // 2
    half_rows = half_devices * rows
    blocks = block_order.shape[1]
    smem = pl.BlockSpec(memory_space=pltpu.SMEM)
    vmem = pl.BlockSpec(memory_space=pltpu.VMEM)
    results = pl.pallas_call(
        functools.partial(plan_kernel, groups, rows, width),
        in_specs=[smem, smem, smem, smem, vmem, vmem],
        out_specs=[vmem, vmem, smem, vmem, vmem] + [vmem] * half_devices,
        out_shape=[
            jax.ShapeDtypeStruct((rows + rows // 2, half_rows), jnp.bfloat16),
            jax.ShapeDtypeStruct((rows, half_rows + half_rows // 2), jnp.bfloat16),
            jax.ShapeDtypeStruct((2,), jnp.int32),
            jax.ShapeDtypeStruct((rows, LANES), jnp.float32),
            jax.ShapeDtypeStruct((rows, LANES), jnp.float32),
        ]
        + [jax.ShapeDtypeStruct((rows, LANES), jnp.int32)] * half_devices,
        scratch_shapes=[pltpu.VMEM((blocks, LANES), jnp.int32)],
        compiler_params=pltpu.CompilerParams(vmem_limit_bytes=VMEM_LIMIT),
        cost_estimate=pl.CostEstimate(
            flops=2**31, bytes_accessed=4 * rows * half_rows, transcendentals=0
        ),
        name="plan",
    )(
        member,
        seq_len,
        seq_adapter,
        block_order,
        variate.reshape(blocks, LANES),
        jnp.asarray(rope_frequency(width)),
    )
    return (*results[:5], results[5:])


def pick_kernel(counts, later_count, chosen_ref, *refs):
    outs = refs[sum(counts) + later_count : sum(counts) + later_count + len(counts)]
    refs = iter(refs[: sum(counts)])
    for count, out_ref in zip(counts, outs):
        total = jnp.zeros(out_ref.shape, jnp.float32)
        column = 0
        for _ in range(count):
            ref = next(refs)
            rows = ref.shape[0]
            total = total + dot(chosen_ref[:, column : column + rows], ref[...])
            column += rows
        out_ref[...] = total.astype(out_ref.dtype)


def pick(chosen, first, count, *helds, later=()):
    features = helds[0][0].shape[1]
    tile = features // 2
    parts = [part for held in helds for part in held]
    return pl.pallas_call(
        functools.partial(pick_kernel, [len(held) for held in helds], len(later)),
        grid=(features // tile,),
        in_specs=[pl.BlockSpec((count, chosen.shape[1]), lambda step: (first // count, 0))]
        + [pl.BlockSpec((part.shape[0], tile), lambda step: (0, step)) for part in parts]
        + [pl.BlockSpec(memory_space=pl.ANY)] * len(later),
        out_specs=[pl.BlockSpec((count, tile), lambda step: (0, step))] * len(helds)
        + [pl.BlockSpec(memory_space=pl.ANY)] * len(later),
        out_shape=[jax.ShapeDtypeStruct((count, features), jnp.bfloat16)] * len(helds)
        + [jax.ShapeDtypeStruct(array.shape, array.dtype) for array in later],
        input_output_aliases={1 + len(parts) + i: len(helds) + i for i in range(len(later))},
        compiler_params=pltpu.CompilerParams(vmem_limit_bytes=VMEM_LIMIT),
        cost_estimate=pl.CostEstimate(
            flops=2 * count * chosen.shape[1] * features * len(helds),
            bytes_accessed=8 * count * features * len(helds),
            transcendentals=0,
        ),
        name="pick",
    )(chosen, *parts, *later)


def axis_count(names):
    count = 1
    for name in names:
        count *= lax.axis_size(name)
    return count


def within_half(array, shift, groups):
    half = groups // 2
    pairs = [
        (base + (place + shift) % half, base + place)
        for base in (0, half)
        for place in range(half)
    ]
    return lax.ppermute(array, GROUP, pairs)


def gather_half(array, groups):
    return [array] + [within_half(array, shift, groups) for shift in range(1, groups // 2)]


def to_other_half(array, groups):
    half = groups // 2
    return lax.ppermute(array, GROUP, [(i, (i + half) % groups) for i in range(groups)])


def scatter_sum(array, axis_sizes):
    for name, size in reversed(axis_sizes):
        outer = array.shape[0] // size
        array = array.reshape((outer, size) + array.shape[1:])
        bit = 1
        while bit < size:
            index = lax.axis_index(name)
            own = (index // bit) % 2
            spread = array.reshape((outer, size // (2 * bit), 2) + array.shape[2:])
            keep = lax.dynamic_index_in_dim(spread, own, 2, keepdims=False)
            send = lax.dynamic_index_in_dim(spread, 1 - own, 2, keepdims=False)
            got = lax.ppermute(send, name, [(i, i ^ bit) for i in range(size)])
            array = (keep.astype(jnp.float32) + got.astype(jnp.float32)).astype(jnp.bfloat16)
            bit *= 2
        array = array.reshape((outer,) + array.shape[2:])
    return array


LANES = 128
MOMENT_ROWS = 24
PACKS = ("far", "near")
GROUP = ("half", "core")
ALL = PACKS + GROUP


def adam(current, first_old, second_old, grad):
    first_moment = BETA_ONE * first_old + (1.0 - BETA_ONE) * grad
    second_moment = BETA_TWO * second_old + (1.0 - BETA_TWO) * grad * grad
    first_fix = first_moment / (1.0 - BETA_ONE**update_count)
    second_fix = second_moment / (1.0 - BETA_TWO**update_count)
    updated = current - LEARN_RATE * (
        first_fix / (jnp.sqrt(second_fix) + ADAM_EPS) + WEIGHT_DECAY * current
    )
    return first_moment, second_moment, updated.astype(jnp.bfloat16)


def settle_shards(grads, few_choice, adapters, moment1, moment2, groups):
    a_qkv, b_qkv, a_guo, a_down, b_gu, b_do = grads
    features, few = a_qkv.shape[0], few_choice.shape[1]
    quarters = a_down.shape[1] // few
    down = jnp.concatenate([a_down[:, i * few : (i + 1) * few] for i in range(quarters)])
    wide = [a_qkv[:, i * few : (i + 1) * few] for i in range(3)]
    wide += [a_guo[:, i * few : (i + 1) * few] for i in (2, 0, 1)] + [down]
    tall = [b_qkv[i * few : (i + 1) * few] for i in range(3)]
    tall += [b_do[2 * few : 3 * few], b_gu[:few], b_gu[few : 2 * few], b_do[:few]]
    pieces = []
    for grad_a, grad_b in zip(wide, tall):
        pieces.append(lax.dot_general(grad_a, few_choice, (((1,), (1,)), ((), ()))).reshape(-1))
        pieces.append(jnp.dot(few_choice, grad_b).reshape(-1))
    axis_sizes = [(PACKS, axis_count(PACKS)), (GROUP, groups)]
    shards = axis_sizes[0][1] * groups
    flat_grads = jnp.concatenate(pieces).astype(jnp.bfloat16).reshape(shards, -1)
    grad_shard = scatter_sum(flat_grads, axis_sizes).reshape(-1).astype(jnp.float32)
    shard_count = grad_shard.shape[0]
    shard_start = lax.axis_index(ALL) * shard_count
    current = lax.dynamic_slice_in_dim(adapters, shard_start, shard_count).astype(jnp.float32)
    first_moment, second_moment, updated = adam(current, moment1, moment2, grad_shard)
    adapters_new = lax.all_gather(updated, ALL, axis=0, tiled=True)
    return grad_shard, first_moment, second_moment, adapters_new


def spreads_evenly(devices, groups, features, hidden, total):
    rows = total // LANES
    chunks = features // LANES
    return (
        groups == 4
        and ADAPTERS * RANK == LANES
        and devices * chunks == 256
        and chunks == 8
        and hidden == devices * LANES
        and hidden == 4 * features
        and rows % (devices * devices) == 0
        and devices & (devices - 1) == 0
    )


def one_hot(condition):
    return jnp.where(condition, 1.0, 0.0).astype(jnp.bfloat16)


def sum_wide(adapter_row, arrived_ref, first, width):
    sources = arrived_ref.shape[0]
    rows = lax.broadcasted_iota(jnp.int32, (LANES, width * LANES), 0)
    columns = lax.broadcasted_iota(jnp.int32, (LANES, width * LANES), 1)
    fits = (rows // (2 * RANK) == columns // LANES) & (rows % RANK == columns % RANK)
    second = (rows // RANK) % 2 == 1
    adapter = jnp.where(fits, (columns % LANES) // RANK, -1)
    total = jnp.zeros((32, width * LANES), jnp.float32)
    for source in range(sources):
        at = source * 2 * RANK
        chosen = jnp.where(
            second, adapter_row[:, at + RANK : at + RANK + 1], adapter_row[:, at : at + 1]
        )
        total = total + dot(
            arrived_ref[source, first : first + 32, :], one_hot(adapter == chosen)
        )
    return total


def sum_tall(adapter_row, arrived_ref, first):
    sources = arrived_ref.shape[0]
    depth = sources * 2 * RANK
    rows = lax.broadcasted_iota(jnp.int32, (LANES, depth), 0)
    columns = lax.broadcasted_iota(jnp.int32, (LANES, depth), 1)
    choice = one_hot((rows // RANK == adapter_row) & (rows % RANK == columns % RANK))
    held = arrived_ref[:, first : first + 2 * RANK, :].reshape(depth, LANES)
    return jnp.dot(choice, held, preferred_element_type=jnp.float32)


def sum_square(adapter_row, arrived_ref, first):
    sources = arrived_ref.shape[0]
    depth = sources * 16
    rows = lax.broadcasted_iota(jnp.int32, (64, depth), 0)
    columns = lax.broadcasted_iota(jnp.int32, (64, depth), 1)
    choice = one_hot(
        ((rows % 32) // 4 == adapter_row)
        & (rows % 4 == columns % 4)
        & (rows // 32 == (columns % 16) // 8)
    )
    held = arrived_ref[:, first : first + 16, :].reshape(depth, LANES)
    return jnp.dot(choice, held, preferred_element_type=jnp.float32)


def settle_rows(parts, skip, param_ref, m1_ref, m2_ref, m_skip, grad_ref, new_refs):
    row = 0
    for part in parts:
        here = slice(row, row + part.shape[0])
        there = slice(skip + row, skip + row + part.shape[0])
        at = slice(m_skip + row, m_skip + row + part.shape[0])
        row += part.shape[0]
        low = part.astype(jnp.bfloat16)
        grad_ref[here, :] = low
        new = adam(
            param_ref[there, :].astype(jnp.float32),
            m1_ref[at, :],
            m2_ref[at, :],
            low.astype(jnp.float32),
        )[2]
        for new_ref in new_refs:
            new_ref[here, :] = new


def settle_early_kernel(own_rows, arrived_ref, moments_ref, param_ref, *refs):
    grad_ref, new_ref, late_m1_ref, late_m2_ref, tall_ref, square_ref, m1_ref, m2_ref = refs[-8:]
    sources = arrived_ref.shape[0]
    told = 6 * RANK
    tall_column = lax.broadcasted_iota(jnp.int32, tall_ref.shape, 1)
    square_column = lax.broadcasted_iota(jnp.int32, square_ref.shape, 1)
    tall = jnp.zeros(tall_ref.shape, jnp.float32)
    square = jnp.zeros(square_ref.shape, jnp.float32)
    for source in range(sources):
        row = arrived_ref[source, 0:16, :].astype(jnp.float32)
        first, second = row[0:1, told : told + 1], row[0:1, told + 1 : told + 2]
        tall = jnp.where(
            tall_column // (2 * RANK) == source,
            jnp.where((tall_column // RANK) % 2 == 1, second, first),
            tall,
        )
        square = jnp.where(
            square_column // RANK == source,
            jnp.where((square_column // 4) % 2 == 1, second, first),
            square,
        )
        held = moments_ref[source].astype(jnp.float32)
        here = slice(source * own_rows, (source + 1) * own_rows)
        m1_ref[here, :] = held[:own_rows]
        m2_ref[here, :] = held[MOMENT_ROWS : MOMENT_ROWS + own_rows]
    tall = tall.astype(jnp.int32)
    square = square.astype(jnp.int32)
    tall_ref[...] = tall
    square_ref[...] = square
    late = late_m1_ref.shape[0]
    late_m1_ref[...] = m1_ref[:late, :]
    late_m2_ref[...] = m2_ref[:late, :]
    wide = sum_wide(tall, arrived_ref, 0, 3)
    last = sum_wide(tall, arrived_ref, 32, 4)
    pair = sum_square(square, arrived_ref, 128)
    parts = [
        wide[:, 2 * LANES :],
        pair[32:],
        wide[:, :LANES],
        sum_tall(tall, arrived_ref, 64),
        wide[:, LANES : 2 * LANES],
        sum_tall(tall, arrived_ref, 96),
    ]
    parts += [last[:, i * LANES : (i + 1) * LANES] for i in range(4)]
    parts.append(pair[:32])
    copies = [new_ref.at[copy] for copy in range(new_ref.shape[0])]
    settle_rows(parts, late, param_ref, m1_ref, m2_ref, late, grad_ref, copies)


def settle_early(arrived, moments, params, late_rows, after):
    sources = arrived.shape[0]
    rows = params.shape[0] - late_rows
    vmem = pl.BlockSpec(memory_space=pltpu.VMEM)
    low = jax.ShapeDtypeStruct((rows, LANES), jnp.bfloat16)
    late = jax.ShapeDtypeStruct((late_rows, LANES), jnp.float32)
    return pl.pallas_call(
        functools.partial(settle_early_kernel, params.shape[0] // sources),
        in_specs=[vmem, vmem, vmem] + [pl.BlockSpec(memory_space=pl.ANY)] * len(after),
        out_specs=[vmem] * 6,
        out_shape=[
            low,
            jax.ShapeDtypeStruct((lax.axis_size("far"), rows, LANES), jnp.bfloat16),
            late,
            late,
            jax.ShapeDtypeStruct((1, sources * 2 * RANK), jnp.int32),
            jax.ShapeDtypeStruct((1, sources * RANK), jnp.int32),
        ],
        scratch_shapes=[pltpu.VMEM(params.shape, jnp.float32)] * 2,
        compiler_params=pltpu.CompilerParams(vmem_limit_bytes=VMEM_LIMIT),
        cost_estimate=pl.CostEstimate(
            flops=sources * 2**24, bytes_accessed=4 * arrived.size, transcendentals=0
        ),
        name="settle_early",
    )(arrived, moments, params, *after)


def settle_late_kernel(
    tall_ref, square_ref, arrived_ref, param_ref, m1_ref, m2_ref, *refs
):
    early_grad_ref = refs[0]
    own_ref, new_ref, _, grad_ref = refs[-4:]
    wide = sum_wide(tall_ref[...], arrived_ref, 0, 3)
    pairs = [sum_square(square_ref[...], arrived_ref, first) for first in (32, 48)]
    parts = []
    for index in range(3):
        parts.append(wide[:, index * LANES : (index + 1) * LANES])
        parts.append(pairs[index // 2][(index % 2) * 32 : (index % 2) * 32 + 32])
    copies = [new_ref.at[copy] for copy in range(new_ref.shape[0])]
    settle_rows(parts, 0, param_ref, m1_ref, m2_ref, 0, grad_ref, copies)
    low = jnp.concatenate(
        [ref[...].astype(jnp.float32) for ref in (grad_ref, early_grad_ref)], axis=0
    )
    each = low.shape[0] // own_ref.shape[0]
    zeros = jnp.zeros((own_ref.shape[1] - each, LANES), jnp.float32)
    for owner in range(own_ref.shape[0]):
        own_ref[owner] = jnp.concatenate(
            [low[owner * each : (owner + 1) * each], zeros], axis=0
        ).astype(jnp.bfloat16)


def settle_late(tall, square, arrived, params, late_m1, late_m2, early_grad, later, after):
    rows = late_m1.shape[0]
    anywhere = pl.BlockSpec(memory_space=pl.ANY)
    vmem = pl.BlockSpec(memory_space=pltpu.VMEM)
    return pl.pallas_call(
        settle_late_kernel,
        in_specs=[vmem] * 7 + [anywhere] * (1 + len(after)),
        out_specs=[vmem, vmem, anywhere],
        scratch_shapes=[pltpu.VMEM((rows, LANES), jnp.bfloat16)],
        input_output_aliases={7: 2},
        out_shape=[
            jax.ShapeDtypeStruct((arrived.shape[0], MOMENT_ROWS, LANES), jnp.bfloat16),
            jax.ShapeDtypeStruct((axis_count(PACKS), rows, LANES), jnp.bfloat16),
            jax.ShapeDtypeStruct(later.shape, later.dtype),
        ],
        compiler_params=pltpu.CompilerParams(vmem_limit_bytes=VMEM_LIMIT),
        cost_estimate=pl.CostEstimate(
            flops=arrived.shape[0] * 2**24, bytes_accessed=4 * arrived.size, transcendentals=0
        ),
        name="settle_late",
    )(tall, square, arrived, params, late_m1, late_m2, early_grad, later, *after)


def gather_inner(piece, groups):
    pieces = [piece]
    bit = groups // 2
    while bit:
        pairs = [(i, i ^ bit) for i in range(groups)]
        pieces = pieces + [lax.ppermute(piece, GROUP, pairs) for piece in pieces]
        bit //= 2
    return pieces


def placing_order(device, unit):
    size = unit * device.shape[0]
    to_row = lax.broadcasted_iota(jnp.int32, (size, size), 0)
    from_row = jnp.arange(size, dtype=jnp.int32)
    source = (from_row % unit) * device.shape[0] + jnp.repeat(device, unit)
    return (to_row == source[None, :]).astype(jnp.bfloat16)


def piece_devices(groups, devices):
    member = lax.axis_index(GROUP)
    piece = jnp.arange(groups, dtype=jnp.int32)
    mask = jnp.zeros_like(piece)
    bit = 1
    while bit < groups:
        mask = mask * 2 + (piece // bit) % 2
        bit *= 2
    outer = jnp.arange(devices // groups, dtype=jnp.int32)
    return (outer[None, :] * groups + (member ^ mask)[:, None]).reshape(-1)


def hand_on(after, *arrays):
    anywhere = pl.BlockSpec(memory_space=pl.ANY)
    return pl.pallas_call(
        lambda *refs: None,
        in_specs=[anywhere] * (1 + len(arrays)),
        out_specs=[anywhere] * len(arrays),
        out_shape=[jax.ShapeDtypeStruct(array.shape, array.dtype) for array in arrays],
        input_output_aliases={1 + index: index for index in range(len(arrays))},
        name="hand_on",
    )(after, *arrays)


def assemble_kernel(counts, devices, chunks, first, order_ref, *refs):
    piece_refs = []
    for count in counts:
        piece_refs.append(refs[:count])
        refs = refs[count:]
    out_any, placed_ref, sems = refs[-3:]

    def held_rows(part_refs, start, stop):
        before = 0
        for ref in part_refs:
            if start < before + ref.shape[1]:
                return ref[:, start - before : stop - before, :]
            before += ref.shape[1]

    unit = order_ref.shape[0] // devices
    copies = []
    for index, (begin, end) in enumerate(chunks):
        for start in range(begin, end, 2 * unit):
            sides = []
            for side in (start, start + unit):
                held = jnp.concatenate(
                    [held_rows(part_refs, side, side + unit) for part_refs in piece_refs], axis=0
                )
                sides.append(held.reshape(unit * devices, LANES))
            placed = dot(order_ref[...], jnp.concatenate(sides, axis=1)).astype(jnp.bfloat16)
            for half, side in enumerate((start, start + unit)):
                placed_ref[side * devices : (side + unit) * devices, :] = placed[
                    :, half * LANES : (half + 1) * LANES
                ]
        here = slice(begin * devices, end * devices)
        there = slice((first + begin) * devices, (first + end) * devices)
        copies.append(
            pltpu.make_async_copy(placed_ref.at[here, :], out_any.at[there, :], sems.at[index])
        )
        copies[-1].start()
    for copy in copies:
        copy.wait()


def assemble(order, pieces, total_rows, first, before, after):
    devices = len(pieces) * pieces[0][0].shape[0]
    rows = pieces[0][0].shape[1]
    parts = [part for piece in pieces for part in piece]
    step = 32 * max(1, rows // 128)
    chunks = [(begin, min(begin + step, rows)) for begin in range(0, rows, step)]
    vmem, anywhere = pl.BlockSpec(memory_space=pltpu.VMEM), pl.BlockSpec(memory_space=pl.ANY)
    in_specs = [vmem] * (1 + len(parts)) + [anywhere] * len(after)
    operands = [order, *parts, *after]
    aliases = {}
    if before is not None:
        aliases = {len(operands): 0}
        in_specs.append(anywhere)
        operands.append(before)
    return pl.pallas_call(
        functools.partial(assemble_kernel, [len(piece) for piece in pieces], devices, chunks, first),
        in_specs=in_specs,
        out_specs=anywhere,
        out_shape=jax.ShapeDtypeStruct((total_rows, LANES), jnp.bfloat16),
        scratch_shapes=[
            pltpu.VMEM((rows * devices, LANES), jnp.bfloat16),
            pltpu.SemaphoreType.DMA((len(chunks),)),
        ],
        input_output_aliases=aliases,
        compiler_params=pltpu.CompilerParams(vmem_limit_bytes=VMEM_LIMIT),
        cost_estimate=pl.CostEstimate(
            flops=rows * devices * 2**17, bytes_accessed=rows * devices * 512, transcendentals=0
        ),
        name="assemble",
    )(*operands)


def rope_frequency(head_width):
    index = np.arange(LANES) % (head_width // 2)
    return (ROPE_BASE ** (-2.0 * index / head_width)).astype(np.float32)[None, :]


def gain_rows(attn_gain, ffn_gain, q_gain, k_gain):
    repeats = attn_gain.shape[0] // q_gain.shape[0]
    return jnp.concatenate(
        [attn_gain, ffn_gain] + [q_gain] * repeats + [k_gain] * repeats
    ).astype(jnp.float32).reshape(4, -1)


def select_kernel(features, hidden, devices, turn_ref, me_ref, flat_ref, *refs):
    m1_ref, m2_ref = refs[:2]
    out_refs = refs[3:]
    a_qkv_ref, a_guo_ref, a_down_ref, b_qkv_ref, b_gu_ref, b_do_ref = out_refs[:6]
    if devices:
        own_ref, moments_ref, wide_ref = out_refs[6:]
        count = m1_ref.shape[0] // devices
        for device in range(devices):
            rows = []
            for ref in (m1_ref, m2_ref):
                rows.append(ref[pl.ds(device, count, stride=devices), :])
                rows.append(jnp.zeros((MOMENT_ROWS - count, LANES), jnp.float32))
            moments_ref[device] = jnp.concatenate(rows, axis=0).astype(jnp.bfloat16)
        size = wide_ref.shape[0]
        each = size // devices
        for chunk in range(flat_ref.shape[0] // size):
            wide_ref[...] = flat_ref[chunk * size : (chunk + 1) * size, :].astype(jnp.float32)
            own_ref[chunk * each : (chunk + 1) * each, :] = wide_ref[
                pl.ds(me_ref[0], each, stride=devices), :
            ].astype(jnp.bfloat16)
    few = 2 * RANK
    rows = lax.broadcasted_iota(jnp.int32, (LANES, LANES), 0)
    columns = lax.broadcasted_iota(jnp.int32, (LANES, LANES), 1)
    chosen = jnp.where((columns // RANK) % 2 == 1, turn_ref[1], turn_ref[0])
    fits = (rows // RANK == chosen) & (rows % RANK == columns % RANK)
    start = {}
    row = 0
    for name, rows_in, rows_out in (
        ("q", features, features),
        ("k", features, features),
        ("v", features, features),
        ("o", features, features),
        ("g", features, hidden),
        ("u", features, hidden),
        ("d", hidden, features),
    ):
        start[name] = (row, row + rows_in)
        row += rows_in + rows_out

    def wide(names, length):
        total = jnp.zeros((length, LANES), jnp.float32)
        for place, name in enumerate(names):
            first = start[name][0]
            total = total + jnp.dot(
                flat_ref[first : first + length, :],
                one_hot(fits & (columns // few == place)),
                preferred_element_type=jnp.float32,
            )
        return total.astype(jnp.bfloat16)

    a_qkv_ref[...] = wide("qkv", features)
    a_guo_ref[...] = wide("guo", features)
    for first in range(0, hidden, features):
        a_down_ref[first : first + features, :] = jnp.dot(
            flat_ref[start["d"][0] + first : start["d"][0] + first + features, :],
            one_hot(fits & (columns // few == 0)),
            preferred_element_type=jnp.float32,
        ).astype(jnp.bfloat16)

    def tall(name, length, out_ref, place):
        chunks = length // LANES
        size = RANK * chunks
        to_row = lax.broadcasted_iota(jnp.int32, (size, size), 0)
        from_row = lax.broadcasted_iota(jnp.int32, (size, size), 1)
        turned = one_hot(
            (to_row // RANK == from_row % chunks) & (to_row % RANK == from_row // chunks)
        )
        for turn in range(2):
            first = start[name][1] + pl.multiple_of(turn_ref[turn] * size, LANES)
            block = jnp.dot(
                turned, flat_ref[pl.ds(first, size), :], preferred_element_type=jnp.float32
            ).astype(jnp.bfloat16)
            here = place * few + turn * RANK
            for chunk in range(chunks):
                out_ref[here : here + RANK, chunk * LANES : (chunk + 1) * LANES] = block[
                    chunk * RANK : (chunk + 1) * RANK
                ]

    for out_ref, names in ((b_qkv_ref, "qkv"), (b_gu_ref, "gu"), (b_do_ref, "d.o")):
        out_ref[...] = jnp.zeros(out_ref.shape, out_ref.dtype)
        for place, name in enumerate(names):
            if name != ".":
                tall(name, out_ref.shape[1], out_ref, place)


def select(devices, turn_adapter, me, adapters, moments, features, hidden, after):
    shapes = [(features, LANES), (features, LANES), (hidden, LANES)]
    shapes += [(LANES, features), (LANES, hidden), (LANES, features)]
    scratch = []
    if devices:
        shapes.append((adapters.shape[0] // (LANES * devices), LANES))
        shapes.append((devices, 2 * MOMENT_ROWS, LANES))
        scratch.append(pltpu.VMEM((1024, LANES), jnp.float32))
    return pl.pallas_call(
        functools.partial(select_kernel, features, hidden, devices),
        in_specs=[
            pl.BlockSpec(memory_space=pltpu.SMEM),
            pl.BlockSpec(memory_space=pltpu.SMEM),
            pl.BlockSpec(memory_space=pltpu.VMEM),
            pl.BlockSpec(memory_space=pltpu.VMEM),
            pl.BlockSpec(memory_space=pltpu.VMEM),
            pl.BlockSpec(memory_space=pl.ANY),
        ],
        out_specs=[pl.BlockSpec(memory_space=pltpu.VMEM)] * len(shapes),
        out_shape=[jax.ShapeDtypeStruct(shape, jnp.bfloat16) for shape in shapes],
        scratch_shapes=scratch,
        compiler_params=pltpu.CompilerParams(vmem_limit_bytes=VMEM_LIMIT),
        cost_estimate=pl.CostEstimate(
            flops=2**31, bytes_accessed=4 * adapters.shape[0], transcendentals=0
        ),
        name="select",
    )(turn_adapter, me, adapters.reshape(-1, LANES), *moments, after)


def dot(left, right):
    return jnp.dot(left, right, preferred_element_type=jnp.float32)


def beside(*arrays):
    return jnp.concatenate(arrays, axis=1)


def above(*arrays):
    return jnp.concatenate(arrays, axis=0)


def turn_mask(meta_ref):
    rows = meta_ref.shape[0]
    lane = lax.broadcasted_iota(jnp.int32, (rows, LANES), 1)
    mask = jnp.where((lane // RANK) % 2 == meta_ref[:, 2:3], 1.0, 0.0)
    return mask, lane // (2 * RANK)


def row_norm(values):
    return lax.rsqrt(jnp.mean(values * values, axis=1, keepdims=True) + NORM_EPS)


def row_norm_back(values, gain, grad):
    scale = row_norm(values)
    unit = values * scale
    grad = grad * gain
    return scale * (grad - unit * jnp.mean(grad * unit, axis=1, keepdims=True))


def head_mean(values, width):
    lanes = values.shape[1]
    rows = lax.broadcasted_iota(jnp.int32, (lanes, lanes), 0)
    columns = lax.broadcasted_iota(jnp.int32, (lanes, lanes), 1)
    ones = one_hot(rows // width == columns // width)
    return dot(values.astype(jnp.bfloat16), ones) * (1.0 / width)


def swap_halves(values, width):
    lanes = values.shape[1]
    lane = lax.broadcasted_iota(jnp.int32, values.shape, 1)
    ahead = pltpu.roll(values, lanes - width // 2, 1)
    behind = pltpu.roll(values, width // 2, 1)
    return jnp.where(lane % width < width // 2, ahead, behind)


def widen(table, lanes):
    return jnp.concatenate([table] * (lanes // table.shape[1]), axis=1)


def joined(kept_ref, arrived_ref):
    first = kept_ref.shape[0] - arrived_ref.shape[0]
    kept = kept_ref[...]
    return jnp.concatenate([kept[:first], kept[first:] + arrived_ref[...]], axis=0)


def turned_heads(raw, gain, cosine, sine, width):
    unit = raw * lax.rsqrt(head_mean(raw * raw, width) + NORM_EPS) * gain
    return (unit * cosine + swap_halves(unit, width) * sine).astype(jnp.bfloat16)


def project_own(normed, inner, place, index, weight_ref, b_ref):
    own = jnp.where(place == index, ADAPTER_SCALE * inner, 0.0).astype(jnp.bfloat16)
    return dot(beside(normed, own), above(weight_ref[...], b_ref[...]))


def project_key_value_kernel(
    width,
    kept_ref,
    arrived_ref,
    gains_ref,
    wk_ref,
    wv_ref,
    a_ref,
    b_ref,
    meta_ref,
    cos_ref,
    sin_ref,
    _,
    x_ref,
    normed_ref,
    inner_ref,
    raw_ref,
    k_ref,
    v_ref,
    __,
):
    mask, place = turn_mask(meta_ref)

    @pl.when(pl.program_id(0) == 0)
    def _():
        rows = joined(kept_ref, arrived_ref)
        x_ref[...] = rows
        values = rows.astype(jnp.float32)
        normed = (values * row_norm(values) * gains_ref[0:1, :]).astype(
            jnp.bfloat16
        )
        normed_ref[...] = normed
        inner_ref[...] = (dot(normed, a_ref[...]) * mask).astype(jnp.bfloat16)

    normed = normed_ref[...]
    inner = inner_ref[...].astype(jnp.float32)
    lanes = wk_ref.shape[1]
    cosine, sine = widen(cos_ref[...], lanes), widen(sin_ref[...], lanes)
    key = project_own(normed, inner, place, 1, wk_ref, b_ref)
    raw_ref[...] = key.astype(jnp.bfloat16)
    k_ref[...] = turned_heads(key, gains_ref[3:4, :lanes], cosine, sine, width)
    v_ref[...] = project_own(normed, inner, place, 2, wv_ref, b_ref).astype(jnp.bfloat16)


def project_query_kernel(
    width, normed_ref, inner_ref, wq_ref, b_ref, cos_ref, sin_ref, gains_ref, raw_ref, q_ref
):
    lanes = wq_ref.shape[1]
    place = lax.broadcasted_iota(jnp.int32, inner_ref.shape, 1) // (2 * RANK)
    cosine, sine = widen(cos_ref[...], lanes), widen(sin_ref[...], lanes)
    inner = inner_ref[...].astype(jnp.float32)
    query = project_own(normed_ref[...], inner, place, 0, wq_ref, b_ref)
    raw_ref[...] = query.astype(jnp.bfloat16)
    q_ref[...] = turned_heads(query, gains_ref[2:3, :lanes], cosine, sine, width)


def project_heads(
    kept,
    arrived,
    later,
    gains,
    weights,
    a_qkv,
    b_qkv,
    meta,
    cos_table,
    sin_table,
    width,
):
    rows, features = kept.shape
    tile = 512
    grid = (features // tile,)

    def tiled(height):
        return pl.BlockSpec((height, tile), lambda step: (0, step))

    def shape(dtype):
        return jax.ShapeDtypeStruct((rows, features), dtype)

    full, few = whole_block((rows, features)), whole_block((rows, LANES))
    low = shape(jnp.bfloat16)
    anywhere = pl.BlockSpec(memory_space=pl.ANY)
    x, normed, inner, key_raw, key, value, later = pl.pallas_call(
        functools.partial(project_key_value_kernel, width),
        grid=grid,
        in_specs=[full, whole_block(arrived.shape), whole_block(gains.shape)]
        + [tiled(features)] * 2
        + [whole_block((features, LANES)), tiled(LANES), few, few, few]
        + [anywhere],
        out_specs=[full, full, few] + [tiled(rows)] * 3 + [anywhere],
        input_output_aliases={10: 6},
        out_shape=[
            low,
            low,
            jax.ShapeDtypeStruct((rows, LANES), jnp.bfloat16),
            low,
            low,
            low,
            jax.ShapeDtypeStruct(later.shape, later.dtype),
        ],
        compiler_params=pltpu.CompilerParams(vmem_limit_bytes=VMEM_LIMIT),
        cost_estimate=pl.CostEstimate(
            flops=6 * rows * features * features,
            bytes_accessed=4 * features * features + 14 * rows * features,
            transcendentals=0,
        ),
        name="project_key_value",
    )(
        kept,
        arrived,
        gains,
        *weights[1:],
        a_qkv,
        b_qkv,
        meta,
        cos_table,
        sin_table,
        later,
    )
    query_raw, query = pl.pallas_call(
        functools.partial(project_query_kernel, width),
        grid=grid,
        in_specs=[full, few, tiled(features), tiled(LANES), few, few, whole_block(gains.shape)],
        out_specs=[tiled(rows)] * 2,
        out_shape=[low, low],
        compiler_params=pltpu.CompilerParams(vmem_limit_bytes=VMEM_LIMIT),
        cost_estimate=pl.CostEstimate(
            flops=3 * rows * features * features,
            bytes_accessed=2 * features * features + 8 * rows * features,
            transcendentals=0,
        ),
        name="project_query",
    )(normed, inner, weights[0], b_qkv, cos_table, sin_table, gains)
    return x, normed, inner, query_raw, key_raw, query, key, value, later


def project_heads_back_kernel(
    count,
    width,
    devices,
    gq_ref,
    *refs,
):
    gk_refs, gv_refs, refs = refs[:count], refs[count : 2 * count], refs[2 * count :]
    (
        q_raw_ref,
        k_raw_ref,
        normed_any,
        inner_ref,
        x_any,
        residual_any,
        gains_ref,
        wq_ref,
        wk_ref,
        wv_ref,
        a_ref,
        b_ref,
        meta_ref,
        cos_ref,
        sin_ref,
    ) = refs[:15]
    if devices:
        out_ref, tail_ref, spread_ref = refs[-9:-6]
    else:
        out_ref, tail_ref, grad_a_ref, grad_b_ref = refs[-10:-6]
    total_ref, few_ref, tall_ref, square_ref, held_ref, sems = refs[-6:]
    step = pl.program_id(0)
    lanes = wq_ref.shape[1]
    mask, place = turn_mask(meta_ref)
    cosine, sine = widen(cos_ref[...], lanes), widen(sin_ref[...], lanes)

    def turned_back(grad, raw, head_gain):
        raw = raw.astype(jnp.float32)
        grad = grad * cosine - swap_halves(grad, width) * sine
        scale = lax.rsqrt(head_mean(raw * raw, width) + NORM_EPS)
        unit = raw * scale
        grad = grad * head_gain
        return (scale * (grad - unit * head_mean(grad * unit, width))).astype(jnp.bfloat16)

    def summed(term_refs):
        total = term_refs[0][...].astype(jnp.float32)
        for ref in term_refs[1:]:
            total = total + ref[...].astype(jnp.float32)
        return total

    copies = [
        pltpu.make_async_copy(source, held_ref.at[index], sems.at[index])
        for index, source in enumerate((normed_any, x_any, residual_any))
    ]

    @pl.when(step == 0)
    def _():
        for copy in copies:
            copy.start()
        total_ref[...] = jnp.zeros(total_ref.shape, jnp.float32)
        few_ref[...] = jnp.zeros(few_ref.shape, jnp.float32)

    inner_turned = jnp.transpose(inner_ref[...].astype(jnp.float32) * ADAPTER_SCALE).astype(
        jnp.bfloat16
    )
    errors = [
        turned_back(gq_ref[...].astype(jnp.float32), q_raw_ref[...], gains_ref[2:3, :lanes]),
        turned_back(summed(gk_refs), k_raw_ref[...], gains_ref[3:4, :lanes]),
        summed(gv_refs).astype(jnp.bfloat16),
    ]
    total_ref[...] += contract_last(
        beside(*errors), beside(wq_ref[...], wk_ref[...], wv_ref[...])
    )
    few = few_ref[...]
    wide = 2 * RANK
    for index, error in enumerate(errors):
        few = few + jnp.where(place == index, contract_last(error, b_ref[...]), 0.0)
        here = slice(index * wide, (index + 1) * wide)
        grad_b = dot(inner_turned[here], error)
        for part in range(lanes // LANES):
            square_ref[part, here, :] = grad_b[:, part * LANES : (part + 1) * LANES]
    square_ref[:, 3 * wide :, :] = jnp.zeros(
        (lanes // LANES, LANES - 3 * wide, LANES), jnp.float32
    )
    if devices:
        chunks = held_ref.shape[2] // LANES
        for index in range(lanes // LANES):
            for first, starts in ((wide, (0, wide)), (wide + RANK, (2 * wide, 3 * wide))):
                spread_square_to(
                    spread_ref,
                    first,
                    square_ref,
                    starts,
                    step * (lanes // LANES) + index,
                    chunks,
                    index,
                )
    else:
        for part in range(lanes // LANES):
            grad_b_ref[:, part * LANES : (part + 1) * LANES] = square_ref[part].astype(
                jnp.bfloat16
            )
    few_ref[...] = few

    @pl.when(step == pl.num_programs(0) - 1)
    def _():
        low = (ADAPTER_SCALE * few_ref[...] * mask).astype(jnp.bfloat16)
        low_turned = jnp.transpose(low.astype(jnp.float32)).astype(jnp.bfloat16)
        for copy in copies:
            copy.wait()
        tall_ref[...] = jnp.transpose(dot(low_turned, held_ref[0]))
        if devices:
            spread_wide_to(spread_ref, 0, tall_ref)
        else:
            grad_a_ref[...] = tall_ref[...].astype(jnp.bfloat16)
        grad = total_ref[...] + contract_last(low, a_ref[...])
        out = held_ref[2].astype(jnp.float32) + row_norm_back(
            held_ref[1].astype(jnp.float32), gains_ref[0:1, :], grad
        )
        out_ref[...] = out.astype(jnp.bfloat16)
        tail_ref[...] = out[out.shape[0] - tail_ref.shape[0] :].astype(jnp.bfloat16)


def project_heads_back(
    devices,
    after,
    grad_query,
    key_terms,
    value_terms,
    query_raw,
    key_raw,
    normed,
    inner,
    rows_in,
    grad_residual,
    gains,
    weights,
    a_qkv,
    b_qkv,
    meta,
    cos_table,
    sin_table,
    width,
):
    rows, features = rows_in.shape
    count = len(key_terms)
    tile = 256

    def tiled(height):
        return pl.BlockSpec((height, tile), lambda step: (0, step))

    full = whole_block((rows, features))
    anywhere = pl.BlockSpec(memory_space=pl.ANY)
    if devices:
        spread = (devices, 4 * RANK, LANES)
        grad_specs = [whole_block(spread)]
        grad_shapes = [jax.ShapeDtypeStruct(spread, jnp.bfloat16)]
    else:
        grad_specs = [whole_block((features, LANES)), tiled(LANES)]
        grad_shapes = [
            jax.ShapeDtypeStruct((features, LANES), jnp.bfloat16),
            jax.ShapeDtypeStruct((LANES, features), jnp.bfloat16),
        ]
    return pl.pallas_call(
        functools.partial(project_heads_back_kernel, count, width, devices),
        grid=(features // tile,),
        in_specs=[tiled(rows)] * (3 + 2 * count)
        + [anywhere, whole_block((rows, LANES)), anywhere, anywhere, whole_block(gains.shape)]
        + [tiled(features)] * 3
        + [whole_block((features, LANES)), tiled(LANES), whole_block(meta.shape)]
        + [whole_block((rows, LANES))] * 2
        + [anywhere] * len(after),
        out_specs=[full, whole_block((rows // 2, features)), *grad_specs],
        out_shape=[
            jax.ShapeDtypeStruct((rows, features), jnp.bfloat16),
            jax.ShapeDtypeStruct((rows // 2, features), jnp.bfloat16),
            *grad_shapes,
        ],
        scratch_shapes=[
            pltpu.VMEM((rows, features), jnp.float32),
            pltpu.VMEM((rows, LANES), jnp.float32),
            pltpu.VMEM((features, LANES), jnp.float32),
            pltpu.VMEM((tile // LANES, LANES, LANES), jnp.float32),
            pltpu.VMEM((3, rows, features), jnp.bfloat16),
            pltpu.SemaphoreType.DMA((3,)),
        ],
        compiler_params=pltpu.CompilerParams(vmem_limit_bytes=VMEM_LIMIT),
        cost_estimate=pl.CostEstimate(
            flops=8 * rows * features * features,
            bytes_accessed=6 * features * features + 30 * rows * features,
            transcendentals=0,
        ),
        name="project_heads_back",
    )(
        grad_query,
        *key_terms,
        *value_terms,
        query_raw,
        key_raw,
        normed,
        inner,
        rows_in,
        grad_residual,
        gains,
        *weights,
        a_qkv,
        b_qkv,
        meta,
        cos_table,
        sin_table,
        *after,
    )


def spread_wide_to(spread_ref, first, held_ref):
    devices = spread_ref.shape[0]
    count = held_ref.shape[0] // devices
    for device in range(devices):
        spread_ref[device, first : first + count, :] = held_ref[
            pl.ds(device, count, stride=devices), :
        ].astype(jnp.bfloat16)


def spread_square_to(spread_ref, first, held_ref, starts, chunk, chunks, index):
    classes = spread_ref.shape[0] // chunks
    count = 2 * RANK // classes
    for part in range(classes):
        rows = [
            held_ref[index, pl.ds(start + part, count, stride=classes), :]
            for start in starts
        ]
        spread_ref[part * chunks + chunk, first : first + 2 * count, :] = jnp.concatenate(
            rows, axis=0
        ).astype(jnp.bfloat16)


def feed_forward_kernel(
    devices,
    turn_ref,
    att_ref,
    x_any,
    kept_any,
    arrived_any,
    gains_ref,
    wo_ref,
    wg_any,
    wu_any,
    wd_any,
    a_guo_ref,
    a_down_ref,
    b_gu_ref,
    b_do_ref,
    meta_ref,
    out_any,
    tail_any,
    grad_res_any,
    grad_att_ref,
    *refs,
):
    if devices:
        spread_ref, refs = refs[0], refs[1:]
    else:
        (grad_a_ref, grad_ad_ref, grad_bgu_ref, grad_bdo_ref), refs = refs[:4], refs[4:]
    (
        res_ref,
        hidden_ref,
        inner_ref,
        inner_turned_ref,
        sum_ref,
        grad_hidden_ref,
        inner_down_ref,
        few_ref,
        few_down_ref,
        few_down_turned_ref,
        down_ref,
        tall_ref,
        square_ref,
        e_ref,
        x_ref,
        arrived_ref,
        wg_ref,
        wu_ref,
        wd_ref,
        out_ref,
        grad_res_ref,
        rows_sems,
        tile_sems,
        out_sems,
    ) = refs
    step = pl.program_id(0)
    steps = pl.num_programs(0)
    mask, place = turn_mask(meta_ref)
    tile = wg_ref.shape[2]
    swap_rows = arrived_ref.shape[0]
    row_copies = [
        pltpu.make_async_copy(source, target, rows_sems.at[index])
        for index, (source, target) in enumerate(
            ((x_any, x_ref), (kept_any, e_ref), (arrived_any, arrived_ref))
        )
    ]

    def tile_copies(number):
        slot = number % 2
        here = pl.ds(pl.multiple_of(number * tile, tile), tile)
        pairs = (
            (wg_any.at[:, here], wg_ref.at[slot]),
            (wu_any.at[:, here], wu_ref.at[slot]),
            (wd_any.at[here, :], wd_ref.at[slot]),
        )
        return [
            pltpu.make_async_copy(source, target, tile_sems.at[slot, index])
            for index, (source, target) in enumerate(pairs)
        ]

    features = wo_ref.shape[0]
    wide = 2 * RANK

    def only(values, index):
        return jnp.where(place == index, values, 0.0).astype(jnp.bfloat16)

    def turn(values):
        return jnp.transpose(values.astype(jnp.float32)).astype(jnp.bfloat16)

    @pl.when(step == 0)
    def _():
        for copy in row_copies:
            copy.start()
        for copy in tile_copies(0):
            copy.start()
        att = att_ref[...]
        inner_out = dot(att, a_guo_ref[...]) * mask
        attention_out = dot(
            beside(att, only(ADAPTER_SCALE * inner_out, 2)), above(wo_ref[...], b_do_ref[...])
        )
        row_copies[0].wait()
        res = x_ref[...].astype(jnp.float32) + attention_out
        res_ref[...] = res
        hidden = (res * row_norm(res) * gains_ref[1:2, :]).astype(jnp.bfloat16)
        hidden_ref[...] = hidden
        inner = dot(hidden, a_guo_ref[...]) * mask
        inner = jnp.where(place == 2, inner_out, inner).astype(jnp.bfloat16)
        inner_ref[...] = inner
        inner_turned_ref[...] = turn(inner.astype(jnp.float32) * ADAPTER_SCALE)
        for copy in row_copies[1:]:
            copy.wait()
        e_ref[e_ref.shape[0] - swap_rows :, :] += arrived_ref[...]
        few_down = only(ADAPTER_SCALE * contract_last(e_ref[...], b_do_ref[...]) * mask, 0)
        few_down_ref[...] = few_down
        few_down_turned_ref[...] = turn(few_down)[:wide]
        sum_ref[...] = jnp.zeros(sum_ref.shape, jnp.float32)
        grad_hidden_ref[...] = jnp.zeros(grad_hidden_ref.shape, jnp.float32)
        inner_down_ref[...] = jnp.zeros(inner_down_ref.shape, jnp.float32)
        few_ref[...] = jnp.zeros(few_ref.shape, jnp.float32)

    @pl.when(step + 1 < steps)
    def _():
        for copy in tile_copies(step + 1):
            copy.start()

    for copy in tile_copies(step):
        copy.wait()
    slot = step % 2
    hidden = hidden_ref[...]
    inner = ADAPTER_SCALE * inner_ref[...].astype(jnp.float32)
    gate_weight, up_weight, down_weight = wg_ref[slot], wu_ref[slot], wd_ref[slot]
    b_tile = b_gu_ref[...]
    gate = dot(beside(hidden, only(inner, 0)), above(gate_weight, b_tile))
    up = dot(beside(hidden, only(inner, 1)), above(up_weight, b_tile))
    grad_act = contract_last(
        beside(e_ref[...], few_down_ref[...]), beside(down_weight, a_down_ref[...])
    )
    sigmoid = 1.0 / (1.0 + jnp.exp(-gate))
    silu = gate * sigmoid
    act = (silu * up).astype(jnp.bfloat16)
    grad_up = (grad_act * silu).astype(jnp.bfloat16)
    grad_gate = (grad_act * up * (sigmoid * (1.0 + gate * (1.0 - sigmoid)))).astype(jnp.bfloat16)
    sum_ref[...] += dot(act, down_weight)
    inner_down_ref[...] += dot(act, a_down_ref[...])
    grad_hidden_ref[...] += contract_last(
        beside(grad_gate, grad_up), beside(gate_weight, up_weight)
    )
    few_ref[...] += jnp.where(
        place == 0, contract_last(grad_gate, b_tile), contract_last(grad_up, b_tile)
    )
    grad_b_gate = dot(inner_turned_ref[:wide, :], grad_gate).astype(jnp.bfloat16)
    grad_b_up = dot(inner_turned_ref[wide : 2 * wide, :], grad_up).astype(jnp.bfloat16)
    if devices:
        for index in range(tile // LANES):
            device = step * (tile // LANES) + index
            chunk = slice(index * LANES, (index + 1) * LANES)
            spread_ref[device, 2 * wide : 3 * wide, :] = grad_b_gate[:, chunk]
            spread_ref[device, 3 * wide : 4 * wide, :] = grad_b_up[:, chunk]
    else:
        grad_bgu_ref[:wide, :] = grad_b_gate
        grad_bgu_ref[wide:, :] = grad_b_up
    per_quarter = features // tile
    down_ref[
        pl.ds(pl.multiple_of((step // per_quarter) * wide, wide), wide),
        pl.ds(pl.multiple_of((step % per_quarter) * tile, tile), tile),
    ] = dot(few_down_turned_ref[...], act)

    out_copies = [
        pltpu.make_async_copy(source, target, out_sems.at[index])
        for index, (source, target) in enumerate(
            (
                (out_ref, out_any),
                (out_ref.at[out_ref.shape[0] - swap_rows :, :], tail_any),
                (grad_res_ref, grad_res_any),
            )
        )
    ]

    @pl.when(step == steps - 1)
    def _():
        grads_out = e_ref[...]
        inner_down = only(inner_down_ref[...] * mask, 0)
        res = res_ref[...]
        out_ref[...] = (
            res + sum_ref[...] + ADAPTER_SCALE * dot(inner_down, b_do_ref[...])
        ).astype(jnp.bfloat16)
        for copy in out_copies[:2]:
            copy.start()
        few = jnp.where(place < 2, ADAPTER_SCALE * few_ref[...] * mask, 0.0).astype(jnp.bfloat16)
        grad_hidden = grad_hidden_ref[...] + contract_last(few, a_guo_ref[...])
        grad_res = grads_out.astype(jnp.float32) + row_norm_back(
            res, gains_ref[1:2, :], grad_hidden
        )
        low = grad_res.astype(jnp.bfloat16)
        grad_res_ref[...] = low
        out_copies[2].start()
        few_out = only(ADAPTER_SCALE * contract_last(low, b_do_ref[...]) * mask, 2)
        grad_att_ref[...] = contract_last(
            beside(low, few_out), beside(wo_ref[...], a_guo_ref[...])
        ).astype(jnp.bfloat16)
        grad_a = dot(turn(few), hidden_ref[...]) + dot(turn(few_out), att_ref[...])
        inner_out = only(inner_ref[...].astype(jnp.float32), 2)
        grad_b = ADAPTER_SCALE * (
            dot(turn(inner_down), grads_out) + dot(turn(inner_out), low)
        )
        if devices:
            lane = lax.broadcasted_iota(jnp.int32, (features, LANES), 1)
            told = jnp.where(
                lane == 3 * wide, turn_ref[0], jnp.where(lane == 3 * wide + 1, turn_ref[1], 0)
            )
            tall_ref[...] = jnp.transpose(grad_a) + told.astype(jnp.float32)
            spread_wide_to(spread_ref, 0, tall_ref)
            tall_ref[...] = jnp.transpose(down_ref[...])
            spread_wide_to(spread_ref, wide, tall_ref)
            chunks = features // LANES
            for chunk in range(chunks):
                square_ref[chunk] = grad_b[:, chunk * LANES : (chunk + 1) * LANES]
                spread_square_to(
                    spread_ref, 4 * wide, square_ref, (0, 2 * wide), chunk, chunks, chunk
                )
        else:
            grad_a_ref[...] = jnp.transpose(grad_a).astype(jnp.bfloat16)
            grad_ad_ref[...] = jnp.transpose(down_ref[...]).astype(jnp.bfloat16)
            grad_bdo_ref[...] = grad_b.astype(jnp.bfloat16)
        for copy in out_copies:
            copy.wait()


def feed_forward(
    devices,
    turn_adapter,
    attended,
    rows_in,
    kept,
    arrived,
    gains,
    weights,
    selected,
    meta,
):
    rows, features = rows_in.shape
    hidden = weights[1].shape[1]
    tile = 512
    full = whole_block((rows, features))
    square = whole_block((features, features))
    anywhere = pl.BlockSpec(memory_space=pl.ANY)

    def shape(height, length, dtype):
        return jax.ShapeDtypeStruct((height, length), dtype)

    if devices:
        spread = (devices, 9 * RANK, LANES)
        grad_specs = [whole_block(spread)]
        grad_shapes = [jax.ShapeDtypeStruct(spread, jnp.bfloat16)]
    else:
        grad_specs = [
            whole_block((features, LANES)),
            whole_block((features, LANES)),
            pl.BlockSpec((4 * RANK, tile), lambda step: (0, step)),
            whole_block((LANES, features)),
        ]
        grad_shapes = [
            shape(features, LANES, jnp.bfloat16),
            shape(features, LANES, jnp.bfloat16),
            shape(4 * RANK, hidden, jnp.bfloat16),
            shape(LANES, features, jnp.bfloat16),
        ]
    return pl.pallas_call(
        functools.partial(feed_forward_kernel, devices),
        grid=(hidden // tile,),
        in_specs=[
            pl.BlockSpec(memory_space=pltpu.SMEM),
            full,
            anywhere,
            anywhere,
            anywhere,
            whole_block(gains.shape),
            square,
            anywhere,
            anywhere,
            anywhere,
            whole_block((features, LANES)),
            pl.BlockSpec((tile, LANES), lambda step: (step, 0)),
            pl.BlockSpec((LANES, tile), lambda step: (0, step)),
            whole_block((LANES, features)),
            whole_block(meta.shape),
        ],
        out_specs=[anywhere, anywhere, anywhere, full, *grad_specs],
        out_shape=[
            shape(rows, features, jnp.bfloat16),
            shape(*arrived.shape, jnp.bfloat16),
            shape(rows, features, jnp.bfloat16),
            shape(rows, features, jnp.bfloat16),
            *grad_shapes,
        ],
        scratch_shapes=[
            pltpu.VMEM((rows, features), jnp.float32),
            pltpu.VMEM((rows, features), jnp.bfloat16),
            pltpu.VMEM((rows, LANES), jnp.bfloat16),
            pltpu.VMEM((LANES, rows), jnp.bfloat16),
            pltpu.VMEM((rows, features), jnp.float32),
            pltpu.VMEM((rows, features), jnp.float32),
            pltpu.VMEM((rows, LANES), jnp.float32),
            pltpu.VMEM((rows, LANES), jnp.float32),
            pltpu.VMEM((rows, LANES), jnp.bfloat16),
            pltpu.VMEM((2 * RANK, rows), jnp.bfloat16),
            pltpu.VMEM((LANES, features), jnp.float32),
            pltpu.VMEM((features, LANES), jnp.float32),
            pltpu.VMEM((features // LANES, LANES, LANES), jnp.float32),
            pltpu.VMEM((rows, features), jnp.bfloat16),
            pltpu.VMEM((rows, features), jnp.bfloat16),
            pltpu.VMEM(arrived.shape, jnp.bfloat16),
            pltpu.VMEM((2, features, tile), jnp.bfloat16),
            pltpu.VMEM((2, features, tile), jnp.bfloat16),
            pltpu.VMEM((2, tile, features), jnp.bfloat16),
            pltpu.VMEM((rows, features), jnp.bfloat16),
            pltpu.VMEM((rows, features), jnp.bfloat16),
            pltpu.SemaphoreType.DMA((3,)),
            pltpu.SemaphoreType.DMA((2, 3)),
            pltpu.SemaphoreType.DMA((3,)),
        ],
        compiler_params=pltpu.CompilerParams(vmem_limit_bytes=VMEM_LIMIT),
        cost_estimate=pl.CostEstimate(
            flops=14 * rows * features * hidden,
            bytes_accessed=8 * features * hidden + 16 * rows * features,
            transcendentals=0,
        ),
        name="feed_forward",
    )(
        turn_adapter,
        attended,
        rows_in,
        kept,
        arrived,
        gains,
        *weights,
        *selected,
        meta,
    )


def settle_owned(grads, moment1, moment2, devices):
    grads = lax.all_to_all(grads, ALL, 0, 0, tiled=True)
    grads = grads[:, : moment1.shape[0] // (LANES * devices)]
    grad_shard = jnp.transpose(grads, (1, 0, 2)).reshape(-1).astype(jnp.float32)
    current = jnp.zeros((), jnp.float32)
    first_moment, second_moment, _ = adam(current, moment1, moment2, grad_shard)
    return grad_shard, first_moment, second_moment


def per_device(
    tokens,
    cotangent,
    variate,
    seq_len,
    seq_adapter,
    block_order,
    attn_gain,
    ffn_gain,
    q_gain,
    k_gain,
    attn_bias,
    query_weight,
    key_weight,
    value_weight,
    output_weight,
    gate_weight,
    up_weight,
    down_weight,
    adapters,
    moment1,
    moment2,
):
    groups = axis_count(GROUP)
    member = lax.axis_index(GROUP)
    row_count, feature_width = tokens.shape
    hidden_width = gate_weight.shape[1]
    head_width = q_gain.shape[0]
    half_devices = groups // 2
    segments = seq_len.shape[1]
    chosen, back, turn_adapter, cos_table, sin_table, key_metas = plan(
        groups, row_count, head_width, member[None], seq_len, seq_adapter, block_order, variate
    )
    meta = key_metas[0]
    axes = ALL
    devices = axis_count(PACKS) * groups
    even = spreads_evenly(devices, groups, feature_width, hidden_width, adapters.shape[0])
    spread = devices if even else 0
    gains = gain_rows(attn_gain, ffn_gain, q_gain, k_gain)


    held = (gather_half(tokens, groups), gather_half(cotangent, groups))
    sent_tokens, sent_grads = pick(chosen, row_count, row_count // 2, *held)
    arrived_tokens = to_other_half(sent_tokens, groups)
    a_qkv, a_guo, a_down, b_qkv, b_gu, b_do, *spread_state = select(
        spread,
        turn_adapter,
        lax.axis_index(axes)[None],
        adapters,
        (moment1.reshape(-1, LANES), moment2.reshape(-1, LANES)),
        feature_width,
        hidden_width,
        sent_tokens,
    )
    if even:
        params, moments = spread_state
        moments = lax.all_to_all(moments, axes, 0, 0, tiled=True)
    kept_tokens, kept_grads = pick(chosen, 0, row_count, *held)
    (
        my_tokens,
        normed,
        inner,
        query_raw,
        key_raw,
        query_low,
        key_low,
        value_low,
        sent_grads,
    ) = project_heads(
        kept_tokens,
        arrived_tokens,
        sent_grads,
        gains,
        (query_weight, key_weight, value_weight),
        a_qkv,
        b_qkv,
        meta,
        cos_table,
        sin_table,
        head_width,
    )
    arrived_grads = to_other_half(sent_grads, groups)
    keys = gather_half(key_low, groups)
    values = gather_half(value_low, groups)
    attended_low, log_total = attend(
        attn_bias, query_low, meta, keys, values, key_metas, segments, head_width
    )
    layer_rows, layer_tail, grad_residual, grad_attended, *forward_grads = feed_forward(
        spread,
        turn_adapter,
        attended_low,
        my_tokens,
        kept_grads,
        arrived_grads,
        gains,
        (output_weight, gate_weight, up_weight, down_weight),
        (a_guo, a_down, b_gu, b_do),
        meta,
    )
    layer_back = to_other_half(layer_tail, groups)
    layer_held = gather_half(layer_rows, groups) + gather_half(layer_back, groups)

    results = attend_back(
        attn_bias,
        query_low,
        meta,
        log_total,
        attended_low,
        grad_attended,
        keys,
        values,
        key_metas,
        segments,
        head_width,
    )
    after = []
    if even:
        total_rows = adapters.shape[0] // LANES
        late_rows = 6 * feature_width // devices
        early = lax.all_to_all(forward_grads[0], axes, 0, 0, tiled=True)
        early_grad, early_new, late_m1, late_m2, tall, square = settle_early(
            early, moments, params, late_rows, [results[0]]
        )
        early_outer = lax.all_to_all(early_new, "far", 0, 0, tiled=True)
        swap = [(0, 1), (1, 0)]
        early_near = lax.ppermute(early_outer, "near", swap)
        early_half = lax.ppermute(early_outer, "half", swap)
        after = [early_new, layer_back]
    grad_query = results[0]
    grad_keys = results[1 : 1 + half_devices]
    grad_values = results[1 + half_devices :]
    key_terms, value_terms = [grad_keys[0]], [grad_values[0]]
    for shift in range(1, half_devices):
        back_shift = half_devices - shift
        key_terms.append(within_half(grad_keys[shift], back_shift, groups))
        value_terms.append(within_half(grad_values[shift], back_shift, groups))
    grad_rows, grad_tail, *back_grads = project_heads_back(
        spread,
        after,
        grad_query,
        key_terms,
        value_terms,
        query_raw,
        key_raw,
        normed,
        inner,
        my_tokens,
        grad_residual,
        gains,
        (query_weight, key_weight, value_weight),
        a_qkv,
        b_qkv,
        meta,
        cos_table,
        sin_table,
        head_width,
    )
    def bring_back(tail):
        return gather_half(grad_rows, groups) + gather_half(to_other_half(tail, groups), groups)

    if not even:
        grads = (*back_grads, *forward_grads)
        column = jnp.arange(2 * RANK, dtype=jnp.int32)
        few_choice = one_hot(
            jnp.arange(LANES, dtype=jnp.int32)[:, None]
            == (jnp.repeat(turn_adapter, RANK) * RANK + column % RANK)[None, :]
        )
        settled = settle_shards(grads, few_choice, adapters, moment1, moment2, groups)
        layer_out = pick(back, 0, row_count, layer_held)[0]
        input_grad = pick(back, 0, row_count, bring_back(grad_tail))[0]
        return (layer_out, input_grad) + settled
    late = lax.all_to_all(back_grads[0], axes, 0, 0, tiled=True)
    layer_out = pick(back, 0, row_count, layer_held)[0]
    own_grads, late_new, grad_tail = settle_late(
        tall, square, late, params, late_m1, late_m2, early_grad, grad_tail, [layer_out, early_near, early_half]
    )
    late_outer = lax.all_to_all(late_new, PACKS, 0, 0, tiled=True)
    late_pieces = gather_inner(late_outer, groups)
    own_grads, early_half = hand_on(late_outer, own_grads, early_half)
    early_far = lax.ppermute(early_half, "near", swap)
    input_grad = pick(back, 0, row_count, bring_back(grad_tail))[0]
    early_pieces = [[early_outer], [early_near], [early_half], [early_far]]
    early_pieces += [
        [lax.ppermute(part, "core", swap) for part in piece] for piece in early_pieces
    ]
    far = jnp.arange(lax.axis_size("far"), dtype=jnp.int32)
    near, half, core = [lax.axis_index(name) for name in ALL[1:]]
    early_device = jnp.concatenate(
        [
            ((far * 2 + (near ^ flip_near)) * 2 + (half ^ flip_half)) * 2 + (core ^ flip_core)
            for flip_core in (0, 1)
            for flip_near, flip_half in ((0, 0), (1, 0), (0, 1), (1, 1))
        ]
    )
    late_pieces = [[piece] for piece in late_pieces]
    order = placing_order(piece_devices(groups, devices), 16)
    adapters_new = assemble(
        placing_order(early_device, 16),
        early_pieces,
        total_rows,
        late_rows,
        None,
        [input_grad, late_pieces[1][0]],
    )
    adapters_new = assemble(order, late_pieces, total_rows, 0, adapters_new, [])
    owned = settle_owned(own_grads, moment1, moment2, devices)
    return (layer_out, input_grad, *owned, adapters_new.reshape(-1))


def solution(mesh):
    packs, groups = mesh.shape["dp"], mesh.shape["group"]
    cut = jax.sharding.Mesh(mesh.devices.reshape(packs // 2, 2, groups // 2, 2), ALL)
    in_specs = (
        P(ALL, None),
        P(ALL, None),
        P(PACKS),
        P(PACKS, None),
        P(PACKS, None),
        P(PACKS, None),
        P(),
        P(),
        P(),
        P(),
        P(),
        P(),
        P(),
        P(),
        P(),
        P(),
        P(),
        P(),
        P(),
        P(ALL),
        P(ALL),
    )
    out_specs = (
        P(ALL, None),
        P(ALL, None),
        P(ALL),
        P(ALL),
        P(ALL),
        P(),
    )
    return jax.shard_map(
        per_device, mesh=cut, in_specs=in_specs, out_specs=out_specs, check_vma=False
    )
```

```python
import functools

import jax
import jax.numpy as jnp
import numpy as np
from jax import lax
from jax.experimental import pallas as pl
from jax.experimental.pallas import tpu as pltpu
from jax.sharding import PartitionSpec as P

RANK = 16
ADAPTERS = 8
NORM_EPS = 1e-06
ADAPTER_SCALE = 2.0
ROPE_BASE = 10000.0
MASKED = -1e30
LEARN_RATE = 0.01
BETA_ONE = 0.9
BETA_TWO = 0.999
ADAM_EPS = 1e-08
WEIGHT_DECAY = 0.01
update_count = 10.0
VARIATES = 4
VMEM_LIMIT = 56 * 1024 * 1024
EXACT_PARTS = 3


def contract_last(left, right):
    return lax.dot_general(
        left, right, (((1,), (1,)), ((), ())), preferred_element_type=jnp.float32
    )


def exact_parts(values):
    parts = []
    for _ in range(EXACT_PARTS):
        part = values.astype(jnp.bfloat16).astype(jnp.float32)
        parts.append(part)
        values = values - part
    return parts


def parts_in_lanes(values, first, column):
    result = jnp.zeros(values.shape, jnp.float32)
    for index, part in enumerate(exact_parts(values)):
        result = jnp.where(column == first + index, part, result)
    return result


def note_keys(side_ref, kmeta_refs, column, lane, width, segments):
    seg_column = column - EXACT_PARTS * VARIATES
    ones = (seg_column >= segments) & (seg_column < segments + EXACT_PARTS)
    for block, kmeta_ref in enumerate(kmeta_refs):
        one = (column < EXACT_PARTS * VARIATES) & ((column % VARIATES) == kmeta_ref[:, 0:1])
        in_seg = (seg_column >= 0) & (seg_column < segments) & (seg_column == kmeta_ref[:, 1:2])
        for head in range(2):
            outside = (lane // width) != head
            side_ref[head, block] = one_hot((one | in_seg | ones) & outside)


def note_queries(match_ref, apart_ref, qmeta_ref, column, segments):
    same = (column < EXACT_PARTS * VARIATES) & ((column % VARIATES) == qmeta_ref[:, 0:1])
    match_ref[...] = jnp.where(same, 1.0, 0.0)
    seg_column = column - EXACT_PARTS * VARIATES
    apart = (seg_column >= 0) & (seg_column < segments) & (seg_column != qmeta_ref[:, 1:2])
    apart_ref[...] = jnp.where(apart, MASKED, 0.0)


def bias_rows(bias_ref, head, column):
    rows = []
    for which in range(2):
        row = jnp.zeros(column.shape, jnp.float32)
        value = jnp.full(column.shape, bias_ref[which, head], jnp.float32)
        for index, part in enumerate(exact_parts(value)):
            row = jnp.where(column // VARIATES == index, part, row)
        rows.append(row)
    return rows


def query_side(match_ref, apart_ref, bias_ref, head, column):
    same, other = bias_rows(bias_ref, head, column[:1])
    return jnp.where(match_ref[...] > 0.0, same, other) + apart_ref[...]


def head_lanes(head, width, lanes):
    lane = lax.broadcasted_iota(jnp.int32, (1, lanes), 1)
    return jnp.where(lane // width == head, 1.0, 0.0).astype(jnp.bfloat16)


def attend_kernel(key_blocks, segments, width, bias_ref, query_ref, qmeta_ref, *refs):
    key_refs, value_refs, kmeta_refs = (
        refs[:key_blocks],
        refs[key_blocks : 2 * key_blocks],
        refs[2 * key_blocks : 3 * key_blocks],
    )
    out_ref, total_ref, side_ref, match_ref, apart_ref = refs[3 * key_blocks :]
    pair = pl.program_id(0)
    rows, lanes = query_ref.shape
    lane = lax.broadcasted_iota(jnp.int32, (rows, lanes), 1)
    column = lane % width

    @pl.when(pair == 0)
    def _():
        note_keys(side_ref, kmeta_refs, column, lane, width, segments)
        note_queries(match_ref, apart_ref, qmeta_ref, column, segments)

    scaled = query_ref[...].astype(jnp.float32) * width ** (-0.5)
    heads = range(lanes // width)
    scores = []
    for head in heads:
        extension = query_side(
            match_ref, apart_ref, bias_ref, pair * (lanes // width) + head, column
        )
        left = jnp.where((lane // width) == head, scaled, extension).astype(jnp.bfloat16)
        inside = head_lanes(head, width, lanes)
        for block in range(key_blocks):
            right = key_refs[block][...] * inside + side_ref[head, block]
            scores.append(contract_last(left, right))
    results = []
    for head in heads:
        inside = head_lanes(head, width, lanes)
        outside = head_lanes(1 - head, width, lanes)
        weights = [
            jnp.exp(score).astype(jnp.bfloat16)
            for score in scores[head * key_blocks : (head + 1) * key_blocks]
        ]
        values = [ref[...] * inside + outside for ref in value_refs]
        results.append(dot(beside(*weights), above(*values)))
    first = (lane // width) == 0
    numerator = jnp.where(first, results[0], results[1])
    crossed = jnp.where(first, results[1], results[0])
    out_ref[...] = (numerator / pltpu.roll(crossed, width, 1)).astype(jnp.bfloat16)
    total_ref[...] = jnp.log(crossed)


def lane_block(rows, lanes):
    return pl.BlockSpec((rows, lanes), lambda pair: (0, pair))


def whole_block(shape):
    return pl.BlockSpec(shape, lambda pair: (0,) * len(shape))


def attend(attn_bias, query_low, query_meta, keys, values, key_metas, segments, width):
    rows, features = query_low.shape
    lanes = 2 * width
    count = len(keys)
    flops = 4 * rows * rows * count * features
    return pl.pallas_call(
        functools.partial(attend_kernel, count, segments, width),
        grid=(features // lanes,),
        in_specs=[
            pl.BlockSpec(memory_space=pltpu.SMEM),
            lane_block(rows, lanes),
            whole_block(query_meta.shape),
        ]
        + [lane_block(rows, lanes)] * (2 * count)
        + [whole_block(query_meta.shape)] * count,
        out_specs=[lane_block(rows, lanes)] * 2,
        out_shape=[
            jax.ShapeDtypeStruct((rows, features), jnp.bfloat16),
            jax.ShapeDtypeStruct((rows, features), jnp.float32),
        ],
        scratch_shapes=[
            pltpu.VMEM((2, count, rows, lanes), jnp.bfloat16),
            pltpu.VMEM((rows, lanes), jnp.float32),
            pltpu.VMEM((rows, lanes), jnp.float32),
        ],
        compiler_params=pltpu.CompilerParams(vmem_limit_bytes=VMEM_LIMIT),
        cost_estimate=pl.CostEstimate(
            flops=flops, bytes_accessed=12 * rows * features, transcendentals=0
        ),
        name="attend",
    )(attn_bias, query_low, query_meta, *keys, *values, *key_metas)


def attend_back_kernel(
    key_blocks,
    segments,
    width,
    bias_ref,
    query_ref,
    qmeta_ref,
    total_ref,
    attended_ref,
    grad_ref,
    *refs,
):
    key_refs, value_refs, kmeta_refs = (
        refs[:key_blocks],
        refs[key_blocks : 2 * key_blocks],
        refs[2 * key_blocks : 3 * key_blocks],
    )
    results = refs[len(refs) - 4 - 2 * key_blocks :]
    grad_query_ref = results[0]
    grad_key_refs = results[1 : key_blocks + 1]
    grad_value_refs = results[key_blocks + 1 : 2 * key_blocks + 1]
    side_ref, match_ref, apart_ref = results[2 * key_blocks + 1 :]
    pair = pl.program_id(0)
    rows, lanes = query_ref.shape
    lane = lax.broadcasted_iota(jnp.int32, (rows, lanes), 1)
    column = lane % width
    ones_at = EXACT_PARTS * VARIATES + segments

    @pl.when(pair == 0)
    def _():
        note_keys(side_ref, kmeta_refs, column, lane, width, segments)
        note_queries(match_ref, apart_ref, qmeta_ref, column, segments)

    scaled = query_ref[...].astype(jnp.float32) * width ** (-0.5)
    scaled_low = scaled.astype(jnp.bfloat16)
    grad_low = grad_ref[...]
    grad = grad_low.astype(jnp.float32)
    overlap = grad * attended_ref[...].astype(jnp.float32)
    square_row = lax.broadcasted_iota(jnp.int32, (lanes, lanes), 0)
    square_column = lax.broadcasted_iota(jnp.int32, (lanes, lanes), 1)
    across = one_hot(square_row // width != square_column // width)
    high = overlap.astype(jnp.bfloat16)
    rest = (overlap - high.astype(jnp.float32)).astype(jnp.bfloat16)
    dot_side = parts_in_lanes(-(dot(high, across) + dot(rest, across)), ones_at, column)
    total_side = parts_in_lanes(-total_ref[...], ones_at, column)
    heads = range(lanes // width)
    blocks = range(key_blocks)
    probs, grad_probs = {}, {}
    for head in heads:
        inside = (lane // width) == head
        extension = total_side + query_side(
            match_ref, apart_ref, bias_ref, pair * (lanes // width) + head, column
        )
        right = jnp.where(inside, scaled, extension).astype(jnp.bfloat16)
        grad_right = jnp.where(inside, grad, dot_side).astype(jnp.bfloat16)
        own_lanes = head_lanes(head, width, lanes)
        for block in blocks:
            side = side_ref[head, block]
            probs[head, block] = contract_last(key_refs[block][...] * own_lanes + side, right)
            grad_probs[head, block] = contract_last(
                value_refs[block][...] * own_lanes + side, grad_right
            )
    grad_query_parts = []
    grad_keys = [[] for _ in blocks]
    grad_values = [[] for _ in blocks]
    keys_turned = beside(*[jnp.transpose(ref[...]) for ref in key_refs])
    for head in heads:
        grad_scores = []
        for block in blocks:
            prob = jnp.exp(probs[head, block])
            grad_score = (prob * grad_probs[head, block]).astype(jnp.bfloat16)
            grad_values[block].append(dot(prob.astype(jnp.bfloat16), grad_low))
            grad_keys[block].append(dot(grad_score, scaled_low))
            grad_scores.append(grad_score)
        grad_query_parts.append(
            dot(keys_turned[head * width : (head + 1) * width], above(*grad_scores))
        )
    first = (lane // width) == 0
    stacked = jnp.concatenate(grad_query_parts, axis=0) * width ** (-0.5)
    grad_query_ref[...] = jnp.transpose(stacked).astype(jnp.bfloat16)
    for block in range(key_blocks):
        grad_key_refs[block][...] = jnp.where(first, *grad_keys[block]).astype(
            grad_key_refs[block].dtype
        )
        grad_value_refs[block][...] = jnp.where(first, *grad_values[block]).astype(
            grad_value_refs[block].dtype
        )


def attend_back(
    attn_bias,
    query_low,
    query_meta,
    log_total,
    attended_low,
    grad_attended,
    keys,
    values,
    key_metas,
    segments,
    width,
):
    rows, features = query_low.shape
    lanes = 2 * width
    count = len(keys)
    here = lane_block(rows, lanes)
    flops = 10 * rows * rows * count * features
    low = jax.ShapeDtypeStruct((rows, features), jnp.bfloat16)
    results = pl.pallas_call(
        functools.partial(attend_back_kernel, count, segments, width),
        grid=(features // lanes,),
        in_specs=[
            pl.BlockSpec(memory_space=pltpu.SMEM),
            here,
            whole_block(query_meta.shape),
        ]
        + [here] * (3 + 2 * count)
        + [whole_block(query_meta.shape)] * count,
        out_specs=[here] * (1 + 2 * count),
        out_shape=[low] * (1 + 2 * count),
        scratch_shapes=[
            pltpu.VMEM((2, count, rows, lanes), jnp.bfloat16),
            pltpu.VMEM((rows, lanes), jnp.float32),
            pltpu.VMEM((rows, lanes), jnp.float32),
        ],
        compiler_params=pltpu.CompilerParams(vmem_limit_bytes=VMEM_LIMIT),
        cost_estimate=pl.CostEstimate(
            flops=flops, bytes_accessed=20 * rows * features, transcendentals=0
        ),
        name="attend_back",
    )(
        attn_bias,
        query_low,
        query_meta,
        log_total,
        attended_low,
        grad_attended,
        *keys,
        *values,
        *key_metas,
    )
    return results


def plan_kernel(
    groups,
    rows,
    width,
    member_ref,
    length_ref,
    adapter_ref,
    order_ref,
    variate_ref,
    frequency_ref,
    chosen_ref,
    back_ref,
    turn_ref,
    cos_ref,
    sin_ref,
    *refs,
):
    meta_refs, slot_ref = refs[:-1], refs[-1]
    blocks = variate_ref.shape[0]
    half_devices = groups // 2
    half_blocks = blocks // 2
    half_rows = half_blocks * LANES
    swap_rows = rows // 2
    member = member_ref[0]
    my_half, my_place = member // half_devices, member % half_devices
    places = [lax.rem(my_place + shift, half_devices) for shift in range(half_devices)]
    segments = length_ref.shape[1]
    starts = [jnp.int32(0)]
    for segment in range(segments):
        starts.append(starts[-1] + length_ref[0, segment])
    long_start, long_index = jnp.int32(0), jnp.int32(0)
    for segment in range(segments):
        is_half = length_ref[0, segment] == half_rows
        long_start = jnp.where(is_half, starts[segment], long_start)
        long_index = jnp.where(is_half, segment, long_index)

    block = lax.broadcasted_iota(jnp.int32, (blocks, LANES), 0)
    lane = lax.broadcasted_iota(jnp.int32, (blocks, LANES), 1)
    work_block = jnp.zeros((blocks, LANES), jnp.int32)
    for index in range(blocks):
        work_block = jnp.where(block == order_ref[0, index], index, work_block)
    work_row = work_block * LANES + lane
    is_long = (work_row >= long_start) & (work_row < long_start + half_rows)
    in_first = block < half_blocks
    long_count = jnp.sum(jnp.where(is_long & in_first, 1.0, 0.0)).astype(jnp.int32)
    long_half = jnp.where(2 * long_count < half_rows, 1, 0)
    side = jnp.where(in_first, 0, 1)
    target = jnp.where(is_long, long_half, 1 - long_half)
    foreign = target != side
    flags = jnp.where(foreign, 1.0, 0.0)
    moved = jnp.sum(jnp.where(in_first, flags, 0.0)).astype(jnp.int32)
    square_row = lax.broadcasted_iota(jnp.int32, (LANES, LANES), 0)
    square_column = lax.broadcasted_iota(jnp.int32, (LANES, LANES), 1)
    within = dot(flags.astype(jnp.bfloat16), one_hot(square_row < square_column))
    block_sum = jnp.broadcast_to(jnp.sum(flags, axis=1, keepdims=True), (blocks, LANES))
    from_block = lax.broadcasted_iota(jnp.int32, (blocks, blocks), 1)
    to_block = lax.broadcasted_iota(jnp.int32, (blocks, blocks), 0)
    earlier = (from_block < to_block) & ((from_block < half_blocks) == (to_block < half_blocks))
    before = dot(one_hot(earlier), block_sum.astype(jnp.bfloat16))
    foreign_rank = (within + before).astype(jnp.int32)
    kept_rank = (block - side * half_blocks) * LANES + lane - foreign_rank
    kept_slot = side * half_rows + kept_rank
    foreign_slot = (1 - side) * half_rows + rows + foreign_rank
    foreign_slot = foreign_slot - jnp.clip(moved, 0, swap_rows)
    for index in range(1, half_devices):
        start = index * rows - jnp.minimum(moved, index * swap_rows)
        last = (index - 1) * rows - jnp.minimum(moved, (index - 1) * swap_rows)
        kept_slot = jnp.where(kept_rank >= start, kept_slot + rows - (start - last), kept_slot)
        received = jnp.clip(moved - index * swap_rows, 0, swap_rows)
        previous = jnp.clip(moved - (index - 1) * swap_rows, 0, swap_rows)
        foreign_slot = jnp.where(
            foreign_rank >= index * swap_rows,
            foreign_slot + rows - swap_rows + previous - received,
            foreign_slot,
        )
    slot = jnp.where(foreign, foreign_slot, kept_slot)
    slot_ref[...] = slot

    per_device = rows // LANES
    wanted = lax.broadcasted_iota(jnp.int32, (rows + swap_rows, 1), 0)
    wanted = jnp.where(
        wanted < rows,
        my_half * half_rows + my_place * rows + wanted,
        (1 - my_half) * half_rows + my_place * rows + wanted - swap_rows,
    )
    for shift in range(half_devices):
        for index in range(per_device):
            held = my_half * half_blocks + places[shift] * per_device + index
            column = (shift * per_device + index) * LANES
            chosen_ref[:, column : column + LANES] = one_hot(
                wanted == slot_ref[pl.ds(held, 1), :]
            )

    slot_turned = jnp.transpose(slot.astype(jnp.float32))
    turned_lane = lax.broadcasted_iota(jnp.int32, (LANES, blocks), 1)
    first_lane = lax.broadcasted_iota(jnp.int32, (1, LANES), 1)
    for index in range(per_device):
        held = my_half * half_blocks + my_place * per_device + index
        mine = jnp.sum(
            jnp.where(turned_lane == held, slot_turned, 0.0), axis=1, keepdims=True
        ).astype(jnp.int32)
        here = slice(index * LANES, (index + 1) * LANES)
        column = 0
        for first, half, length in ((0, my_half, rows), (swap_rows, 1 - my_half, swap_rows)):
            for shift in range(half_devices):
                for chunk in range(0, length, LANES):
                    number = half * half_rows + places[shift] * rows + first + chunk
                    back_ref[here, column : column + LANES] = one_hot(mine == number + first_lane)
                    column += LANES

    on_long = my_half == long_half
    for turn in range(2):
        chosen_segment = jnp.where(
            on_long, long_index, jnp.where(long_index <= turn, turn + 1, turn)
        )
        adapter = adapter_ref[0, 0]
        for segment in range(1, segments):
            adapter = jnp.where(chosen_segment == segment, adapter_ref[0, segment], adapter)
        turn_ref[turn] = adapter

    variate_turned = jnp.transpose(variate_ref[...].astype(jnp.float32))
    known = []
    for index in range(blocks):
        values = jnp.where(
            square_column == 0,
            work_block[index : index + 1, :].astype(jnp.float32),
            jnp.where(
                square_column == 1,
                square_row.astype(jnp.float32),
                variate_turned[:, index : index + 1],
            ),
        )
        known.append(jnp.where(square_column < 3, values, 0.0).astype(jnp.bfloat16))
    number = lax.broadcasted_iota(jnp.int32, (rows, 1), 0)
    wide_lane = lax.broadcasted_iota(jnp.int32, (rows, LANES), 1)
    for shift in range(half_devices):
        slots = my_half * half_rows + places[shift] * rows + number
        facts = jnp.zeros((rows, LANES), jnp.float32)
        for index in range(blocks):
            facts = facts + dot(one_hot(slots == slot[index : index + 1, :]), known[index])
        facts = facts.astype(jnp.int32)
        row = facts[:, 0:1] * LANES + facts[:, 1:2]
        segment = jnp.zeros((rows, 1), jnp.int32)
        first_row = jnp.zeros((rows, 1), jnp.int32)
        for index in range(1, segments):
            segment = jnp.where(row >= starts[index], index, segment)
            first_row = jnp.where(row >= starts[index], starts[index], first_row)
        turn = jnp.where(segment > long_index, segment - 1, segment)
        turn = jnp.where(on_long, 0, turn)
        meta_refs[shift][...] = jnp.where(
            wide_lane == 0, facts[:, 2:3], jnp.where(wide_lane == 1, segment, turn)
        )
        if shift == 0:
            angles = (row - first_row).astype(jnp.float32) * frequency_ref[...]
            sign = jnp.where(wide_lane % width < width // 2, -1.0, 1.0)
            cos_ref[...] = jnp.cos(angles)
            sin_ref[...] = jnp.sin(angles) * sign


def plan(groups, rows, width, member, seq_len, seq_adapter, block_order, variate):
    half_devices = groups // 2
    half_rows = half_devices * rows
    blocks = block_order.shape[1]
    smem = pl.BlockSpec(memory_space=pltpu.SMEM)
    vmem = pl.BlockSpec(memory_space=pltpu.VMEM)
    results = pl.pallas_call(
        functools.partial(plan_kernel, groups, rows, width),
        in_specs=[smem, smem, smem, smem, vmem, vmem],
        out_specs=[vmem, vmem, smem, vmem, vmem] + [vmem] * half_devices,
        out_shape=[
            jax.ShapeDtypeStruct((rows + rows // 2, half_rows), jnp.bfloat16),
            jax.ShapeDtypeStruct((rows, half_rows + half_rows // 2), jnp.bfloat16),
            jax.ShapeDtypeStruct((2,), jnp.int32),
            jax.ShapeDtypeStruct((rows, LANES), jnp.float32),
            jax.ShapeDtypeStruct((rows, LANES), jnp.float32),
        ]
        + [jax.ShapeDtypeStruct((rows, LANES), jnp.int32)] * half_devices,
        scratch_shapes=[pltpu.VMEM((blocks, LANES), jnp.int32)],
        compiler_params=pltpu.CompilerParams(vmem_limit_bytes=VMEM_LIMIT),
        cost_estimate=pl.CostEstimate(
            flops=2**31, bytes_accessed=4 * rows * half_rows, transcendentals=0
        ),
        name="plan",
    )(
        member,
        seq_len,
        seq_adapter,
        block_order,
        variate.reshape(blocks, LANES),
        jnp.asarray(rope_frequency(width)),
    )
    return (*results[:5], results[5:])


def pick_kernel(counts, later_count, chosen_ref, *refs):
    outs = refs[sum(counts) + later_count : sum(counts) + later_count + len(counts)]
    refs = iter(refs[: sum(counts)])
    for count, out_ref in zip(counts, outs):
        total = jnp.zeros(out_ref.shape, jnp.float32)
        column = 0
        for _ in range(count):
            ref = next(refs)
            rows = ref.shape[0]
            total = total + dot(chosen_ref[:, column : column + rows], ref[...])
            column += rows
        out_ref[...] = total.astype(out_ref.dtype)


def pick(chosen, first, count, *helds, later=()):
    features = helds[0][0].shape[1]
    tile = features // 2
    parts = [part for held in helds for part in held]
    return pl.pallas_call(
        functools.partial(pick_kernel, [len(held) for held in helds], len(later)),
        grid=(features // tile,),
        in_specs=[pl.BlockSpec((count, chosen.shape[1]), lambda step: (first // count, 0))]
        + [pl.BlockSpec((part.shape[0], tile), lambda step: (0, step)) for part in parts]
        + [pl.BlockSpec(memory_space=pl.ANY)] * len(later),
        out_specs=[pl.BlockSpec((count, tile), lambda step: (0, step))] * len(helds)
        + [pl.BlockSpec(memory_space=pl.ANY)] * len(later),
        out_shape=[jax.ShapeDtypeStruct((count, features), jnp.bfloat16)] * len(helds)
        + [jax.ShapeDtypeStruct(array.shape, array.dtype) for array in later],
        input_output_aliases={1 + len(parts) + i: len(helds) + i for i in range(len(later))},
        compiler_params=pltpu.CompilerParams(vmem_limit_bytes=VMEM_LIMIT),
        cost_estimate=pl.CostEstimate(
            flops=2 * count * chosen.shape[1] * features * len(helds),
            bytes_accessed=8 * count * features * len(helds),
            transcendentals=0,
        ),
        name="pick",
    )(chosen, *parts, *later)


def axis_count(names):
    count = 1
    for name in names:
        count *= lax.axis_size(name)
    return count


def within_half(array, shift, groups):
    half = groups // 2
    pairs = [
        (base + (place + shift) % half, base + place)
        for base in (0, half)
        for place in range(half)
    ]
    return lax.ppermute(array, GROUP, pairs)


def gather_half(array, groups):
    return [array] + [within_half(array, shift, groups) for shift in range(1, groups // 2)]


def to_other_half(array, groups):
    half = groups // 2
    return lax.ppermute(array, GROUP, [(i, (i + half) % groups) for i in range(groups)])


def scatter_sum(array, axis_sizes):
    for name, size in reversed(axis_sizes):
        outer = array.shape[0] // size
        array = array.reshape((outer, size) + array.shape[1:])
        bit = 1
        while bit < size:
            index = lax.axis_index(name)
            own = (index // bit) % 2
            spread = array.reshape((outer, size // (2 * bit), 2) + array.shape[2:])
            keep = lax.dynamic_index_in_dim(spread, own, 2, keepdims=False)
            send = lax.dynamic_index_in_dim(spread, 1 - own, 2, keepdims=False)
            got = lax.ppermute(send, name, [(i, i ^ bit) for i in range(size)])
            array = (keep.astype(jnp.float32) + got.astype(jnp.float32)).astype(jnp.bfloat16)
            bit *= 2
        array = array.reshape((outer,) + array.shape[2:])
    return array


LANES = 128
MOMENT_ROWS = 24
PACKS = ("far", "near")
GROUP = ("half", "core")
ALL = PACKS + GROUP


def adam(current, first_old, second_old, grad):
    first_moment = BETA_ONE * first_old + (1.0 - BETA_ONE) * grad
    second_moment = BETA_TWO * second_old + (1.0 - BETA_TWO) * grad * grad
    first_fix = first_moment / (1.0 - BETA_ONE**update_count)
    second_fix = second_moment / (1.0 - BETA_TWO**update_count)
    updated = current - LEARN_RATE * (
        first_fix / (jnp.sqrt(second_fix) + ADAM_EPS) + WEIGHT_DECAY * current
    )
    return first_moment, second_moment, updated.astype(jnp.bfloat16)


def settle_shards(grads, few_choice, adapters, moment1, moment2, groups):
    a_qkv, b_qkv, a_guo, a_down, b_gu, b_do = grads
    features, few = a_qkv.shape[0], few_choice.shape[1]
    quarters = a_down.shape[1] // few
    down = jnp.concatenate([a_down[:, i * few : (i + 1) * few] for i in range(quarters)])
    wide = [a_qkv[:, i * few : (i + 1) * few] for i in range(3)]
    wide += [a_guo[:, i * few : (i + 1) * few] for i in (2, 0, 1)] + [down]
    tall = [b_qkv[i * few : (i + 1) * few] for i in range(3)]
    tall += [b_do[2 * few : 3 * few], b_gu[:few], b_gu[few : 2 * few], b_do[:few]]
    pieces = []
    for grad_a, grad_b in zip(wide, tall):
        pieces.append(lax.dot_general(grad_a, few_choice, (((1,), (1,)), ((), ()))).reshape(-1))
        pieces.append(jnp.dot(few_choice, grad_b).reshape(-1))
    axis_sizes = [(PACKS, axis_count(PACKS)), (GROUP, groups)]
    shards = axis_sizes[0][1] * groups
    flat_grads = jnp.concatenate(pieces).astype(jnp.bfloat16).reshape(shards, -1)
    grad_shard = scatter_sum(flat_grads, axis_sizes).reshape(-1).astype(jnp.float32)
    shard_count = grad_shard.shape[0]
    shard_start = lax.axis_index(ALL) * shard_count
    current = lax.dynamic_slice_in_dim(adapters, shard_start, shard_count).astype(jnp.float32)
    first_moment, second_moment, updated = adam(current, moment1, moment2, grad_shard)
    adapters_new = lax.all_gather(updated, ALL, axis=0, tiled=True)
    return grad_shard, first_moment, second_moment, adapters_new


def spreads_evenly(devices, groups, features, hidden, total):
    rows = total // LANES
    chunks = features // LANES
    return (
        groups == 4
        and ADAPTERS * RANK == LANES
        and devices * chunks == 256
        and chunks == 8
        and hidden == devices * LANES
        and hidden == 4 * features
        and rows % (devices * devices) == 0
        and devices & (devices - 1) == 0
    )


def one_hot(condition):
    return jnp.where(condition, 1.0, 0.0).astype(jnp.bfloat16)


def sum_wide(adapter_row, arrived_ref, first, width):
    sources = arrived_ref.shape[0]
    rows = lax.broadcasted_iota(jnp.int32, (LANES, width * LANES), 0)
    columns = lax.broadcasted_iota(jnp.int32, (LANES, width * LANES), 1)
    fits = (rows // (2 * RANK) == columns // LANES) & (rows % RANK == columns % RANK)
    second = (rows // RANK) % 2 == 1
    adapter = jnp.where(fits, (columns % LANES) // RANK, -1)
    total = jnp.zeros((32, width * LANES), jnp.float32)
    for source in range(sources):
        at = source * 2 * RANK
        chosen = jnp.where(
            second, adapter_row[:, at + RANK : at + RANK + 1], adapter_row[:, at : at + 1]
        )
        total = total + dot(
            arrived_ref[source, first : first + 32, :], one_hot(adapter == chosen)
        )
    return total


def sum_tall(adapter_row, arrived_ref, first):
    sources = arrived_ref.shape[0]
    depth = sources * 2 * RANK
    rows = lax.broadcasted_iota(jnp.int32, (LANES, depth), 0)
    columns = lax.broadcasted_iota(jnp.int32, (LANES, depth), 1)
    choice = one_hot((rows // RANK == adapter_row) & (rows % RANK == columns % RANK))
    held = arrived_ref[:, first : first + 2 * RANK, :].reshape(depth, LANES)
    return jnp.dot(choice, held, preferred_element_type=jnp.float32)


def sum_square(adapter_row, arrived_ref, first):
    sources = arrived_ref.shape[0]
    depth = sources * 16
    rows = lax.broadcasted_iota(jnp.int32, (64, depth), 0)
    columns = lax.broadcasted_iota(jnp.int32, (64, depth), 1)
    choice = one_hot(
        ((rows % 32) // 4 == adapter_row)
        & (rows % 4 == columns % 4)
        & (rows // 32 == (columns % 16) // 8)
    )
    held = arrived_ref[:, first : first + 16, :].reshape(depth, LANES)
    return jnp.dot(choice, held, preferred_element_type=jnp.float32)


def settle_rows(parts, skip, param_ref, m1_ref, m2_ref, m_skip, grad_ref, new_refs):
    row = 0
    for part in parts:
        here = slice(row, row + part.shape[0])
        there = slice(skip + row, skip + row + part.shape[0])
        at = slice(m_skip + row, m_skip + row + part.shape[0])
        row += part.shape[0]
        low = part.astype(jnp.bfloat16)
        grad_ref[here, :] = low
        new = adam(
            param_ref[there, :].astype(jnp.float32),
            m1_ref[at, :],
            m2_ref[at, :],
            low.astype(jnp.float32),
        )[2]
        for new_ref in new_refs:
            new_ref[here, :] = new


def settle_early_kernel(own_rows, arrived_ref, moments_ref, param_ref, *refs):
    grad_ref, new_ref, late_m1_ref, late_m2_ref, tall_ref, square_ref, m1_ref, m2_ref = refs[-8:]
    sources = arrived_ref.shape[0]
    told = 6 * RANK
    tall_column = lax.broadcasted_iota(jnp.int32, tall_ref.shape, 1)
    square_column = lax.broadcasted_iota(jnp.int32, square_ref.shape, 1)
    tall = jnp.zeros(tall_ref.shape, jnp.float32)
    square = jnp.zeros(square_ref.shape, jnp.float32)
    for source in range(sources):
        row = arrived_ref[source, 0:16, :].astype(jnp.float32)
        first, second = row[0:1, told : told + 1], row[0:1, told + 1 : told + 2]
        tall = jnp.where(
            tall_column // (2 * RANK) == source,
            jnp.where((tall_column // RANK) % 2 == 1, second, first),
            tall,
        )
        square = jnp.where(
            square_column // RANK == source,
            jnp.where((square_column // 4) % 2 == 1, second, first),
            square,
        )
        held = moments_ref[source].astype(jnp.float32)
        here = slice(source * own_rows, (source + 1) * own_rows)
        m1_ref[here, :] = held[:own_rows]
        m2_ref[here, :] = held[MOMENT_ROWS : MOMENT_ROWS + own_rows]
    tall = tall.astype(jnp.int32)
    square = square.astype(jnp.int32)
    tall_ref[...] = tall
    square_ref[...] = square
    late = late_m1_ref.shape[0]
    late_m1_ref[...] = m1_ref[:late, :]
    late_m2_ref[...] = m2_ref[:late, :]
    wide = sum_wide(tall, arrived_ref, 0, 3)
    last = sum_wide(tall, arrived_ref, 32, 4)
    pair = sum_square(square, arrived_ref, 128)
    parts = [
        wide[:, 2 * LANES :],
        pair[32:],
        wide[:, :LANES],
        sum_tall(tall, arrived_ref, 64),
        wide[:, LANES : 2 * LANES],
        sum_tall(tall, arrived_ref, 96),
    ]
    parts += [last[:, i * LANES : (i + 1) * LANES] for i in range(4)]
    parts.append(pair[:32])
    copies = [new_ref.at[copy] for copy in range(new_ref.shape[0])]
    settle_rows(parts, late, param_ref, m1_ref, m2_ref, late, grad_ref, copies)


def settle_early(arrived, moments, params, late_rows, after):
    sources = arrived.shape[0]
    rows = params.shape[0] - late_rows
    vmem = pl.BlockSpec(memory_space=pltpu.VMEM)
    low = jax.ShapeDtypeStruct((rows, LANES), jnp.bfloat16)
    late = jax.ShapeDtypeStruct((late_rows, LANES), jnp.float32)
    return pl.pallas_call(
        functools.partial(settle_early_kernel, params.shape[0] // sources),
        in_specs=[vmem, vmem, vmem] + [pl.BlockSpec(memory_space=pl.ANY)] * len(after),
        out_specs=[vmem] * 6,
        out_shape=[
            low,
            jax.ShapeDtypeStruct((lax.axis_size("far"), rows, LANES), jnp.bfloat16),
            late,
            late,
            jax.ShapeDtypeStruct((1, sources * 2 * RANK), jnp.int32),
            jax.ShapeDtypeStruct((1, sources * RANK), jnp.int32),
        ],
        scratch_shapes=[pltpu.VMEM(params.shape, jnp.float32)] * 2,
        compiler_params=pltpu.CompilerParams(vmem_limit_bytes=VMEM_LIMIT),
        cost_estimate=pl.CostEstimate(
            flops=sources * 2**24, bytes_accessed=4 * arrived.size, transcendentals=0
        ),
        name="settle_early",
    )(arrived, moments, params, *after)


def settle_late_kernel(
    tall_ref, square_ref, arrived_ref, param_ref, m1_ref, m2_ref, *refs
):
    early_grad_ref = refs[0]
    own_ref, new_ref, _, grad_ref = refs[-4:]
    wide = sum_wide(tall_ref[...], arrived_ref, 0, 3)
    pairs = [sum_square(square_ref[...], arrived_ref, first) for first in (32, 48)]
    parts = []
    for index in range(3):
        parts.append(wide[:, index * LANES : (index + 1) * LANES])
        parts.append(pairs[index // 2][(index % 2) * 32 : (index % 2) * 32 + 32])
    copies = [new_ref.at[copy] for copy in range(new_ref.shape[0])]
    settle_rows(parts, 0, param_ref, m1_ref, m2_ref, 0, grad_ref, copies)
    low = jnp.concatenate(
        [ref[...].astype(jnp.float32) for ref in (grad_ref, early_grad_ref)], axis=0
    )
    each = low.shape[0] // own_ref.shape[0]
    zeros = jnp.zeros((own_ref.shape[1] - each, LANES), jnp.float32)
    for owner in range(own_ref.shape[0]):
        own_ref[owner] = jnp.concatenate(
            [low[owner * each : (owner + 1) * each], zeros], axis=0
        ).astype(jnp.bfloat16)


def settle_late(tall, square, arrived, params, late_m1, late_m2, early_grad, later, after):
    rows = late_m1.shape[0]
    anywhere = pl.BlockSpec(memory_space=pl.ANY)
    vmem = pl.BlockSpec(memory_space=pltpu.VMEM)
    return pl.pallas_call(
        settle_late_kernel,
        in_specs=[vmem] * 7 + [anywhere] * (1 + len(after)),
        out_specs=[vmem, vmem, anywhere],
        scratch_shapes=[pltpu.VMEM((rows, LANES), jnp.bfloat16)],
        input_output_aliases={7: 2},
        out_shape=[
            jax.ShapeDtypeStruct((arrived.shape[0], MOMENT_ROWS, LANES), jnp.bfloat16),
            jax.ShapeDtypeStruct((axis_count(PACKS), rows, LANES), jnp.bfloat16),
            jax.ShapeDtypeStruct(later.shape, later.dtype),
        ],
        compiler_params=pltpu.CompilerParams(vmem_limit_bytes=VMEM_LIMIT),
        cost_estimate=pl.CostEstimate(
            flops=arrived.shape[0] * 2**24, bytes_accessed=4 * arrived.size, transcendentals=0
        ),
        name="settle_late",
    )(tall, square, arrived, params, late_m1, late_m2, early_grad, later, *after)


def gather_inner(piece, groups):
    pieces = [piece]
    bit = groups // 2
    while bit:
        pairs = [(i, i ^ bit) for i in range(groups)]
        pieces = pieces + [lax.ppermute(piece, GROUP, pairs) for piece in pieces]
        bit //= 2
    return pieces


def placing_order(device, unit):
    size = unit * device.shape[0]
    to_row = lax.broadcasted_iota(jnp.int32, (size, size), 0)
    from_row = jnp.arange(size, dtype=jnp.int32)
    source = (from_row % unit) * device.shape[0] + jnp.repeat(device, unit)
    return (to_row == source[None, :]).astype(jnp.bfloat16)


def piece_devices(groups, devices):
    member = lax.axis_index(GROUP)
    piece = jnp.arange(groups, dtype=jnp.int32)
    mask = jnp.zeros_like(piece)
    bit = 1
    while bit < groups:
        mask = mask * 2 + (piece // bit) % 2
        bit *= 2
    outer = jnp.arange(devices // groups, dtype=jnp.int32)
    return (outer[None, :] * groups + (member ^ mask)[:, None]).reshape(-1)


def hand_on(after, *arrays):
    anywhere = pl.BlockSpec(memory_space=pl.ANY)
    return pl.pallas_call(
        lambda *refs: None,
        in_specs=[anywhere] * (1 + len(arrays)),
        out_specs=[anywhere] * len(arrays),
        out_shape=[jax.ShapeDtypeStruct(array.shape, array.dtype) for array in arrays],
        input_output_aliases={1 + index: index for index in range(len(arrays))},
        name="hand_on",
    )(after, *arrays)


def assemble_kernel(counts, devices, chunks, first, order_ref, *refs):
    piece_refs = []
    for count in counts:
        piece_refs.append(refs[:count])
        refs = refs[count:]
    out_any, placed_ref, sems = refs[-3:]

    def held_rows(part_refs, start, stop):
        before = 0
        for ref in part_refs:
            if start < before + ref.shape[1]:
                return ref[:, start - before : stop - before, :]
            before += ref.shape[1]

    unit = order_ref.shape[0] // devices
    copies = []
    for index, (begin, end) in enumerate(chunks):
        for start in range(begin, end, 2 * unit):
            sides = []
            for side in (start, start + unit):
                held = jnp.concatenate(
                    [held_rows(part_refs, side, side + unit) for part_refs in piece_refs], axis=0
                )
                sides.append(held.reshape(unit * devices, LANES))
            placed = dot(order_ref[...], jnp.concatenate(sides, axis=1)).astype(jnp.bfloat16)
            for half, side in enumerate((start, start + unit)):
                placed_ref[side * devices : (side + unit) * devices, :] = placed[
                    :, half * LANES : (half + 1) * LANES
                ]
        here = slice(begin * devices, end * devices)
        there = slice((first + begin) * devices, (first + end) * devices)
        copies.append(
            pltpu.make_async_copy(placed_ref.at[here, :], out_any.at[there, :], sems.at[index])
        )
        copies[-1].start()
    for copy in copies:
        copy.wait()


def assemble(order, pieces, total_rows, first, before, after):
    devices = len(pieces) * pieces[0][0].shape[0]
    rows = pieces[0][0].shape[1]
    parts = [part for piece in pieces for part in piece]
    step = 32 * max(1, rows // 128)
    chunks = [(begin, min(begin + step, rows)) for begin in range(0, rows, step)]
    vmem, anywhere = pl.BlockSpec(memory_space=pltpu.VMEM), pl.BlockSpec(memory_space=pl.ANY)
    in_specs = [vmem] * (1 + len(parts)) + [anywhere] * len(after)
    operands = [order, *parts, *after]
    aliases = {}
    if before is not None:
        aliases = {len(operands): 0}
        in_specs.append(anywhere)
        operands.append(before)
    return pl.pallas_call(
        functools.partial(assemble_kernel, [len(piece) for piece in pieces], devices, chunks, first),
        in_specs=in_specs,
        out_specs=anywhere,
        out_shape=jax.ShapeDtypeStruct((total_rows, LANES), jnp.bfloat16),
        scratch_shapes=[
            pltpu.VMEM((rows * devices, LANES), jnp.bfloat16),
            pltpu.SemaphoreType.DMA((len(chunks),)),
        ],
        input_output_aliases=aliases,
        compiler_params=pltpu.CompilerParams(vmem_limit_bytes=VMEM_LIMIT),
        cost_estimate=pl.CostEstimate(
            flops=rows * devices * 2**17, bytes_accessed=rows * devices * 512, transcendentals=0
        ),
        name="assemble",
    )(*operands)


def rope_frequency(head_width):
    index = np.arange(LANES) % (head_width // 2)
    return (ROPE_BASE ** (-2.0 * index / head_width)).astype(np.float32)[None, :]


def gain_rows(attn_gain, ffn_gain, q_gain, k_gain):
    repeats = attn_gain.shape[0] // q_gain.shape[0]
    return jnp.concatenate(
        [attn_gain, ffn_gain] + [q_gain] * repeats + [k_gain] * repeats
    ).astype(jnp.float32).reshape(4, -1)


def select_kernel(features, hidden, devices, turn_ref, me_ref, flat_any, *refs):
    m1_ref, m2_ref = refs[:2]
    out_refs, flat_ref, sems = refs[3:-2], refs[-2], refs[-1]
    size = flat_ref.shape[0] // sems.shape[0]
    copies = [
        pltpu.make_async_copy(
            flat_any.at[pl.ds(chunk * size, size), :],
            flat_ref.at[pl.ds(chunk * size, size), :],
            sems.at[chunk],
        )
        for chunk in range(sems.shape[0])
    ]
    for copy in copies:
        copy.start()
    a_qkv_ref, a_guo_ref, a_down_ref, b_qkv_ref, b_gu_ref, b_do_ref = out_refs[:6]
    if devices:
        own_ref, moments_ref, wide_ref = out_refs[6:]
        count = m1_ref.shape[0] // devices
        for device in range(devices):
            rows = []
            for ref in (m1_ref, m2_ref):
                rows.append(ref[pl.ds(device, count, stride=devices), :])
                rows.append(jnp.zeros((MOMENT_ROWS - count, LANES), jnp.float32))
            moments_ref[device] = jnp.concatenate(rows, axis=0).astype(jnp.bfloat16)
        each = size // devices
        for chunk, copy in enumerate(copies):
            copy.wait()
            wide_ref[...] = flat_ref[chunk * size : (chunk + 1) * size, :].astype(jnp.float32)
            own_ref[chunk * each : (chunk + 1) * each, :] = wide_ref[
                pl.ds(me_ref[0], each, stride=devices), :
            ].astype(jnp.bfloat16)
    if not devices:
        for copy in copies:
            copy.wait()
    few = 2 * RANK
    rows = lax.broadcasted_iota(jnp.int32, (LANES, LANES), 0)
    columns = lax.broadcasted_iota(jnp.int32, (LANES, LANES), 1)
    chosen = jnp.where((columns // RANK) % 2 == 1, turn_ref[1], turn_ref[0])
    fits = (rows // RANK == chosen) & (rows % RANK == columns % RANK)
    start = {}
    row = 0
    for name, rows_in, rows_out in (
        ("q", features, features),
        ("k", features, features),
        ("v", features, features),
        ("o", features, features),
        ("g", features, hidden),
        ("u", features, hidden),
        ("d", hidden, features),
    ):
        start[name] = (row, row + rows_in)
        row += rows_in + rows_out

    def wide(names, length):
        total = jnp.zeros((length, LANES), jnp.float32)
        for place, name in enumerate(names):
            first = start[name][0]
            total = total + jnp.dot(
                flat_ref[first : first + length, :],
                one_hot(fits & (columns // few == place)),
                preferred_element_type=jnp.float32,
            )
        return total.astype(jnp.bfloat16)

    a_qkv_ref[...] = wide("qkv", features)
    a_guo_ref[...] = wide("guo", features)
    for first in range(0, hidden, features):
        a_down_ref[first : first + features, :] = jnp.dot(
            flat_ref[start["d"][0] + first : start["d"][0] + first + features, :],
            one_hot(fits & (columns // few == 0)),
            preferred_element_type=jnp.float32,
        ).astype(jnp.bfloat16)

    def tall(name, length, out_ref, place):
        chunks = length // LANES
        size = RANK * chunks
        to_row = lax.broadcasted_iota(jnp.int32, (size, size), 0)
        from_row = lax.broadcasted_iota(jnp.int32, (size, size), 1)
        turned = one_hot(
            (to_row // RANK == from_row % chunks) & (to_row % RANK == from_row // chunks)
        )
        for turn in range(2):
            first = start[name][1] + pl.multiple_of(turn_ref[turn] * size, LANES)
            block = jnp.dot(
                turned, flat_ref[pl.ds(first, size), :], preferred_element_type=jnp.float32
            ).astype(jnp.bfloat16)
            here = place * few + turn * RANK
            for chunk in range(chunks):
                out_ref[here : here + RANK, chunk * LANES : (chunk + 1) * LANES] = block[
                    chunk * RANK : (chunk + 1) * RANK
                ]

    for out_ref, names in ((b_qkv_ref, "qkv"), (b_gu_ref, "gu"), (b_do_ref, "d.o")):
        out_ref[...] = jnp.zeros(out_ref.shape, out_ref.dtype)
        for place, name in enumerate(names):
            if name != ".":
                tall(name, out_ref.shape[1], out_ref, place)


def select(devices, turn_adapter, me, adapters, moments, features, hidden, after):
    shapes = [(features, LANES), (features, LANES), (hidden, LANES)]
    shapes += [(LANES, features), (LANES, hidden), (LANES, features)]
    scratch = []
    if devices:
        shapes.append((adapters.shape[0] // (LANES * devices), LANES))
        shapes.append((devices, 2 * MOMENT_ROWS, LANES))
        scratch.append(pltpu.VMEM((1024, LANES), jnp.float32))
    rows = adapters.shape[0] // LANES
    scratch += [pltpu.VMEM((rows, LANES), jnp.bfloat16), pltpu.SemaphoreType.DMA((rows // 1024,))]
    return pl.pallas_call(
        functools.partial(select_kernel, features, hidden, devices),
        in_specs=[
            pl.BlockSpec(memory_space=pltpu.SMEM),
            pl.BlockSpec(memory_space=pltpu.SMEM),
            pl.BlockSpec(memory_space=pl.ANY),
            pl.BlockSpec(memory_space=pltpu.VMEM),
            pl.BlockSpec(memory_space=pltpu.VMEM),
            pl.BlockSpec(memory_space=pl.ANY),
        ],
        out_specs=[pl.BlockSpec(memory_space=pltpu.VMEM)] * len(shapes),
        out_shape=[jax.ShapeDtypeStruct(shape, jnp.bfloat16) for shape in shapes],
        scratch_shapes=scratch,
        compiler_params=pltpu.CompilerParams(vmem_limit_bytes=VMEM_LIMIT),
        cost_estimate=pl.CostEstimate(
            flops=2**31, bytes_accessed=4 * adapters.shape[0], transcendentals=0
        ),
        name="select",
    )(turn_adapter, me, adapters.reshape(-1, LANES), *moments, after)


def dot(left, right):
    return jnp.dot(left, right, preferred_element_type=jnp.float32)


def beside(*arrays):
    return jnp.concatenate(arrays, axis=1)


def above(*arrays):
    return jnp.concatenate(arrays, axis=0)


def turn_mask(meta_ref):
    rows = meta_ref.shape[0]
    lane = lax.broadcasted_iota(jnp.int32, (rows, LANES), 1)
    mask = jnp.where((lane // RANK) % 2 == meta_ref[:, 2:3], 1.0, 0.0)
    return mask, lane // (2 * RANK)


def row_norm(values):
    return lax.rsqrt(jnp.mean(values * values, axis=1, keepdims=True) + NORM_EPS)


def row_norm_back(values, gain, grad):
    scale = row_norm(values)
    unit = values * scale
    grad = grad * gain
    return scale * (grad - unit * jnp.mean(grad * unit, axis=1, keepdims=True))


def head_mean(values, width):
    lanes = values.shape[1]
    rows = lax.broadcasted_iota(jnp.int32, (lanes, lanes), 0)
    columns = lax.broadcasted_iota(jnp.int32, (lanes, lanes), 1)
    ones = one_hot(rows // width == columns // width)
    return dot(values.astype(jnp.bfloat16), ones) * (1.0 / width)


def swap_halves(values, width):
    lanes = values.shape[1]
    lane = lax.broadcasted_iota(jnp.int32, values.shape, 1)
    ahead = pltpu.roll(values, lanes - width // 2, 1)
    behind = pltpu.roll(values, width // 2, 1)
    return jnp.where(lane % width < width // 2, ahead, behind)


def widen(table, lanes):
    return jnp.concatenate([table] * (lanes // table.shape[1]), axis=1)


def joined(kept_ref, arrived_ref):
    first = kept_ref.shape[0] - arrived_ref.shape[0]
    kept = kept_ref[...]
    return jnp.concatenate([kept[:first], kept[first:] + arrived_ref[...]], axis=0)


def turned_heads(raw, gain, cosine, sine, width):
    unit = raw * lax.rsqrt(head_mean(raw * raw, width) + NORM_EPS) * gain
    return (unit * cosine + swap_halves(unit, width) * sine).astype(jnp.bfloat16)


def project_own(normed, inner, place, index, weight_ref, b_ref):
    own = jnp.where(place == index, ADAPTER_SCALE * inner, 0.0).astype(jnp.bfloat16)
    return dot(beside(normed, own), above(weight_ref[...], b_ref[...]))


def project_key_value_kernel(
    width,
    kept_ref,
    arrived_ref,
    gains_ref,
    wk_ref,
    wv_ref,
    a_ref,
    b_ref,
    meta_ref,
    cos_ref,
    sin_ref,
    _,
    x_ref,
    normed_ref,
    inner_ref,
    raw_ref,
    k_ref,
    v_ref,
    __,
):
    mask, place = turn_mask(meta_ref)

    @pl.when(pl.program_id(0) == 0)
    def _():
        rows = joined(kept_ref, arrived_ref)
        x_ref[...] = rows
        values = rows.astype(jnp.float32)
        normed = (values * row_norm(values) * gains_ref[0:1, :]).astype(
            jnp.bfloat16
        )
        normed_ref[...] = normed
        inner_ref[...] = (dot(normed, a_ref[...]) * mask).astype(jnp.bfloat16)

    normed = normed_ref[...]
    inner = inner_ref[...].astype(jnp.float32)
    lanes = wk_ref.shape[1]
    cosine, sine = widen(cos_ref[...], lanes), widen(sin_ref[...], lanes)
    key = project_own(normed, inner, place, 1, wk_ref, b_ref)
    raw_ref[...] = key.astype(jnp.bfloat16)
    k_ref[...] = turned_heads(key, gains_ref[3:4, :lanes], cosine, sine, width)
    v_ref[...] = project_own(normed, inner, place, 2, wv_ref, b_ref).astype(jnp.bfloat16)


def project_query_kernel(
    width, normed_ref, inner_ref, wq_ref, b_ref, cos_ref, sin_ref, gains_ref, raw_ref, q_ref
):
    lanes = wq_ref.shape[1]
    place = lax.broadcasted_iota(jnp.int32, inner_ref.shape, 1) // (2 * RANK)
    cosine, sine = widen(cos_ref[...], lanes), widen(sin_ref[...], lanes)
    inner = inner_ref[...].astype(jnp.float32)
    query = project_own(normed_ref[...], inner, place, 0, wq_ref, b_ref)
    raw_ref[...] = query.astype(jnp.bfloat16)
    q_ref[...] = turned_heads(query, gains_ref[2:3, :lanes], cosine, sine, width)


def project_heads(
    kept,
    arrived,
    later,
    gains,
    weights,
    a_qkv,
    b_qkv,
    meta,
    cos_table,
    sin_table,
    width,
):
    rows, features = kept.shape
    tile = 512
    grid = (features // tile,)

    def tiled(height):
        return pl.BlockSpec((height, tile), lambda step: (0, step))

    def shape(dtype):
        return jax.ShapeDtypeStruct((rows, features), dtype)

    full, few = whole_block((rows, features)), whole_block((rows, LANES))
    low = shape(jnp.bfloat16)
    anywhere = pl.BlockSpec(memory_space=pl.ANY)
    x, normed, inner, key_raw, key, value, later = pl.pallas_call(
        functools.partial(project_key_value_kernel, width),
        grid=grid,
        in_specs=[full, whole_block(arrived.shape), whole_block(gains.shape)]
        + [tiled(features)] * 2
        + [whole_block((features, LANES)), tiled(LANES), few, few, few]
        + [anywhere],
        out_specs=[full, full, few] + [tiled(rows)] * 3 + [anywhere],
        input_output_aliases={10: 6},
        out_shape=[
            low,
            low,
            jax.ShapeDtypeStruct((rows, LANES), jnp.bfloat16),
            low,
            low,
            low,
            jax.ShapeDtypeStruct(later.shape, later.dtype),
        ],
        compiler_params=pltpu.CompilerParams(vmem_limit_bytes=VMEM_LIMIT),
        cost_estimate=pl.CostEstimate(
            flops=6 * rows * features * features,
            bytes_accessed=4 * features * features + 14 * rows * features,
            transcendentals=0,
        ),
        name="project_key_value",
    )(
        kept,
        arrived,
        gains,
        *weights[1:],
        a_qkv,
        b_qkv,
        meta,
        cos_table,
        sin_table,
        later,
    )
    query_raw, query = pl.pallas_call(
        functools.partial(project_query_kernel, width),
        grid=grid,
        in_specs=[full, few, tiled(features), tiled(LANES), few, few, whole_block(gains.shape)],
        out_specs=[tiled(rows)] * 2,
        out_shape=[low, low],
        compiler_params=pltpu.CompilerParams(vmem_limit_bytes=VMEM_LIMIT),
        cost_estimate=pl.CostEstimate(
            flops=3 * rows * features * features,
            bytes_accessed=2 * features * features + 8 * rows * features,
            transcendentals=0,
        ),
        name="project_query",
    )(normed, inner, weights[0], b_qkv, cos_table, sin_table, gains)
    return x, normed, inner, query_raw, key_raw, query, key, value, later


def project_heads_back_kernel(
    count,
    width,
    devices,
    gq_ref,
    *refs,
):
    gk_refs, gv_refs, refs = refs[:count], refs[count : 2 * count], refs[2 * count :]
    (
        q_raw_ref,
        k_raw_ref,
        normed_any,
        inner_ref,
        x_any,
        residual_any,
        gains_ref,
        wq_ref,
        wk_ref,
        wv_ref,
        a_ref,
        b_ref,
        meta_ref,
        cos_ref,
        sin_ref,
    ) = refs[:15]
    if devices:
        out_ref, tail_ref, spread_ref = refs[-9:-6]
    else:
        out_ref, tail_ref, grad_a_ref, grad_b_ref = refs[-10:-6]
    total_ref, few_ref, tall_ref, square_ref, held_ref, sems = refs[-6:]
    step = pl.program_id(0)
    lanes = wq_ref.shape[1]
    mask, place = turn_mask(meta_ref)
    cosine, sine = widen(cos_ref[...], lanes), widen(sin_ref[...], lanes)

    def turned_back(grad, raw, head_gain):
        raw = raw.astype(jnp.float32)
        grad = grad * cosine - swap_halves(grad, width) * sine
        scale = lax.rsqrt(head_mean(raw * raw, width) + NORM_EPS)
        unit = raw * scale
        grad = grad * head_gain
        return (scale * (grad - unit * head_mean(grad * unit, width))).astype(jnp.bfloat16)

    def summed(term_refs):
        total = term_refs[0][...].astype(jnp.float32)
        for ref in term_refs[1:]:
            total = total + ref[...].astype(jnp.float32)
        return total

    copies = [
        pltpu.make_async_copy(source, held_ref.at[index], sems.at[index])
        for index, source in enumerate((normed_any, x_any, residual_any))
    ]

    @pl.when(step == 0)
    def _():
        for copy in copies:
            copy.start()
        total_ref[...] = jnp.zeros(total_ref.shape, jnp.float32)
        few_ref[...] = jnp.zeros(few_ref.shape, jnp.float32)

    inner_turned = jnp.transpose(inner_ref[...].astype(jnp.float32) * ADAPTER_SCALE).astype(
        jnp.bfloat16
    )
    errors = [
        turned_back(gq_ref[...].astype(jnp.float32), q_raw_ref[...], gains_ref[2:3, :lanes]),
        turned_back(summed(gk_refs), k_raw_ref[...], gains_ref[3:4, :lanes]),
        summed(gv_refs).astype(jnp.bfloat16),
    ]
    total_ref[...] += contract_last(
        beside(*errors), beside(wq_ref[...], wk_ref[...], wv_ref[...])
    )
    few = few_ref[...]
    wide = 2 * RANK
    for index, error in enumerate(errors):
        few = few + jnp.where(place == index, contract_last(error, b_ref[...]), 0.0)
        here = slice(index * wide, (index + 1) * wide)
        grad_b = dot(inner_turned[here], error)
        for part in range(lanes // LANES):
            square_ref[part, here, :] = grad_b[:, part * LANES : (part + 1) * LANES]
    square_ref[:, 3 * wide :, :] = jnp.zeros(
        (lanes // LANES, LANES - 3 * wide, LANES), jnp.float32
    )
    if devices:
        chunks = held_ref.shape[2] // LANES
        for index in range(lanes // LANES):
            for first, starts in ((wide, (0, wide)), (wide + RANK, (2 * wide, 3 * wide))):
                spread_square_to(
                    spread_ref,
                    first,
                    square_ref,
                    starts,
                    step * (lanes // LANES) + index,
                    chunks,
                    index,
                )
    else:
        for part in range(lanes // LANES):
            grad_b_ref[:, part * LANES : (part + 1) * LANES] = square_ref[part].astype(
                jnp.bfloat16
            )
    few_ref[...] = few

    @pl.when(step == pl.num_programs(0) - 1)
    def _():
        low = (ADAPTER_SCALE * few_ref[...] * mask).astype(jnp.bfloat16)
        low_turned = jnp.transpose(low.astype(jnp.float32)).astype(jnp.bfloat16)
        for copy in copies:
            copy.wait()
        tall_ref[...] = jnp.transpose(dot(low_turned, held_ref[0]))
        if devices:
            spread_wide_to(spread_ref, 0, tall_ref)
        else:
            grad_a_ref[...] = tall_ref[...].astype(jnp.bfloat16)
        grad = total_ref[...] + contract_last(low, a_ref[...])
        out = held_ref[2].astype(jnp.float32) + row_norm_back(
            held_ref[1].astype(jnp.float32), gains_ref[0:1, :], grad
        )
        out_ref[...] = out.astype(jnp.bfloat16)
        tail_ref[...] = out[out.shape[0] - tail_ref.shape[0] :].astype(jnp.bfloat16)


def project_heads_back(
    devices,
    after,
    grad_query,
    key_terms,
    value_terms,
    query_raw,
    key_raw,
    normed,
    inner,
    rows_in,
    grad_residual,
    gains,
    weights,
    a_qkv,
    b_qkv,
    meta,
    cos_table,
    sin_table,
    width,
):
    rows, features = rows_in.shape
    count = len(key_terms)
    tile = 256

    def tiled(height):
        return pl.BlockSpec((height, tile), lambda step: (0, step))

    full = whole_block((rows, features))
    anywhere = pl.BlockSpec(memory_space=pl.ANY)
    if devices:
        spread = (devices, 4 * RANK, LANES)
        grad_specs = [whole_block(spread)]
        grad_shapes = [jax.ShapeDtypeStruct(spread, jnp.bfloat16)]
    else:
        grad_specs = [whole_block((features, LANES)), tiled(LANES)]
        grad_shapes = [
            jax.ShapeDtypeStruct((features, LANES), jnp.bfloat16),
            jax.ShapeDtypeStruct((LANES, features), jnp.bfloat16),
        ]
    return pl.pallas_call(
        functools.partial(project_heads_back_kernel, count, width, devices),
        grid=(features // tile,),
        in_specs=[tiled(rows)] * (3 + 2 * count)
        + [anywhere, whole_block((rows, LANES)), anywhere, anywhere, whole_block(gains.shape)]
        + [tiled(features)] * 3
        + [whole_block((features, LANES)), tiled(LANES), whole_block(meta.shape)]
        + [whole_block((rows, LANES))] * 2
        + [anywhere] * len(after),
        out_specs=[full, whole_block((rows // 2, features)), *grad_specs],
        out_shape=[
            jax.ShapeDtypeStruct((rows, features), jnp.bfloat16),
            jax.ShapeDtypeStruct((rows // 2, features), jnp.bfloat16),
            *grad_shapes,
        ],
        scratch_shapes=[
            pltpu.VMEM((rows, features), jnp.float32),
            pltpu.VMEM((rows, LANES), jnp.float32),
            pltpu.VMEM((features, LANES), jnp.float32),
            pltpu.VMEM((tile // LANES, LANES, LANES), jnp.float32),
            pltpu.VMEM((3, rows, features), jnp.bfloat16),
            pltpu.SemaphoreType.DMA((3,)),
        ],
        compiler_params=pltpu.CompilerParams(vmem_limit_bytes=VMEM_LIMIT),
        cost_estimate=pl.CostEstimate(
            flops=8 * rows * features * features,
            bytes_accessed=6 * features * features + 30 * rows * features,
            transcendentals=0,
        ),
        name="project_heads_back",
    )(
        grad_query,
        *key_terms,
        *value_terms,
        query_raw,
        key_raw,
        normed,
        inner,
        rows_in,
        grad_residual,
        gains,
        *weights,
        a_qkv,
        b_qkv,
        meta,
        cos_table,
        sin_table,
        *after,
    )


def spread_wide_to(spread_ref, first, held_ref):
    devices = spread_ref.shape[0]
    count = held_ref.shape[0] // devices
    for device in range(devices):
        spread_ref[device, first : first + count, :] = held_ref[
            pl.ds(device, count, stride=devices), :
        ].astype(jnp.bfloat16)


def spread_square_to(spread_ref, first, held_ref, starts, chunk, chunks, index):
    classes = spread_ref.shape[0] // chunks
    count = 2 * RANK // classes
    for part in range(classes):
        rows = [
            held_ref[index, pl.ds(start + part, count, stride=classes), :]
            for start in starts
        ]
        spread_ref[part * chunks + chunk, first : first + 2 * count, :] = jnp.concatenate(
            rows, axis=0
        ).astype(jnp.bfloat16)


def feed_forward_kernel(
    devices,
    turn_ref,
    att_ref,
    x_any,
    kept_any,
    arrived_any,
    gains_ref,
    wo_ref,
    wg_any,
    wu_any,
    wd_any,
    a_guo_ref,
    a_down_ref,
    b_gu_ref,
    b_do_ref,
    meta_ref,
    out_any,
    tail_any,
    grad_res_any,
    grad_att_ref,
    *refs,
):
    if devices:
        spread_ref, refs = refs[0], refs[1:]
    else:
        (grad_a_ref, grad_ad_ref, grad_bgu_ref, grad_bdo_ref), refs = refs[:4], refs[4:]
    (
        res_ref,
        hidden_ref,
        inner_ref,
        inner_turned_ref,
        sum_ref,
        grad_hidden_ref,
        inner_down_ref,
        few_ref,
        few_down_ref,
        few_down_turned_ref,
        down_ref,
        tall_ref,
        square_ref,
        e_ref,
        x_ref,
        arrived_ref,
        wg_ref,
        wu_ref,
        wd_ref,
        out_ref,
        grad_res_ref,
        rows_sems,
        tile_sems,
        out_sems,
    ) = refs
    step = pl.program_id(0)
    steps = pl.num_programs(0)
    mask, place = turn_mask(meta_ref)
    tile = wg_ref.shape[2]
    swap_rows = arrived_ref.shape[0]
    row_copies = [
        pltpu.make_async_copy(source, target, rows_sems.at[index])
        for index, (source, target) in enumerate(
            ((x_any, x_ref), (kept_any, e_ref), (arrived_any, arrived_ref))
        )
    ]

    def tile_copies(number):
        slot = number % 2
        here = pl.ds(pl.multiple_of(number * tile, tile), tile)
        pairs = (
            (wg_any.at[:, here], wg_ref.at[slot]),
            (wu_any.at[:, here], wu_ref.at[slot]),
            (wd_any.at[here, :], wd_ref.at[slot]),
        )
        return [
            pltpu.make_async_copy(source, target, tile_sems.at[slot, index])
            for index, (source, target) in enumerate(pairs)
        ]

    features = wo_ref.shape[0]
    wide = 2 * RANK

    def only(values, index):
        return jnp.where(place == index, values, 0.0).astype(jnp.bfloat16)

    def turn(values):
        return jnp.transpose(values.astype(jnp.float32)).astype(jnp.bfloat16)

    @pl.when(step == 0)
    def _():
        for copy in row_copies:
            copy.start()
        for copy in tile_copies(0):
            copy.start()
        att = att_ref[...]
        inner_out = dot(att, a_guo_ref[...]) * mask
        attention_out = dot(
            beside(att, only(ADAPTER_SCALE * inner_out, 2)), above(wo_ref[...], b_do_ref[...])
        )
        row_copies[0].wait()
        res = x_ref[...].astype(jnp.float32) + attention_out
        res_ref[...] = res
        hidden = (res * row_norm(res) * gains_ref[1:2, :]).astype(jnp.bfloat16)
        hidden_ref[...] = hidden
        inner = dot(hidden, a_guo_ref[...]) * mask
        inner = jnp.where(place == 2, inner_out, inner).astype(jnp.bfloat16)
        inner_ref[...] = inner
        inner_turned_ref[...] = turn(inner.astype(jnp.float32) * ADAPTER_SCALE)
        for copy in row_copies[1:]:
            copy.wait()
        e_ref[e_ref.shape[0] - swap_rows :, :] += arrived_ref[...]
        few_down = only(ADAPTER_SCALE * contract_last(e_ref[...], b_do_ref[...]) * mask, 0)
        few_down_ref[...] = few_down
        few_down_turned_ref[...] = turn(few_down)[:wide]
        sum_ref[...] = jnp.zeros(sum_ref.shape, jnp.float32)
        grad_hidden_ref[...] = jnp.zeros(grad_hidden_ref.shape, jnp.float32)
        inner_down_ref[...] = jnp.zeros(inner_down_ref.shape, jnp.float32)
        few_ref[...] = jnp.zeros(few_ref.shape, jnp.float32)

    @pl.when(step + 1 < steps)
    def _():
        for copy in tile_copies(step + 1):
            copy.start()

    for copy in tile_copies(step):
        copy.wait()
    slot = step % 2
    hidden = hidden_ref[...]
    inner = ADAPTER_SCALE * inner_ref[...].astype(jnp.float32)
    gate_weight, up_weight, down_weight = wg_ref[slot], wu_ref[slot], wd_ref[slot]
    b_tile = b_gu_ref[...]
    gate = dot(beside(hidden, only(inner, 0)), above(gate_weight, b_tile))
    up = dot(beside(hidden, only(inner, 1)), above(up_weight, b_tile))
    grad_act = contract_last(
        beside(e_ref[...], few_down_ref[...]), beside(down_weight, a_down_ref[...])
    )
    sigmoid = 1.0 / (1.0 + jnp.exp(-gate))
    silu = gate * sigmoid
    act = (silu * up).astype(jnp.bfloat16)
    grad_up = (grad_act * silu).astype(jnp.bfloat16)
    grad_gate = (grad_act * up * (sigmoid * (1.0 + gate * (1.0 - sigmoid)))).astype(jnp.bfloat16)
    sum_ref[...] += dot(act, down_weight)
    inner_down_ref[...] += dot(act, a_down_ref[...])
    grad_hidden_ref[...] += contract_last(
        beside(grad_gate, grad_up), beside(gate_weight, up_weight)
    )
    few_ref[...] += jnp.where(
        place == 0, contract_last(grad_gate, b_tile), contract_last(grad_up, b_tile)
    )
    grad_b_gate = dot(inner_turned_ref[:wide, :], grad_gate).astype(jnp.bfloat16)
    grad_b_up = dot(inner_turned_ref[wide : 2 * wide, :], grad_up).astype(jnp.bfloat16)
    if devices:
        for index in range(tile // LANES):
            device = step * (tile // LANES) + index
            chunk = slice(index * LANES, (index + 1) * LANES)
            spread_ref[device, 2 * wide : 3 * wide, :] = grad_b_gate[:, chunk]
            spread_ref[device, 3 * wide : 4 * wide, :] = grad_b_up[:, chunk]
    else:
        grad_bgu_ref[:wide, :] = grad_b_gate
        grad_bgu_ref[wide:, :] = grad_b_up
    per_quarter = features // tile
    down_ref[
        pl.ds(pl.multiple_of((step // per_quarter) * wide, wide), wide),
        pl.ds(pl.multiple_of((step % per_quarter) * tile, tile), tile),
    ] = dot(few_down_turned_ref[...], act)

    out_copies = [
        pltpu.make_async_copy(source, target, out_sems.at[index])
        for index, (source, target) in enumerate(
            (
                (out_ref, out_any),
                (out_ref.at[out_ref.shape[0] - swap_rows :, :], tail_any),
                (grad_res_ref, grad_res_any),
            )
        )
    ]

    @pl.when(step == steps - 1)
    def _():
        grads_out = e_ref[...]
        inner_down = only(inner_down_ref[...] * mask, 0)
        res = res_ref[...]
        out_ref[...] = (
            res + sum_ref[...] + ADAPTER_SCALE * dot(inner_down, b_do_ref[...])
        ).astype(jnp.bfloat16)
        for copy in out_copies[:2]:
            copy.start()
        few = jnp.where(place < 2, ADAPTER_SCALE * few_ref[...] * mask, 0.0).astype(jnp.bfloat16)
        grad_hidden = grad_hidden_ref[...] + contract_last(few, a_guo_ref[...])
        grad_res = grads_out.astype(jnp.float32) + row_norm_back(
            res, gains_ref[1:2, :], grad_hidden
        )
        low = grad_res.astype(jnp.bfloat16)
        grad_res_ref[...] = low
        out_copies[2].start()
        few_out = only(ADAPTER_SCALE * contract_last(low, b_do_ref[...]) * mask, 2)
        grad_att_ref[...] = contract_last(
            beside(low, few_out), beside(wo_ref[...], a_guo_ref[...])
        ).astype(jnp.bfloat16)
        grad_a = dot(turn(few), hidden_ref[...]) + dot(turn(few_out), att_ref[...])
        inner_out = only(inner_ref[...].astype(jnp.float32), 2)
        grad_b = ADAPTER_SCALE * (
            dot(turn(inner_down), grads_out) + dot(turn(inner_out), low)
        )
        if devices:
            lane = lax.broadcasted_iota(jnp.int32, (features, LANES), 1)
            told = jnp.where(
                lane == 3 * wide, turn_ref[0], jnp.where(lane == 3 * wide + 1, turn_ref[1], 0)
            )
            tall_ref[...] = jnp.transpose(grad_a) + told.astype(jnp.float32)
            spread_wide_to(spread_ref, 0, tall_ref)
            tall_ref[...] = jnp.transpose(down_ref[...])
            spread_wide_to(spread_ref, wide, tall_ref)
            chunks = features // LANES
            for chunk in range(chunks):
                square_ref[chunk] = grad_b[:, chunk * LANES : (chunk + 1) * LANES]
                spread_square_to(
                    spread_ref, 4 * wide, square_ref, (0, 2 * wide), chunk, chunks, chunk
                )
        else:
            grad_a_ref[...] = jnp.transpose(grad_a).astype(jnp.bfloat16)
            grad_ad_ref[...] = jnp.transpose(down_ref[...]).astype(jnp.bfloat16)
            grad_bdo_ref[...] = grad_b.astype(jnp.bfloat16)
        for copy in out_copies:
            copy.wait()


def feed_forward(
    devices,
    turn_adapter,
    attended,
    rows_in,
    kept,
    arrived,
    gains,
    weights,
    selected,
    meta,
):
    rows, features = rows_in.shape
    hidden = weights[1].shape[1]
    tile = 512
    full = whole_block((rows, features))
    square = whole_block((features, features))
    anywhere = pl.BlockSpec(memory_space=pl.ANY)

    def shape(height, length, dtype):
        return jax.ShapeDtypeStruct((height, length), dtype)

    if devices:
        spread = (devices, 9 * RANK, LANES)
        grad_specs = [whole_block(spread)]
        grad_shapes = [jax.ShapeDtypeStruct(spread, jnp.bfloat16)]
    else:
        grad_specs = [
            whole_block((features, LANES)),
            whole_block((features, LANES)),
            pl.BlockSpec((4 * RANK, tile), lambda step: (0, step)),
            whole_block((LANES, features)),
        ]
        grad_shapes = [
            shape(features, LANES, jnp.bfloat16),
            shape(features, LANES, jnp.bfloat16),
            shape(4 * RANK, hidden, jnp.bfloat16),
            shape(LANES, features, jnp.bfloat16),
        ]
    return pl.pallas_call(
        functools.partial(feed_forward_kernel, devices),
        grid=(hidden // tile,),
        in_specs=[
            pl.BlockSpec(memory_space=pltpu.SMEM),
            full,
            anywhere,
            anywhere,
            anywhere,
            whole_block(gains.shape),
            square,
            anywhere,
            anywhere,
            anywhere,
            whole_block((features, LANES)),
            pl.BlockSpec((tile, LANES), lambda step: (step, 0)),
            pl.BlockSpec((LANES, tile), lambda step: (0, step)),
            whole_block((LANES, features)),
            whole_block(meta.shape),
        ],
        out_specs=[anywhere, anywhere, anywhere, full, *grad_specs],
        out_shape=[
            shape(rows, features, jnp.bfloat16),
            shape(*arrived.shape, jnp.bfloat16),
            shape(rows, features, jnp.bfloat16),
            shape(rows, features, jnp.bfloat16),
            *grad_shapes,
        ],
        scratch_shapes=[
            pltpu.VMEM((rows, features), jnp.float32),
            pltpu.VMEM((rows, features), jnp.bfloat16),
            pltpu.VMEM((rows, LANES), jnp.bfloat16),
            pltpu.VMEM((LANES, rows), jnp.bfloat16),
            pltpu.VMEM((rows, features), jnp.float32),
            pltpu.VMEM((rows, features), jnp.float32),
            pltpu.VMEM((rows, LANES), jnp.float32),
            pltpu.VMEM((rows, LANES), jnp.float32),
            pltpu.VMEM((rows, LANES), jnp.bfloat16),
            pltpu.VMEM((2 * RANK, rows), jnp.bfloat16),
            pltpu.VMEM((LANES, features), jnp.float32),
            pltpu.VMEM((features, LANES), jnp.float32),
            pltpu.VMEM((features // LANES, LANES, LANES), jnp.float32),
            pltpu.VMEM((rows, features), jnp.bfloat16),
            pltpu.VMEM((rows, features), jnp.bfloat16),
            pltpu.VMEM(arrived.shape, jnp.bfloat16),
            pltpu.VMEM((2, features, tile), jnp.bfloat16),
            pltpu.VMEM((2, features, tile), jnp.bfloat16),
            pltpu.VMEM((2, tile, features), jnp.bfloat16),
            pltpu.VMEM((rows, features), jnp.bfloat16),
            pltpu.VMEM((rows, features), jnp.bfloat16),
            pltpu.SemaphoreType.DMA((3,)),
            pltpu.SemaphoreType.DMA((2, 3)),
            pltpu.SemaphoreType.DMA((3,)),
        ],
        compiler_params=pltpu.CompilerParams(vmem_limit_bytes=VMEM_LIMIT),
        cost_estimate=pl.CostEstimate(
            flops=14 * rows * features * hidden,
            bytes_accessed=8 * features * hidden + 16 * rows * features,
            transcendentals=0,
        ),
        name="feed_forward",
    )(
        turn_adapter,
        attended,
        rows_in,
        kept,
        arrived,
        gains,
        *weights,
        *selected,
        meta,
    )


def settle_owned(grads, moment1, moment2, devices):
    grads = lax.all_to_all(grads, ALL, 0, 0, tiled=True)
    grads = grads[:, : moment1.shape[0] // (LANES * devices)]
    grad_shard = jnp.transpose(grads, (1, 0, 2)).reshape(-1).astype(jnp.float32)
    current = jnp.zeros((), jnp.float32)
    first_moment, second_moment, _ = adam(current, moment1, moment2, grad_shard)
    return grad_shard, first_moment, second_moment


def per_device(
    tokens,
    cotangent,
    variate,
    seq_len,
    seq_adapter,
    block_order,
    attn_gain,
    ffn_gain,
    q_gain,
    k_gain,
    attn_bias,
    query_weight,
    key_weight,
    value_weight,
    output_weight,
    gate_weight,
    up_weight,
    down_weight,
    adapters,
    moment1,
    moment2,
):
    groups = axis_count(GROUP)
    member = lax.axis_index(GROUP)
    row_count, feature_width = tokens.shape
    hidden_width = gate_weight.shape[1]
    head_width = q_gain.shape[0]
    half_devices = groups // 2
    segments = seq_len.shape[1]
    chosen, back, turn_adapter, cos_table, sin_table, key_metas = plan(
        groups, row_count, head_width, member[None], seq_len, seq_adapter, block_order, variate
    )
    meta = key_metas[0]
    axes = ALL
    devices = axis_count(PACKS) * groups
    even = spreads_evenly(devices, groups, feature_width, hidden_width, adapters.shape[0])
    spread = devices if even else 0
    gains = gain_rows(attn_gain, ffn_gain, q_gain, k_gain)


    held = (gather_half(tokens, groups), gather_half(cotangent, groups))
    sent_tokens, sent_grads = pick(chosen, row_count, row_count // 2, *held)
    arrived_tokens = to_other_half(sent_tokens, groups)
    a_qkv, a_guo, a_down, b_qkv, b_gu, b_do, *spread_state = select(
        spread,
        turn_adapter,
        lax.axis_index(axes)[None],
        adapters,
        (moment1.reshape(-1, LANES), moment2.reshape(-1, LANES)),
        feature_width,
        hidden_width,
        sent_tokens,
    )
    if even:
        params, moments = spread_state
        moments = lax.all_to_all(moments, axes, 0, 0, tiled=True)
    kept_tokens, kept_grads = pick(chosen, 0, row_count, *held)
    (
        my_tokens,
        normed,
        inner,
        query_raw,
        key_raw,
        query_low,
        key_low,
        value_low,
        sent_grads,
    ) = project_heads(
        kept_tokens,
        arrived_tokens,
        sent_grads,
        gains,
        (query_weight, key_weight, value_weight),
        a_qkv,
        b_qkv,
        meta,
        cos_table,
        sin_table,
        head_width,
    )
    arrived_grads = to_other_half(sent_grads, groups)
    keys = gather_half(key_low, groups)
    values = gather_half(value_low, groups)
    attended_low, log_total = attend(
        attn_bias, query_low, meta, keys, values, key_metas, segments, head_width
    )
    layer_rows, layer_tail, grad_residual, grad_attended, *forward_grads = feed_forward(
        spread,
        turn_adapter,
        attended_low,
        my_tokens,
        kept_grads,
        arrived_grads,
        gains,
        (output_weight, gate_weight, up_weight, down_weight),
        (a_guo, a_down, b_gu, b_do),
        meta,
    )
    layer_back = to_other_half(layer_tail, groups)
    layer_held = gather_half(layer_rows, groups) + gather_half(layer_back, groups)

    results = attend_back(
        attn_bias,
        query_low,
        meta,
        log_total,
        attended_low,
        grad_attended,
        keys,
        values,
        key_metas,
        segments,
        head_width,
    )
    after = []
    if even:
        total_rows = adapters.shape[0] // LANES
        late_rows = 6 * feature_width // devices
        early = lax.all_to_all(forward_grads[0], axes, 0, 0, tiled=True)
        early_grad, early_new, late_m1, late_m2, tall, square = settle_early(
            early, moments, params, late_rows, [results[0]]
        )
        early_outer = lax.all_to_all(early_new, "far", 0, 0, tiled=True)
        swap = [(0, 1), (1, 0)]
        early_near = lax.ppermute(early_outer, "near", swap)
        early_half = lax.ppermute(early_outer, "half", swap)
        after = [early_new, layer_back]
    grad_query = results[0]
    grad_keys = results[1 : 1 + half_devices]
    grad_values = results[1 + half_devices :]
    key_terms, value_terms = [grad_keys[0]], [grad_values[0]]
    for shift in range(1, half_devices):
        back_shift = half_devices - shift
        key_terms.append(within_half(grad_keys[shift], back_shift, groups))
        value_terms.append(within_half(grad_values[shift], back_shift, groups))
    grad_rows, grad_tail, *back_grads = project_heads_back(
        spread,
        after,
        grad_query,
        key_terms,
        value_terms,
        query_raw,
        key_raw,
        normed,
        inner,
        my_tokens,
        grad_residual,
        gains,
        (query_weight, key_weight, value_weight),
        a_qkv,
        b_qkv,
        meta,
        cos_table,
        sin_table,
        head_width,
    )
    def bring_back(tail):
        return gather_half(grad_rows, groups) + gather_half(to_other_half(tail, groups), groups)

    if not even:
        grads = (*back_grads, *forward_grads)
        column = jnp.arange(2 * RANK, dtype=jnp.int32)
        few_choice = one_hot(
            jnp.arange(LANES, dtype=jnp.int32)[:, None]
            == (jnp.repeat(turn_adapter, RANK) * RANK + column % RANK)[None, :]
        )
        settled = settle_shards(grads, few_choice, adapters, moment1, moment2, groups)
        layer_out = pick(back, 0, row_count, layer_held)[0]
        input_grad = pick(back, 0, row_count, bring_back(grad_tail))[0]
        return (layer_out, input_grad) + settled
    late = lax.all_to_all(back_grads[0], axes, 0, 0, tiled=True)
    layer_out = pick(back, 0, row_count, layer_held)[0]
    own_grads, late_new, grad_tail = settle_late(
        tall, square, late, params, late_m1, late_m2, early_grad, grad_tail, [layer_out, early_near, early_half]
    )
    late_outer = lax.all_to_all(late_new, PACKS, 0, 0, tiled=True)
    late_pieces = gather_inner(late_outer, groups)
    own_grads, early_half = hand_on(late_outer, own_grads, early_half)
    early_far = lax.ppermute(early_half, "near", swap)
    input_grad = pick(back, 0, row_count, bring_back(grad_tail))[0]
    early_pieces = [[early_outer], [early_near], [early_half], [early_far]]
    early_pieces += [
        [lax.ppermute(part, "core", swap) for part in piece] for piece in early_pieces
    ]
    far = jnp.arange(lax.axis_size("far"), dtype=jnp.int32)
    near, half, core = [lax.axis_index(name) for name in ALL[1:]]
    early_device = jnp.concatenate(
        [
            ((far * 2 + (near ^ flip_near)) * 2 + (half ^ flip_half)) * 2 + (core ^ flip_core)
            for flip_core in (0, 1)
            for flip_near, flip_half in ((0, 0), (1, 0), (0, 1), (1, 1))
        ]
    )
    late_pieces = [[piece] for piece in late_pieces]
    order = placing_order(piece_devices(groups, devices), 16)
    adapters_new = assemble(
        placing_order(early_device, 16),
        early_pieces,
        total_rows,
        late_rows,
        None,
        [input_grad, late_pieces[1][0]],
    )
    adapters_new = assemble(order, late_pieces, total_rows, 0, adapters_new, [])
    owned = settle_owned(own_grads, moment1, moment2, devices)
    return (layer_out, input_grad, *owned, adapters_new.reshape(-1))


def solution(mesh):
    packs, groups = mesh.shape["dp"], mesh.shape["group"]
    cut = jax.sharding.Mesh(mesh.devices.reshape(packs // 2, 2, groups // 2, 2), ALL)
    in_specs = (
        P(ALL, None),
        P(ALL, None),
        P(PACKS),
        P(PACKS, None),
        P(PACKS, None),
        P(PACKS, None),
        P(),
        P(),
        P(),
        P(),
        P(),
        P(),
        P(),
        P(),
        P(),
        P(),
        P(),
        P(),
        P(),
        P(ALL),
        P(ALL),
    )
    out_specs = (
        P(ALL, None),
        P(ALL, None),
        P(ALL),
        P(ALL),
        P(ALL),
        P(),
    )
    return jax.shard_map(
        per_device, mesh=cut, in_specs=in_specs, out_specs=out_specs, check_vma=False
    )
```

```python
import functools

import jax
import jax.numpy as jnp
import numpy as np
from jax import lax
from jax.experimental import pallas as pl
from jax.experimental.pallas import tpu as pltpu
from jax.sharding import PartitionSpec as P

RANK = 16
ADAPTERS = 8
NORM_EPS = 1e-06
ADAPTER_SCALE = 2.0
ROPE_BASE = 10000.0
MASKED = -1e30
LEARN_RATE = 0.01
BETA_ONE = 0.9
BETA_TWO = 0.999
ADAM_EPS = 1e-08
WEIGHT_DECAY = 0.01
update_count = 10.0
VARIATES = 4
VMEM_LIMIT = 62 * 1024 * 1024
EXACT_PARTS = 3


def contract_last(left, right):
    return lax.dot_general(
        left, right, (((1,), (1,)), ((), ())), preferred_element_type=jnp.float32
    )


def exact_parts(values):
    parts = []
    for _ in range(EXACT_PARTS):
        part = values.astype(jnp.bfloat16).astype(jnp.float32)
        parts.append(part)
        values = values - part
    return parts


def parts_in_lanes(values, first, column):
    result = jnp.zeros(values.shape, jnp.float32)
    for index, part in enumerate(exact_parts(values)):
        result = jnp.where(column == first + index, part, result)
    return result


def note_keys(side_ref, kmeta_refs, column, lane, width, segments):
    seg_column = column - EXACT_PARTS * VARIATES
    ones = (seg_column >= segments) & (seg_column < segments + EXACT_PARTS)
    for block, kmeta_ref in enumerate(kmeta_refs):
        one = (column < EXACT_PARTS * VARIATES) & ((column % VARIATES) == kmeta_ref[:, 0:1])
        in_seg = (seg_column >= 0) & (seg_column < segments) & (seg_column == kmeta_ref[:, 1:2])
        for head in range(2):
            outside = (lane // width) != head
            side_ref[head, block] = one_hot((one | in_seg | ones) & outside)


def note_queries(match_ref, apart_ref, qmeta_ref, column, segments):
    same = (column < EXACT_PARTS * VARIATES) & ((column % VARIATES) == qmeta_ref[:, 0:1])
    match_ref[...] = jnp.where(same, 1.0, 0.0)
    seg_column = column - EXACT_PARTS * VARIATES
    apart = (seg_column >= 0) & (seg_column < segments) & (seg_column != qmeta_ref[:, 1:2])
    apart_ref[...] = jnp.where(apart, MASKED, 0.0)


def bias_rows(bias_ref, head, column):
    rows = []
    for which in range(2):
        row = jnp.zeros(column.shape, jnp.float32)
        value = jnp.full(column.shape, bias_ref[which, head], jnp.float32)
        for index, part in enumerate(exact_parts(value)):
            row = jnp.where(column // VARIATES == index, part, row)
        rows.append(row)
    return rows


def query_side(match_ref, apart_ref, bias_ref, head, column):
    same, other = bias_rows(bias_ref, head, column[:1])
    return jnp.where(match_ref[...] > 0.0, same, other) + apart_ref[...]


def head_lanes(head, width, lanes):
    lane = lax.broadcasted_iota(jnp.int32, (1, lanes), 1)
    return jnp.where(lane // width == head, 1.0, 0.0).astype(jnp.bfloat16)


def attend_kernel(key_blocks, segments, width, bias_ref, query_ref, qmeta_ref, *refs):
    key_refs, value_refs, kmeta_refs = (
        refs[:key_blocks],
        refs[key_blocks : 2 * key_blocks],
        refs[2 * key_blocks : 3 * key_blocks],
    )
    out_ref, total_ref, side_ref, match_ref, apart_ref = refs[3 * key_blocks :]
    pair = pl.program_id(0)
    rows, lanes = query_ref.shape
    lane = lax.broadcasted_iota(jnp.int32, (rows, lanes), 1)
    column = lane % width

    @pl.when(pair == 0)
    def _():
        note_keys(side_ref, kmeta_refs, column, lane, width, segments)
        note_queries(match_ref, apart_ref, qmeta_ref, column, segments)

    scaled = query_ref[...].astype(jnp.float32) * width ** (-0.5)
    heads = range(lanes // width)
    scores = []
    for head in heads:
        extension = query_side(
            match_ref, apart_ref, bias_ref, pair * (lanes // width) + head, column
        )
        left = jnp.where((lane // width) == head, scaled, extension).astype(jnp.bfloat16)
        inside = head_lanes(head, width, lanes)
        for block in range(key_blocks):
            right = key_refs[block][...] * inside + side_ref[head, block]
            scores.append(contract_last(left, right))
    results = []
    for head in heads:
        inside = head_lanes(head, width, lanes)
        outside = head_lanes(1 - head, width, lanes)
        weights = [
            jnp.exp(score).astype(jnp.bfloat16)
            for score in scores[head * key_blocks : (head + 1) * key_blocks]
        ]
        values = [ref[...] * inside + outside for ref in value_refs]
        results.append(dot(beside(*weights), above(*values)))
    first = (lane // width) == 0
    numerator = jnp.where(first, results[0], results[1])
    crossed = jnp.where(first, results[1], results[0])
    out_ref[...] = (numerator / pltpu.roll(crossed, width, 1)).astype(jnp.bfloat16)
    total_ref[...] = jnp.log(crossed)


def lane_block(rows, lanes):
    return pl.BlockSpec((rows, lanes), lambda pair: (0, pair))


def whole_block(shape):
    return pl.BlockSpec(shape, lambda pair: (0,) * len(shape))


def attend(attn_bias, query_low, query_meta, keys, values, key_metas, segments, width):
    rows, features = query_low.shape
    lanes = 2 * width
    count = len(keys)
    flops = 4 * rows * rows * count * features
    return pl.pallas_call(
        functools.partial(attend_kernel, count, segments, width),
        grid=(features // lanes,),
        in_specs=[
            pl.BlockSpec(memory_space=pltpu.SMEM),
            lane_block(rows, lanes),
            whole_block(query_meta.shape),
        ]
        + [lane_block(rows, lanes)] * (2 * count)
        + [whole_block(query_meta.shape)] * count,
        out_specs=[lane_block(rows, lanes)] * 2,
        out_shape=[
            jax.ShapeDtypeStruct((rows, features), jnp.bfloat16),
            jax.ShapeDtypeStruct((rows, features), jnp.float32),
        ],
        scratch_shapes=[
            pltpu.VMEM((2, count, rows, lanes), jnp.bfloat16),
            pltpu.VMEM((rows, lanes), jnp.float32),
            pltpu.VMEM((rows, lanes), jnp.float32),
        ],
        compiler_params=pltpu.CompilerParams(vmem_limit_bytes=VMEM_LIMIT),
        cost_estimate=pl.CostEstimate(
            flops=flops, bytes_accessed=12 * rows * features, transcendentals=0
        ),
        name="attend",
    )(attn_bias, query_low, query_meta, *keys, *values, *key_metas)


def attend_back_kernel(
    key_blocks,
    segments,
    width,
    bias_ref,
    query_ref,
    qmeta_ref,
    total_ref,
    attended_ref,
    grad_ref,
    *refs,
):
    key_refs, value_refs, kmeta_refs = (
        refs[:key_blocks],
        refs[key_blocks : 2 * key_blocks],
        refs[2 * key_blocks : 3 * key_blocks],
    )
    results = refs[len(refs) - 4 - 2 * key_blocks :]
    grad_query_ref = results[0]
    grad_key_refs = results[1 : key_blocks + 1]
    grad_value_refs = results[key_blocks + 1 : 2 * key_blocks + 1]
    side_ref, match_ref, apart_ref = results[2 * key_blocks + 1 :]
    pair = pl.program_id(0)
    rows, lanes = query_ref.shape
    lane = lax.broadcasted_iota(jnp.int32, (rows, lanes), 1)
    column = lane % width
    ones_at = EXACT_PARTS * VARIATES + segments

    @pl.when(pair == 0)
    def _():
        note_keys(side_ref, kmeta_refs, column, lane, width, segments)
        note_queries(match_ref, apart_ref, qmeta_ref, column, segments)

    scaled = query_ref[...].astype(jnp.float32) * width ** (-0.5)
    scaled_low = scaled.astype(jnp.bfloat16)
    grad_low = grad_ref[...]
    grad = grad_low.astype(jnp.float32)
    overlap = grad * attended_ref[...].astype(jnp.float32)
    square_row = lax.broadcasted_iota(jnp.int32, (lanes, lanes), 0)
    square_column = lax.broadcasted_iota(jnp.int32, (lanes, lanes), 1)
    across = one_hot(square_row // width != square_column // width)
    high = overlap.astype(jnp.bfloat16)
    rest = (overlap - high.astype(jnp.float32)).astype(jnp.bfloat16)
    dot_side = parts_in_lanes(-(dot(high, across) + dot(rest, across)), ones_at, column)
    total_side = parts_in_lanes(-total_ref[...], ones_at, column)
    heads = range(lanes // width)
    blocks = range(key_blocks)
    probs, grad_probs = {}, {}
    for head in heads:
        inside = (lane // width) == head
        extension = total_side + query_side(
            match_ref, apart_ref, bias_ref, pair * (lanes // width) + head, column
        )
        right = jnp.where(inside, scaled, extension).astype(jnp.bfloat16)
        grad_right = jnp.where(inside, grad, dot_side).astype(jnp.bfloat16)
        own_lanes = head_lanes(head, width, lanes)
        for block in blocks:
            side = side_ref[head, block]
            probs[head, block] = contract_last(key_refs[block][...] * own_lanes + side, right)
            grad_probs[head, block] = contract_last(
                value_refs[block][...] * own_lanes + side, grad_right
            )
    grad_query_parts = []
    grad_keys = [[] for _ in blocks]
    grad_values = [[] for _ in blocks]
    keys_turned = beside(*[jnp.transpose(ref[...]) for ref in key_refs])
    for head in heads:
        grad_scores = []
        for block in blocks:
            prob = jnp.exp(probs[head, block])
            grad_score = (prob * grad_probs[head, block]).astype(jnp.bfloat16)
            grad_values[block].append(dot(prob.astype(jnp.bfloat16), grad_low))
            grad_keys[block].append(dot(grad_score, scaled_low))
            grad_scores.append(grad_score)
        grad_query_parts.append(
            dot(keys_turned[head * width : (head + 1) * width], above(*grad_scores))
        )
    first = (lane // width) == 0
    stacked = jnp.concatenate(grad_query_parts, axis=0) * width ** (-0.5)
    grad_query_ref[...] = jnp.transpose(stacked).astype(jnp.bfloat16)
    for block in range(key_blocks):
        grad_key_refs[block][...] = jnp.where(first, *grad_keys[block]).astype(
            grad_key_refs[block].dtype
        )
        grad_value_refs[block][...] = jnp.where(first, *grad_values[block]).astype(
            grad_value_refs[block].dtype
        )


def attend_back(
    attn_bias,
    query_low,
    query_meta,
    log_total,
    attended_low,
    grad_attended,
    keys,
    values,
    key_metas,
    segments,
    width,
):
    rows, features = query_low.shape
    lanes = 2 * width
    count = len(keys)
    here = lane_block(rows, lanes)
    flops = 10 * rows * rows * count * features
    low = jax.ShapeDtypeStruct((rows, features), jnp.bfloat16)
    results = pl.pallas_call(
        functools.partial(attend_back_kernel, count, segments, width),
        grid=(features // lanes,),
        in_specs=[
            pl.BlockSpec(memory_space=pltpu.SMEM),
            here,
            whole_block(query_meta.shape),
        ]
        + [here] * (3 + 2 * count)
        + [whole_block(query_meta.shape)] * count,
        out_specs=[here] * (1 + 2 * count),
        out_shape=[low] * (1 + 2 * count),
        scratch_shapes=[
            pltpu.VMEM((2, count, rows, lanes), jnp.bfloat16),
            pltpu.VMEM((rows, lanes), jnp.float32),
            pltpu.VMEM((rows, lanes), jnp.float32),
        ],
        compiler_params=pltpu.CompilerParams(vmem_limit_bytes=VMEM_LIMIT),
        cost_estimate=pl.CostEstimate(
            flops=flops, bytes_accessed=20 * rows * features, transcendentals=0
        ),
        name="attend_back",
    )(
        attn_bias,
        query_low,
        query_meta,
        log_total,
        attended_low,
        grad_attended,
        *keys,
        *values,
        *key_metas,
    )
    return results


def plan_kernel(
    groups,
    rows,
    width,
    member_ref,
    length_ref,
    adapter_ref,
    order_ref,
    variate_ref,
    frequency_ref,
    chosen_ref,
    back_ref,
    turn_ref,
    cos_ref,
    sin_ref,
    *refs,
):
    meta_refs, slot_ref = refs[:-1], refs[-1]
    blocks = variate_ref.shape[0]
    half_devices = groups // 2
    half_blocks = blocks // 2
    half_rows = half_blocks * LANES
    swap_rows = rows // 2
    member = member_ref[0]
    my_half, my_place = member // half_devices, member % half_devices
    places = [lax.rem(my_place + shift, half_devices) for shift in range(half_devices)]
    segments = length_ref.shape[1]
    starts = [jnp.int32(0)]
    for segment in range(segments):
        starts.append(starts[-1] + length_ref[0, segment])
    long_start, long_index = jnp.int32(0), jnp.int32(0)
    for segment in range(segments):
        is_half = length_ref[0, segment] == half_rows
        long_start = jnp.where(is_half, starts[segment], long_start)
        long_index = jnp.where(is_half, segment, long_index)

    block = lax.broadcasted_iota(jnp.int32, (blocks, LANES), 0)
    lane = lax.broadcasted_iota(jnp.int32, (blocks, LANES), 1)
    work_block = jnp.zeros((blocks, LANES), jnp.int32)
    for index in range(blocks):
        work_block = jnp.where(block == order_ref[0, index], index, work_block)
    work_row = work_block * LANES + lane
    is_long = (work_row >= long_start) & (work_row < long_start + half_rows)
    in_first = block < half_blocks
    long_count = jnp.sum(jnp.where(is_long & in_first, 1.0, 0.0)).astype(jnp.int32)
    long_half = jnp.where(2 * long_count < half_rows, 1, 0)
    side = jnp.where(in_first, 0, 1)
    target = jnp.where(is_long, long_half, 1 - long_half)
    foreign = target != side
    flags = jnp.where(foreign, 1.0, 0.0)
    moved = jnp.sum(jnp.where(in_first, flags, 0.0)).astype(jnp.int32)
    square_row = lax.broadcasted_iota(jnp.int32, (LANES, LANES), 0)
    square_column = lax.broadcasted_iota(jnp.int32, (LANES, LANES), 1)
    within = dot(flags.astype(jnp.bfloat16), one_hot(square_row < square_column))
    block_sum = jnp.broadcast_to(jnp.sum(flags, axis=1, keepdims=True), (blocks, LANES))
    from_block = lax.broadcasted_iota(jnp.int32, (blocks, blocks), 1)
    to_block = lax.broadcasted_iota(jnp.int32, (blocks, blocks), 0)
    earlier = (from_block < to_block) & ((from_block < half_blocks) == (to_block < half_blocks))
    before = dot(one_hot(earlier), block_sum.astype(jnp.bfloat16))
    foreign_rank = (within + before).astype(jnp.int32)
    kept_rank = (block - side * half_blocks) * LANES + lane - foreign_rank
    kept_slot = side * half_rows + kept_rank
    foreign_slot = (1 - side) * half_rows + rows + foreign_rank
    foreign_slot = foreign_slot - jnp.clip(moved, 0, swap_rows)
    for index in range(1, half_devices):
        start = index * rows - jnp.minimum(moved, index * swap_rows)
        last = (index - 1) * rows - jnp.minimum(moved, (index - 1) * swap_rows)
        kept_slot = jnp.where(kept_rank >= start, kept_slot + rows - (start - last), kept_slot)
        received = jnp.clip(moved - index * swap_rows, 0, swap_rows)
        previous = jnp.clip(moved - (index - 1) * swap_rows, 0, swap_rows)
        foreign_slot = jnp.where(
            foreign_rank >= index * swap_rows,
            foreign_slot + rows - swap_rows + previous - received,
            foreign_slot,
        )
    slot = jnp.where(foreign, foreign_slot, kept_slot)
    slot_ref[...] = slot

    per_device = rows // LANES
    wanted = lax.broadcasted_iota(jnp.int32, (rows + swap_rows, 1), 0)
    wanted = jnp.where(
        wanted < rows,
        my_half * half_rows + my_place * rows + wanted,
        (1 - my_half) * half_rows + my_place * rows + wanted - swap_rows,
    )
    for shift in range(half_devices):
        for index in range(per_device):
            held = my_half * half_blocks + places[shift] * per_device + index
            column = (shift * per_device + index) * LANES
            chosen_ref[:, column : column + LANES] = one_hot(
                wanted == slot_ref[pl.ds(held, 1), :]
            )

    slot_turned = jnp.transpose(slot.astype(jnp.float32))
    turned_lane = lax.broadcasted_iota(jnp.int32, (LANES, blocks), 1)
    first_lane = lax.broadcasted_iota(jnp.int32, (1, LANES), 1)
    for index in range(per_device):
        held = my_half * half_blocks + my_place * per_device + index
        mine = jnp.sum(
            jnp.where(turned_lane == held, slot_turned, 0.0), axis=1, keepdims=True
        ).astype(jnp.int32)
        here = slice(index * LANES, (index + 1) * LANES)
        column = 0
        for first, half, length in ((0, my_half, rows), (swap_rows, 1 - my_half, swap_rows)):
            for shift in range(half_devices):
                for chunk in range(0, length, LANES):
                    number = half * half_rows + places[shift] * rows + first + chunk
                    back_ref[here, column : column + LANES] = one_hot(mine == number + first_lane)
                    column += LANES

    on_long = my_half == long_half
    for turn in range(2):
        chosen_segment = jnp.where(
            on_long, long_index, jnp.where(long_index <= turn, turn + 1, turn)
        )
        adapter = adapter_ref[0, 0]
        for segment in range(1, segments):
            adapter = jnp.where(chosen_segment == segment, adapter_ref[0, segment], adapter)
        turn_ref[turn] = adapter

    variate_turned = jnp.transpose(variate_ref[...].astype(jnp.float32))
    known = []
    for index in range(blocks):
        values = jnp.where(
            square_column == 0,
            work_block[index : index + 1, :].astype(jnp.float32),
            jnp.where(
                square_column == 1,
                square_row.astype(jnp.float32),
                variate_turned[:, index : index + 1],
            ),
        )
        known.append(jnp.where(square_column < 3, values, 0.0).astype(jnp.bfloat16))
    number = lax.broadcasted_iota(jnp.int32, (rows, 1), 0)
    wide_lane = lax.broadcasted_iota(jnp.int32, (rows, LANES), 1)
    for shift in range(half_devices):
        slots = my_half * half_rows + places[shift] * rows + number
        facts = jnp.zeros((rows, LANES), jnp.float32)
        for index in range(blocks):
            facts = facts + dot(one_hot(slots == slot[index : index + 1, :]), known[index])
        facts = facts.astype(jnp.int32)
        row = facts[:, 0:1] * LANES + facts[:, 1:2]
        segment = jnp.zeros((rows, 1), jnp.int32)
        first_row = jnp.zeros((rows, 1), jnp.int32)
        for index in range(1, segments):
            segment = jnp.where(row >= starts[index], index, segment)
            first_row = jnp.where(row >= starts[index], starts[index], first_row)
        turn = jnp.where(segment > long_index, segment - 1, segment)
        turn = jnp.where(on_long, 0, turn)
        meta_refs[shift][...] = jnp.where(
            wide_lane == 0, facts[:, 2:3], jnp.where(wide_lane == 1, segment, turn)
        )
        if shift == 0:
            angles = (row - first_row).astype(jnp.float32) * frequency_ref[...]
            sign = jnp.where(wide_lane % width < width // 2, -1.0, 1.0)
            cos_ref[...] = jnp.cos(angles)
            sin_ref[...] = jnp.sin(angles) * sign


def plan(groups, rows, width, member, seq_len, seq_adapter, block_order, variate):
    half_devices = groups // 2
    half_rows = half_devices * rows
    blocks = block_order.shape[1]
    smem = pl.BlockSpec(memory_space=pltpu.SMEM)
    vmem = pl.BlockSpec(memory_space=pltpu.VMEM)
    results = pl.pallas_call(
        functools.partial(plan_kernel, groups, rows, width),
        in_specs=[smem, smem, smem, smem, vmem, vmem],
        out_specs=[vmem, vmem, smem, vmem, vmem] + [vmem] * half_devices,
        out_shape=[
            jax.ShapeDtypeStruct((rows + rows // 2, half_rows), jnp.bfloat16),
            jax.ShapeDtypeStruct((rows, half_rows + half_rows // 2), jnp.bfloat16),
            jax.ShapeDtypeStruct((2,), jnp.int32),
            jax.ShapeDtypeStruct((rows, LANES), jnp.float32),
            jax.ShapeDtypeStruct((rows, LANES), jnp.float32),
        ]
        + [jax.ShapeDtypeStruct((rows, LANES), jnp.int32)] * half_devices,
        scratch_shapes=[pltpu.VMEM((blocks, LANES), jnp.int32)],
        compiler_params=pltpu.CompilerParams(vmem_limit_bytes=VMEM_LIMIT),
        cost_estimate=pl.CostEstimate(
            flops=2**31, bytes_accessed=4 * rows * half_rows, transcendentals=0
        ),
        name="plan",
    )(
        member,
        seq_len,
        seq_adapter,
        block_order,
        variate.reshape(blocks, LANES),
        jnp.asarray(rope_frequency(width)),
    )
    return (*results[:5], results[5:])


def pick_kernel(counts, later_count, chosen_ref, *refs):
    outs = refs[sum(counts) + later_count : sum(counts) + later_count + len(counts)]
    refs = iter(refs[: sum(counts)])
    for count, out_ref in zip(counts, outs):
        total = jnp.zeros(out_ref.shape, jnp.float32)
        column = 0
        for _ in range(count):
            ref = next(refs)
            rows = ref.shape[0]
            total = total + dot(chosen_ref[:, column : column + rows], ref[...])
            column += rows
        out_ref[...] = total.astype(out_ref.dtype)


def pick(chosen, first, count, *helds, later=()):
    features = helds[0][0].shape[1]
    tile = features // 2
    parts = [part for held in helds for part in held]
    return pl.pallas_call(
        functools.partial(pick_kernel, [len(held) for held in helds], len(later)),
        grid=(features // tile,),
        in_specs=[pl.BlockSpec((count, chosen.shape[1]), lambda step: (first // count, 0))]
        + [pl.BlockSpec((part.shape[0], tile), lambda step: (0, step)) for part in parts]
        + [pl.BlockSpec(memory_space=pl.ANY)] * len(later),
        out_specs=[pl.BlockSpec((count, tile), lambda step: (0, step))] * len(helds)
        + [pl.BlockSpec(memory_space=pl.ANY)] * len(later),
        out_shape=[jax.ShapeDtypeStruct((count, features), jnp.bfloat16)] * len(helds)
        + [jax.ShapeDtypeStruct(array.shape, array.dtype) for array in later],
        input_output_aliases={1 + len(parts) + i: len(helds) + i for i in range(len(later))},
        compiler_params=pltpu.CompilerParams(vmem_limit_bytes=VMEM_LIMIT),
        cost_estimate=pl.CostEstimate(
            flops=2 * count * chosen.shape[1] * features * len(helds),
            bytes_accessed=8 * count * features * len(helds),
            transcendentals=0,
        ),
        name="pick",
    )(chosen, *parts, *later)


def axis_count(names):
    count = 1
    for name in names:
        count *= lax.axis_size(name)
    return count


def within_half(array, shift, groups):
    half = groups // 2
    pairs = [
        (base + (place + shift) % half, base + place)
        for base in (0, half)
        for place in range(half)
    ]
    return lax.ppermute(array, GROUP, pairs)


def gather_half(array, groups):
    return [array] + [within_half(array, shift, groups) for shift in range(1, groups // 2)]


def to_other_half(array, groups):
    half = groups // 2
    return lax.ppermute(array, GROUP, [(i, (i + half) % groups) for i in range(groups)])


def scatter_sum(array, axis_sizes):
    for name, size in reversed(axis_sizes):
        outer = array.shape[0] // size
        array = array.reshape((outer, size) + array.shape[1:])
        bit = 1
        while bit < size:
            index = lax.axis_index(name)
            own = (index // bit) % 2
            spread = array.reshape((outer, size // (2 * bit), 2) + array.shape[2:])
            keep = lax.dynamic_index_in_dim(spread, own, 2, keepdims=False)
            send = lax.dynamic_index_in_dim(spread, 1 - own, 2, keepdims=False)
            got = lax.ppermute(send, name, [(i, i ^ bit) for i in range(size)])
            array = (keep.astype(jnp.float32) + got.astype(jnp.float32)).astype(jnp.bfloat16)
            bit *= 2
        array = array.reshape((outer,) + array.shape[2:])
    return array


LANES = 128
MOMENT_ROWS = 24
PACKS = ("far", "near")
GROUP = ("half", "core")
ALL = PACKS + GROUP


def adam(current, first_old, second_old, grad):
    first_moment = BETA_ONE * first_old + (1.0 - BETA_ONE) * grad
    second_moment = BETA_TWO * second_old + (1.0 - BETA_TWO) * grad * grad
    first_fix = first_moment / (1.0 - BETA_ONE**update_count)
    second_fix = second_moment / (1.0 - BETA_TWO**update_count)
    updated = current - LEARN_RATE * (
        first_fix / (jnp.sqrt(second_fix) + ADAM_EPS) + WEIGHT_DECAY * current
    )
    return first_moment, second_moment, updated.astype(jnp.bfloat16)


def settle_shards(grads, few_choice, adapters, moment1, moment2, groups):
    a_qkv, b_qkv, a_guo, a_down, b_gu, b_do = grads
    features, few = a_qkv.shape[0], few_choice.shape[1]
    quarters = a_down.shape[1] // few
    down = jnp.concatenate([a_down[:, i * few : (i + 1) * few] for i in range(quarters)])
    wide = [a_qkv[:, i * few : (i + 1) * few] for i in range(3)]
    wide += [a_guo[:, i * few : (i + 1) * few] for i in (2, 0, 1)] + [down]
    tall = [b_qkv[i * few : (i + 1) * few] for i in range(3)]
    tall += [b_do[2 * few : 3 * few], b_gu[:few], b_gu[few : 2 * few], b_do[:few]]
    pieces = []
    for grad_a, grad_b in zip(wide, tall):
        pieces.append(lax.dot_general(grad_a, few_choice, (((1,), (1,)), ((), ()))).reshape(-1))
        pieces.append(jnp.dot(few_choice, grad_b).reshape(-1))
    axis_sizes = [(PACKS, axis_count(PACKS)), (GROUP, groups)]
    shards = axis_sizes[0][1] * groups
    flat_grads = jnp.concatenate(pieces).astype(jnp.bfloat16).reshape(shards, -1)
    grad_shard = scatter_sum(flat_grads, axis_sizes).reshape(-1).astype(jnp.float32)
    shard_count = grad_shard.shape[0]
    shard_start = lax.axis_index(ALL) * shard_count
    current = lax.dynamic_slice_in_dim(adapters, shard_start, shard_count).astype(jnp.float32)
    first_moment, second_moment, updated = adam(current, moment1, moment2, grad_shard)
    adapters_new = lax.all_gather(updated, ALL, axis=0, tiled=True)
    return grad_shard, first_moment, second_moment, adapters_new


def spreads_evenly(devices, groups, features, hidden, total):
    rows = total // LANES
    chunks = features // LANES
    return (
        groups == 4
        and ADAPTERS * RANK == LANES
        and devices * chunks == 256
        and chunks == 8
        and hidden == devices * LANES
        and hidden == 4 * features
        and rows % (devices * devices) == 0
        and devices & (devices - 1) == 0
    )


def one_hot(condition):
    return jnp.where(condition, 1.0, 0.0).astype(jnp.bfloat16)


def sum_wide(adapter_row, arrived_ref, first, width):
    sources = arrived_ref.shape[0]
    rows = lax.broadcasted_iota(jnp.int32, (LANES, width * LANES), 0)
    columns = lax.broadcasted_iota(jnp.int32, (LANES, width * LANES), 1)
    fits = (rows // (2 * RANK) == columns // LANES) & (rows % RANK == columns % RANK)
    second = (rows // RANK) % 2 == 1
    adapter = jnp.where(fits, (columns % LANES) // RANK, -1)
    total = jnp.zeros((32, width * LANES), jnp.float32)
    for source in range(sources):
        at = source * 2 * RANK
        chosen = jnp.where(
            second, adapter_row[:, at + RANK : at + RANK + 1], adapter_row[:, at : at + 1]
        )
        total = total + dot(
            arrived_ref[source, first : first + 32, :], one_hot(adapter == chosen)
        )
    return total


def sum_tall(adapter_row, arrived_ref, first):
    sources = arrived_ref.shape[0]
    depth = sources * 2 * RANK
    rows = lax.broadcasted_iota(jnp.int32, (LANES, depth), 0)
    columns = lax.broadcasted_iota(jnp.int32, (LANES, depth), 1)
    choice = one_hot((rows // RANK == adapter_row) & (rows % RANK == columns % RANK))
    held = arrived_ref[:, first : first + 2 * RANK, :].reshape(depth, LANES)
    return jnp.dot(choice, held, preferred_element_type=jnp.float32)


def sum_square(adapter_row, arrived_ref, first):
    sources = arrived_ref.shape[0]
    depth = sources * 16
    rows = lax.broadcasted_iota(jnp.int32, (64, depth), 0)
    columns = lax.broadcasted_iota(jnp.int32, (64, depth), 1)
    choice = one_hot(
        ((rows % 32) // 4 == adapter_row)
        & (rows % 4 == columns % 4)
        & (rows // 32 == (columns % 16) // 8)
    )
    held = arrived_ref[:, first : first + 16, :].reshape(depth, LANES)
    return jnp.dot(choice, held, preferred_element_type=jnp.float32)


def settle_rows(parts, skip, param_ref, m1_ref, m2_ref, m_skip, grad_ref, new_refs):
    row = 0
    for part in parts:
        here = slice(row, row + part.shape[0])
        there = slice(skip + row, skip + row + part.shape[0])
        at = slice(m_skip + row, m_skip + row + part.shape[0])
        row += part.shape[0]
        low = part.astype(jnp.bfloat16)
        grad_ref[here, :] = low
        new = adam(
            param_ref[there, :].astype(jnp.float32),
            m1_ref[at, :],
            m2_ref[at, :],
            low.astype(jnp.float32),
        )[2]
        for new_ref in new_refs:
            new_ref[here, :] = new


def settle_early_kernel(own_rows, arrived_ref, moments_ref, param_ref, *refs):
    grad_ref, new_ref, late_m1_ref, late_m2_ref, tall_ref, square_ref, m1_ref, m2_ref = refs[-8:]
    sources = arrived_ref.shape[0]
    told = 6 * RANK
    tall_column = lax.broadcasted_iota(jnp.int32, tall_ref.shape, 1)
    square_column = lax.broadcasted_iota(jnp.int32, square_ref.shape, 1)
    tall = jnp.zeros(tall_ref.shape, jnp.float32)
    square = jnp.zeros(square_ref.shape, jnp.float32)
    for source in range(sources):
        row = arrived_ref[source, 0:16, :].astype(jnp.float32)
        first, second = row[0:1, told : told + 1], row[0:1, told + 1 : told + 2]
        tall = jnp.where(
            tall_column // (2 * RANK) == source,
            jnp.where((tall_column // RANK) % 2 == 1, second, first),
            tall,
        )
        square = jnp.where(
            square_column // RANK == source,
            jnp.where((square_column // 4) % 2 == 1, second, first),
            square,
        )
        held = moments_ref[source].astype(jnp.float32)
        here = slice(source * own_rows, (source + 1) * own_rows)
        m1_ref[here, :] = held[:own_rows]
        m2_ref[here, :] = held[MOMENT_ROWS : MOMENT_ROWS + own_rows]
    tall = tall.astype(jnp.int32)
    square = square.astype(jnp.int32)
    tall_ref[...] = tall
    square_ref[...] = square
    late = late_m1_ref.shape[0]
    late_m1_ref[...] = m1_ref[:late, :]
    late_m2_ref[...] = m2_ref[:late, :]
    wide = sum_wide(tall, arrived_ref, 0, 3)
    last = sum_wide(tall, arrived_ref, 32, 4)
    pair = sum_square(square, arrived_ref, 128)
    parts = [
        wide[:, 2 * LANES :],
        pair[32:],
        wide[:, :LANES],
        sum_tall(tall, arrived_ref, 64),
        wide[:, LANES : 2 * LANES],
        sum_tall(tall, arrived_ref, 96),
    ]
    parts += [last[:, i * LANES : (i + 1) * LANES] for i in range(4)]
    parts.append(pair[:32])
    copies = [new_ref.at[copy] for copy in range(new_ref.shape[0])]
    settle_rows(parts, late, param_ref, m1_ref, m2_ref, late, grad_ref, copies)


def settle_early(arrived, moments, params, late_rows, after):
    sources = arrived.shape[0]
    rows = params.shape[0] - late_rows
    vmem = pl.BlockSpec(memory_space=pltpu.VMEM)
    low = jax.ShapeDtypeStruct((rows, LANES), jnp.bfloat16)
    late = jax.ShapeDtypeStruct((late_rows, LANES), jnp.float32)
    return pl.pallas_call(
        functools.partial(settle_early_kernel, params.shape[0] // sources),
        in_specs=[vmem, vmem, vmem] + [pl.BlockSpec(memory_space=pl.ANY)] * len(after),
        out_specs=[vmem] * 6,
        out_shape=[
            low,
            jax.ShapeDtypeStruct((lax.axis_size("far"), rows, LANES), jnp.bfloat16),
            late,
            late,
            jax.ShapeDtypeStruct((1, sources * 2 * RANK), jnp.int32),
            jax.ShapeDtypeStruct((1, sources * RANK), jnp.int32),
        ],
        scratch_shapes=[pltpu.VMEM(params.shape, jnp.float32)] * 2,
        compiler_params=pltpu.CompilerParams(vmem_limit_bytes=VMEM_LIMIT),
        cost_estimate=pl.CostEstimate(
            flops=sources * 2**24, bytes_accessed=4 * arrived.size, transcendentals=0
        ),
        name="settle_early",
    )(arrived, moments, params, *after)


def settle_late_kernel(
    tall_ref, square_ref, arrived_ref, param_ref, m1_ref, m2_ref, *refs
):
    early_grad_ref = refs[0]
    own_ref, new_ref, _, grad_ref = refs[-4:]
    wide = sum_wide(tall_ref[...], arrived_ref, 0, 3)
    pairs = [sum_square(square_ref[...], arrived_ref, first) for first in (32, 48)]
    parts = []
    for index in range(3):
        parts.append(wide[:, index * LANES : (index + 1) * LANES])
        parts.append(pairs[index // 2][(index % 2) * 32 : (index % 2) * 32 + 32])
    copies = [new_ref.at[copy] for copy in range(new_ref.shape[0])]
    settle_rows(parts, 0, param_ref, m1_ref, m2_ref, 0, grad_ref, copies)
    low = jnp.concatenate(
        [ref[...].astype(jnp.float32) for ref in (grad_ref, early_grad_ref)], axis=0
    )
    each = low.shape[0] // own_ref.shape[0]
    zeros = jnp.zeros((own_ref.shape[1] - each, LANES), jnp.float32)
    for owner in range(own_ref.shape[0]):
        own_ref[owner] = jnp.concatenate(
            [low[owner * each : (owner + 1) * each], zeros], axis=0
        ).astype(jnp.bfloat16)


def settle_late(tall, square, arrived, params, late_m1, late_m2, early_grad, later, after):
    rows = late_m1.shape[0]
    anywhere = pl.BlockSpec(memory_space=pl.ANY)
    vmem = pl.BlockSpec(memory_space=pltpu.VMEM)
    return pl.pallas_call(
        settle_late_kernel,
        in_specs=[vmem] * 7 + [anywhere] * (1 + len(after)),
        out_specs=[vmem, vmem, anywhere],
        scratch_shapes=[pltpu.VMEM((rows, LANES), jnp.bfloat16)],
        input_output_aliases={7: 2},
        out_shape=[
            jax.ShapeDtypeStruct((arrived.shape[0], MOMENT_ROWS, LANES), jnp.bfloat16),
            jax.ShapeDtypeStruct((axis_count(PACKS), rows, LANES), jnp.bfloat16),
            jax.ShapeDtypeStruct(later.shape, later.dtype),
        ],
        compiler_params=pltpu.CompilerParams(vmem_limit_bytes=VMEM_LIMIT),
        cost_estimate=pl.CostEstimate(
            flops=arrived.shape[0] * 2**24, bytes_accessed=4 * arrived.size, transcendentals=0
        ),
        name="settle_late",
    )(tall, square, arrived, params, late_m1, late_m2, early_grad, later, *after)


def gather_inner(piece, groups):
    pieces = [piece]
    bit = groups // 2
    while bit:
        pairs = [(i, i ^ bit) for i in range(groups)]
        pieces = pieces + [lax.ppermute(piece, GROUP, pairs) for piece in pieces]
        bit //= 2
    return pieces


def placing_order(device, unit):
    size = unit * device.shape[0]
    to_row = lax.broadcasted_iota(jnp.int32, (size, size), 0)
    from_row = jnp.arange(size, dtype=jnp.int32)
    source = (from_row % unit) * device.shape[0] + jnp.repeat(device, unit)
    return (to_row == source[None, :]).astype(jnp.bfloat16)


def piece_devices(groups, devices):
    member = lax.axis_index(GROUP)
    piece = jnp.arange(groups, dtype=jnp.int32)
    mask = jnp.zeros_like(piece)
    bit = 1
    while bit < groups:
        mask = mask * 2 + (piece // bit) % 2
        bit *= 2
    outer = jnp.arange(devices // groups, dtype=jnp.int32)
    return (outer[None, :] * groups + (member ^ mask)[:, None]).reshape(-1)


def hand_on(after, *arrays):
    anywhere = pl.BlockSpec(memory_space=pl.ANY)
    return pl.pallas_call(
        lambda *refs: None,
        in_specs=[anywhere] * (1 + len(arrays)),
        out_specs=[anywhere] * len(arrays),
        out_shape=[jax.ShapeDtypeStruct(array.shape, array.dtype) for array in arrays],
        input_output_aliases={1 + index: index for index in range(len(arrays))},
        name="hand_on",
    )(after, *arrays)


def assemble_kernel(counts, devices, chunks, first, order_ref, *refs):
    piece_refs = []
    for count in counts:
        piece_refs.append(refs[:count])
        refs = refs[count:]
    out_any, placed_ref, sems = refs[-3:]

    def held_rows(part_refs, start, stop):
        before = 0
        for ref in part_refs:
            if start < before + ref.shape[1]:
                return ref[:, start - before : stop - before, :]
            before += ref.shape[1]

    unit = order_ref.shape[0] // devices
    copies = []
    for index, (begin, end) in enumerate(chunks):
        for start in range(begin, end, 2 * unit):
            sides = []
            for side in (start, start + unit):
                held = jnp.concatenate(
                    [held_rows(part_refs, side, side + unit) for part_refs in piece_refs], axis=0
                )
                sides.append(held.reshape(unit * devices, LANES))
            placed = dot(order_ref[...], jnp.concatenate(sides, axis=1)).astype(jnp.bfloat16)
            for half, side in enumerate((start, start + unit)):
                placed_ref[side * devices : (side + unit) * devices, :] = placed[
                    :, half * LANES : (half + 1) * LANES
                ]
        here = slice(begin * devices, end * devices)
        there = slice((first + begin) * devices, (first + end) * devices)
        copies.append(
            pltpu.make_async_copy(placed_ref.at[here, :], out_any.at[there, :], sems.at[index])
        )
        copies[-1].start()
    for copy in copies:
        copy.wait()


def assemble(order, pieces, total_rows, first, before, after):
    devices = len(pieces) * pieces[0][0].shape[0]
    rows = pieces[0][0].shape[1]
    parts = [part for piece in pieces for part in piece]
    step = 32 * max(1, rows // 128)
    chunks = [(begin, min(begin + step, rows)) for begin in range(0, rows, step)]
    vmem, anywhere = pl.BlockSpec(memory_space=pltpu.VMEM), pl.BlockSpec(memory_space=pl.ANY)
    in_specs = [vmem] * (1 + len(parts)) + [anywhere] * len(after)
    operands = [order, *parts, *after]
    aliases = {}
    if before is not None:
        aliases = {len(operands): 0}
        in_specs.append(anywhere)
        operands.append(before)
    return pl.pallas_call(
        functools.partial(assemble_kernel, [len(piece) for piece in pieces], devices, chunks, first),
        in_specs=in_specs,
        out_specs=anywhere,
        out_shape=jax.ShapeDtypeStruct((total_rows, LANES), jnp.bfloat16),
        scratch_shapes=[
            pltpu.VMEM((rows * devices, LANES), jnp.bfloat16),
            pltpu.SemaphoreType.DMA((len(chunks),)),
        ],
        input_output_aliases=aliases,
        compiler_params=pltpu.CompilerParams(vmem_limit_bytes=VMEM_LIMIT),
        cost_estimate=pl.CostEstimate(
            flops=rows * devices * 2**17, bytes_accessed=rows * devices * 512, transcendentals=0
        ),
        name="assemble",
    )(*operands)


def rope_frequency(head_width):
    index = np.arange(LANES) % (head_width // 2)
    return (ROPE_BASE ** (-2.0 * index / head_width)).astype(np.float32)[None, :]


def gain_rows(attn_gain, ffn_gain, q_gain, k_gain):
    repeats = attn_gain.shape[0] // q_gain.shape[0]
    return jnp.concatenate(
        [attn_gain, ffn_gain] + [q_gain] * repeats + [k_gain] * repeats
    ).astype(jnp.float32).reshape(4, -1)


def select_kernel(features, hidden, devices, turn_ref, me_ref, flat_any, *refs):
    m1_ref, m2_ref = refs[:2]
    out_refs, flat_ref, sems = refs[3:-2], refs[-2], refs[-1]
    size = flat_ref.shape[0] // sems.shape[0]
    copies = [
        pltpu.make_async_copy(
            flat_any.at[pl.ds(chunk * size, size), :],
            flat_ref.at[pl.ds(chunk * size, size), :],
            sems.at[chunk],
        )
        for chunk in range(sems.shape[0])
    ]
    for copy in copies:
        copy.start()
    a_qkv_ref, a_guo_ref, a_down_ref, b_qkv_ref, b_gu_ref, b_do_ref = out_refs[:6]
    if devices:
        own_ref, moments_ref, wide_ref = out_refs[6:]
        count = m1_ref.shape[0] // devices
        for device in range(devices):
            rows = []
            for ref in (m1_ref, m2_ref):
                rows.append(ref[pl.ds(device, count, stride=devices), :])
                rows.append(jnp.zeros((MOMENT_ROWS - count, LANES), jnp.float32))
            moments_ref[device] = jnp.concatenate(rows, axis=0).astype(jnp.bfloat16)
        each = size // devices
        for chunk, copy in enumerate(copies):
            copy.wait()
            wide_ref[...] = flat_ref[chunk * size : (chunk + 1) * size, :].astype(jnp.float32)
            own_ref[chunk * each : (chunk + 1) * each, :] = wide_ref[
                pl.ds(me_ref[0], each, stride=devices), :
            ].astype(jnp.bfloat16)
    if not devices:
        for copy in copies:
            copy.wait()
    few = 2 * RANK
    rows = lax.broadcasted_iota(jnp.int32, (LANES, LANES), 0)
    columns = lax.broadcasted_iota(jnp.int32, (LANES, LANES), 1)
    chosen = jnp.where((columns // RANK) % 2 == 1, turn_ref[1], turn_ref[0])
    fits = (rows // RANK == chosen) & (rows % RANK == columns % RANK)
    start = {}
    row = 0
    for name, rows_in, rows_out in (
        ("q", features, features),
        ("k", features, features),
        ("v", features, features),
        ("o", features, features),
        ("g", features, hidden),
        ("u", features, hidden),
        ("d", hidden, features),
    ):
        start[name] = (row, row + rows_in)
        row += rows_in + rows_out

    def wide(names, length):
        total = jnp.zeros((length, LANES), jnp.float32)
        for place, name in enumerate(names):
            first = start[name][0]
            total = total + jnp.dot(
                flat_ref[first : first + length, :],
                one_hot(fits & (columns // few == place)),
                preferred_element_type=jnp.float32,
            )
        return total.astype(jnp.bfloat16)

    a_qkv_ref[...] = wide("qkv", features)
    a_guo_ref[...] = wide("guo", features)
    for first in range(0, hidden, features):
        a_down_ref[first : first + features, :] = jnp.dot(
            flat_ref[start["d"][0] + first : start["d"][0] + first + features, :],
            one_hot(fits & (columns // few == 0)),
            preferred_element_type=jnp.float32,
        ).astype(jnp.bfloat16)

    def tall(name, length, out_ref, place):
        chunks = length // LANES
        size = RANK * chunks
        to_row = lax.broadcasted_iota(jnp.int32, (size, size), 0)
        from_row = lax.broadcasted_iota(jnp.int32, (size, size), 1)
        turned = one_hot(
            (to_row // RANK == from_row % chunks) & (to_row % RANK == from_row // chunks)
        )
        for turn in range(2):
            first = start[name][1] + pl.multiple_of(turn_ref[turn] * size, LANES)
            block = jnp.dot(
                turned, flat_ref[pl.ds(first, size), :], preferred_element_type=jnp.float32
            ).astype(jnp.bfloat16)
            here = place * few + turn * RANK
            for chunk in range(chunks):
                out_ref[here : here + RANK, chunk * LANES : (chunk + 1) * LANES] = block[
                    chunk * RANK : (chunk + 1) * RANK
                ]

    for out_ref, names in ((b_qkv_ref, "qkv"), (b_gu_ref, "gu"), (b_do_ref, "d.o")):
        out_ref[...] = jnp.zeros(out_ref.shape, out_ref.dtype)
        for place, name in enumerate(names):
            if name != ".":
                tall(name, out_ref.shape[1], out_ref, place)


def select(devices, turn_adapter, me, adapters, moments, features, hidden, after):
    shapes = [(features, LANES), (features, LANES), (hidden, LANES)]
    shapes += [(LANES, features), (LANES, hidden), (LANES, features)]
    scratch = []
    if devices:
        shapes.append((adapters.shape[0] // (LANES * devices), LANES))
        shapes.append((devices, 2 * MOMENT_ROWS, LANES))
        scratch.append(pltpu.VMEM((1024, LANES), jnp.float32))
    rows = adapters.shape[0] // LANES
    scratch += [pltpu.VMEM((rows, LANES), jnp.bfloat16), pltpu.SemaphoreType.DMA((rows // 1024,))]
    return pl.pallas_call(
        functools.partial(select_kernel, features, hidden, devices),
        in_specs=[
            pl.BlockSpec(memory_space=pltpu.SMEM),
            pl.BlockSpec(memory_space=pltpu.SMEM),
            pl.BlockSpec(memory_space=pl.ANY),
            pl.BlockSpec(memory_space=pltpu.VMEM),
            pl.BlockSpec(memory_space=pltpu.VMEM),
            pl.BlockSpec(memory_space=pl.ANY),
        ],
        out_specs=[pl.BlockSpec(memory_space=pltpu.VMEM)] * len(shapes),
        out_shape=[jax.ShapeDtypeStruct(shape, jnp.bfloat16) for shape in shapes],
        scratch_shapes=scratch,
        compiler_params=pltpu.CompilerParams(vmem_limit_bytes=VMEM_LIMIT),
        cost_estimate=pl.CostEstimate(
            flops=2**31, bytes_accessed=4 * adapters.shape[0], transcendentals=0
        ),
        name="select",
    )(turn_adapter, me, adapters.reshape(-1, LANES), *moments, after)


def dot(left, right):
    return jnp.dot(left, right, preferred_element_type=jnp.float32)


def beside(*arrays):
    return jnp.concatenate(arrays, axis=1)


def above(*arrays):
    return jnp.concatenate(arrays, axis=0)


def turn_mask(meta_ref):
    rows = meta_ref.shape[0]
    lane = lax.broadcasted_iota(jnp.int32, (rows, LANES), 1)
    mask = jnp.where((lane // RANK) % 2 == meta_ref[:, 2:3], 1.0, 0.0)
    return mask, lane // (2 * RANK)


def row_norm(values):
    return lax.rsqrt(jnp.mean(values * values, axis=1, keepdims=True) + NORM_EPS)


def row_norm_back(values, gain, grad):
    scale = row_norm(values)
    unit = values * scale
    grad = grad * gain
    return scale * (grad - unit * jnp.mean(grad * unit, axis=1, keepdims=True))


def head_mean(values, width):
    lanes = values.shape[1]
    rows = lax.broadcasted_iota(jnp.int32, (lanes, lanes), 0)
    columns = lax.broadcasted_iota(jnp.int32, (lanes, lanes), 1)
    ones = one_hot(rows // width == columns // width)
    return dot(values.astype(jnp.bfloat16), ones) * (1.0 / width)


def swap_halves(values, width):
    lanes = values.shape[1]
    lane = lax.broadcasted_iota(jnp.int32, values.shape, 1)
    ahead = pltpu.roll(values, lanes - width // 2, 1)
    behind = pltpu.roll(values, width // 2, 1)
    return jnp.where(lane % width < width // 2, ahead, behind)


def widen(table, lanes):
    return jnp.concatenate([table] * (lanes // table.shape[1]), axis=1)


def joined(kept_ref, arrived_ref):
    first = kept_ref.shape[0] - arrived_ref.shape[0]
    kept = kept_ref[...]
    return jnp.concatenate([kept[:first], kept[first:] + arrived_ref[...]], axis=0)


def turned_heads(raw, gain, cosine, sine, width):
    unit = raw * lax.rsqrt(head_mean(raw * raw, width) + NORM_EPS) * gain
    return (unit * cosine + swap_halves(unit, width) * sine).astype(jnp.bfloat16)


def project_own(normed, inner, place, index, weight_ref, b_ref):
    own = jnp.where(place == index, ADAPTER_SCALE * inner, 0.0).astype(jnp.bfloat16)
    return dot(beside(normed, own), above(weight_ref[...], b_ref[...]))


def project_heads_kernel(
    width,
    kept_ref,
    arrived_ref,
    gains_ref,
    wq_ref,
    wk_ref,
    wv_ref,
    a_ref,
    b_ref,
    meta_ref,
    cos_ref,
    sin_ref,
    _,
    x_ref,
    normed_ref,
    inner_ref,
    q_raw_ref,
    k_raw_ref,
    q_ref,
    k_ref,
    v_ref,
    __,
):
    mask, place = turn_mask(meta_ref)

    @pl.when(pl.program_id(0) == 0)
    def _():
        rows = joined(kept_ref, arrived_ref)
        x_ref[...] = rows
        values = rows.astype(jnp.float32)
        normed = (values * row_norm(values) * gains_ref[0:1, :]).astype(
            jnp.bfloat16
        )
        normed_ref[...] = normed
        inner_ref[...] = (dot(normed, a_ref[...]) * mask).astype(jnp.bfloat16)

    normed = normed_ref[...]
    inner = inner_ref[...].astype(jnp.float32)
    lanes = wk_ref.shape[1]
    cosine, sine = widen(cos_ref[...], lanes), widen(sin_ref[...], lanes)
    query = project_own(normed, inner, place, 0, wq_ref, b_ref)
    q_raw_ref[...] = query.astype(jnp.bfloat16)
    q_ref[...] = turned_heads(query, gains_ref[2:3, :lanes], cosine, sine, width)
    key = project_own(normed, inner, place, 1, wk_ref, b_ref)
    k_raw_ref[...] = key.astype(jnp.bfloat16)
    k_ref[...] = turned_heads(key, gains_ref[3:4, :lanes], cosine, sine, width)
    v_ref[...] = project_own(normed, inner, place, 2, wv_ref, b_ref).astype(jnp.bfloat16)


def project_heads(
    kept,
    arrived,
    later,
    gains,
    weights,
    a_qkv,
    b_qkv,
    meta,
    cos_table,
    sin_table,
    width,
):
    rows, features = kept.shape
    tile = 512
    grid = (features // tile,)

    def tiled(height):
        return pl.BlockSpec((height, tile), lambda step: (0, step))

    def shape(dtype):
        return jax.ShapeDtypeStruct((rows, features), dtype)

    full, few = whole_block((rows, features)), whole_block((rows, LANES))
    low = shape(jnp.bfloat16)
    anywhere = pl.BlockSpec(memory_space=pl.ANY)
    results = pl.pallas_call(
        functools.partial(project_heads_kernel, width),
        grid=grid,
        in_specs=[full, whole_block(arrived.shape), whole_block(gains.shape)]
        + [tiled(features)] * 3
        + [whole_block((features, LANES)), tiled(LANES), few, few, few]
        + [anywhere],
        out_specs=[full, full, few] + [tiled(rows)] * 5 + [anywhere],
        input_output_aliases={11: 8},
        out_shape=[
            low,
            low,
            jax.ShapeDtypeStruct((rows, LANES), jnp.bfloat16),
            low,
            low,
            low,
            low,
            low,
            jax.ShapeDtypeStruct(later.shape, later.dtype),
        ],
        compiler_params=pltpu.CompilerParams(vmem_limit_bytes=VMEM_LIMIT),
        cost_estimate=pl.CostEstimate(
            flops=9 * rows * features * features,
            bytes_accessed=4 * features * features + 14 * rows * features,
            transcendentals=0,
        ),
        name="project_heads",
    )(
        kept,
        arrived,
        gains,
        *weights,
        a_qkv,
        b_qkv,
        meta,
        cos_table,
        sin_table,
        later,
    )
    return results


def project_heads_back_kernel(
    count,
    width,
    devices,
    gq_ref,
    *refs,
):
    gk_refs, gv_refs, refs = refs[:count], refs[count : 2 * count], refs[2 * count :]
    (
        q_raw_ref,
        k_raw_ref,
        normed_any,
        inner_ref,
        x_any,
        residual_any,
        gains_ref,
        wq_ref,
        wk_ref,
        wv_ref,
        a_ref,
        b_ref,
        meta_ref,
        cos_ref,
        sin_ref,
    ) = refs[:15]
    if devices:
        out_ref, tail_ref, spread_ref = refs[-9:-6]
    else:
        out_ref, tail_ref, grad_a_ref, grad_b_ref = refs[-10:-6]
    total_ref, few_ref, tall_ref, square_ref, held_ref, sems = refs[-6:]
    step = pl.program_id(0)
    lanes = wq_ref.shape[1]
    mask, place = turn_mask(meta_ref)
    cosine, sine = widen(cos_ref[...], lanes), widen(sin_ref[...], lanes)

    def turned_back(grad, raw, head_gain):
        raw = raw.astype(jnp.float32)
        grad = grad * cosine - swap_halves(grad, width) * sine
        scale = lax.rsqrt(head_mean(raw * raw, width) + NORM_EPS)
        unit = raw * scale
        grad = grad * head_gain
        return (scale * (grad - unit * head_mean(grad * unit, width))).astype(jnp.bfloat16)

    def summed(term_refs):
        total = term_refs[0][...].astype(jnp.float32)
        for ref in term_refs[1:]:
            total = total + ref[...].astype(jnp.float32)
        return total

    copies = [
        pltpu.make_async_copy(source, held_ref.at[index], sems.at[index])
        for index, source in enumerate((normed_any, x_any, residual_any))
    ]

    @pl.when(step == 0)
    def _():
        for copy in copies:
            copy.start()
        total_ref[...] = jnp.zeros(total_ref.shape, jnp.float32)
        few_ref[...] = jnp.zeros(few_ref.shape, jnp.float32)

    inner_turned = jnp.transpose(inner_ref[...].astype(jnp.float32) * ADAPTER_SCALE).astype(
        jnp.bfloat16
    )
    errors = [
        turned_back(gq_ref[...].astype(jnp.float32), q_raw_ref[...], gains_ref[2:3, :lanes]),
        turned_back(summed(gk_refs), k_raw_ref[...], gains_ref[3:4, :lanes]),
        summed(gv_refs).astype(jnp.bfloat16),
    ]
    total_ref[...] += contract_last(
        beside(*errors), beside(wq_ref[...], wk_ref[...], wv_ref[...])
    )
    few = few_ref[...]
    wide = 2 * RANK
    for index, error in enumerate(errors):
        few = few + jnp.where(place == index, contract_last(error, b_ref[...]), 0.0)
        here = slice(index * wide, (index + 1) * wide)
        grad_b = dot(inner_turned[here], error)
        for part in range(lanes // LANES):
            square_ref[part, here, :] = grad_b[:, part * LANES : (part + 1) * LANES]
    square_ref[:, 3 * wide :, :] = jnp.zeros(
        (lanes // LANES, LANES - 3 * wide, LANES), jnp.float32
    )
    if devices:
        chunks = held_ref.shape[2] // LANES
        for index in range(lanes // LANES):
            for first, starts in ((wide, (0, wide)), (wide + RANK, (2 * wide, 3 * wide))):
                spread_square_to(
                    spread_ref,
                    first,
                    square_ref,
                    starts,
                    step * (lanes // LANES) + index,
                    chunks,
                    index,
                )
    else:
        for part in range(lanes // LANES):
            grad_b_ref[:, part * LANES : (part + 1) * LANES] = square_ref[part].astype(
                jnp.bfloat16
            )
    few_ref[...] = few

    @pl.when(step == pl.num_programs(0) - 1)
    def _():
        low = (ADAPTER_SCALE * few_ref[...] * mask).astype(jnp.bfloat16)
        low_turned = jnp.transpose(low.astype(jnp.float32)).astype(jnp.bfloat16)
        for copy in copies:
            copy.wait()
        tall_ref[...] = jnp.transpose(dot(low_turned, held_ref[0]))
        if devices:
            spread_wide_to(spread_ref, 0, tall_ref)
        else:
            grad_a_ref[...] = tall_ref[...].astype(jnp.bfloat16)
        grad = total_ref[...] + contract_last(low, a_ref[...])
        out = held_ref[2].astype(jnp.float32) + row_norm_back(
            held_ref[1].astype(jnp.float32), gains_ref[0:1, :], grad
        )
        out_ref[...] = out.astype(jnp.bfloat16)
        tail_ref[...] = out[out.shape[0] - tail_ref.shape[0] :].astype(jnp.bfloat16)


def project_heads_back(
    devices,
    after,
    grad_query,
    key_terms,
    value_terms,
    query_raw,
    key_raw,
    normed,
    inner,
    rows_in,
    grad_residual,
    gains,
    weights,
    a_qkv,
    b_qkv,
    meta,
    cos_table,
    sin_table,
    width,
):
    rows, features = rows_in.shape
    count = len(key_terms)
    tile = 256

    def tiled(height):
        return pl.BlockSpec((height, tile), lambda step: (0, step))

    full = whole_block((rows, features))
    anywhere = pl.BlockSpec(memory_space=pl.ANY)
    if devices:
        spread = (devices, 4 * RANK, LANES)
        grad_specs = [whole_block(spread)]
        grad_shapes = [jax.ShapeDtypeStruct(spread, jnp.bfloat16)]
    else:
        grad_specs = [whole_block((features, LANES)), tiled(LANES)]
        grad_shapes = [
            jax.ShapeDtypeStruct((features, LANES), jnp.bfloat16),
            jax.ShapeDtypeStruct((LANES, features), jnp.bfloat16),
        ]
    return pl.pallas_call(
        functools.partial(project_heads_back_kernel, count, width, devices),
        grid=(features // tile,),
        in_specs=[tiled(rows)] * (3 + 2 * count)
        + [anywhere, whole_block((rows, LANES)), anywhere, anywhere, whole_block(gains.shape)]
        + [tiled(features)] * 3
        + [whole_block((features, LANES)), tiled(LANES), whole_block(meta.shape)]
        + [whole_block((rows, LANES))] * 2
        + [anywhere] * len(after),
        out_specs=[full, whole_block((rows // 2, features)), *grad_specs],
        out_shape=[
            jax.ShapeDtypeStruct((rows, features), jnp.bfloat16),
            jax.ShapeDtypeStruct((rows // 2, features), jnp.bfloat16),
            *grad_shapes,
        ],
        scratch_shapes=[
            pltpu.VMEM((rows, features), jnp.float32),
            pltpu.VMEM((rows, LANES), jnp.float32),
            pltpu.VMEM((features, LANES), jnp.float32),
            pltpu.VMEM((tile // LANES, LANES, LANES), jnp.float32),
            pltpu.VMEM((3, rows, features), jnp.bfloat16),
            pltpu.SemaphoreType.DMA((3,)),
        ],
        compiler_params=pltpu.CompilerParams(vmem_limit_bytes=VMEM_LIMIT),
        cost_estimate=pl.CostEstimate(
            flops=8 * rows * features * features,
            bytes_accessed=6 * features * features + 30 * rows * features,
            transcendentals=0,
        ),
        name="project_heads_back",
    )(
        grad_query,
        *key_terms,
        *value_terms,
        query_raw,
        key_raw,
        normed,
        inner,
        rows_in,
        grad_residual,
        gains,
        *weights,
        a_qkv,
        b_qkv,
        meta,
        cos_table,
        sin_table,
        *after,
    )


def spread_wide_to(spread_ref, first, held_ref):
    devices = spread_ref.shape[0]
    count = held_ref.shape[0] // devices
    for device in range(devices):
        spread_ref[device, first : first + count, :] = held_ref[
            pl.ds(device, count, stride=devices), :
        ].astype(jnp.bfloat16)


def spread_square_to(spread_ref, first, held_ref, starts, chunk, chunks, index):
    classes = spread_ref.shape[0] // chunks
    count = 2 * RANK // classes
    for part in range(classes):
        rows = [
            held_ref[index, pl.ds(start + part, count, stride=classes), :]
            for start in starts
        ]
        spread_ref[part * chunks + chunk, first : first + 2 * count, :] = jnp.concatenate(
            rows, axis=0
        ).astype(jnp.bfloat16)


def feed_forward_kernel(
    devices,
    turn_ref,
    att_ref,
    x_any,
    kept_any,
    arrived_any,
    gains_ref,
    wo_ref,
    wg_any,
    wu_any,
    wd_any,
    a_guo_ref,
    a_down_ref,
    b_gu_ref,
    b_do_ref,
    meta_ref,
    out_any,
    tail_any,
    grad_res_any,
    grad_att_ref,
    *refs,
):
    if devices:
        spread_ref, refs = refs[0], refs[1:]
    else:
        (grad_a_ref, grad_ad_ref, grad_bgu_ref, grad_bdo_ref), refs = refs[:4], refs[4:]
    (
        res_ref,
        hidden_ref,
        inner_ref,
        inner_turned_ref,
        sum_ref,
        grad_hidden_ref,
        inner_down_ref,
        few_ref,
        few_down_ref,
        few_down_turned_ref,
        down_ref,
        tall_ref,
        square_ref,
        e_ref,
        x_ref,
        arrived_ref,
        wg_ref,
        wu_ref,
        wd_ref,
        out_ref,
        grad_res_ref,
        rows_sems,
        tile_sems,
        out_sems,
    ) = refs
    step = pl.program_id(0)
    steps = pl.num_programs(0)
    mask, place = turn_mask(meta_ref)
    tile = wg_ref.shape[2]
    swap_rows = arrived_ref.shape[0]
    row_copies = [
        pltpu.make_async_copy(source, target, rows_sems.at[index])
        for index, (source, target) in enumerate(
            ((x_any, x_ref), (kept_any, e_ref), (arrived_any, arrived_ref))
        )
    ]

    def tile_copies(number):
        slot = number % 2
        here = pl.ds(pl.multiple_of(number * tile, tile), tile)
        pairs = (
            (wg_any.at[:, here], wg_ref.at[slot]),
            (wu_any.at[:, here], wu_ref.at[slot]),
            (wd_any.at[here, :], wd_ref.at[slot]),
        )
        return [
            pltpu.make_async_copy(source, target, tile_sems.at[slot, index])
            for index, (source, target) in enumerate(pairs)
        ]

    features = wo_ref.shape[0]
    wide = 2 * RANK

    def only(values, index):
        return jnp.where(place == index, values, 0.0).astype(jnp.bfloat16)

    def turn(values):
        return jnp.transpose(values.astype(jnp.float32)).astype(jnp.bfloat16)

    @pl.when(step == 0)
    def _():
        for copy in row_copies:
            copy.start()
        for copy in tile_copies(0):
            copy.start()
        att = att_ref[...]
        inner_out = dot(att, a_guo_ref[...]) * mask
        attention_out = dot(
            beside(att, only(ADAPTER_SCALE * inner_out, 2)), above(wo_ref[...], b_do_ref[...])
        )
        row_copies[0].wait()
        res = x_ref[...].astype(jnp.float32) + attention_out
        res_ref[...] = res
        hidden = (res * row_norm(res) * gains_ref[1:2, :]).astype(jnp.bfloat16)
        hidden_ref[...] = hidden
        inner = dot(hidden, a_guo_ref[...]) * mask
        inner = jnp.where(place == 2, inner_out, inner).astype(jnp.bfloat16)
        inner_ref[...] = inner
        inner_turned_ref[...] = turn(inner.astype(jnp.float32) * ADAPTER_SCALE)
        for copy in row_copies[1:]:
            copy.wait()
        e_ref[e_ref.shape[0] - swap_rows :, :] += arrived_ref[...]
        few_down = only(ADAPTER_SCALE * contract_last(e_ref[...], b_do_ref[...]) * mask, 0)
        few_down_ref[...] = few_down
        few_down_turned_ref[...] = turn(few_down)[:wide]
        sum_ref[...] = jnp.zeros(sum_ref.shape, jnp.float32)
        grad_hidden_ref[...] = jnp.zeros(grad_hidden_ref.shape, jnp.float32)
        inner_down_ref[...] = jnp.zeros(inner_down_ref.shape, jnp.float32)
        few_ref[...] = jnp.zeros(few_ref.shape, jnp.float32)

    @pl.when(step + 1 < steps)
    def _():
        for copy in tile_copies(step + 1):
            copy.start()

    for copy in tile_copies(step):
        copy.wait()
    slot = step % 2
    hidden = hidden_ref[...]
    inner = ADAPTER_SCALE * inner_ref[...].astype(jnp.float32)
    gate_weight, up_weight, down_weight = wg_ref[slot], wu_ref[slot], wd_ref[slot]
    b_tile = b_gu_ref[...]
    gate = dot(beside(hidden, only(inner, 0)), above(gate_weight, b_tile))
    up = dot(beside(hidden, only(inner, 1)), above(up_weight, b_tile))
    grad_act = contract_last(
        beside(e_ref[...], few_down_ref[...]), beside(down_weight, a_down_ref[...])
    )
    sigmoid = 1.0 / (1.0 + jnp.exp(-gate))
    silu = gate * sigmoid
    act = (silu * up).astype(jnp.bfloat16)
    grad_up = (grad_act * silu).astype(jnp.bfloat16)
    grad_gate = (grad_act * up * (sigmoid * (1.0 + gate * (1.0 - sigmoid)))).astype(jnp.bfloat16)
    sum_ref[...] += dot(act, down_weight)
    inner_down_ref[...] += dot(act, a_down_ref[...])
    grad_hidden_ref[...] += contract_last(
        beside(grad_gate, grad_up), beside(gate_weight, up_weight)
    )
    few_ref[...] += jnp.where(
        place == 0, contract_last(grad_gate, b_tile), contract_last(grad_up, b_tile)
    )
    grad_b_gate = dot(inner_turned_ref[:wide, :], grad_gate).astype(jnp.bfloat16)
    grad_b_up = dot(inner_turned_ref[wide : 2 * wide, :], grad_up).astype(jnp.bfloat16)
    if devices:
        for index in range(tile // LANES):
            device = step * (tile // LANES) + index
            chunk = slice(index * LANES, (index + 1) * LANES)
            spread_ref[device, 2 * wide : 3 * wide, :] = grad_b_gate[:, chunk]
            spread_ref[device, 3 * wide : 4 * wide, :] = grad_b_up[:, chunk]
    else:
        grad_bgu_ref[:wide, :] = grad_b_gate
        grad_bgu_ref[wide:, :] = grad_b_up
    per_quarter = features // tile
    down_ref[
        pl.ds(pl.multiple_of((step // per_quarter) * wide, wide), wide),
        pl.ds(pl.multiple_of((step % per_quarter) * tile, tile), tile),
    ] = dot(few_down_turned_ref[...], act)

    out_copies = [
        pltpu.make_async_copy(source, target, out_sems.at[index])
        for index, (source, target) in enumerate(
            (
                (out_ref, out_any),
                (out_ref.at[out_ref.shape[0] - swap_rows :, :], tail_any),
                (grad_res_ref, grad_res_any),
            )
        )
    ]

    @pl.when(step == steps - 1)
    def _():
        grads_out = e_ref[...]
        inner_down = only(inner_down_ref[...] * mask, 0)
        res = res_ref[...]
        out_ref[...] = (
            res + sum_ref[...] + ADAPTER_SCALE * dot(inner_down, b_do_ref[...])
        ).astype(jnp.bfloat16)
        for copy in out_copies[:2]:
            copy.start()
        few = jnp.where(place < 2, ADAPTER_SCALE * few_ref[...] * mask, 0.0).astype(jnp.bfloat16)
        grad_hidden = grad_hidden_ref[...] + contract_last(few, a_guo_ref[...])
        grad_res = grads_out.astype(jnp.float32) + row_norm_back(
            res, gains_ref[1:2, :], grad_hidden
        )
        low = grad_res.astype(jnp.bfloat16)
        grad_res_ref[...] = low
        out_copies[2].start()
        few_out = only(ADAPTER_SCALE * contract_last(low, b_do_ref[...]) * mask, 2)
        grad_att_ref[...] = contract_last(
            beside(low, few_out), beside(wo_ref[...], a_guo_ref[...])
        ).astype(jnp.bfloat16)
        grad_a = dot(turn(few), hidden_ref[...]) + dot(turn(few_out), att_ref[...])
        inner_out = only(inner_ref[...].astype(jnp.float32), 2)
        grad_b = ADAPTER_SCALE * (
            dot(turn(inner_down), grads_out) + dot(turn(inner_out), low)
        )
        if devices:
            lane = lax.broadcasted_iota(jnp.int32, (features, LANES), 1)
            told = jnp.where(
                lane == 3 * wide, turn_ref[0], jnp.where(lane == 3 * wide + 1, turn_ref[1], 0)
            )
            tall_ref[...] = jnp.transpose(grad_a) + told.astype(jnp.float32)
            spread_wide_to(spread_ref, 0, tall_ref)
            tall_ref[...] = jnp.transpose(down_ref[...])
            spread_wide_to(spread_ref, wide, tall_ref)
            chunks = features // LANES
            for chunk in range(chunks):
                square_ref[chunk] = grad_b[:, chunk * LANES : (chunk + 1) * LANES]
                spread_square_to(
                    spread_ref, 4 * wide, square_ref, (0, 2 * wide), chunk, chunks, chunk
                )
        else:
            grad_a_ref[...] = jnp.transpose(grad_a).astype(jnp.bfloat16)
            grad_ad_ref[...] = jnp.transpose(down_ref[...]).astype(jnp.bfloat16)
            grad_bdo_ref[...] = grad_b.astype(jnp.bfloat16)
        for copy in out_copies:
            copy.wait()


def feed_forward(
    devices,
    turn_adapter,
    attended,
    rows_in,
    kept,
    arrived,
    gains,
    weights,
    selected,
    meta,
):
    rows, features = rows_in.shape
    hidden = weights[1].shape[1]
    tile = 512
    full = whole_block((rows, features))
    square = whole_block((features, features))
    anywhere = pl.BlockSpec(memory_space=pl.ANY)

    def shape(height, length, dtype):
        return jax.ShapeDtypeStruct((height, length), dtype)

    if devices:
        spread = (devices, 9 * RANK, LANES)
        grad_specs = [whole_block(spread)]
        grad_shapes = [jax.ShapeDtypeStruct(spread, jnp.bfloat16)]
    else:
        grad_specs = [
            whole_block((features, LANES)),
            whole_block((features, LANES)),
            pl.BlockSpec((4 * RANK, tile), lambda step: (0, step)),
            whole_block((LANES, features)),
        ]
        grad_shapes = [
            shape(features, LANES, jnp.bfloat16),
            shape(features, LANES, jnp.bfloat16),
            shape(4 * RANK, hidden, jnp.bfloat16),
            shape(LANES, features, jnp.bfloat16),
        ]
    return pl.pallas_call(
        functools.partial(feed_forward_kernel, devices),
        grid=(hidden // tile,),
        in_specs=[
            pl.BlockSpec(memory_space=pltpu.SMEM),
            full,
            anywhere,
            anywhere,
            anywhere,
            whole_block(gains.shape),
            square,
            anywhere,
            anywhere,
            anywhere,
            whole_block((features, LANES)),
            pl.BlockSpec((tile, LANES), lambda step: (step, 0)),
            pl.BlockSpec((LANES, tile), lambda step: (0, step)),
            whole_block((LANES, features)),
            whole_block(meta.shape),
        ],
        out_specs=[anywhere, anywhere, anywhere, full, *grad_specs],
        out_shape=[
            shape(rows, features, jnp.bfloat16),
            shape(*arrived.shape, jnp.bfloat16),
            shape(rows, features, jnp.bfloat16),
            shape(rows, features, jnp.bfloat16),
            *grad_shapes,
        ],
        scratch_shapes=[
            pltpu.VMEM((rows, features), jnp.float32),
            pltpu.VMEM((rows, features), jnp.bfloat16),
            pltpu.VMEM((rows, LANES), jnp.bfloat16),
            pltpu.VMEM((LANES, rows), jnp.bfloat16),
            pltpu.VMEM((rows, features), jnp.float32),
            pltpu.VMEM((rows, features), jnp.float32),
            pltpu.VMEM((rows, LANES), jnp.float32),
            pltpu.VMEM((rows, LANES), jnp.float32),
            pltpu.VMEM((rows, LANES), jnp.bfloat16),
            pltpu.VMEM((2 * RANK, rows), jnp.bfloat16),
            pltpu.VMEM((LANES, features), jnp.float32),
            pltpu.VMEM((features, LANES), jnp.float32),
            pltpu.VMEM((features // LANES, LANES, LANES), jnp.float32),
            pltpu.VMEM((rows, features), jnp.bfloat16),
            pltpu.VMEM((rows, features), jnp.bfloat16),
            pltpu.VMEM(arrived.shape, jnp.bfloat16),
            pltpu.VMEM((2, features, tile), jnp.bfloat16),
            pltpu.VMEM((2, features, tile), jnp.bfloat16),
            pltpu.VMEM((2, tile, features), jnp.bfloat16),
            pltpu.VMEM((rows, features), jnp.bfloat16),
            pltpu.VMEM((rows, features), jnp.bfloat16),
            pltpu.SemaphoreType.DMA((3,)),
            pltpu.SemaphoreType.DMA((2, 3)),
            pltpu.SemaphoreType.DMA((3,)),
        ],
        compiler_params=pltpu.CompilerParams(vmem_limit_bytes=VMEM_LIMIT),
        cost_estimate=pl.CostEstimate(
            flops=14 * rows * features * hidden,
            bytes_accessed=8 * features * hidden + 16 * rows * features,
            transcendentals=0,
        ),
        name="feed_forward",
    )(
        turn_adapter,
        attended,
        rows_in,
        kept,
        arrived,
        gains,
        *weights,
        *selected,
        meta,
    )


def settle_owned(grads, moment1, moment2, devices):
    grads = lax.all_to_all(grads, ALL, 0, 0, tiled=True)
    grads = grads[:, : moment1.shape[0] // (LANES * devices)]
    grad_shard = jnp.transpose(grads, (1, 0, 2)).reshape(-1).astype(jnp.float32)
    current = jnp.zeros((), jnp.float32)
    first_moment, second_moment, _ = adam(current, moment1, moment2, grad_shard)
    return grad_shard, first_moment, second_moment


def per_device(
    tokens,
    cotangent,
    variate,
    seq_len,
    seq_adapter,
    block_order,
    attn_gain,
    ffn_gain,
    q_gain,
    k_gain,
    attn_bias,
    query_weight,
    key_weight,
    value_weight,
    output_weight,
    gate_weight,
    up_weight,
    down_weight,
    adapters,
    moment1,
    moment2,
):
    groups = axis_count(GROUP)
    member = lax.axis_index(GROUP)
    row_count, feature_width = tokens.shape
    hidden_width = gate_weight.shape[1]
    head_width = q_gain.shape[0]
    half_devices = groups // 2
    segments = seq_len.shape[1]
    chosen, back, turn_adapter, cos_table, sin_table, key_metas = plan(
        groups, row_count, head_width, member[None], seq_len, seq_adapter, block_order, variate
    )
    meta = key_metas[0]
    axes = ALL
    devices = axis_count(PACKS) * groups
    even = spreads_evenly(devices, groups, feature_width, hidden_width, adapters.shape[0])
    spread = devices if even else 0
    gains = gain_rows(attn_gain, ffn_gain, q_gain, k_gain)


    held = (gather_half(tokens, groups), gather_half(cotangent, groups))
    sent_tokens, sent_grads = pick(chosen, row_count, row_count // 2, *held)
    arrived_tokens = to_other_half(sent_tokens, groups)
    a_qkv, a_guo, a_down, b_qkv, b_gu, b_do, *spread_state = select(
        spread,
        turn_adapter,
        lax.axis_index(axes)[None],
        adapters,
        (moment1.reshape(-1, LANES), moment2.reshape(-1, LANES)),
        feature_width,
        hidden_width,
        sent_tokens,
    )
    if even:
        params, moments = spread_state
        moments = lax.all_to_all(moments, axes, 0, 0, tiled=True)
    kept_tokens, kept_grads = pick(chosen, 0, row_count, *held)
    (
        my_tokens,
        normed,
        inner,
        query_raw,
        key_raw,
        query_low,
        key_low,
        value_low,
        sent_grads,
    ) = project_heads(
        kept_tokens,
        arrived_tokens,
        sent_grads,
        gains,
        (query_weight, key_weight, value_weight),
        a_qkv,
        b_qkv,
        meta,
        cos_table,
        sin_table,
        head_width,
    )
    arrived_grads = to_other_half(sent_grads, groups)
    keys = gather_half(key_low, groups)
    values = gather_half(value_low, groups)
    attended_low, log_total = attend(
        attn_bias, query_low, meta, keys, values, key_metas, segments, head_width
    )
    layer_rows, layer_tail, grad_residual, grad_attended, *forward_grads = feed_forward(
        spread,
        turn_adapter,
        attended_low,
        my_tokens,
        kept_grads,
        arrived_grads,
        gains,
        (output_weight, gate_weight, up_weight, down_weight),
        (a_guo, a_down, b_gu, b_do),
        meta,
    )
    layer_back = to_other_half(layer_tail, groups)
    layer_held = gather_half(layer_rows, groups) + gather_half(layer_back, groups)

    results = attend_back(
        attn_bias,
        query_low,
        meta,
        log_total,
        attended_low,
        grad_attended,
        keys,
        values,
        key_metas,
        segments,
        head_width,
    )
    after = []
    if even:
        total_rows = adapters.shape[0] // LANES
        late_rows = 6 * feature_width // devices
        early = lax.all_to_all(forward_grads[0], axes, 0, 0, tiled=True)
        early_grad, early_new, late_m1, late_m2, tall, square = settle_early(
            early, moments, params, late_rows, [results[0]]
        )
        early_outer = lax.all_to_all(early_new, "far", 0, 0, tiled=True)
        swap = [(0, 1), (1, 0)]
        early_near = lax.ppermute(early_outer, "near", swap)
        early_half = lax.ppermute(early_outer, "half", swap)
        after = [early_new, layer_back]
    grad_query = results[0]
    grad_keys = results[1 : 1 + half_devices]
    grad_values = results[1 + half_devices :]
    key_terms, value_terms = [grad_keys[0]], [grad_values[0]]
    for shift in range(1, half_devices):
        back_shift = half_devices - shift
        key_terms.append(within_half(grad_keys[shift], back_shift, groups))
        value_terms.append(within_half(grad_values[shift], back_shift, groups))
    grad_rows, grad_tail, *back_grads = project_heads_back(
        spread,
        after,
        grad_query,
        key_terms,
        value_terms,
        query_raw,
        key_raw,
        normed,
        inner,
        my_tokens,
        grad_residual,
        gains,
        (query_weight, key_weight, value_weight),
        a_qkv,
        b_qkv,
        meta,
        cos_table,
        sin_table,
        head_width,
    )
    def bring_back(tail):
        return gather_half(grad_rows, groups) + gather_half(to_other_half(tail, groups), groups)

    if not even:
        grads = (*back_grads, *forward_grads)
        column = jnp.arange(2 * RANK, dtype=jnp.int32)
        few_choice = one_hot(
            jnp.arange(LANES, dtype=jnp.int32)[:, None]
            == (jnp.repeat(turn_adapter, RANK) * RANK + column % RANK)[None, :]
        )
        settled = settle_shards(grads, few_choice, adapters, moment1, moment2, groups)
        layer_out = pick(back, 0, row_count, layer_held)[0]
        input_grad = pick(back, 0, row_count, bring_back(grad_tail))[0]
        return (layer_out, input_grad) + settled
    late = lax.all_to_all(back_grads[0], axes, 0, 0, tiled=True)
    layer_out = pick(back, 0, row_count, layer_held)[0]
    own_grads, late_new, grad_tail = settle_late(
        tall, square, late, params, late_m1, late_m2, early_grad, grad_tail, [layer_out, early_near, early_half]
    )
    late_outer = lax.all_to_all(late_new, PACKS, 0, 0, tiled=True)
    late_pieces = gather_inner(late_outer, groups)
    own_grads, early_half = hand_on(late_outer, own_grads, early_half)
    early_far = lax.ppermute(early_half, "near", swap)
    input_grad = pick(back, 0, row_count, bring_back(grad_tail))[0]
    early_pieces = [[early_outer], [early_near], [early_half], [early_far]]
    early_pieces += [
        [lax.ppermute(part, "core", swap) for part in piece] for piece in early_pieces
    ]
    far = jnp.arange(lax.axis_size("far"), dtype=jnp.int32)
    near, half, core = [lax.axis_index(name) for name in ALL[1:]]
    early_device = jnp.concatenate(
        [
            ((far * 2 + (near ^ flip_near)) * 2 + (half ^ flip_half)) * 2 + (core ^ flip_core)
            for flip_core in (0, 1)
            for flip_near, flip_half in ((0, 0), (1, 0), (0, 1), (1, 1))
        ]
    )
    late_pieces = [[piece] for piece in late_pieces]
    order = placing_order(piece_devices(groups, devices), 16)
    adapters_new = assemble(order, late_pieces, total_rows, 0, None, [input_grad])
    adapters_new = assemble(
        placing_order(early_device, 16), early_pieces, total_rows, late_rows, adapters_new, []
    )
    owned = settle_owned(own_grads, moment1, moment2, devices)
    return (layer_out, input_grad, *owned, adapters_new.reshape(-1))


def solution(mesh):
    packs, groups = mesh.shape["dp"], mesh.shape["group"]
    cut = jax.sharding.Mesh(mesh.devices.reshape(packs // 2, 2, groups // 2, 2), ALL)
    in_specs = (
        P(ALL, None),
        P(ALL, None),
        P(PACKS),
        P(PACKS, None),
        P(PACKS, None),
        P(PACKS, None),
        P(),
        P(),
        P(),
        P(),
        P(),
        P(),
        P(),
        P(),
        P(),
        P(),
        P(),
        P(),
        P(),
        P(ALL),
        P(ALL),
    )
    out_specs = (
        P(ALL, None),
        P(ALL, None),
        P(ALL),
        P(ALL),
        P(ALL),
        P(),
    )
    return jax.shard_map(
        per_device, mesh=cut, in_specs=in_specs, out_specs=out_specs, check_vma=False
    )
```

```python
import functools

import jax
import jax.numpy as jnp
import numpy as np
from jax import lax
from jax.experimental import pallas as pl
from jax.experimental.pallas import tpu as pltpu
from jax.sharding import PartitionSpec as P

RANK = 16
ADAPTERS = 8
NORM_EPS = 1e-06
ADAPTER_SCALE = 2.0
ROPE_BASE = 10000.0
MASKED = -1e30
LEARN_RATE = 0.01
BETA_ONE = 0.9
BETA_TWO = 0.999
ADAM_EPS = 1e-08
WEIGHT_DECAY = 0.01
update_count = 10.0
VARIATES = 4
VMEM_LIMIT = 62 * 1024 * 1024
EXACT_PARTS = 3
PAIRS = 2


def contract_last(left, right):
    return lax.dot_general(
        left, right, (((1,), (1,)), ((), ())), preferred_element_type=jnp.float32
    )


def exact_parts(values):
    parts = []
    for _ in range(EXACT_PARTS):
        part = values.astype(jnp.bfloat16).astype(jnp.float32)
        parts.append(part)
        values = values - part
    return parts


def parts_in_lanes(values, first, column):
    result = jnp.zeros(values.shape, jnp.float32)
    for index, part in enumerate(exact_parts(values)):
        result = jnp.where(column == first + index, part, result)
    return result


def note_keys(side_ref, kmeta_refs, column, lane, width, segments):
    seg_column = column - EXACT_PARTS * VARIATES
    ones = (seg_column >= segments) & (seg_column < segments + EXACT_PARTS)
    for block, kmeta_ref in enumerate(kmeta_refs):
        one = (column < EXACT_PARTS * VARIATES) & ((column % VARIATES) == kmeta_ref[:, 0:1])
        in_seg = (seg_column >= 0) & (seg_column < segments) & (seg_column == kmeta_ref[:, 1:2])
        for head in range(2):
            outside = (lane // width) != head
            side_ref[head, block] = one_hot((one | in_seg | ones) & outside)


def note_queries(match_ref, apart_ref, qmeta_ref, column, segments):
    same = (column < EXACT_PARTS * VARIATES) & ((column % VARIATES) == qmeta_ref[:, 0:1])
    match_ref[...] = jnp.where(same, 1.0, 0.0)
    seg_column = column - EXACT_PARTS * VARIATES
    apart = (seg_column >= 0) & (seg_column < segments) & (seg_column != qmeta_ref[:, 1:2])
    apart_ref[...] = jnp.where(apart, MASKED, 0.0)


def bias_rows(bias_ref, head, column):
    rows = []
    for which in range(2):
        row = jnp.zeros(column.shape, jnp.float32)
        value = jnp.full(column.shape, bias_ref[which, head], jnp.float32)
        for index, part in enumerate(exact_parts(value)):
            row = jnp.where(column // VARIATES == index, part, row)
        rows.append(row)
    return rows


def query_side(match_ref, apart_ref, bias_ref, head, column):
    same, other = bias_rows(bias_ref, head, column[:1])
    return jnp.where(match_ref[...] > 0.0, same, other) + apart_ref[...]


def head_lanes(head, width, lanes):
    lane = lax.broadcasted_iota(jnp.int32, (1, lanes), 1)
    return jnp.where(lane // width == head, 1.0, 0.0).astype(jnp.bfloat16)


def attend_kernel(key_blocks, segments, width, bias_ref, query_ref, qmeta_ref, *refs):
    key_refs, value_refs, kmeta_refs = (
        refs[:key_blocks],
        refs[key_blocks : 2 * key_blocks],
        refs[2 * key_blocks : 3 * key_blocks],
    )
    out_ref, total_ref, side_ref, match_ref, apart_ref = refs[3 * key_blocks :]
    step = pl.program_id(0)
    rows = query_ref.shape[0]
    lanes = 2 * width
    pairs = query_ref.shape[1] // lanes
    lane = lax.broadcasted_iota(jnp.int32, (rows, lanes), 1)
    column = lane % width

    @pl.when(step == 0)
    def _():
        note_keys(side_ref, kmeta_refs, column, lane, width, segments)
        note_queries(match_ref, apart_ref, qmeta_ref, column, segments)

    first = (lane // width) == 0
    heads = [(pair, head) for pair in range(pairs) for head in range(2)]
    scores = []
    for pair, head in heads:
        here = slice(pair * lanes, (pair + 1) * lanes)
        scaled = query_ref[:, here].astype(jnp.float32) * width ** (-0.5)
        extension = query_side(
            match_ref, apart_ref, bias_ref, (step * pairs + pair) * 2 + head, column
        )
        left = jnp.where((lane // width) == head, scaled, extension).astype(jnp.bfloat16)
        inside = head_lanes(head, width, lanes)
        for block in range(key_blocks):
            right = key_refs[block][:, here] * inside + side_ref[head, block]
            scores.append(contract_last(left, right))
    results = []
    for index, (pair, head) in enumerate(heads):
        here = slice(pair * lanes, (pair + 1) * lanes)
        inside = head_lanes(head, width, lanes)
        outside = head_lanes(1 - head, width, lanes)
        weights = [
            jnp.exp(score).astype(jnp.bfloat16)
            for score in scores[index * key_blocks : (index + 1) * key_blocks]
        ]
        values = [ref[:, here] * inside + outside for ref in value_refs]
        results.append(dot(beside(*weights), above(*values)))
        if head == 1:
            numerator = jnp.where(first, results[-2], results[-1])
            crossed = jnp.where(first, results[-1], results[-2])
            out_ref[:, here] = (numerator / pltpu.roll(crossed, width, 1)).astype(jnp.bfloat16)
            total_ref[:, here] = jnp.log(crossed)


def lane_block(rows, lanes):
    return pl.BlockSpec((rows, lanes), lambda pair: (0, pair))


def whole_block(shape):
    return pl.BlockSpec(shape, lambda pair: (0,) * len(shape))


def attend(attn_bias, query_low, query_meta, keys, values, key_metas, segments, width):
    rows, features = query_low.shape
    lanes = 2 * width
    wide = PAIRS * lanes
    count = len(keys)
    flops = 4 * rows * rows * count * features
    return pl.pallas_call(
        functools.partial(attend_kernel, count, segments, width),
        grid=(features // wide,),
        in_specs=[
            pl.BlockSpec(memory_space=pltpu.SMEM),
            lane_block(rows, wide),
            whole_block(query_meta.shape),
        ]
        + [lane_block(rows, wide)] * (2 * count)
        + [whole_block(query_meta.shape)] * count,
        out_specs=[lane_block(rows, wide)] * 2,
        out_shape=[
            jax.ShapeDtypeStruct((rows, features), jnp.bfloat16),
            jax.ShapeDtypeStruct((rows, features), jnp.float32),
        ],
        scratch_shapes=[
            pltpu.VMEM((2, count, rows, lanes), jnp.bfloat16),
            pltpu.VMEM((rows, lanes), jnp.float32),
            pltpu.VMEM((rows, lanes), jnp.float32),
        ],
        compiler_params=pltpu.CompilerParams(vmem_limit_bytes=VMEM_LIMIT),
        cost_estimate=pl.CostEstimate(
            flops=flops, bytes_accessed=12 * rows * features, transcendentals=0
        ),
        name="attend",
    )(attn_bias, query_low, query_meta, *keys, *values, *key_metas)


def attend_back_kernel(
    key_blocks,
    segments,
    width,
    bias_ref,
    query_ref,
    qmeta_ref,
    total_ref,
    attended_ref,
    grad_ref,
    *refs,
):
    key_refs, value_refs, kmeta_refs = (
        refs[:key_blocks],
        refs[key_blocks : 2 * key_blocks],
        refs[2 * key_blocks : 3 * key_blocks],
    )
    results = refs[len(refs) - 4 - 2 * key_blocks :]
    grad_query_ref = results[0]
    grad_key_refs = results[1 : key_blocks + 1]
    grad_value_refs = results[key_blocks + 1 : 2 * key_blocks + 1]
    side_ref, match_ref, apart_ref = results[2 * key_blocks + 1 :]
    pair = pl.program_id(0)
    rows, lanes = query_ref.shape
    lane = lax.broadcasted_iota(jnp.int32, (rows, lanes), 1)
    column = lane % width
    ones_at = EXACT_PARTS * VARIATES + segments

    @pl.when(pair == 0)
    def _():
        note_keys(side_ref, kmeta_refs, column, lane, width, segments)
        note_queries(match_ref, apart_ref, qmeta_ref, column, segments)

    scaled = query_ref[...].astype(jnp.float32) * width ** (-0.5)
    scaled_low = scaled.astype(jnp.bfloat16)
    grad_low = grad_ref[...]
    grad = grad_low.astype(jnp.float32)
    overlap = grad * attended_ref[...].astype(jnp.float32)
    square_row = lax.broadcasted_iota(jnp.int32, (lanes, lanes), 0)
    square_column = lax.broadcasted_iota(jnp.int32, (lanes, lanes), 1)
    across = one_hot(square_row // width != square_column // width)
    high = overlap.astype(jnp.bfloat16)
    rest = (overlap - high.astype(jnp.float32)).astype(jnp.bfloat16)
    dot_side = parts_in_lanes(-(dot(high, across) + dot(rest, across)), ones_at, column)
    total_side = parts_in_lanes(-total_ref[...], ones_at, column)
    heads = range(lanes // width)
    blocks = range(key_blocks)
    probs, grad_probs = {}, {}
    for head in heads:
        inside = (lane // width) == head
        extension = total_side + query_side(
            match_ref, apart_ref, bias_ref, pair * (lanes // width) + head, column
        )
        right = jnp.where(inside, scaled, extension).astype(jnp.bfloat16)
        grad_right = jnp.where(inside, grad, dot_side).astype(jnp.bfloat16)
        own_lanes = head_lanes(head, width, lanes)
        for block in blocks:
            side = side_ref[head, block]
            probs[head, block] = contract_last(key_refs[block][...] * own_lanes + side, right)
            grad_probs[head, block] = contract_last(
                value_refs[block][...] * own_lanes + side, grad_right
            )
    grad_query_parts = []
    grad_keys = [[] for _ in blocks]
    grad_values = [[] for _ in blocks]
    keys_turned = beside(*[jnp.transpose(ref[...]) for ref in key_refs])
    for head in heads:
        grad_scores = []
        for block in blocks:
            prob = jnp.exp(probs[head, block])
            grad_score = (prob * grad_probs[head, block]).astype(jnp.bfloat16)
            grad_values[block].append(dot(prob.astype(jnp.bfloat16), grad_low))
            grad_keys[block].append(dot(grad_score, scaled_low))
            grad_scores.append(grad_score)
        grad_query_parts.append(
            dot(keys_turned[head * width : (head + 1) * width], above(*grad_scores))
        )
    first = (lane // width) == 0
    stacked = jnp.concatenate(grad_query_parts, axis=0) * width ** (-0.5)
    grad_query_ref[...] = jnp.transpose(stacked).astype(jnp.bfloat16)
    for block in range(key_blocks):
        grad_key_refs[block][...] = jnp.where(first, *grad_keys[block]).astype(
            grad_key_refs[block].dtype
        )
        grad_value_refs[block][...] = jnp.where(first, *grad_values[block]).astype(
            grad_value_refs[block].dtype
        )


def attend_back(
    attn_bias,
    query_low,
    query_meta,
    log_total,
    attended_low,
    grad_attended,
    keys,
    values,
    key_metas,
    segments,
    width,
):
    rows, features = query_low.shape
    lanes = 2 * width
    count = len(keys)
    here = lane_block(rows, lanes)
    flops = 10 * rows * rows * count * features
    low = jax.ShapeDtypeStruct((rows, features), jnp.bfloat16)
    results = pl.pallas_call(
        functools.partial(attend_back_kernel, count, segments, width),
        grid=(features // lanes,),
        in_specs=[
            pl.BlockSpec(memory_space=pltpu.SMEM),
            here,
            whole_block(query_meta.shape),
        ]
        + [here] * (3 + 2 * count)
        + [whole_block(query_meta.shape)] * count,
        out_specs=[here] * (1 + 2 * count),
        out_shape=[low] * (1 + 2 * count),
        scratch_shapes=[
            pltpu.VMEM((2, count, rows, lanes), jnp.bfloat16),
            pltpu.VMEM((rows, lanes), jnp.float32),
            pltpu.VMEM((rows, lanes), jnp.float32),
        ],
        compiler_params=pltpu.CompilerParams(vmem_limit_bytes=VMEM_LIMIT),
        cost_estimate=pl.CostEstimate(
            flops=flops, bytes_accessed=20 * rows * features, transcendentals=0
        ),
        name="attend_back",
    )(
        attn_bias,
        query_low,
        query_meta,
        log_total,
        attended_low,
        grad_attended,
        *keys,
        *values,
        *key_metas,
    )
    return results


def plan_kernel(
    groups,
    rows,
    width,
    member_ref,
    length_ref,
    adapter_ref,
    order_ref,
    variate_ref,
    frequency_ref,
    chosen_ref,
    back_ref,
    turn_ref,
    cos_ref,
    sin_ref,
    *refs,
):
    meta_refs, slot_ref = refs[:-1], refs[-1]
    blocks = variate_ref.shape[0]
    half_devices = groups // 2
    half_blocks = blocks // 2
    half_rows = half_blocks * LANES
    swap_rows = rows // 2
    member = member_ref[0]
    my_half, my_place = member // half_devices, member % half_devices
    places = [lax.rem(my_place + shift, half_devices) for shift in range(half_devices)]
    segments = length_ref.shape[1]
    starts = [jnp.int32(0)]
    for segment in range(segments):
        starts.append(starts[-1] + length_ref[0, segment])
    long_start, long_index = jnp.int32(0), jnp.int32(0)
    for segment in range(segments):
        is_half = length_ref[0, segment] == half_rows
        long_start = jnp.where(is_half, starts[segment], long_start)
        long_index = jnp.where(is_half, segment, long_index)

    block = lax.broadcasted_iota(jnp.int32, (blocks, LANES), 0)
    lane = lax.broadcasted_iota(jnp.int32, (blocks, LANES), 1)
    work_block = jnp.zeros((blocks, LANES), jnp.int32)
    for index in range(blocks):
        work_block = jnp.where(block == order_ref[0, index], index, work_block)
    work_row = work_block * LANES + lane
    is_long = (work_row >= long_start) & (work_row < long_start + half_rows)
    in_first = block < half_blocks
    long_count = jnp.sum(jnp.where(is_long & in_first, 1.0, 0.0)).astype(jnp.int32)
    long_half = jnp.where(2 * long_count < half_rows, 1, 0)
    side = jnp.where(in_first, 0, 1)
    target = jnp.where(is_long, long_half, 1 - long_half)
    foreign = target != side
    flags = jnp.where(foreign, 1.0, 0.0)
    moved = jnp.sum(jnp.where(in_first, flags, 0.0)).astype(jnp.int32)
    square_row = lax.broadcasted_iota(jnp.int32, (LANES, LANES), 0)
    square_column = lax.broadcasted_iota(jnp.int32, (LANES, LANES), 1)
    within = dot(flags.astype(jnp.bfloat16), one_hot(square_row < square_column))
    block_sum = jnp.broadcast_to(jnp.sum(flags, axis=1, keepdims=True), (blocks, LANES))
    from_block = lax.broadcasted_iota(jnp.int32, (blocks, blocks), 1)
    to_block = lax.broadcasted_iota(jnp.int32, (blocks, blocks), 0)
    earlier = (from_block < to_block) & ((from_block < half_blocks) == (to_block < half_blocks))
    before = dot(one_hot(earlier), block_sum.astype(jnp.bfloat16))
    foreign_rank = (within + before).astype(jnp.int32)
    kept_rank = (block - side * half_blocks) * LANES + lane - foreign_rank
    kept_slot = side * half_rows + kept_rank
    foreign_slot = (1 - side) * half_rows + rows + foreign_rank
    foreign_slot = foreign_slot - jnp.clip(moved, 0, swap_rows)
    for index in range(1, half_devices):
        start = index * rows - jnp.minimum(moved, index * swap_rows)
        last = (index - 1) * rows - jnp.minimum(moved, (index - 1) * swap_rows)
        kept_slot = jnp.where(kept_rank >= start, kept_slot + rows - (start - last), kept_slot)
        received = jnp.clip(moved - index * swap_rows, 0, swap_rows)
        previous = jnp.clip(moved - (index - 1) * swap_rows, 0, swap_rows)
        foreign_slot = jnp.where(
            foreign_rank >= index * swap_rows,
            foreign_slot + rows - swap_rows + previous - received,
            foreign_slot,
        )
    slot = jnp.where(foreign, foreign_slot, kept_slot)
    slot_ref[...] = slot

    per_device = rows // LANES
    wanted = lax.broadcasted_iota(jnp.int32, (rows + swap_rows, 1), 0)
    wanted = jnp.where(
        wanted < rows,
        my_half * half_rows + my_place * rows + wanted,
        (1 - my_half) * half_rows + my_place * rows + wanted - swap_rows,
    )
    for shift in range(half_devices):
        for index in range(per_device):
            held = my_half * half_blocks + places[shift] * per_device + index
            column = (shift * per_device + index) * LANES
            chosen_ref[:, column : column + LANES] = one_hot(
                wanted == slot_ref[pl.ds(held, 1), :]
            )

    slot_turned = jnp.transpose(slot.astype(jnp.float32))
    turned_lane = lax.broadcasted_iota(jnp.int32, (LANES, blocks), 1)
    first_lane = lax.broadcasted_iota(jnp.int32, (1, LANES), 1)
    for index in range(per_device):
        held = my_half * half_blocks + my_place * per_device + index
        mine = jnp.sum(
            jnp.where(turned_lane == held, slot_turned, 0.0), axis=1, keepdims=True
        ).astype(jnp.int32)
        here = slice(index * LANES, (index + 1) * LANES)
        column = 0
        for first, half, length in ((0, my_half, rows), (swap_rows, 1 - my_half, swap_rows)):
            for shift in range(half_devices):
                for chunk in range(0, length, LANES):
                    number = half * half_rows + places[shift] * rows + first + chunk
                    back_ref[here, column : column + LANES] = one_hot(mine == number + first_lane)
                    column += LANES

    on_long = my_half == long_half
    for turn in range(2):
        chosen_segment = jnp.where(
            on_long, long_index, jnp.where(long_index <= turn, turn + 1, turn)
        )
        adapter = adapter_ref[0, 0]
        for segment in range(1, segments):
            adapter = jnp.where(chosen_segment == segment, adapter_ref[0, segment], adapter)
        turn_ref[turn] = adapter

    variate_turned = jnp.transpose(variate_ref[...].astype(jnp.float32))
    known = []
    for index in range(blocks):
        values = jnp.where(
            square_column == 0,
            work_block[index : index + 1, :].astype(jnp.float32),
            jnp.where(
                square_column == 1,
                square_row.astype(jnp.float32),
                variate_turned[:, index : index + 1],
            ),
        )
        known.append(jnp.where(square_column < 3, values, 0.0).astype(jnp.bfloat16))
    number = lax.broadcasted_iota(jnp.int32, (rows, 1), 0)
    wide_lane = lax.broadcasted_iota(jnp.int32, (rows, LANES), 1)
    for shift in range(half_devices):
        slots = my_half * half_rows + places[shift] * rows + number
        facts = jnp.zeros((rows, LANES), jnp.float32)
        for index in range(blocks):
            facts = facts + dot(one_hot(slots == slot[index : index + 1, :]), known[index])
        facts = facts.astype(jnp.int32)
        row = facts[:, 0:1] * LANES + facts[:, 1:2]
        segment = jnp.zeros((rows, 1), jnp.int32)
        first_row = jnp.zeros((rows, 1), jnp.int32)
        for index in range(1, segments):
            segment = jnp.where(row >= starts[index], index, segment)
            first_row = jnp.where(row >= starts[index], starts[index], first_row)
        turn = jnp.where(segment > long_index, segment - 1, segment)
        turn = jnp.where(on_long, 0, turn)
        meta_refs[shift][...] = jnp.where(
            wide_lane == 0, facts[:, 2:3], jnp.where(wide_lane == 1, segment, turn)
        )
        if shift == 0:
            angles = (row - first_row).astype(jnp.float32) * frequency_ref[...]
            sign = jnp.where(wide_lane % width < width // 2, -1.0, 1.0)
            cos_ref[...] = jnp.cos(angles)
            sin_ref[...] = jnp.sin(angles) * sign


def plan(groups, rows, width, member, seq_len, seq_adapter, block_order, variate):
    half_devices = groups // 2
    half_rows = half_devices * rows
    blocks = block_order.shape[1]
    smem = pl.BlockSpec(memory_space=pltpu.SMEM)
    vmem = pl.BlockSpec(memory_space=pltpu.VMEM)
    results = pl.pallas_call(
        functools.partial(plan_kernel, groups, rows, width),
        in_specs=[smem, smem, smem, smem, vmem, vmem],
        out_specs=[vmem, vmem, smem, vmem, vmem] + [vmem] * half_devices,
        out_shape=[
            jax.ShapeDtypeStruct((rows + rows // 2, half_rows), jnp.bfloat16),
            jax.ShapeDtypeStruct((rows, half_rows + half_rows // 2), jnp.bfloat16),
            jax.ShapeDtypeStruct((2,), jnp.int32),
            jax.ShapeDtypeStruct((rows, LANES), jnp.float32),
            jax.ShapeDtypeStruct((rows, LANES), jnp.float32),
        ]
        + [jax.ShapeDtypeStruct((rows, LANES), jnp.int32)] * half_devices,
        scratch_shapes=[pltpu.VMEM((blocks, LANES), jnp.int32)],
        compiler_params=pltpu.CompilerParams(vmem_limit_bytes=VMEM_LIMIT),
        cost_estimate=pl.CostEstimate(
            flops=2**31, bytes_accessed=4 * rows * half_rows, transcendentals=0
        ),
        name="plan",
    )(
        member,
        seq_len,
        seq_adapter,
        block_order,
        variate.reshape(blocks, LANES),
        jnp.asarray(rope_frequency(width)),
    )
    return (*results[:5], results[5:])


def pick_kernel(counts, later_count, chosen_ref, *refs):
    outs = refs[sum(counts) + later_count : sum(counts) + later_count + len(counts)]
    refs = iter(refs[: sum(counts)])
    for count, out_ref in zip(counts, outs):
        total = jnp.zeros(out_ref.shape, jnp.float32)
        column = 0
        for _ in range(count):
            ref = next(refs)
            rows = ref.shape[0]
            total = total + dot(chosen_ref[:, column : column + rows], ref[...])
            column += rows
        out_ref[...] = total.astype(out_ref.dtype)


def pick(chosen, first, count, *helds, later=()):
    features = helds[0][0].shape[1]
    tile = features // 2
    parts = [part for held in helds for part in held]
    return pl.pallas_call(
        functools.partial(pick_kernel, [len(held) for held in helds], len(later)),
        grid=(features // tile,),
        in_specs=[pl.BlockSpec((count, chosen.shape[1]), lambda step: (first // count, 0))]
        + [pl.BlockSpec((part.shape[0], tile), lambda step: (0, step)) for part in parts]
        + [pl.BlockSpec(memory_space=pl.ANY)] * len(later),
        out_specs=[pl.BlockSpec((count, tile), lambda step: (0, step))] * len(helds)
        + [pl.BlockSpec(memory_space=pl.ANY)] * len(later),
        out_shape=[jax.ShapeDtypeStruct((count, features), jnp.bfloat16)] * len(helds)
        + [jax.ShapeDtypeStruct(array.shape, array.dtype) for array in later],
        input_output_aliases={1 + len(parts) + i: len(helds) + i for i in range(len(later))},
        compiler_params=pltpu.CompilerParams(vmem_limit_bytes=VMEM_LIMIT),
        cost_estimate=pl.CostEstimate(
            flops=2 * count * chosen.shape[1] * features * len(helds),
            bytes_accessed=8 * count * features * len(helds),
            transcendentals=0,
        ),
        name="pick",
    )(chosen, *parts, *later)


def axis_count(names):
    count = 1
    for name in names:
        count *= lax.axis_size(name)
    return count


def within_half(array, shift, groups):
    half = groups // 2
    pairs = [
        (base + (place + shift) % half, base + place)
        for base in (0, half)
        for place in range(half)
    ]
    return lax.ppermute(array, GROUP, pairs)


def gather_half(array, groups):
    return [array] + [within_half(array, shift, groups) for shift in range(1, groups // 2)]


def to_other_half(array, groups):
    half = groups // 2
    return lax.ppermute(array, GROUP, [(i, (i + half) % groups) for i in range(groups)])


def scatter_sum(array, axis_sizes):
    for name, size in reversed(axis_sizes):
        outer = array.shape[0] // size
        array = array.reshape((outer, size) + array.shape[1:])
        bit = 1
        while bit < size:
            index = lax.axis_index(name)
            own = (index // bit) % 2
            spread = array.reshape((outer, size // (2 * bit), 2) + array.shape[2:])
            keep = lax.dynamic_index_in_dim(spread, own, 2, keepdims=False)
            send = lax.dynamic_index_in_dim(spread, 1 - own, 2, keepdims=False)
            got = lax.ppermute(send, name, [(i, i ^ bit) for i in range(size)])
            array = (keep.astype(jnp.float32) + got.astype(jnp.float32)).astype(jnp.bfloat16)
            bit *= 2
        array = array.reshape((outer,) + array.shape[2:])
    return array


LANES = 128
MOMENT_ROWS = 24
PACKS = ("far", "near")
GROUP = ("half", "core")
ALL = PACKS + GROUP


def adam(current, first_old, second_old, grad):
    first_moment = BETA_ONE * first_old + (1.0 - BETA_ONE) * grad
    second_moment = BETA_TWO * second_old + (1.0 - BETA_TWO) * grad * grad
    first_fix = first_moment / (1.0 - BETA_ONE**update_count)
    second_fix = second_moment / (1.0 - BETA_TWO**update_count)
    updated = current - LEARN_RATE * (
        first_fix / (jnp.sqrt(second_fix) + ADAM_EPS) + WEIGHT_DECAY * current
    )
    return first_moment, second_moment, updated.astype(jnp.bfloat16)


def settle_shards(grads, few_choice, adapters, moment1, moment2, groups):
    a_qkv, b_qkv, a_guo, a_down, b_gu, b_do = grads
    features, few = a_qkv.shape[0], few_choice.shape[1]
    quarters = a_down.shape[1] // few
    down = jnp.concatenate([a_down[:, i * few : (i + 1) * few] for i in range(quarters)])
    wide = [a_qkv[:, i * few : (i + 1) * few] for i in range(3)]
    wide += [a_guo[:, i * few : (i + 1) * few] for i in (2, 0, 1)] + [down]
    tall = [b_qkv[i * few : (i + 1) * few] for i in range(3)]
    tall += [b_do[2 * few : 3 * few], b_gu[:few], b_gu[few : 2 * few], b_do[:few]]
    pieces = []
    for grad_a, grad_b in zip(wide, tall):
        pieces.append(lax.dot_general(grad_a, few_choice, (((1,), (1,)), ((), ()))).reshape(-1))
        pieces.append(jnp.dot(few_choice, grad_b).reshape(-1))
    axis_sizes = [(PACKS, axis_count(PACKS)), (GROUP, groups)]
    shards = axis_sizes[0][1] * groups
    flat_grads = jnp.concatenate(pieces).astype(jnp.bfloat16).reshape(shards, -1)
    grad_shard = scatter_sum(flat_grads, axis_sizes).reshape(-1).astype(jnp.float32)
    shard_count = grad_shard.shape[0]
    shard_start = lax.axis_index(ALL) * shard_count
    current = lax.dynamic_slice_in_dim(adapters, shard_start, shard_count).astype(jnp.float32)
    first_moment, second_moment, updated = adam(current, moment1, moment2, grad_shard)
    adapters_new = lax.all_gather(updated, ALL, axis=0, tiled=True)
    return grad_shard, first_moment, second_moment, adapters_new


def spreads_evenly(devices, groups, features, hidden, total):
    rows = total // LANES
    chunks = features // LANES
    return (
        groups == 4
        and ADAPTERS * RANK == LANES
        and devices * chunks == 256
        and chunks == 8
        and hidden == devices * LANES
        and hidden == 4 * features
        and rows % (devices * devices) == 0
        and devices & (devices - 1) == 0
    )


def one_hot(condition):
    return jnp.where(condition, 1.0, 0.0).astype(jnp.bfloat16)


def sum_wide(adapter_row, arrived_ref, first, width):
    sources = arrived_ref.shape[0]
    rows = lax.broadcasted_iota(jnp.int32, (LANES, width * LANES), 0)
    columns = lax.broadcasted_iota(jnp.int32, (LANES, width * LANES), 1)
    fits = (rows // (2 * RANK) == columns // LANES) & (rows % RANK == columns % RANK)
    second = (rows // RANK) % 2 == 1
    adapter = jnp.where(fits, (columns % LANES) // RANK, -1)
    total = jnp.zeros((32, width * LANES), jnp.float32)
    for source in range(sources):
        at = source * 2 * RANK
        chosen = jnp.where(
            second, adapter_row[:, at + RANK : at + RANK + 1], adapter_row[:, at : at + 1]
        )
        total = total + dot(
            arrived_ref[source, first : first + 32, :], one_hot(adapter == chosen)
        )
    return total


def sum_tall(adapter_row, arrived_ref, first):
    sources = arrived_ref.shape[0]
    depth = sources * 2 * RANK
    rows = lax.broadcasted_iota(jnp.int32, (LANES, depth), 0)
    columns = lax.broadcasted_iota(jnp.int32, (LANES, depth), 1)
    choice = one_hot((rows // RANK == adapter_row) & (rows % RANK == columns % RANK))
    held = arrived_ref[:, first : first + 2 * RANK, :].reshape(depth, LANES)
    return jnp.dot(choice, held, preferred_element_type=jnp.float32)


def sum_square(adapter_row, arrived_ref, first):
    sources = arrived_ref.shape[0]
    depth = sources * 16
    rows = lax.broadcasted_iota(jnp.int32, (64, depth), 0)
    columns = lax.broadcasted_iota(jnp.int32, (64, depth), 1)
    choice = one_hot(
        ((rows % 32) // 4 == adapter_row)
        & (rows % 4 == columns % 4)
        & (rows // 32 == (columns % 16) // 8)
    )
    held = arrived_ref[:, first : first + 16, :].reshape(depth, LANES)
    return jnp.dot(choice, held, preferred_element_type=jnp.float32)


def settle_rows(parts, skip, param_ref, m1_ref, m2_ref, m_skip, grad_ref, new_refs):
    row = 0
    for part in parts:
        here = slice(row, row + part.shape[0])
        there = slice(skip + row, skip + row + part.shape[0])
        at = slice(m_skip + row, m_skip + row + part.shape[0])
        row += part.shape[0]
        low = part.astype(jnp.bfloat16)
        grad_ref[here, :] = low
        new = adam(
            param_ref[there, :].astype(jnp.float32),
            m1_ref[at, :],
            m2_ref[at, :],
            low.astype(jnp.float32),
        )[2]
        for new_ref in new_refs:
            new_ref[here, :] = new


def settle_early_kernel(own_rows, arrived_ref, moments_ref, param_ref, *refs):
    grad_ref, new_ref, late_m1_ref, late_m2_ref, tall_ref, square_ref, m1_ref, m2_ref = refs[-8:]
    sources = arrived_ref.shape[0]
    told = 6 * RANK
    tall_column = lax.broadcasted_iota(jnp.int32, tall_ref.shape, 1)
    square_column = lax.broadcasted_iota(jnp.int32, square_ref.shape, 1)
    tall = jnp.zeros(tall_ref.shape, jnp.float32)
    square = jnp.zeros(square_ref.shape, jnp.float32)
    for source in range(sources):
        row = arrived_ref[source, 0:16, :].astype(jnp.float32)
        first, second = row[0:1, told : told + 1], row[0:1, told + 1 : told + 2]
        tall = jnp.where(
            tall_column // (2 * RANK) == source,
            jnp.where((tall_column // RANK) % 2 == 1, second, first),
            tall,
        )
        square = jnp.where(
            square_column // RANK == source,
            jnp.where((square_column // 4) % 2 == 1, second, first),
            square,
        )
        held = moments_ref[source].astype(jnp.float32)
        here = slice(source * own_rows, (source + 1) * own_rows)
        m1_ref[here, :] = held[:own_rows]
        m2_ref[here, :] = held[MOMENT_ROWS : MOMENT_ROWS + own_rows]
    tall = tall.astype(jnp.int32)
    square = square.astype(jnp.int32)
    tall_ref[...] = tall
    square_ref[...] = square
    late = late_m1_ref.shape[0]
    late_m1_ref[...] = m1_ref[:late, :]
    late_m2_ref[...] = m2_ref[:late, :]
    wide = sum_wide(tall, arrived_ref, 0, 3)
    last = sum_wide(tall, arrived_ref, 32, 4)
    pair = sum_square(square, arrived_ref, 128)
    parts = [
        wide[:, 2 * LANES :],
        pair[32:],
        wide[:, :LANES],
        sum_tall(tall, arrived_ref, 64),
        wide[:, LANES : 2 * LANES],
        sum_tall(tall, arrived_ref, 96),
    ]
    parts += [last[:, i * LANES : (i + 1) * LANES] for i in range(4)]
    parts.append(pair[:32])
    copies = [new_ref.at[copy] for copy in range(new_ref.shape[0])]
    settle_rows(parts, late, param_ref, m1_ref, m2_ref, late, grad_ref, copies)


def settle_early(arrived, moments, params, late_rows, after):
    sources = arrived.shape[0]
    rows = params.shape[0] - late_rows
    vmem = pl.BlockSpec(memory_space=pltpu.VMEM)
    low = jax.ShapeDtypeStruct((rows, LANES), jnp.bfloat16)
    late = jax.ShapeDtypeStruct((late_rows, LANES), jnp.float32)
    return pl.pallas_call(
        functools.partial(settle_early_kernel, params.shape[0] // sources),
        in_specs=[vmem, vmem, vmem] + [pl.BlockSpec(memory_space=pl.ANY)] * len(after),
        out_specs=[vmem] * 6,
        out_shape=[
            low,
            jax.ShapeDtypeStruct((1, rows, LANES), jnp.bfloat16),
            late,
            late,
            jax.ShapeDtypeStruct((1, sources * 2 * RANK), jnp.int32),
            jax.ShapeDtypeStruct((1, sources * RANK), jnp.int32),
        ],
        scratch_shapes=[pltpu.VMEM(params.shape, jnp.float32)] * 2,
        compiler_params=pltpu.CompilerParams(vmem_limit_bytes=VMEM_LIMIT),
        cost_estimate=pl.CostEstimate(
            flops=sources * 2**24, bytes_accessed=4 * arrived.size, transcendentals=0
        ),
        name="settle_early",
    )(arrived, moments, params, *after)


def settle_late_kernel(
    later_count, tall_ref, square_ref, arrived_ref, param_ref, m1_ref, m2_ref, *refs
):
    early_grad_ref = refs[0]
    own_ref, new_ref = refs[-3 - later_count : -1 - later_count]
    grad_ref = refs[-1]
    wide = sum_wide(tall_ref[...], arrived_ref, 0, 3)
    pairs = [sum_square(square_ref[...], arrived_ref, first) for first in (32, 48)]
    parts = []
    for index in range(3):
        parts.append(wide[:, index * LANES : (index + 1) * LANES])
        parts.append(pairs[index // 2][(index % 2) * 32 : (index % 2) * 32 + 32])
    copies = [new_ref.at[copy] for copy in range(new_ref.shape[0])]
    settle_rows(parts, 0, param_ref, m1_ref, m2_ref, 0, grad_ref, copies)
    low = jnp.concatenate(
        [ref[...].astype(jnp.float32) for ref in (grad_ref, early_grad_ref)], axis=0
    )
    each = low.shape[0] // own_ref.shape[0]
    zeros = jnp.zeros((own_ref.shape[1] - each, LANES), jnp.float32)
    for owner in range(own_ref.shape[0]):
        own_ref[owner] = jnp.concatenate(
            [low[owner * each : (owner + 1) * each], zeros], axis=0
        ).astype(jnp.bfloat16)


def settle_late(tall, square, arrived, params, late_m1, late_m2, early_grad, later, after):
    rows = late_m1.shape[0]
    anywhere = pl.BlockSpec(memory_space=pl.ANY)
    vmem = pl.BlockSpec(memory_space=pltpu.VMEM)
    return pl.pallas_call(
        functools.partial(settle_late_kernel, len(later)),
        in_specs=[vmem] * 7 + [anywhere] * (len(later) + len(after)),
        out_specs=[vmem, vmem] + [anywhere] * len(later),
        scratch_shapes=[pltpu.VMEM((rows, LANES), jnp.bfloat16)],
        input_output_aliases={7 + index: 2 + index for index in range(len(later))},
        out_shape=[
            jax.ShapeDtypeStruct((arrived.shape[0], MOMENT_ROWS, LANES), jnp.bfloat16),
            jax.ShapeDtypeStruct((axis_count(PACKS), rows, LANES), jnp.bfloat16),
        ]
        + [jax.ShapeDtypeStruct(array.shape, array.dtype) for array in later],
        compiler_params=pltpu.CompilerParams(vmem_limit_bytes=VMEM_LIMIT),
        cost_estimate=pl.CostEstimate(
            flops=arrived.shape[0] * 2**24, bytes_accessed=4 * arrived.size, transcendentals=0
        ),
        name="settle_late",
    )(tall, square, arrived, params, late_m1, late_m2, early_grad, *later, *after)


def gather_inner(piece, groups):
    pieces = [piece]
    bit = groups // 2
    while bit:
        pairs = [(i, i ^ bit) for i in range(groups)]
        pieces = pieces + [lax.ppermute(piece, GROUP, pairs) for piece in pieces]
        bit //= 2
    return pieces


def placing_order(device, unit):
    size = unit * device.shape[0]
    to_row = lax.broadcasted_iota(jnp.int32, (size, size), 0)
    from_row = jnp.arange(size, dtype=jnp.int32)
    source = (from_row % unit) * device.shape[0] + jnp.repeat(device, unit)
    return (to_row == source[None, :]).astype(jnp.bfloat16)


def piece_devices(groups, devices):
    member = lax.axis_index(GROUP)
    piece = jnp.arange(groups, dtype=jnp.int32)
    mask = jnp.zeros_like(piece)
    bit = 1
    while bit < groups:
        mask = mask * 2 + (piece // bit) % 2
        bit *= 2
    outer = jnp.arange(devices // groups, dtype=jnp.int32)
    return (outer[None, :] * groups + (member ^ mask)[:, None]).reshape(-1)


def hand_on(after, *arrays):
    anywhere = pl.BlockSpec(memory_space=pl.ANY)
    return pl.pallas_call(
        lambda *refs: None,
        in_specs=[anywhere] * (len(after) + len(arrays)),
        out_specs=[anywhere] * len(arrays),
        out_shape=[jax.ShapeDtypeStruct(array.shape, array.dtype) for array in arrays],
        input_output_aliases={len(after) + index: index for index in range(len(arrays))},
        name="hand_on",
    )(*after, *arrays)


def assemble_kernel(counts, devices, chunks, first, order_ref, *refs):
    piece_refs = []
    for count in counts:
        piece_refs.append(refs[:count])
        refs = refs[count:]
    out_any, placed_ref, sems = refs[-3:]

    def held_rows(part_refs, start, stop):
        before = 0
        for ref in part_refs:
            if start < before + ref.shape[1]:
                return ref[:, start - before : stop - before, :]
            before += ref.shape[1]

    unit = order_ref.shape[0] // devices
    copies = []
    for index, (begin, end) in enumerate(chunks):
        for start in range(begin, end, 2 * unit):
            sides = []
            for side in (start, start + unit):
                held = jnp.concatenate(
                    [held_rows(part_refs, side, side + unit) for part_refs in piece_refs], axis=0
                )
                sides.append(held.reshape(unit * devices, LANES))
            placed = dot(order_ref[...], jnp.concatenate(sides, axis=1)).astype(jnp.bfloat16)
            for half, side in enumerate((start, start + unit)):
                placed_ref[side * devices : (side + unit) * devices, :] = placed[
                    :, half * LANES : (half + 1) * LANES
                ]
        here = slice(begin * devices, end * devices)
        there = slice((first + begin) * devices, (first + end) * devices)
        copies.append(
            pltpu.make_async_copy(placed_ref.at[here, :], out_any.at[there, :], sems.at[index])
        )
        copies[-1].start()
    for copy in copies:
        copy.wait()


def assemble(order, pieces, total_rows, first, before, after):
    devices = len(pieces) * pieces[0][0].shape[0]
    rows = pieces[0][0].shape[1]
    parts = [part for piece in pieces for part in piece]
    step = 32 * max(1, rows // 128)
    chunks = [(begin, min(begin + step, rows)) for begin in range(0, rows, step)]
    vmem, anywhere = pl.BlockSpec(memory_space=pltpu.VMEM), pl.BlockSpec(memory_space=pl.ANY)
    in_specs = [vmem] * (1 + len(parts)) + [anywhere] * len(after)
    operands = [order, *parts, *after]
    aliases = {}
    if before is not None:
        aliases = {len(operands): 0}
        in_specs.append(anywhere)
        operands.append(before)
    return pl.pallas_call(
        functools.partial(assemble_kernel, [len(piece) for piece in pieces], devices, chunks, first),
        in_specs=in_specs,
        out_specs=anywhere,
        out_shape=jax.ShapeDtypeStruct((total_rows, LANES), jnp.bfloat16),
        scratch_shapes=[
            pltpu.VMEM((rows * devices, LANES), jnp.bfloat16),
            pltpu.SemaphoreType.DMA((len(chunks),)),
        ],
        input_output_aliases=aliases,
        compiler_params=pltpu.CompilerParams(vmem_limit_bytes=VMEM_LIMIT),
        cost_estimate=pl.CostEstimate(
            flops=rows * devices * 2**17, bytes_accessed=rows * devices * 512, transcendentals=0
        ),
        name="assemble",
    )(*operands)


def rope_frequency(head_width):
    index = np.arange(LANES) % (head_width // 2)
    return (ROPE_BASE ** (-2.0 * index / head_width)).astype(np.float32)[None, :]


def gain_rows(attn_gain, ffn_gain, q_gain, k_gain):
    repeats = attn_gain.shape[0] // q_gain.shape[0]
    return jnp.concatenate(
        [attn_gain, ffn_gain] + [q_gain] * repeats + [k_gain] * repeats
    ).astype(jnp.float32).reshape(4, -1)


def select_kernel(features, hidden, devices, turn_ref, me_ref, flat_any, *refs):
    m1_ref, m2_ref = refs[:2]
    out_refs, flat_ref, sems = refs[3:-2], refs[-2], refs[-1]
    size = flat_ref.shape[0] // sems.shape[0]
    copies = [
        pltpu.make_async_copy(
            flat_any.at[pl.ds(chunk * size, size), :],
            flat_ref.at[pl.ds(chunk * size, size), :],
            sems.at[chunk],
        )
        for chunk in range(sems.shape[0])
    ]
    for copy in copies:
        copy.start()
    a_qkv_ref, a_guo_ref, a_down_ref, b_qkv_ref, b_gu_ref, b_do_ref = out_refs[:6]
    if devices:
        own_ref, moments_ref, wide_ref = out_refs[6:]
        count = m1_ref.shape[0] // devices
        for device in range(devices):
            rows = []
            for ref in (m1_ref, m2_ref):
                rows.append(ref[pl.ds(device, count, stride=devices), :])
                rows.append(jnp.zeros((MOMENT_ROWS - count, LANES), jnp.float32))
            moments_ref[device] = jnp.concatenate(rows, axis=0).astype(jnp.bfloat16)
        each = size // devices
        for chunk, copy in enumerate(copies):
            copy.wait()
            wide_ref[...] = flat_ref[chunk * size : (chunk + 1) * size, :].astype(jnp.float32)
            own_ref[chunk * each : (chunk + 1) * each, :] = wide_ref[
                pl.ds(me_ref[0], each, stride=devices), :
            ].astype(jnp.bfloat16)
    if not devices:
        for copy in copies:
            copy.wait()
    few = 2 * RANK
    rows = lax.broadcasted_iota(jnp.int32, (LANES, LANES), 0)
    columns = lax.broadcasted_iota(jnp.int32, (LANES, LANES), 1)
    chosen = jnp.where((columns // RANK) % 2 == 1, turn_ref[1], turn_ref[0])
    fits = (rows // RANK == chosen) & (rows % RANK == columns % RANK)
    start = {}
    row = 0
    for name, rows_in, rows_out in (
        ("q", features, features),
        ("k", features, features),
        ("v", features, features),
        ("o", features, features),
        ("g", features, hidden),
        ("u", features, hidden),
        ("d", hidden, features),
    ):
        start[name] = (row, row + rows_in)
        row += rows_in + rows_out

    def wide(names, length):
        total = jnp.zeros((length, LANES), jnp.float32)
        for place, name in enumerate(names):
            first = start[name][0]
            total = total + jnp.dot(
                flat_ref[first : first + length, :],
                one_hot(fits & (columns // few == place)),
                preferred_element_type=jnp.float32,
            )
        return total.astype(jnp.bfloat16)

    a_qkv_ref[...] = wide("qkv", features)
    a_guo_ref[...] = wide("guo", features)
    for first in range(0, hidden, features):
        a_down_ref[first : first + features, :] = jnp.dot(
            flat_ref[start["d"][0] + first : start["d"][0] + first + features, :],
            one_hot(fits & (columns // few == 0)),
            preferred_element_type=jnp.float32,
        ).astype(jnp.bfloat16)

    def tall(name, length, out_ref, place):
        chunks = length // LANES
        size = RANK * chunks
        to_row = lax.broadcasted_iota(jnp.int32, (size, size), 0)
        from_row = lax.broadcasted_iota(jnp.int32, (size, size), 1)
        turned = one_hot(
            (to_row // RANK == from_row % chunks) & (to_row % RANK == from_row // chunks)
        )
        for turn in range(2):
            first = start[name][1] + pl.multiple_of(turn_ref[turn] * size, LANES)
            block = jnp.dot(
                turned, flat_ref[pl.ds(first, size), :], preferred_element_type=jnp.float32
            ).astype(jnp.bfloat16)
            here = place * few + turn * RANK
            for chunk in range(chunks):
                out_ref[here : here + RANK, chunk * LANES : (chunk + 1) * LANES] = block[
                    chunk * RANK : (chunk + 1) * RANK
                ]

    for out_ref, names in ((b_qkv_ref, "qkv"), (b_gu_ref, "gu"), (b_do_ref, "d.o")):
        out_ref[...] = jnp.zeros(out_ref.shape, out_ref.dtype)
        for place, name in enumerate(names):
            if name != ".":
                tall(name, out_ref.shape[1], out_ref, place)


def select(devices, turn_adapter, me, adapters, moments, features, hidden, after):
    shapes = [(features, LANES), (features, LANES), (hidden, LANES)]
    shapes += [(LANES, features), (LANES, hidden), (LANES, features)]
    scratch = []
    if devices:
        shapes.append((adapters.shape[0] // (LANES * devices), LANES))
        shapes.append((devices, 2 * MOMENT_ROWS, LANES))
        scratch.append(pltpu.VMEM((1024, LANES), jnp.float32))
    rows = adapters.shape[0] // LANES
    scratch += [pltpu.VMEM((rows, LANES), jnp.bfloat16), pltpu.SemaphoreType.DMA((rows // 1024,))]
    return pl.pallas_call(
        functools.partial(select_kernel, features, hidden, devices),
        in_specs=[
            pl.BlockSpec(memory_space=pltpu.SMEM),
            pl.BlockSpec(memory_space=pltpu.SMEM),
            pl.BlockSpec(memory_space=pl.ANY),
            pl.BlockSpec(memory_space=pltpu.VMEM),
            pl.BlockSpec(memory_space=pltpu.VMEM),
            pl.BlockSpec(memory_space=pl.ANY),
        ],
        out_specs=[pl.BlockSpec(memory_space=pltpu.VMEM)] * len(shapes),
        out_shape=[jax.ShapeDtypeStruct(shape, jnp.bfloat16) for shape in shapes],
        scratch_shapes=scratch,
        compiler_params=pltpu.CompilerParams(vmem_limit_bytes=VMEM_LIMIT),
        cost_estimate=pl.CostEstimate(
            flops=2**31, bytes_accessed=4 * adapters.shape[0], transcendentals=0
        ),
        name="select",
    )(turn_adapter, me, adapters.reshape(-1, LANES), *moments, after)


def dot(left, right):
    return jnp.dot(left, right, preferred_element_type=jnp.float32)


def beside(*arrays):
    return jnp.concatenate(arrays, axis=1)


def above(*arrays):
    return jnp.concatenate(arrays, axis=0)


def turn_mask(meta_ref):
    rows = meta_ref.shape[0]
    lane = lax.broadcasted_iota(jnp.int32, (rows, LANES), 1)
    mask = jnp.where((lane // RANK) % 2 == meta_ref[:, 2:3], 1.0, 0.0)
    return mask, lane // (2 * RANK)


def row_norm(values):
    return lax.rsqrt(jnp.mean(values * values, axis=1, keepdims=True) + NORM_EPS)


def row_norm_back(values, gain, grad):
    scale = row_norm(values)
    unit = values * scale
    grad = grad * gain
    return scale * (grad - unit * jnp.mean(grad * unit, axis=1, keepdims=True))


def head_mean(values, width):
    lanes = values.shape[1]
    rows = lax.broadcasted_iota(jnp.int32, (lanes, lanes), 0)
    columns = lax.broadcasted_iota(jnp.int32, (lanes, lanes), 1)
    ones = one_hot(rows // width == columns // width)
    return dot(values.astype(jnp.bfloat16), ones) * (1.0 / width)


def swap_halves(values, width):
    lanes = values.shape[1]
    lane = lax.broadcasted_iota(jnp.int32, values.shape, 1)
    ahead = pltpu.roll(values, lanes - width // 2, 1)
    behind = pltpu.roll(values, width // 2, 1)
    return jnp.where(lane % width < width // 2, ahead, behind)


def widen(table, lanes):
    return jnp.concatenate([table] * (lanes // table.shape[1]), axis=1)


def joined(kept_ref, arrived_ref):
    first = kept_ref.shape[0] - arrived_ref.shape[0]
    kept = kept_ref[...]
    return jnp.concatenate([kept[:first], kept[first:] + arrived_ref[...]], axis=0)


def turned_heads(raw, gain, cosine, sine, width):
    unit = raw * lax.rsqrt(head_mean(raw * raw, width) + NORM_EPS) * gain
    return (unit * cosine + swap_halves(unit, width) * sine).astype(jnp.bfloat16)


def project_own(normed, inner, place, index, weight_ref, b_ref):
    own = jnp.where(place == index, ADAPTER_SCALE * inner, 0.0).astype(jnp.bfloat16)
    return dot(beside(normed, own), above(weight_ref[...], b_ref[...]))


def project_heads_kernel(
    width,
    kept_ref,
    arrived_ref,
    gains_ref,
    wq_ref,
    wk_ref,
    wv_ref,
    a_ref,
    b_ref,
    meta_ref,
    cos_ref,
    sin_ref,
    _,
    x_ref,
    normed_ref,
    inner_ref,
    q_raw_ref,
    k_raw_ref,
    q_ref,
    k_ref,
    v_ref,
    __,
):
    mask, place = turn_mask(meta_ref)

    @pl.when(pl.program_id(0) == 0)
    def _():
        rows = joined(kept_ref, arrived_ref)
        x_ref[...] = rows
        values = rows.astype(jnp.float32)
        normed = (values * row_norm(values) * gains_ref[0:1, :]).astype(
            jnp.bfloat16
        )
        normed_ref[...] = normed
        inner_ref[...] = (dot(normed, a_ref[...]) * mask).astype(jnp.bfloat16)

    normed = normed_ref[...]
    inner = inner_ref[...].astype(jnp.float32)
    lanes = wk_ref.shape[1]
    cosine, sine = widen(cos_ref[...], lanes), widen(sin_ref[...], lanes)
    query = project_own(normed, inner, place, 0, wq_ref, b_ref)
    q_raw_ref[...] = query.astype(jnp.bfloat16)
    q_ref[...] = turned_heads(query, gains_ref[2:3, :lanes], cosine, sine, width)
    key = project_own(normed, inner, place, 1, wk_ref, b_ref)
    k_raw_ref[...] = key.astype(jnp.bfloat16)
    k_ref[...] = turned_heads(key, gains_ref[3:4, :lanes], cosine, sine, width)
    v_ref[...] = project_own(normed, inner, place, 2, wv_ref, b_ref).astype(jnp.bfloat16)


def project_heads(
    kept,
    arrived,
    later,
    gains,
    weights,
    a_qkv,
    b_qkv,
    meta,
    cos_table,
    sin_table,
    width,
):
    rows, features = kept.shape
    tile = 512
    grid = (features // tile,)

    def tiled(height):
        return pl.BlockSpec((height, tile), lambda step: (0, step))

    def shape(dtype):
        return jax.ShapeDtypeStruct((rows, features), dtype)

    full, few = whole_block((rows, features)), whole_block((rows, LANES))
    low = shape(jnp.bfloat16)
    anywhere = pl.BlockSpec(memory_space=pl.ANY)
    results = pl.pallas_call(
        functools.partial(project_heads_kernel, width),
        grid=grid,
        in_specs=[full, whole_block(arrived.shape), whole_block(gains.shape)]
        + [tiled(features)] * 3
        + [whole_block((features, LANES)), tiled(LANES), few, few, few]
        + [anywhere],
        out_specs=[full, full, few] + [tiled(rows)] * 5 + [anywhere],
        input_output_aliases={11: 8},
        out_shape=[
            low,
            low,
            jax.ShapeDtypeStruct((rows, LANES), jnp.bfloat16),
            low,
            low,
            low,
            low,
            low,
            jax.ShapeDtypeStruct(later.shape, later.dtype),
        ],
        compiler_params=pltpu.CompilerParams(vmem_limit_bytes=VMEM_LIMIT),
        cost_estimate=pl.CostEstimate(
            flops=9 * rows * features * features,
            bytes_accessed=4 * features * features + 14 * rows * features,
            transcendentals=0,
        ),
        name="project_heads",
    )(
        kept,
        arrived,
        gains,
        *weights,
        a_qkv,
        b_qkv,
        meta,
        cos_table,
        sin_table,
        later,
    )
    return results


def project_heads_back_kernel(
    count,
    width,
    devices,
    gq_ref,
    *refs,
):
    gk_refs, gv_refs, refs = refs[:count], refs[count : 2 * count], refs[2 * count :]
    (
        q_raw_ref,
        k_raw_ref,
        normed_any,
        inner_ref,
        x_any,
        residual_any,
        gains_ref,
        wq_ref,
        wk_ref,
        wv_ref,
        a_ref,
        b_ref,
        meta_ref,
        cos_ref,
        sin_ref,
    ) = refs[:15]
    if devices:
        out_ref, tail_ref, spread_ref = refs[-9:-6]
    else:
        out_ref, tail_ref, grad_a_ref, grad_b_ref = refs[-10:-6]
    total_ref, few_ref, tall_ref, square_ref, held_ref, sems = refs[-6:]
    step = pl.program_id(0)
    lanes = wq_ref.shape[1]
    mask, place = turn_mask(meta_ref)
    cosine, sine = widen(cos_ref[...], lanes), widen(sin_ref[...], lanes)

    def turned_back(grad, raw, head_gain):
        raw = raw.astype(jnp.float32)
        grad = grad * cosine - swap_halves(grad, width) * sine
        scale = lax.rsqrt(head_mean(raw * raw, width) + NORM_EPS)
        unit = raw * scale
        grad = grad * head_gain
        return (scale * (grad - unit * head_mean(grad * unit, width))).astype(jnp.bfloat16)

    def summed(term_refs):
        total = term_refs[0][...].astype(jnp.float32)
        for ref in term_refs[1:]:
            total = total + ref[...].astype(jnp.float32)
        return total

    copies = [
        pltpu.make_async_copy(source, held_ref.at[index], sems.at[index])
        for index, source in enumerate((normed_any, x_any, residual_any))
    ]

    @pl.when(step == 0)
    def _():
        for copy in copies:
            copy.start()
        total_ref[...] = jnp.zeros(total_ref.shape, jnp.float32)
        few_ref[...] = jnp.zeros(few_ref.shape, jnp.float32)

    inner_turned = jnp.transpose(inner_ref[...].astype(jnp.float32) * ADAPTER_SCALE).astype(
        jnp.bfloat16
    )
    errors = [
        turned_back(gq_ref[...].astype(jnp.float32), q_raw_ref[...], gains_ref[2:3, :lanes]),
        turned_back(summed(gk_refs), k_raw_ref[...], gains_ref[3:4, :lanes]),
        summed(gv_refs).astype(jnp.bfloat16),
    ]
    total_ref[...] += contract_last(
        beside(*errors), beside(wq_ref[...], wk_ref[...], wv_ref[...])
    )
    few = few_ref[...]
    wide = 2 * RANK
    for index, error in enumerate(errors):
        few = few + jnp.where(place == index, contract_last(error, b_ref[...]), 0.0)
        here = slice(index * wide, (index + 1) * wide)
        grad_b = dot(inner_turned[here], error)
        for part in range(lanes // LANES):
            square_ref[part, here, :] = grad_b[:, part * LANES : (part + 1) * LANES]
    square_ref[:, 3 * wide :, :] = jnp.zeros(
        (lanes // LANES, LANES - 3 * wide, LANES), jnp.float32
    )
    if devices:
        chunks = held_ref.shape[2] // LANES
        for index in range(lanes // LANES):
            for first, starts in ((wide, (0, wide)), (wide + RANK, (2 * wide, 3 * wide))):
                spread_square_to(
                    spread_ref,
                    first,
                    square_ref,
                    starts,
                    step * (lanes // LANES) + index,
                    chunks,
                    index,
                )
    else:
        for part in range(lanes // LANES):
            grad_b_ref[:, part * LANES : (part + 1) * LANES] = square_ref[part].astype(
                jnp.bfloat16
            )
    few_ref[...] = few

    @pl.when(step == pl.num_programs(0) - 1)
    def _():
        low = (ADAPTER_SCALE * few_ref[...] * mask).astype(jnp.bfloat16)
        low_turned = jnp.transpose(low.astype(jnp.float32)).astype(jnp.bfloat16)
        for copy in copies:
            copy.wait()
        tall_ref[...] = jnp.transpose(dot(low_turned, held_ref[0]))
        if devices:
            spread_wide_to(spread_ref, 0, tall_ref)
        else:
            grad_a_ref[...] = tall_ref[...].astype(jnp.bfloat16)
        grad = total_ref[...] + contract_last(low, a_ref[...])
        out = held_ref[2].astype(jnp.float32) + row_norm_back(
            held_ref[1].astype(jnp.float32), gains_ref[0:1, :], grad
        )
        out_ref[...] = out.astype(jnp.bfloat16)
        tail_ref[...] = out[out.shape[0] - tail_ref.shape[0] :].astype(jnp.bfloat16)


def project_heads_back(
    devices,
    after,
    grad_query,
    key_terms,
    value_terms,
    query_raw,
    key_raw,
    normed,
    inner,
    rows_in,
    grad_residual,
    gains,
    weights,
    a_qkv,
    b_qkv,
    meta,
    cos_table,
    sin_table,
    width,
):
    rows, features = rows_in.shape
    count = len(key_terms)
    tile = 256

    def tiled(height):
        return pl.BlockSpec((height, tile), lambda step: (0, step))

    full = whole_block((rows, features))
    anywhere = pl.BlockSpec(memory_space=pl.ANY)
    if devices:
        spread = (devices, 4 * RANK, LANES)
        grad_specs = [whole_block(spread)]
        grad_shapes = [jax.ShapeDtypeStruct(spread, jnp.bfloat16)]
    else:
        grad_specs = [whole_block((features, LANES)), tiled(LANES)]
        grad_shapes = [
            jax.ShapeDtypeStruct((features, LANES), jnp.bfloat16),
            jax.ShapeDtypeStruct((LANES, features), jnp.bfloat16),
        ]
    return pl.pallas_call(
        functools.partial(project_heads_back_kernel, count, width, devices),
        grid=(features // tile,),
        in_specs=[tiled(rows)] * (3 + 2 * count)
        + [anywhere, whole_block((rows, LANES)), anywhere, anywhere, whole_block(gains.shape)]
        + [tiled(features)] * 3
        + [whole_block((features, LANES)), tiled(LANES), whole_block(meta.shape)]
        + [whole_block((rows, LANES))] * 2
        + [anywhere] * len(after),
        out_specs=[full, whole_block((rows // 2, features)), *grad_specs],
        out_shape=[
            jax.ShapeDtypeStruct((rows, features), jnp.bfloat16),
            jax.ShapeDtypeStruct((rows // 2, features), jnp.bfloat16),
            *grad_shapes,
        ],
        scratch_shapes=[
            pltpu.VMEM((rows, features), jnp.float32),
            pltpu.VMEM((rows, LANES), jnp.float32),
            pltpu.VMEM((features, LANES), jnp.float32),
            pltpu.VMEM((tile // LANES, LANES, LANES), jnp.float32),
            pltpu.VMEM((3, rows, features), jnp.bfloat16),
            pltpu.SemaphoreType.DMA((3,)),
        ],
        compiler_params=pltpu.CompilerParams(vmem_limit_bytes=VMEM_LIMIT),
        cost_estimate=pl.CostEstimate(
            flops=8 * rows * features * features,
            bytes_accessed=6 * features * features + 30 * rows * features,
            transcendentals=0,
        ),
        name="project_heads_back",
    )(
        grad_query,
        *key_terms,
        *value_terms,
        query_raw,
        key_raw,
        normed,
        inner,
        rows_in,
        grad_residual,
        gains,
        *weights,
        a_qkv,
        b_qkv,
        meta,
        cos_table,
        sin_table,
        *after,
    )


def spread_wide_to(spread_ref, first, held_ref):
    devices = spread_ref.shape[0]
    count = held_ref.shape[0] // devices
    for device in range(devices):
        spread_ref[device, first : first + count, :] = held_ref[
            pl.ds(device, count, stride=devices), :
        ].astype(jnp.bfloat16)


def spread_square_to(spread_ref, first, held_ref, starts, chunk, chunks, index):
    classes = spread_ref.shape[0] // chunks
    count = 2 * RANK // classes
    for part in range(classes):
        rows = [
            held_ref[index, pl.ds(start + part, count, stride=classes), :]
            for start in starts
        ]
        spread_ref[part * chunks + chunk, first : first + 2 * count, :] = jnp.concatenate(
            rows, axis=0
        ).astype(jnp.bfloat16)


def feed_forward_kernel(
    devices,
    turn_ref,
    att_ref,
    x_any,
    kept_any,
    arrived_any,
    gains_ref,
    wo_ref,
    wg_any,
    wu_any,
    wd_any,
    a_guo_ref,
    a_down_ref,
    b_gu_ref,
    b_do_ref,
    meta_ref,
    out_any,
    tail_any,
    grad_res_any,
    grad_att_ref,
    *refs,
):
    if devices:
        spread_ref, refs = refs[0], refs[1:]
    else:
        (grad_a_ref, grad_ad_ref, grad_bgu_ref, grad_bdo_ref), refs = refs[:4], refs[4:]
    (
        res_ref,
        hidden_ref,
        inner_ref,
        inner_turned_ref,
        sum_ref,
        grad_hidden_ref,
        inner_down_ref,
        few_ref,
        few_down_ref,
        few_down_turned_ref,
        down_ref,
        tall_ref,
        square_ref,
        e_ref,
        x_ref,
        arrived_ref,
        wg_ref,
        wu_ref,
        wd_ref,
        out_ref,
        grad_res_ref,
        rows_sems,
        tile_sems,
        out_sems,
    ) = refs
    step = pl.program_id(0)
    steps = pl.num_programs(0)
    mask, place = turn_mask(meta_ref)
    tile = wg_ref.shape[2]
    swap_rows = arrived_ref.shape[0]
    row_copies = [
        pltpu.make_async_copy(source, target, rows_sems.at[index])
        for index, (source, target) in enumerate(
            ((x_any, x_ref), (kept_any, e_ref), (arrived_any, arrived_ref))
        )
    ]

    def tile_copies(number):
        slot = number % 2
        here = pl.ds(pl.multiple_of(number * tile, tile), tile)
        pairs = (
            (wg_any.at[:, here], wg_ref.at[slot]),
            (wu_any.at[:, here], wu_ref.at[slot]),
            (wd_any.at[here, :], wd_ref.at[slot]),
        )
        return [
            pltpu.make_async_copy(source, target, tile_sems.at[slot, index])
            for index, (source, target) in enumerate(pairs)
        ]

    features = wo_ref.shape[0]
    wide = 2 * RANK

    def only(values, index):
        return jnp.where(place == index, values, 0.0).astype(jnp.bfloat16)

    def turn(values):
        return jnp.transpose(values.astype(jnp.float32)).astype(jnp.bfloat16)

    @pl.when(step == 0)
    def _():
        for copy in row_copies:
            copy.start()
        for copy in tile_copies(0):
            copy.start()
        att = att_ref[...]
        inner_out = dot(att, a_guo_ref[...]) * mask
        attention_out = dot(
            beside(att, only(ADAPTER_SCALE * inner_out, 2)), above(wo_ref[...], b_do_ref[...])
        )
        row_copies[0].wait()
        res = x_ref[...].astype(jnp.float32) + attention_out
        res_ref[...] = res
        hidden = (res * row_norm(res) * gains_ref[1:2, :]).astype(jnp.bfloat16)
        hidden_ref[...] = hidden
        inner = dot(hidden, a_guo_ref[...]) * mask
        inner = jnp.where(place == 2, inner_out, inner).astype(jnp.bfloat16)
        inner_ref[...] = inner
        inner_turned_ref[...] = turn(inner.astype(jnp.float32) * ADAPTER_SCALE)
        for copy in row_copies[1:]:
            copy.wait()
        e_ref[e_ref.shape[0] - swap_rows :, :] += arrived_ref[...]
        few_down = only(ADAPTER_SCALE * contract_last(e_ref[...], b_do_ref[...]) * mask, 0)
        few_down_ref[...] = few_down
        few_down_turned_ref[...] = turn(few_down)[:wide]
        sum_ref[...] = jnp.zeros(sum_ref.shape, jnp.float32)
        grad_hidden_ref[...] = jnp.zeros(grad_hidden_ref.shape, jnp.float32)
        inner_down_ref[...] = jnp.zeros(inner_down_ref.shape, jnp.float32)
        few_ref[...] = jnp.zeros(few_ref.shape, jnp.float32)

    @pl.when(step + 1 < steps)
    def _():
        for copy in tile_copies(step + 1):
            copy.start()

    for copy in tile_copies(step):
        copy.wait()
    slot = step % 2
    hidden = hidden_ref[...]
    inner = ADAPTER_SCALE * inner_ref[...].astype(jnp.float32)
    gate_weight, up_weight, down_weight = wg_ref[slot], wu_ref[slot], wd_ref[slot]
    b_tile = b_gu_ref[...]
    gate = dot(beside(hidden, only(inner, 0)), above(gate_weight, b_tile))
    up = dot(beside(hidden, only(inner, 1)), above(up_weight, b_tile))
    grad_act = contract_last(
        beside(e_ref[...], few_down_ref[...]), beside(down_weight, a_down_ref[...])
    )
    sigmoid = 1.0 / (1.0 + jnp.exp(-gate))
    silu = gate * sigmoid
    act = (silu * up).astype(jnp.bfloat16)
    grad_up = (grad_act * silu).astype(jnp.bfloat16)
    grad_gate = (grad_act * up * (sigmoid * (1.0 + gate * (1.0 - sigmoid)))).astype(jnp.bfloat16)
    sum_ref[...] += dot(act, down_weight)
    inner_down_ref[...] += dot(act, a_down_ref[...])
    grad_hidden_ref[...] += contract_last(
        beside(grad_gate, grad_up), beside(gate_weight, up_weight)
    )
    few_ref[...] += jnp.where(
        place == 0, contract_last(grad_gate, b_tile), contract_last(grad_up, b_tile)
    )
    grad_b_gate = dot(inner_turned_ref[:wide, :], grad_gate).astype(jnp.bfloat16)
    grad_b_up = dot(inner_turned_ref[wide : 2 * wide, :], grad_up).astype(jnp.bfloat16)
    if devices:
        for index in range(tile // LANES):
            device = step * (tile // LANES) + index
            chunk = slice(index * LANES, (index + 1) * LANES)
            spread_ref[device, 2 * wide : 3 * wide, :] = grad_b_gate[:, chunk]
            spread_ref[device, 3 * wide : 4 * wide, :] = grad_b_up[:, chunk]
    else:
        grad_bgu_ref[:wide, :] = grad_b_gate
        grad_bgu_ref[wide:, :] = grad_b_up
    per_quarter = features // tile
    down_ref[
        pl.ds(pl.multiple_of((step // per_quarter) * wide, wide), wide),
        pl.ds(pl.multiple_of((step % per_quarter) * tile, tile), tile),
    ] = dot(few_down_turned_ref[...], act)

    out_copies = [
        pltpu.make_async_copy(source, target, out_sems.at[index])
        for index, (source, target) in enumerate(
            (
                (out_ref, out_any),
                (out_ref.at[out_ref.shape[0] - swap_rows :, :], tail_any),
                (grad_res_ref, grad_res_any),
            )
        )
    ]

    @pl.when(step == steps - 1)
    def _():
        grads_out = e_ref[...]
        inner_down = only(inner_down_ref[...] * mask, 0)
        res = res_ref[...]
        out_ref[...] = (
            res + sum_ref[...] + ADAPTER_SCALE * dot(inner_down, b_do_ref[...])
        ).astype(jnp.bfloat16)
        for copy in out_copies[:2]:
            copy.start()
        few = jnp.where(place < 2, ADAPTER_SCALE * few_ref[...] * mask, 0.0).astype(jnp.bfloat16)
        grad_hidden = grad_hidden_ref[...] + contract_last(few, a_guo_ref[...])
        grad_res = grads_out.astype(jnp.float32) + row_norm_back(
            res, gains_ref[1:2, :], grad_hidden
        )
        low = grad_res.astype(jnp.bfloat16)
        grad_res_ref[...] = low
        out_copies[2].start()
        few_out = only(ADAPTER_SCALE * contract_last(low, b_do_ref[...]) * mask, 2)
        grad_att_ref[...] = contract_last(
            beside(low, few_out), beside(wo_ref[...], a_guo_ref[...])
        ).astype(jnp.bfloat16)
        grad_a = dot(turn(few), hidden_ref[...]) + dot(turn(few_out), att_ref[...])
        inner_out = only(inner_ref[...].astype(jnp.float32), 2)
        grad_b = ADAPTER_SCALE * (
            dot(turn(inner_down), grads_out) + dot(turn(inner_out), low)
        )
        if devices:
            lane = lax.broadcasted_iota(jnp.int32, (features, LANES), 1)
            told = jnp.where(
                lane == 3 * wide, turn_ref[0], jnp.where(lane == 3 * wide + 1, turn_ref[1], 0)
            )
            tall_ref[...] = jnp.transpose(grad_a) + told.astype(jnp.float32)
            spread_wide_to(spread_ref, 0, tall_ref)
            tall_ref[...] = jnp.transpose(down_ref[...])
            spread_wide_to(spread_ref, wide, tall_ref)
            chunks = features // LANES
            for chunk in range(chunks):
                square_ref[chunk] = grad_b[:, chunk * LANES : (chunk + 1) * LANES]
                spread_square_to(
                    spread_ref, 4 * wide, square_ref, (0, 2 * wide), chunk, chunks, chunk
                )
        else:
            grad_a_ref[...] = jnp.transpose(grad_a).astype(jnp.bfloat16)
            grad_ad_ref[...] = jnp.transpose(down_ref[...]).astype(jnp.bfloat16)
            grad_bdo_ref[...] = grad_b.astype(jnp.bfloat16)
        for copy in out_copies:
            copy.wait()


def feed_forward(
    devices,
    turn_adapter,
    attended,
    rows_in,
    kept,
    arrived,
    gains,
    weights,
    selected,
    meta,
):
    rows, features = rows_in.shape
    hidden = weights[1].shape[1]
    tile = 1024
    full = whole_block((rows, features))
    square = whole_block((features, features))
    anywhere = pl.BlockSpec(memory_space=pl.ANY)

    def shape(height, length, dtype):
        return jax.ShapeDtypeStruct((height, length), dtype)

    if devices:
        spread = (devices, 9 * RANK, LANES)
        grad_specs = [whole_block(spread)]
        grad_shapes = [jax.ShapeDtypeStruct(spread, jnp.bfloat16)]
    else:
        grad_specs = [
            whole_block((features, LANES)),
            whole_block((features, LANES)),
            pl.BlockSpec((4 * RANK, tile), lambda step: (0, step)),
            whole_block((LANES, features)),
        ]
        grad_shapes = [
            shape(features, LANES, jnp.bfloat16),
            shape(features, LANES, jnp.bfloat16),
            shape(4 * RANK, hidden, jnp.bfloat16),
            shape(LANES, features, jnp.bfloat16),
        ]
    return pl.pallas_call(
        functools.partial(feed_forward_kernel, devices),
        grid=(hidden // tile,),
        in_specs=[
            pl.BlockSpec(memory_space=pltpu.SMEM),
            full,
            anywhere,
            anywhere,
            anywhere,
            whole_block(gains.shape),
            square,
            anywhere,
            anywhere,
            anywhere,
            whole_block((features, LANES)),
            pl.BlockSpec((tile, LANES), lambda step: (step, 0)),
            pl.BlockSpec((LANES, tile), lambda step: (0, step)),
            whole_block((LANES, features)),
            whole_block(meta.shape),
        ],
        out_specs=[anywhere, anywhere, anywhere, full, *grad_specs],
        out_shape=[
            shape(rows, features, jnp.bfloat16),
            shape(*arrived.shape, jnp.bfloat16),
            shape(rows, features, jnp.bfloat16),
            shape(rows, features, jnp.bfloat16),
            *grad_shapes,
        ],
        scratch_shapes=[
            pltpu.VMEM((rows, features), jnp.float32),
            pltpu.VMEM((rows, features), jnp.bfloat16),
            pltpu.VMEM((rows, LANES), jnp.bfloat16),
            pltpu.VMEM((LANES, rows), jnp.bfloat16),
            pltpu.VMEM((rows, features), jnp.float32),
            pltpu.VMEM((rows, features), jnp.float32),
            pltpu.VMEM((rows, LANES), jnp.float32),
            pltpu.VMEM((rows, LANES), jnp.float32),
            pltpu.VMEM((rows, LANES), jnp.bfloat16),
            pltpu.VMEM((2 * RANK, rows), jnp.bfloat16),
            pltpu.VMEM((LANES, features), jnp.float32),
            pltpu.VMEM((features, LANES), jnp.float32),
            pltpu.VMEM((features // LANES, LANES, LANES), jnp.float32),
            pltpu.VMEM((rows, features), jnp.bfloat16),
            pltpu.VMEM((rows, features), jnp.bfloat16),
            pltpu.VMEM(arrived.shape, jnp.bfloat16),
            pltpu.VMEM((2, features, tile), jnp.bfloat16),
            pltpu.VMEM((2, features, tile), jnp.bfloat16),
            pltpu.VMEM((2, tile, features), jnp.bfloat16),
            pltpu.VMEM((rows, features), jnp.bfloat16),
            pltpu.VMEM((rows, features), jnp.bfloat16),
            pltpu.SemaphoreType.DMA((3,)),
            pltpu.SemaphoreType.DMA((2, 3)),
            pltpu.SemaphoreType.DMA((3,)),
        ],
        compiler_params=pltpu.CompilerParams(vmem_limit_bytes=VMEM_LIMIT),
        cost_estimate=pl.CostEstimate(
            flops=14 * rows * features * hidden,
            bytes_accessed=8 * features * hidden + 16 * rows * features,
            transcendentals=0,
        ),
        name="feed_forward",
    )(
        turn_adapter,
        attended,
        rows_in,
        kept,
        arrived,
        gains,
        *weights,
        *selected,
        meta,
    )


def settle_owned(grads, moment1, moment2, devices):
    grads = lax.all_to_all(grads, ALL, 0, 0, tiled=True)
    grads = grads[:, : moment1.shape[0] // (LANES * devices)]
    grad_shard = jnp.transpose(grads, (1, 0, 2)).reshape(-1).astype(jnp.float32)
    current = jnp.zeros((), jnp.float32)
    first_moment, second_moment, _ = adam(current, moment1, moment2, grad_shard)
    return grad_shard, first_moment, second_moment


def per_device(
    tokens,
    cotangent,
    variate,
    seq_len,
    seq_adapter,
    block_order,
    attn_gain,
    ffn_gain,
    q_gain,
    k_gain,
    attn_bias,
    query_weight,
    key_weight,
    value_weight,
    output_weight,
    gate_weight,
    up_weight,
    down_weight,
    adapters,
    moment1,
    moment2,
):
    groups = axis_count(GROUP)
    member = lax.axis_index(GROUP)
    row_count, feature_width = tokens.shape
    hidden_width = gate_weight.shape[1]
    head_width = q_gain.shape[0]
    half_devices = groups // 2
    segments = seq_len.shape[1]
    chosen, back, turn_adapter, cos_table, sin_table, key_metas = plan(
        groups, row_count, head_width, member[None], seq_len, seq_adapter, block_order, variate
    )
    meta = key_metas[0]
    axes = ALL
    devices = axis_count(PACKS) * groups
    even = spreads_evenly(devices, groups, feature_width, hidden_width, adapters.shape[0])
    spread = devices if even else 0
    gains = gain_rows(attn_gain, ffn_gain, q_gain, k_gain)


    held = (gather_half(tokens, groups), gather_half(cotangent, groups))
    sent_tokens, sent_grads = pick(chosen, row_count, row_count // 2, *held)
    arrived_tokens = to_other_half(sent_tokens, groups)
    a_qkv, a_guo, a_down, b_qkv, b_gu, b_do, *spread_state = select(
        spread,
        turn_adapter,
        lax.axis_index(axes)[None],
        adapters,
        (moment1.reshape(-1, LANES), moment2.reshape(-1, LANES)),
        feature_width,
        hidden_width,
        sent_tokens,
    )
    if even:
        params, moments = spread_state
        moments = lax.all_to_all(moments, axes, 0, 0, tiled=True)
    kept_tokens, kept_grads = pick(chosen, 0, row_count, *held)
    (
        my_tokens,
        normed,
        inner,
        query_raw,
        key_raw,
        query_low,
        key_low,
        value_low,
        sent_grads,
    ) = project_heads(
        kept_tokens,
        arrived_tokens,
        sent_grads,
        gains,
        (query_weight, key_weight, value_weight),
        a_qkv,
        b_qkv,
        meta,
        cos_table,
        sin_table,
        head_width,
    )
    arrived_grads = to_other_half(sent_grads, groups)
    keys = gather_half(key_low, groups)
    values = gather_half(value_low, groups)
    attended_low, log_total = attend(
        attn_bias, query_low, meta, keys, values, key_metas, segments, head_width
    )
    layer_rows, layer_tail, grad_residual, grad_attended, *forward_grads = feed_forward(
        spread,
        turn_adapter,
        attended_low,
        my_tokens,
        kept_grads,
        arrived_grads,
        gains,
        (output_weight, gate_weight, up_weight, down_weight),
        (a_guo, a_down, b_gu, b_do),
        meta,
    )
    layer_back = to_other_half(layer_tail, groups)

    results = attend_back(
        attn_bias,
        query_low,
        meta,
        log_total,
        attended_low,
        grad_attended,
        keys,
        values,
        key_metas,
        segments,
        head_width,
    )
    after = []
    if even:
        total_rows = adapters.shape[0] // LANES
        late_rows = 6 * feature_width // devices
        early = lax.all_to_all(forward_grads[0], axes, 0, 0, tiled=True)
    grad_query = results[0]
    grad_keys = results[1 : 1 + half_devices]
    grad_values = results[1 + half_devices :]
    key_terms, value_terms = [grad_keys[0]], [grad_values[0]]
    for shift in range(1, half_devices):
        back_shift = half_devices - shift
        key_terms.append(within_half(grad_keys[shift], back_shift, groups))
        value_terms.append(within_half(grad_values[shift], back_shift, groups))
    grad_rows, grad_tail, *back_grads = project_heads_back(
        spread,
        after,
        grad_query,
        key_terms,
        value_terms,
        query_raw,
        key_raw,
        normed,
        inner,
        my_tokens,
        grad_residual,
        gains,
        (query_weight, key_weight, value_weight),
        a_qkv,
        b_qkv,
        meta,
        cos_table,
        sin_table,
        head_width,
    )
    def bring_back(tail):
        return gather_half(grad_rows, groups) + gather_half(to_other_half(tail, groups), groups)

    if not even:
        grads = (*back_grads, *forward_grads)
        column = jnp.arange(2 * RANK, dtype=jnp.int32)
        few_choice = one_hot(
            jnp.arange(LANES, dtype=jnp.int32)[:, None]
            == (jnp.repeat(turn_adapter, RANK) * RANK + column % RANK)[None, :]
        )
        settled = settle_shards(grads, few_choice, adapters, moment1, moment2, groups)
        layer_held = gather_half(layer_rows, groups) + gather_half(layer_back, groups)
        layer_out = pick(back, 0, row_count, layer_held)[0]
        input_grad = pick(back, 0, row_count, bring_back(grad_tail))[0]
        return (layer_out, input_grad) + settled
    late = lax.all_to_all(back_grads[0], axes, 0, 0, tiled=True)
    early_grad, early_new, late_m1, late_m2, tall, square = settle_early(
        early, moments, params, late_rows, [grad_rows]
    )
    swap = [(0, 1), (1, 0)]
    far_count = lax.axis_size("far")
    bit = 1
    early_outer = early_new
    while bit < far_count:
        pairs = [(i, i ^ bit) for i in range(far_count)]
        early_outer = jnp.concatenate([early_outer, lax.ppermute(early_outer, "far", pairs)])
        bit *= 2
    early_near = lax.ppermute(early_outer, "near", swap)
    early_half = lax.ppermute(early_outer, "half", swap)
    early_far = lax.ppermute(early_half, "near", swap)
    own_grads, late_new, grad_tail, layer_back = settle_late(
        tall, square, late, params, late_m1, late_m2, early_grad, [grad_tail, layer_back], []
    )
    layer_held = gather_half(layer_rows, groups) + gather_half(layer_back, groups)
    layer_out = pick(back, 0, row_count, layer_held)[0]
    late_outer = lax.all_to_all(late_new, PACKS, 0, 0, tiled=True)
    late_pieces = gather_inner(late_outer, groups)
    own_grads = hand_on([late_outer, layer_out], own_grads)[0]
    input_grad = pick(back, 0, row_count, bring_back(grad_tail))[0]
    early_pieces = [[early_outer], [early_near], [early_half], [early_far]]
    early_pieces += [
        [lax.ppermute(part, "core", swap) for part in piece] for piece in early_pieces
    ]
    far = lax.axis_index("far") ^ jnp.arange(far_count, dtype=jnp.int32)
    near, half, core = [lax.axis_index(name) for name in ALL[1:]]
    early_device = jnp.concatenate(
        [
            ((far * 2 + (near ^ flip_near)) * 2 + (half ^ flip_half)) * 2 + (core ^ flip_core)
            for flip_core in (0, 1)
            for flip_near, flip_half in ((0, 0), (1, 0), (0, 1), (1, 1))
        ]
    )
    late_pieces = [[piece] for piece in late_pieces]
    order = placing_order(piece_devices(groups, devices), 16)
    adapters_new = assemble(order, late_pieces, total_rows, 0, None, [input_grad])
    adapters_new = assemble(
        placing_order(early_device, 16), early_pieces, total_rows, late_rows, adapters_new, []
    )
    owned = settle_owned(own_grads, moment1, moment2, devices)
    return (layer_out, input_grad, *owned, adapters_new.reshape(-1))


def solution(mesh):
    packs, groups = mesh.shape["dp"], mesh.shape["group"]
    cut = jax.sharding.Mesh(mesh.devices.reshape(packs // 2, 2, groups // 2, 2), ALL)
    in_specs = (
        P(ALL, None),
        P(ALL, None),
        P(PACKS),
        P(PACKS, None),
        P(PACKS, None),
        P(PACKS, None),
        P(),
        P(),
        P(),
        P(),
        P(),
        P(),
        P(),
        P(),
        P(),
        P(),
        P(),
        P(),
        P(),
        P(ALL),
        P(ALL),
    )
    out_specs = (
        P(ALL, None),
        P(ALL, None),
        P(ALL),
        P(ALL),
        P(ALL),
        P(),
    )
    return jax.shard_map(
        per_device, mesh=cut, in_specs=in_specs, out_specs=out_specs, check_vma=False
    )
```

```python
import functools

import jax
import jax.numpy as jnp
import numpy as np
from jax import lax
from jax.experimental import pallas as pl
from jax.experimental.pallas import tpu as pltpu
from jax.sharding import PartitionSpec as P

RANK = 16
ADAPTERS = 8
NORM_EPS = 1e-06
ADAPTER_SCALE = 2.0
ROPE_BASE = 10000.0
MASKED = -1e30
LEARN_RATE = 0.01
BETA_ONE = 0.9
BETA_TWO = 0.999
ADAM_EPS = 1e-08
WEIGHT_DECAY = 0.01
update_count = 10.0
VARIATES = 4
VMEM_LIMIT = 63 * 1024 * 1024
EXACT_PARTS = 3
PAIRS = 2


def contract_last(left, right):
    return lax.dot_general(
        left, right, (((1,), (1,)), ((), ())), preferred_element_type=jnp.float32
    )


def exact_parts(values):
    parts = []
    for _ in range(EXACT_PARTS):
        part = values.astype(jnp.bfloat16).astype(jnp.float32)
        parts.append(part)
        values = values - part
    return parts


def parts_in_lanes(values, first, column):
    result = jnp.zeros(values.shape, jnp.float32)
    for index, part in enumerate(exact_parts(values)):
        result = jnp.where(column == first + index, part, result)
    return result


def note_keys(side_ref, kmeta_refs, column, lane, width, segments):
    seg_column = column - EXACT_PARTS * VARIATES
    ones = (seg_column >= segments) & (seg_column < segments + EXACT_PARTS)
    for block, kmeta_ref in enumerate(kmeta_refs):
        one = (column < EXACT_PARTS * VARIATES) & ((column % VARIATES) == kmeta_ref[:, 0:1])
        in_seg = (seg_column >= 0) & (seg_column < segments) & (seg_column == kmeta_ref[:, 1:2])
        for head in range(2):
            outside = (lane // width) != head
            side_ref[head, block] = one_hot((one | in_seg | ones) & outside)


def note_queries(match_ref, apart_ref, qmeta_ref, column, segments):
    same = (column < EXACT_PARTS * VARIATES) & ((column % VARIATES) == qmeta_ref[:, 0:1])
    match_ref[...] = jnp.where(same, 1.0, 0.0)
    seg_column = column - EXACT_PARTS * VARIATES
    apart = (seg_column >= 0) & (seg_column < segments) & (seg_column != qmeta_ref[:, 1:2])
    apart_ref[...] = jnp.where(apart, MASKED, 0.0)


def bias_rows(bias_ref, head, column):
    rows = []
    for which in range(2):
        row = jnp.zeros(column.shape, jnp.float32)
        value = jnp.full(column.shape, bias_ref[which, head], jnp.float32)
        for index, part in enumerate(exact_parts(value)):
            row = jnp.where(column // VARIATES == index, part, row)
        rows.append(row)
    return rows


def query_side(match_ref, apart_ref, bias_ref, head, column):
    same, other = bias_rows(bias_ref, head, column[:1])
    return jnp.where(match_ref[...] > 0.0, same, other) + apart_ref[...]


def head_lanes(head, width, lanes):
    lane = lax.broadcasted_iota(jnp.int32, (1, lanes), 1)
    return jnp.where(lane // width == head, 1.0, 0.0).astype(jnp.bfloat16)


def attend_kernel(key_blocks, segments, width, bias_ref, query_ref, qmeta_ref, *refs):
    key_refs, value_refs, kmeta_refs = (
        refs[:key_blocks],
        refs[key_blocks : 2 * key_blocks],
        refs[2 * key_blocks : 3 * key_blocks],
    )
    out_ref, total_ref, side_ref, match_ref, apart_ref = refs[3 * key_blocks :]
    step = pl.program_id(0)
    rows = query_ref.shape[0]
    lanes = 2 * width
    pairs = query_ref.shape[1] // lanes
    lane = lax.broadcasted_iota(jnp.int32, (rows, lanes), 1)
    column = lane % width

    @pl.when(step == 0)
    def _():
        note_keys(side_ref, kmeta_refs, column, lane, width, segments)
        note_queries(match_ref, apart_ref, qmeta_ref, column, segments)

    first = (lane // width) == 0
    heads = [(pair, head) for pair in range(pairs) for head in range(2)]
    scores = []
    for pair, head in heads:
        here = slice(pair * lanes, (pair + 1) * lanes)
        scaled = query_ref[:, here].astype(jnp.float32) * width ** (-0.5)
        extension = query_side(
            match_ref, apart_ref, bias_ref, (step * pairs + pair) * 2 + head, column
        )
        left = jnp.where((lane // width) == head, scaled, extension).astype(jnp.bfloat16)
        inside = head_lanes(head, width, lanes)
        for block in range(key_blocks):
            right = key_refs[block][:, here] * inside + side_ref[head, block]
            scores.append(contract_last(left, right))
    results = []
    for index, (pair, head) in enumerate(heads):
        here = slice(pair * lanes, (pair + 1) * lanes)
        inside = head_lanes(head, width, lanes)
        outside = head_lanes(1 - head, width, lanes)
        weights = [
            jnp.exp(score).astype(jnp.bfloat16)
            for score in scores[index * key_blocks : (index + 1) * key_blocks]
        ]
        values = [ref[:, here] * inside + outside for ref in value_refs]
        results.append(dot(beside(*weights), above(*values)))
        if head == 1:
            numerator = jnp.where(first, results[-2], results[-1])
            crossed = jnp.where(first, results[-1], results[-2])
            out_ref[:, here] = (numerator / pltpu.roll(crossed, width, 1)).astype(jnp.bfloat16)
            total_ref[:, here] = jnp.log(crossed)


def lane_block(rows, lanes):
    return pl.BlockSpec((rows, lanes), lambda pair: (0, pair))


def whole_block(shape):
    return pl.BlockSpec(shape, lambda pair: (0,) * len(shape))


def attend(attn_bias, query_low, query_meta, keys, values, key_metas, segments, width):
    rows, features = query_low.shape
    lanes = 2 * width
    wide = PAIRS * lanes
    count = len(keys)
    flops = 4 * rows * rows * count * features
    return pl.pallas_call(
        functools.partial(attend_kernel, count, segments, width),
        grid=(features // wide,),
        in_specs=[
            pl.BlockSpec(memory_space=pltpu.SMEM),
            lane_block(rows, wide),
            whole_block(query_meta.shape),
        ]
        + [lane_block(rows, wide)] * (2 * count)
        + [whole_block(query_meta.shape)] * count,
        out_specs=[lane_block(rows, wide)] * 2,
        out_shape=[
            jax.ShapeDtypeStruct((rows, features), jnp.bfloat16),
            jax.ShapeDtypeStruct((rows, features), jnp.float32),
        ],
        scratch_shapes=[
            pltpu.VMEM((2, count, rows, lanes), jnp.bfloat16),
            pltpu.VMEM((rows, lanes), jnp.float32),
            pltpu.VMEM((rows, lanes), jnp.float32),
        ],
        compiler_params=pltpu.CompilerParams(vmem_limit_bytes=VMEM_LIMIT),
        cost_estimate=pl.CostEstimate(
            flops=flops, bytes_accessed=12 * rows * features, transcendentals=0
        ),
        name="attend",
    )(attn_bias, query_low, query_meta, *keys, *values, *key_metas)


def attend_back_kernel(
    key_blocks,
    segments,
    width,
    bias_ref,
    query_ref,
    qmeta_ref,
    total_ref,
    attended_ref,
    grad_ref,
    *refs,
):
    key_refs, value_refs, kmeta_refs = (
        refs[:key_blocks],
        refs[key_blocks : 2 * key_blocks],
        refs[2 * key_blocks : 3 * key_blocks],
    )
    results = refs[len(refs) - 4 - 2 * key_blocks :]
    grad_query_ref = results[0]
    grad_key_refs = results[1 : key_blocks + 1]
    grad_value_refs = results[key_blocks + 1 : 2 * key_blocks + 1]
    side_ref, match_ref, apart_ref = results[2 * key_blocks + 1 :]
    pair = pl.program_id(0)
    rows, lanes = query_ref.shape
    lane = lax.broadcasted_iota(jnp.int32, (rows, lanes), 1)
    column = lane % width
    ones_at = EXACT_PARTS * VARIATES + segments

    @pl.when(pair == 0)
    def _():
        note_keys(side_ref, kmeta_refs, column, lane, width, segments)
        note_queries(match_ref, apart_ref, qmeta_ref, column, segments)

    scaled = query_ref[...].astype(jnp.float32) * width ** (-0.5)
    scaled_low = scaled.astype(jnp.bfloat16)
    grad_low = grad_ref[...]
    grad = grad_low.astype(jnp.float32)
    overlap = grad * attended_ref[...].astype(jnp.float32)
    square_row = lax.broadcasted_iota(jnp.int32, (lanes, lanes), 0)
    square_column = lax.broadcasted_iota(jnp.int32, (lanes, lanes), 1)
    across = one_hot(square_row // width != square_column // width)
    high = overlap.astype(jnp.bfloat16)
    rest = (overlap - high.astype(jnp.float32)).astype(jnp.bfloat16)
    dot_side = parts_in_lanes(-(dot(high, across) + dot(rest, across)), ones_at, column)
    total_side = parts_in_lanes(-total_ref[...], ones_at, column)
    heads = range(lanes // width)
    blocks = range(key_blocks)
    probs, grad_probs = {}, {}
    for head in heads:
        inside = (lane // width) == head
        extension = total_side + query_side(
            match_ref, apart_ref, bias_ref, pair * (lanes // width) + head, column
        )
        right = jnp.where(inside, scaled, extension).astype(jnp.bfloat16)
        grad_right = jnp.where(inside, grad, dot_side).astype(jnp.bfloat16)
        own_lanes = head_lanes(head, width, lanes)
        for block in blocks:
            side = side_ref[head, block]
            probs[head, block] = contract_last(key_refs[block][...] * own_lanes + side, right)
            grad_probs[head, block] = contract_last(
                value_refs[block][...] * own_lanes + side, grad_right
            )
    grad_query_parts = []
    grad_keys = [[] for _ in blocks]
    grad_values = [[] for _ in blocks]
    keys_turned = beside(*[jnp.transpose(ref[...]) for ref in key_refs])
    for head in heads:
        grad_scores = []
        for block in blocks:
            prob = jnp.exp(probs[head, block])
            grad_score = (prob * grad_probs[head, block]).astype(jnp.bfloat16)
            grad_values[block].append(dot(prob.astype(jnp.bfloat16), grad_low))
            grad_keys[block].append(dot(grad_score, scaled_low))
            grad_scores.append(grad_score)
        grad_query_parts.append(
            dot(keys_turned[head * width : (head + 1) * width], above(*grad_scores))
        )
    first = (lane // width) == 0
    stacked = jnp.concatenate(grad_query_parts, axis=0) * width ** (-0.5)
    grad_query_ref[...] = jnp.transpose(stacked).astype(jnp.bfloat16)
    for block in range(key_blocks):
        grad_key_refs[block][...] = jnp.where(first, *grad_keys[block]).astype(
            grad_key_refs[block].dtype
        )
        grad_value_refs[block][...] = jnp.where(first, *grad_values[block]).astype(
            grad_value_refs[block].dtype
        )


def attend_back(
    attn_bias,
    query_low,
    query_meta,
    log_total,
    attended_low,
    grad_attended,
    keys,
    values,
    key_metas,
    segments,
    width,
):
    rows, features = query_low.shape
    lanes = 2 * width
    count = len(keys)
    here = lane_block(rows, lanes)
    flops = 10 * rows * rows * count * features
    low = jax.ShapeDtypeStruct((rows, features), jnp.bfloat16)
    results = pl.pallas_call(
        functools.partial(attend_back_kernel, count, segments, width),
        grid=(features // lanes,),
        in_specs=[
            pl.BlockSpec(memory_space=pltpu.SMEM),
            here,
            whole_block(query_meta.shape),
        ]
        + [here] * (3 + 2 * count)
        + [whole_block(query_meta.shape)] * count,
        out_specs=[here] * (1 + 2 * count),
        out_shape=[low] * (1 + 2 * count),
        scratch_shapes=[
            pltpu.VMEM((2, count, rows, lanes), jnp.bfloat16),
            pltpu.VMEM((rows, lanes), jnp.float32),
            pltpu.VMEM((rows, lanes), jnp.float32),
        ],
        compiler_params=pltpu.CompilerParams(vmem_limit_bytes=VMEM_LIMIT),
        cost_estimate=pl.CostEstimate(
            flops=flops, bytes_accessed=20 * rows * features, transcendentals=0
        ),
        name="attend_back",
    )(
        attn_bias,
        query_low,
        query_meta,
        log_total,
        attended_low,
        grad_attended,
        *keys,
        *values,
        *key_metas,
    )
    return results


def plan_kernel(
    groups,
    rows,
    width,
    member_ref,
    length_ref,
    adapter_ref,
    order_ref,
    variate_ref,
    frequency_ref,
    chosen_ref,
    back_ref,
    turn_ref,
    cos_ref,
    sin_ref,
    *refs,
):
    meta_refs, slot_ref = refs[:-1], refs[-1]
    blocks = variate_ref.shape[0]
    half_devices = groups // 2
    half_blocks = blocks // 2
    half_rows = half_blocks * LANES
    swap_rows = rows // 2
    member = member_ref[0]
    my_half, my_place = member // half_devices, member % half_devices
    places = [lax.rem(my_place + shift, half_devices) for shift in range(half_devices)]
    segments = length_ref.shape[1]
    starts = [jnp.int32(0)]
    for segment in range(segments):
        starts.append(starts[-1] + length_ref[0, segment])
    long_start, long_index = jnp.int32(0), jnp.int32(0)
    for segment in range(segments):
        is_half = length_ref[0, segment] == half_rows
        long_start = jnp.where(is_half, starts[segment], long_start)
        long_index = jnp.where(is_half, segment, long_index)

    block = lax.broadcasted_iota(jnp.int32, (blocks, LANES), 0)
    lane = lax.broadcasted_iota(jnp.int32, (blocks, LANES), 1)
    work_block = jnp.zeros((blocks, LANES), jnp.int32)
    for index in range(blocks):
        work_block = jnp.where(block == order_ref[0, index], index, work_block)
    work_row = work_block * LANES + lane
    is_long = (work_row >= long_start) & (work_row < long_start + half_rows)
    in_first = block < half_blocks
    long_count = jnp.sum(jnp.where(is_long & in_first, 1.0, 0.0)).astype(jnp.int32)
    long_half = jnp.where(2 * long_count < half_rows, 1, 0)
    side = jnp.where(in_first, 0, 1)
    target = jnp.where(is_long, long_half, 1 - long_half)
    foreign = target != side
    flags = jnp.where(foreign, 1.0, 0.0)
    moved = jnp.sum(jnp.where(in_first, flags, 0.0)).astype(jnp.int32)
    square_row = lax.broadcasted_iota(jnp.int32, (LANES, LANES), 0)
    square_column = lax.broadcasted_iota(jnp.int32, (LANES, LANES), 1)
    within = dot(flags.astype(jnp.bfloat16), one_hot(square_row < square_column))
    block_sum = jnp.broadcast_to(jnp.sum(flags, axis=1, keepdims=True), (blocks, LANES))
    from_block = lax.broadcasted_iota(jnp.int32, (blocks, blocks), 1)
    to_block = lax.broadcasted_iota(jnp.int32, (blocks, blocks), 0)
    earlier = (from_block < to_block) & ((from_block < half_blocks) == (to_block < half_blocks))
    before = dot(one_hot(earlier), block_sum.astype(jnp.bfloat16))
    foreign_rank = (within + before).astype(jnp.int32)
    kept_rank = (block - side * half_blocks) * LANES + lane - foreign_rank
    kept_slot = side * half_rows + kept_rank
    foreign_slot = (1 - side) * half_rows + rows + foreign_rank
    foreign_slot = foreign_slot - jnp.clip(moved, 0, swap_rows)
    for index in range(1, half_devices):
        start = index * rows - jnp.minimum(moved, index * swap_rows)
        last = (index - 1) * rows - jnp.minimum(moved, (index - 1) * swap_rows)
        kept_slot = jnp.where(kept_rank >= start, kept_slot + rows - (start - last), kept_slot)
        received = jnp.clip(moved - index * swap_rows, 0, swap_rows)
        previous = jnp.clip(moved - (index - 1) * swap_rows, 0, swap_rows)
        foreign_slot = jnp.where(
            foreign_rank >= index * swap_rows,
            foreign_slot + rows - swap_rows + previous - received,
            foreign_slot,
        )
    slot = jnp.where(foreign, foreign_slot, kept_slot)
    slot_ref[...] = slot

    per_device = rows // LANES
    wanted = lax.broadcasted_iota(jnp.int32, (rows + swap_rows, 1), 0)
    wanted = jnp.where(
        wanted < rows,
        my_half * half_rows + my_place * rows + wanted,
        (1 - my_half) * half_rows + my_place * rows + wanted - swap_rows,
    )
    for shift in range(half_devices):
        for index in range(per_device):
            held = my_half * half_blocks + places[shift] * per_device + index
            column = (shift * per_device + index) * LANES
            chosen_ref[:, column : column + LANES] = one_hot(
                wanted == slot_ref[pl.ds(held, 1), :]
            )

    slot_turned = jnp.transpose(slot.astype(jnp.float32))
    turned_lane = lax.broadcasted_iota(jnp.int32, (LANES, blocks), 1)
    first_lane = lax.broadcasted_iota(jnp.int32, (1, LANES), 1)
    for index in range(per_device):
        held = my_half * half_blocks + my_place * per_device + index
        mine = jnp.sum(
            jnp.where(turned_lane == held, slot_turned, 0.0), axis=1, keepdims=True
        ).astype(jnp.int32)
        here = slice(index * LANES, (index + 1) * LANES)
        column = 0
        for first, half, length in ((0, my_half, rows), (swap_rows, 1 - my_half, swap_rows)):
            for shift in range(half_devices):
                for chunk in range(0, length, LANES):
                    number = half * half_rows + places[shift] * rows + first + chunk
                    back_ref[here, column : column + LANES] = one_hot(mine == number + first_lane)
                    column += LANES

    on_long = my_half == long_half
    for turn in range(2):
        chosen_segment = jnp.where(
            on_long, long_index, jnp.where(long_index <= turn, turn + 1, turn)
        )
        adapter = adapter_ref[0, 0]
        for segment in range(1, segments):
            adapter = jnp.where(chosen_segment == segment, adapter_ref[0, segment], adapter)
        turn_ref[turn] = adapter

    variate_turned = jnp.transpose(variate_ref[...].astype(jnp.float32))
    known = []
    for index in range(blocks):
        values = jnp.where(
            square_column == 0,
            work_block[index : index + 1, :].astype(jnp.float32),
            jnp.where(
                square_column == 1,
                square_row.astype(jnp.float32),
                variate_turned[:, index : index + 1],
            ),
        )
        known.append(jnp.where(square_column < 3, values, 0.0).astype(jnp.bfloat16))
    number = lax.broadcasted_iota(jnp.int32, (rows, 1), 0)
    wide_lane = lax.broadcasted_iota(jnp.int32, (rows, LANES), 1)
    for shift in range(half_devices):
        slots = my_half * half_rows + places[shift] * rows + number
        facts = jnp.zeros((rows, LANES), jnp.float32)
        for index in range(blocks):
            facts = facts + dot(one_hot(slots == slot[index : index + 1, :]), known[index])
        facts = facts.astype(jnp.int32)
        row = facts[:, 0:1] * LANES + facts[:, 1:2]
        segment = jnp.zeros((rows, 1), jnp.int32)
        first_row = jnp.zeros((rows, 1), jnp.int32)
        for index in range(1, segments):
            segment = jnp.where(row >= starts[index], index, segment)
            first_row = jnp.where(row >= starts[index], starts[index], first_row)
        turn = jnp.where(segment > long_index, segment - 1, segment)
        turn = jnp.where(on_long, 0, turn)
        meta_refs[shift][...] = jnp.where(
            wide_lane == 0, facts[:, 2:3], jnp.where(wide_lane == 1, segment, turn)
        )
        if shift == 0:
            angles = (row - first_row).astype(jnp.float32) * frequency_ref[...]
            sign = jnp.where(wide_lane % width < width // 2, -1.0, 1.0)
            cos_ref[...] = jnp.cos(angles)
            sin_ref[...] = jnp.sin(angles) * sign


def plan(groups, rows, width, member, seq_len, seq_adapter, block_order, variate):
    half_devices = groups // 2
    half_rows = half_devices * rows
    blocks = block_order.shape[1]
    smem = pl.BlockSpec(memory_space=pltpu.SMEM)
    vmem = pl.BlockSpec(memory_space=pltpu.VMEM)
    results = pl.pallas_call(
        functools.partial(plan_kernel, groups, rows, width),
        in_specs=[smem, smem, smem, smem, vmem, vmem],
        out_specs=[vmem, vmem, smem, vmem, vmem] + [vmem] * half_devices,
        out_shape=[
            jax.ShapeDtypeStruct((rows + rows // 2, half_rows), jnp.bfloat16),
            jax.ShapeDtypeStruct((rows, half_rows + half_rows // 2), jnp.bfloat16),
            jax.ShapeDtypeStruct((2,), jnp.int32),
            jax.ShapeDtypeStruct((rows, LANES), jnp.float32),
            jax.ShapeDtypeStruct((rows, LANES), jnp.float32),
        ]
        + [jax.ShapeDtypeStruct((rows, LANES), jnp.int32)] * half_devices,
        scratch_shapes=[pltpu.VMEM((blocks, LANES), jnp.int32)],
        compiler_params=pltpu.CompilerParams(vmem_limit_bytes=VMEM_LIMIT),
        cost_estimate=pl.CostEstimate(
            flops=2**31, bytes_accessed=4 * rows * half_rows, transcendentals=0
        ),
        name="plan",
    )(
        member,
        seq_len,
        seq_adapter,
        block_order,
        variate.reshape(blocks, LANES),
        jnp.asarray(rope_frequency(width)),
    )
    return (*results[:5], results[5:])


def pick_kernel(counts, later_count, chosen_ref, *refs):
    outs = refs[sum(counts) + later_count : sum(counts) + later_count + len(counts)]
    refs = iter(refs[: sum(counts)])
    for count, out_ref in zip(counts, outs):
        total = jnp.zeros(out_ref.shape, jnp.float32)
        column = 0
        for _ in range(count):
            ref = next(refs)
            rows = ref.shape[0]
            total = total + dot(chosen_ref[:, column : column + rows], ref[...])
            column += rows
        out_ref[...] = total.astype(out_ref.dtype)


def pick(chosen, first, count, *helds, later=()):
    features = helds[0][0].shape[1]
    tile = features // 2
    parts = [part for held in helds for part in held]
    return pl.pallas_call(
        functools.partial(pick_kernel, [len(held) for held in helds], len(later)),
        grid=(features // tile,),
        in_specs=[pl.BlockSpec((count, chosen.shape[1]), lambda step: (first // count, 0))]
        + [pl.BlockSpec((part.shape[0], tile), lambda step: (0, step)) for part in parts]
        + [pl.BlockSpec(memory_space=pl.ANY)] * len(later),
        out_specs=[pl.BlockSpec((count, tile), lambda step: (0, step))] * len(helds)
        + [pl.BlockSpec(memory_space=pl.ANY)] * len(later),
        out_shape=[jax.ShapeDtypeStruct((count, features), jnp.bfloat16)] * len(helds)
        + [jax.ShapeDtypeStruct(array.shape, array.dtype) for array in later],
        input_output_aliases={1 + len(parts) + i: len(helds) + i for i in range(len(later))},
        compiler_params=pltpu.CompilerParams(vmem_limit_bytes=VMEM_LIMIT),
        cost_estimate=pl.CostEstimate(
            flops=2 * count * chosen.shape[1] * features * len(helds),
            bytes_accessed=8 * count * features * len(helds),
            transcendentals=0,
        ),
        name="pick",
    )(chosen, *parts, *later)


def axis_count(names):
    count = 1
    for name in names:
        count *= lax.axis_size(name)
    return count


def within_half(array, shift, groups):
    half = groups // 2
    pairs = [
        (base + (place + shift) % half, base + place)
        for base in (0, half)
        for place in range(half)
    ]
    return lax.ppermute(array, GROUP, pairs)


def gather_half(array, groups):
    return [array] + [within_half(array, shift, groups) for shift in range(1, groups // 2)]


def to_other_half(array, groups):
    half = groups // 2
    return lax.ppermute(array, GROUP, [(i, (i + half) % groups) for i in range(groups)])


def scatter_sum(array, axis_sizes):
    for name, size in reversed(axis_sizes):
        outer = array.shape[0] // size
        array = array.reshape((outer, size) + array.shape[1:])
        bit = 1
        while bit < size:
            index = lax.axis_index(name)
            own = (index // bit) % 2
            spread = array.reshape((outer, size // (2 * bit), 2) + array.shape[2:])
            keep = lax.dynamic_index_in_dim(spread, own, 2, keepdims=False)
            send = lax.dynamic_index_in_dim(spread, 1 - own, 2, keepdims=False)
            got = lax.ppermute(send, name, [(i, i ^ bit) for i in range(size)])
            array = (keep.astype(jnp.float32) + got.astype(jnp.float32)).astype(jnp.bfloat16)
            bit *= 2
        array = array.reshape((outer,) + array.shape[2:])
    return array


LANES = 128
MOMENT_ROWS = 24
PACKS = ("far", "near")
GROUP = ("half", "core")
ALL = PACKS + GROUP


def adam(current, first_old, second_old, grad):
    first_moment = BETA_ONE * first_old + (1.0 - BETA_ONE) * grad
    second_moment = BETA_TWO * second_old + (1.0 - BETA_TWO) * grad * grad
    first_fix = first_moment / (1.0 - BETA_ONE**update_count)
    second_fix = second_moment / (1.0 - BETA_TWO**update_count)
    updated = current - LEARN_RATE * (
        first_fix / (jnp.sqrt(second_fix) + ADAM_EPS) + WEIGHT_DECAY * current
    )
    return first_moment, second_moment, updated.astype(jnp.bfloat16)


def settle_shards(grads, few_choice, adapters, moment1, moment2, groups):
    a_qkv, b_qkv, a_guo, a_down, b_gu, b_do = grads
    features, few = a_qkv.shape[0], few_choice.shape[1]
    quarters = a_down.shape[1] // few
    down = jnp.concatenate([a_down[:, i * few : (i + 1) * few] for i in range(quarters)])
    wide = [a_qkv[:, i * few : (i + 1) * few] for i in range(3)]
    wide += [a_guo[:, i * few : (i + 1) * few] for i in (2, 0, 1)] + [down]
    tall = [b_qkv[i * few : (i + 1) * few] for i in range(3)]
    tall += [b_do[2 * few : 3 * few], b_gu[:few], b_gu[few : 2 * few], b_do[:few]]
    pieces = []
    for grad_a, grad_b in zip(wide, tall):
        pieces.append(lax.dot_general(grad_a, few_choice, (((1,), (1,)), ((), ()))).reshape(-1))
        pieces.append(jnp.dot(few_choice, grad_b).reshape(-1))
    axis_sizes = [(PACKS, axis_count(PACKS)), (GROUP, groups)]
    shards = axis_sizes[0][1] * groups
    flat_grads = jnp.concatenate(pieces).astype(jnp.bfloat16).reshape(shards, -1)
    grad_shard = scatter_sum(flat_grads, axis_sizes).reshape(-1).astype(jnp.float32)
    shard_count = grad_shard.shape[0]
    shard_start = lax.axis_index(ALL) * shard_count
    current = lax.dynamic_slice_in_dim(adapters, shard_start, shard_count).astype(jnp.float32)
    first_moment, second_moment, updated = adam(current, moment1, moment2, grad_shard)
    adapters_new = lax.all_gather(updated, ALL, axis=0, tiled=True)
    return grad_shard, first_moment, second_moment, adapters_new


def spreads_evenly(devices, groups, features, hidden, total):
    rows = total // LANES
    chunks = features // LANES
    return (
        groups == 4
        and ADAPTERS * RANK == LANES
        and devices * chunks == 256
        and chunks == 8
        and hidden == devices * LANES
        and hidden == 4 * features
        and rows % (devices * devices) == 0
        and devices & (devices - 1) == 0
    )


def one_hot(condition):
    return jnp.where(condition, 1.0, 0.0).astype(jnp.bfloat16)


def sum_wide(adapter_row, arrived_ref, first, width):
    sources = arrived_ref.shape[0]
    rows = lax.broadcasted_iota(jnp.int32, (LANES, width * LANES), 0)
    columns = lax.broadcasted_iota(jnp.int32, (LANES, width * LANES), 1)
    fits = (rows // (2 * RANK) == columns // LANES) & (rows % RANK == columns % RANK)
    second = (rows // RANK) % 2 == 1
    adapter = jnp.where(fits, (columns % LANES) // RANK, -1)
    total = jnp.zeros((32, width * LANES), jnp.float32)
    for source in range(sources):
        at = source * 2 * RANK
        chosen = jnp.where(
            second, adapter_row[:, at + RANK : at + RANK + 1], adapter_row[:, at : at + 1]
        )
        total = total + dot(
            arrived_ref[source, first : first + 32, :], one_hot(adapter == chosen)
        )
    return total


def sum_tall(adapter_row, arrived_ref, first):
    sources = arrived_ref.shape[0]
    depth = sources * 2 * RANK
    rows = lax.broadcasted_iota(jnp.int32, (LANES, depth), 0)
    columns = lax.broadcasted_iota(jnp.int32, (LANES, depth), 1)
    choice = one_hot((rows // RANK == adapter_row) & (rows % RANK == columns % RANK))
    held = arrived_ref[:, first : first + 2 * RANK, :].reshape(depth, LANES)
    return jnp.dot(choice, held, preferred_element_type=jnp.float32)


def sum_square(adapter_row, arrived_ref, first):
    sources = arrived_ref.shape[0]
    depth = sources * 16
    rows = lax.broadcasted_iota(jnp.int32, (64, depth), 0)
    columns = lax.broadcasted_iota(jnp.int32, (64, depth), 1)
    choice = one_hot(
        ((rows % 32) // 4 == adapter_row)
        & (rows % 4 == columns % 4)
        & (rows // 32 == (columns % 16) // 8)
    )
    held = arrived_ref[:, first : first + 16, :].reshape(depth, LANES)
    return jnp.dot(choice, held, preferred_element_type=jnp.float32)


def settle_rows(parts, skip, param_ref, m1_ref, m2_ref, m_skip, grad_ref, new_refs):
    row = 0
    for part in parts:
        here = slice(row, row + part.shape[0])
        there = slice(skip + row, skip + row + part.shape[0])
        at = slice(m_skip + row, m_skip + row + part.shape[0])
        row += part.shape[0]
        low = part.astype(jnp.bfloat16)
        grad_ref[here, :] = low
        new = adam(
            param_ref[there, :].astype(jnp.float32),
            m1_ref[at, :],
            m2_ref[at, :],
            low.astype(jnp.float32),
        )[2]
        for new_ref in new_refs:
            new_ref[here, :] = new


def settle_early_kernel(own_rows, arrived_ref, moments_ref, param_ref, *refs):
    grad_ref, new_ref, late_m1_ref, late_m2_ref, tall_ref, square_ref, m1_ref, m2_ref = refs[-8:]
    sources = arrived_ref.shape[0]
    told = 6 * RANK
    tall_column = lax.broadcasted_iota(jnp.int32, tall_ref.shape, 1)
    square_column = lax.broadcasted_iota(jnp.int32, square_ref.shape, 1)
    tall = jnp.zeros(tall_ref.shape, jnp.float32)
    square = jnp.zeros(square_ref.shape, jnp.float32)
    for source in range(sources):
        row = arrived_ref[source, 0:16, :].astype(jnp.float32)
        first, second = row[0:1, told : told + 1], row[0:1, told + 1 : told + 2]
        tall = jnp.where(
            tall_column // (2 * RANK) == source,
            jnp.where((tall_column // RANK) % 2 == 1, second, first),
            tall,
        )
        square = jnp.where(
            square_column // RANK == source,
            jnp.where((square_column // 4) % 2 == 1, second, first),
            square,
        )
        held = moments_ref[source].astype(jnp.float32)
        here = slice(source * own_rows, (source + 1) * own_rows)
        m1_ref[here, :] = held[:own_rows]
        m2_ref[here, :] = held[MOMENT_ROWS : MOMENT_ROWS + own_rows]
    tall = tall.astype(jnp.int32)
    square = square.astype(jnp.int32)
    tall_ref[...] = tall
    square_ref[...] = square
    late = late_m1_ref.shape[0]
    late_m1_ref[...] = m1_ref[:late, :]
    late_m2_ref[...] = m2_ref[:late, :]
    wide = sum_wide(tall, arrived_ref, 0, 3)
    last = sum_wide(tall, arrived_ref, 32, 4)
    pair = sum_square(square, arrived_ref, 128)
    parts = [
        wide[:, 2 * LANES :],
        pair[32:],
        wide[:, :LANES],
        sum_tall(tall, arrived_ref, 64),
        wide[:, LANES : 2 * LANES],
        sum_tall(tall, arrived_ref, 96),
    ]
    parts += [last[:, i * LANES : (i + 1) * LANES] for i in range(4)]
    parts.append(pair[:32])
    copies = [new_ref.at[copy] for copy in range(new_ref.shape[0])]
    settle_rows(parts, late, param_ref, m1_ref, m2_ref, late, grad_ref, copies)


def settle_early(arrived, moments, params, late_rows, after):
    sources = arrived.shape[0]
    rows = params.shape[0] - late_rows
    vmem = pl.BlockSpec(memory_space=pltpu.VMEM)
    low = jax.ShapeDtypeStruct((rows, LANES), jnp.bfloat16)
    late = jax.ShapeDtypeStruct((late_rows, LANES), jnp.float32)
    return pl.pallas_call(
        functools.partial(settle_early_kernel, params.shape[0] // sources),
        in_specs=[vmem, vmem, vmem] + [pl.BlockSpec(memory_space=pl.ANY)] * len(after),
        out_specs=[vmem] * 6,
        out_shape=[
            low,
            jax.ShapeDtypeStruct((1, rows, LANES), jnp.bfloat16),
            late,
            late,
            jax.ShapeDtypeStruct((1, sources * 2 * RANK), jnp.int32),
            jax.ShapeDtypeStruct((1, sources * RANK), jnp.int32),
        ],
        scratch_shapes=[pltpu.VMEM(params.shape, jnp.float32)] * 2,
        compiler_params=pltpu.CompilerParams(vmem_limit_bytes=VMEM_LIMIT),
        cost_estimate=pl.CostEstimate(
            flops=sources * 2**24, bytes_accessed=4 * arrived.size, transcendentals=0
        ),
        name="settle_early",
    )(arrived, moments, params, *after)


def settle_late_kernel(
    later_count, tall_ref, square_ref, arrived_ref, param_ref, m1_ref, m2_ref, *refs
):
    early_grad_ref = refs[0]
    own_ref, new_ref = refs[-3 - later_count : -1 - later_count]
    grad_ref = refs[-1]
    wide = sum_wide(tall_ref[...], arrived_ref, 0, 3)
    pairs = [sum_square(square_ref[...], arrived_ref, first) for first in (32, 48)]
    parts = []
    for index in range(3):
        parts.append(wide[:, index * LANES : (index + 1) * LANES])
        parts.append(pairs[index // 2][(index % 2) * 32 : (index % 2) * 32 + 32])
    copies = [new_ref.at[copy] for copy in range(new_ref.shape[0])]
    settle_rows(parts, 0, param_ref, m1_ref, m2_ref, 0, grad_ref, copies)
    low = jnp.concatenate(
        [ref[...].astype(jnp.float32) for ref in (grad_ref, early_grad_ref)], axis=0
    )
    each = low.shape[0] // own_ref.shape[0]
    zeros = jnp.zeros((own_ref.shape[1] - each, LANES), jnp.float32)
    for owner in range(own_ref.shape[0]):
        own_ref[owner] = jnp.concatenate(
            [low[owner * each : (owner + 1) * each], zeros], axis=0
        ).astype(jnp.bfloat16)


def settle_late(tall, square, arrived, params, late_m1, late_m2, early_grad, later, after):
    rows = late_m1.shape[0]
    anywhere = pl.BlockSpec(memory_space=pl.ANY)
    vmem = pl.BlockSpec(memory_space=pltpu.VMEM)
    return pl.pallas_call(
        functools.partial(settle_late_kernel, len(later)),
        in_specs=[vmem] * 7 + [anywhere] * (len(later) + len(after)),
        out_specs=[vmem, vmem] + [anywhere] * len(later),
        scratch_shapes=[pltpu.VMEM((rows, LANES), jnp.bfloat16)],
        input_output_aliases={7 + index: 2 + index for index in range(len(later))},
        out_shape=[
            jax.ShapeDtypeStruct((arrived.shape[0], MOMENT_ROWS, LANES), jnp.bfloat16),
            jax.ShapeDtypeStruct((axis_count(PACKS), rows, LANES), jnp.bfloat16),
        ]
        + [jax.ShapeDtypeStruct(array.shape, array.dtype) for array in later],
        compiler_params=pltpu.CompilerParams(vmem_limit_bytes=VMEM_LIMIT),
        cost_estimate=pl.CostEstimate(
            flops=arrived.shape[0] * 2**24, bytes_accessed=4 * arrived.size, transcendentals=0
        ),
        name="settle_late",
    )(tall, square, arrived, params, late_m1, late_m2, early_grad, *later, *after)


def gather_inner(piece, groups):
    pieces = [piece]
    bit = groups // 2
    while bit:
        pairs = [(i, i ^ bit) for i in range(groups)]
        pieces = pieces + [lax.ppermute(piece, GROUP, pairs) for piece in pieces]
        bit //= 2
    return pieces


def placing_order(device, unit):
    size = unit * device.shape[0]
    to_row = lax.broadcasted_iota(jnp.int32, (size, size), 0)
    from_row = jnp.arange(size, dtype=jnp.int32)
    source = (from_row % unit) * device.shape[0] + jnp.repeat(device, unit)
    return (to_row == source[None, :]).astype(jnp.bfloat16)


def piece_devices(groups, devices):
    member = lax.axis_index(GROUP)
    piece = jnp.arange(groups, dtype=jnp.int32)
    mask = jnp.zeros_like(piece)
    bit = 1
    while bit < groups:
        mask = mask * 2 + (piece // bit) % 2
        bit *= 2
    outer = jnp.arange(devices // groups, dtype=jnp.int32)
    return (outer[None, :] * groups + (member ^ mask)[:, None]).reshape(-1)


def hand_on(after, *arrays):
    anywhere = pl.BlockSpec(memory_space=pl.ANY)
    return pl.pallas_call(
        lambda *refs: None,
        in_specs=[anywhere] * (len(after) + len(arrays)),
        out_specs=[anywhere] * len(arrays),
        out_shape=[jax.ShapeDtypeStruct(array.shape, array.dtype) for array in arrays],
        input_output_aliases={len(after) + index: index for index in range(len(arrays))},
        name="hand_on",
    )(*after, *arrays)


def assemble_kernel(counts, devices, chunks, first, order_ref, *refs):
    piece_refs = []
    for count in counts:
        piece_refs.append(refs[:count])
        refs = refs[count:]
    out_any, placed_ref, sems = refs[-3:]

    def held_rows(part_refs, start, stop):
        before = 0
        for ref in part_refs:
            if start < before + ref.shape[1]:
                return ref[:, start - before : stop - before, :]
            before += ref.shape[1]

    unit = order_ref.shape[0] // devices
    copies = []
    for index, (begin, end) in enumerate(chunks):
        for start in range(begin, end, 2 * unit):
            sides = []
            for side in (start, start + unit):
                held = jnp.concatenate(
                    [held_rows(part_refs, side, side + unit) for part_refs in piece_refs], axis=0
                )
                sides.append(held.reshape(unit * devices, LANES))
            placed = dot(order_ref[...], jnp.concatenate(sides, axis=1)).astype(jnp.bfloat16)
            for half, side in enumerate((start, start + unit)):
                placed_ref[side * devices : (side + unit) * devices, :] = placed[
                    :, half * LANES : (half + 1) * LANES
                ]
        here = slice(begin * devices, end * devices)
        there = slice((first + begin) * devices, (first + end) * devices)
        copies.append(
            pltpu.make_async_copy(placed_ref.at[here, :], out_any.at[there, :], sems.at[index])
        )
        copies[-1].start()
    for copy in copies:
        copy.wait()


def assemble(order, pieces, total_rows, first, before, after):
    devices = len(pieces) * pieces[0][0].shape[0]
    rows = pieces[0][0].shape[1]
    parts = [part for piece in pieces for part in piece]
    step = 32 * max(1, rows // 128)
    chunks = [(begin, min(begin + step, rows)) for begin in range(0, rows, step)]
    vmem, anywhere = pl.BlockSpec(memory_space=pltpu.VMEM), pl.BlockSpec(memory_space=pl.ANY)
    in_specs = [vmem] * (1 + len(parts)) + [anywhere] * len(after)
    operands = [order, *parts, *after]
    aliases = {}
    if before is not None:
        aliases = {len(operands): 0}
        in_specs.append(anywhere)
        operands.append(before)
    return pl.pallas_call(
        functools.partial(assemble_kernel, [len(piece) for piece in pieces], devices, chunks, first),
        in_specs=in_specs,
        out_specs=anywhere,
        out_shape=jax.ShapeDtypeStruct((total_rows, LANES), jnp.bfloat16),
        scratch_shapes=[
            pltpu.VMEM((rows * devices, LANES), jnp.bfloat16),
            pltpu.SemaphoreType.DMA((len(chunks),)),
        ],
        input_output_aliases=aliases,
        compiler_params=pltpu.CompilerParams(vmem_limit_bytes=VMEM_LIMIT),
        cost_estimate=pl.CostEstimate(
            flops=rows * devices * 2**17, bytes_accessed=rows * devices * 512, transcendentals=0
        ),
        name="assemble",
    )(*operands)


def rope_frequency(head_width):
    index = np.arange(LANES) % (head_width // 2)
    return (ROPE_BASE ** (-2.0 * index / head_width)).astype(np.float32)[None, :]


def gain_rows(attn_gain, ffn_gain, q_gain, k_gain):
    repeats = attn_gain.shape[0] // q_gain.shape[0]
    return jnp.concatenate(
        [attn_gain, ffn_gain] + [q_gain] * repeats + [k_gain] * repeats
    ).astype(jnp.float32).reshape(4, -1)


def select_kernel(features, hidden, devices, turn_ref, me_ref, flat_any, *refs):
    m1_ref, m2_ref = refs[:2]
    out_refs, flat_ref, sems = refs[3:-2], refs[-2], refs[-1]
    size = flat_ref.shape[0] // sems.shape[0]
    copies = [
        pltpu.make_async_copy(
            flat_any.at[pl.ds(chunk * size, size), :],
            flat_ref.at[pl.ds(chunk * size, size), :],
            sems.at[chunk],
        )
        for chunk in range(sems.shape[0])
    ]
    for copy in copies:
        copy.start()
    a_qkv_ref, a_guo_ref, a_down_ref, b_qkv_ref, b_gu_ref, b_do_ref = out_refs[:6]
    if devices:
        own_ref, moments_ref, wide_ref = out_refs[6:]
        count = m1_ref.shape[0] // devices
        for device in range(devices):
            rows = []
            for ref in (m1_ref, m2_ref):
                rows.append(ref[pl.ds(device, count, stride=devices), :])
                rows.append(jnp.zeros((MOMENT_ROWS - count, LANES), jnp.float32))
            moments_ref[device] = jnp.concatenate(rows, axis=0).astype(jnp.bfloat16)
        each = size // devices
        for chunk, copy in enumerate(copies):
            copy.wait()
            wide_ref[...] = flat_ref[chunk * size : (chunk + 1) * size, :].astype(jnp.float32)
            own_ref[chunk * each : (chunk + 1) * each, :] = wide_ref[
                pl.ds(me_ref[0], each, stride=devices), :
            ].astype(jnp.bfloat16)
    if not devices:
        for copy in copies:
            copy.wait()
    few = 2 * RANK
    rows = lax.broadcasted_iota(jnp.int32, (LANES, LANES), 0)
    columns = lax.broadcasted_iota(jnp.int32, (LANES, LANES), 1)
    chosen = jnp.where((columns // RANK) % 2 == 1, turn_ref[1], turn_ref[0])
    fits = (rows // RANK == chosen) & (rows % RANK == columns % RANK)
    start = {}
    row = 0
    for name, rows_in, rows_out in (
        ("q", features, features),
        ("k", features, features),
        ("v", features, features),
        ("o", features, features),
        ("g", features, hidden),
        ("u", features, hidden),
        ("d", hidden, features),
    ):
        start[name] = (row, row + rows_in)
        row += rows_in + rows_out

    def wide(names, length):
        total = jnp.zeros((length, LANES), jnp.float32)
        for place, name in enumerate(names):
            first = start[name][0]
            total = total + jnp.dot(
                flat_ref[first : first + length, :],
                one_hot(fits & (columns // few == place)),
                preferred_element_type=jnp.float32,
            )
        return total.astype(jnp.bfloat16)

    a_qkv_ref[...] = wide("qkv", features)
    a_guo_ref[...] = wide("guo", features)
    for first in range(0, hidden, features):
        a_down_ref[first : first + features, :] = jnp.dot(
            flat_ref[start["d"][0] + first : start["d"][0] + first + features, :],
            one_hot(fits & (columns // few == 0)),
            preferred_element_type=jnp.float32,
        ).astype(jnp.bfloat16)

    def tall(name, length, out_ref, place):
        chunks = length // LANES
        size = RANK * chunks
        to_row = lax.broadcasted_iota(jnp.int32, (size, size), 0)
        from_row = lax.broadcasted_iota(jnp.int32, (size, size), 1)
        turned = one_hot(
            (to_row // RANK == from_row % chunks) & (to_row % RANK == from_row // chunks)
        )
        for turn in range(2):
            first = start[name][1] + pl.multiple_of(turn_ref[turn] * size, LANES)
            block = jnp.dot(
                turned, flat_ref[pl.ds(first, size), :], preferred_element_type=jnp.float32
            ).astype(jnp.bfloat16)
            here = place * few + turn * RANK
            for chunk in range(chunks):
                out_ref[here : here + RANK, chunk * LANES : (chunk + 1) * LANES] = block[
                    chunk * RANK : (chunk + 1) * RANK
                ]

    for out_ref, names in ((b_qkv_ref, "qkv"), (b_gu_ref, "gu"), (b_do_ref, "d.o")):
        out_ref[...] = jnp.zeros(out_ref.shape, out_ref.dtype)
        for place, name in enumerate(names):
            if name != ".":
                tall(name, out_ref.shape[1], out_ref, place)


def select(devices, turn_adapter, me, adapters, moments, features, hidden, after):
    shapes = [(features, LANES), (features, LANES), (hidden, LANES)]
    shapes += [(LANES, features), (LANES, hidden), (LANES, features)]
    scratch = []
    if devices:
        shapes.append((adapters.shape[0] // (LANES * devices), LANES))
        shapes.append((devices, 2 * MOMENT_ROWS, LANES))
        scratch.append(pltpu.VMEM((1024, LANES), jnp.float32))
    rows = adapters.shape[0] // LANES
    scratch += [pltpu.VMEM((rows, LANES), jnp.bfloat16), pltpu.SemaphoreType.DMA((rows // 1024,))]
    return pl.pallas_call(
        functools.partial(select_kernel, features, hidden, devices),
        in_specs=[
            pl.BlockSpec(memory_space=pltpu.SMEM),
            pl.BlockSpec(memory_space=pltpu.SMEM),
            pl.BlockSpec(memory_space=pl.ANY),
            pl.BlockSpec(memory_space=pltpu.VMEM),
            pl.BlockSpec(memory_space=pltpu.VMEM),
            pl.BlockSpec(memory_space=pl.ANY),
        ],
        out_specs=[pl.BlockSpec(memory_space=pltpu.VMEM)] * len(shapes),
        out_shape=[jax.ShapeDtypeStruct(shape, jnp.bfloat16) for shape in shapes],
        scratch_shapes=scratch,
        compiler_params=pltpu.CompilerParams(vmem_limit_bytes=VMEM_LIMIT),
        cost_estimate=pl.CostEstimate(
            flops=2**31, bytes_accessed=4 * adapters.shape[0], transcendentals=0
        ),
        name="select",
    )(turn_adapter, me, adapters.reshape(-1, LANES), *moments, after)


def dot(left, right):
    return jnp.dot(left, right, preferred_element_type=jnp.float32)


def beside(*arrays):
    return jnp.concatenate(arrays, axis=1)


def above(*arrays):
    return jnp.concatenate(arrays, axis=0)


def turn_mask(meta_ref):
    rows = meta_ref.shape[0]
    lane = lax.broadcasted_iota(jnp.int32, (rows, LANES), 1)
    mask = jnp.where((lane // RANK) % 2 == meta_ref[:, 2:3], 1.0, 0.0)
    return mask, lane // (2 * RANK)


def row_norm(values):
    return lax.rsqrt(jnp.mean(values * values, axis=1, keepdims=True) + NORM_EPS)


def row_norm_back(values, gain, grad):
    scale = row_norm(values)
    unit = values * scale
    grad = grad * gain
    return scale * (grad - unit * jnp.mean(grad * unit, axis=1, keepdims=True))


def head_mean(values, width):
    lanes = values.shape[1]
    rows = lax.broadcasted_iota(jnp.int32, (lanes, lanes), 0)
    columns = lax.broadcasted_iota(jnp.int32, (lanes, lanes), 1)
    ones = one_hot(rows // width == columns // width)
    return dot(values.astype(jnp.bfloat16), ones) * (1.0 / width)


def swap_halves(values, width):
    lanes = values.shape[1]
    lane = lax.broadcasted_iota(jnp.int32, values.shape, 1)
    ahead = pltpu.roll(values, lanes - width // 2, 1)
    behind = pltpu.roll(values, width // 2, 1)
    return jnp.where(lane % width < width // 2, ahead, behind)


def widen(table, lanes):
    return jnp.concatenate([table] * (lanes // table.shape[1]), axis=1)


def joined(kept_ref, arrived_ref):
    first = kept_ref.shape[0] - arrived_ref.shape[0]
    kept = kept_ref[...]
    return jnp.concatenate([kept[:first], kept[first:] + arrived_ref[...]], axis=0)


def turned_heads(raw, gain, cosine, sine, width):
    unit = raw * lax.rsqrt(head_mean(raw * raw, width) + NORM_EPS) * gain
    return (unit * cosine + swap_halves(unit, width) * sine).astype(jnp.bfloat16)


def project_own(normed, inner, place, index, weight_ref, b_ref):
    own = jnp.where(place == index, ADAPTER_SCALE * inner, 0.0).astype(jnp.bfloat16)
    return dot(beside(normed, own), above(weight_ref[...], b_ref[...]))


def project_heads_kernel(
    width,
    kept_ref,
    arrived_ref,
    gains_ref,
    wq_ref,
    wk_ref,
    wv_ref,
    a_ref,
    b_ref,
    meta_ref,
    cos_ref,
    sin_ref,
    _,
    x_ref,
    normed_ref,
    inner_ref,
    q_raw_ref,
    k_raw_ref,
    q_ref,
    k_ref,
    v_ref,
    __,
):
    mask, place = turn_mask(meta_ref)

    @pl.when(pl.program_id(0) == 0)
    def _():
        rows = joined(kept_ref, arrived_ref)
        x_ref[...] = rows
        values = rows.astype(jnp.float32)
        normed = (values * row_norm(values) * gains_ref[0:1, :]).astype(
            jnp.bfloat16
        )
        normed_ref[...] = normed
        inner_ref[...] = (dot(normed, a_ref[...]) * mask).astype(jnp.bfloat16)

    normed = normed_ref[...]
    inner = inner_ref[...].astype(jnp.float32)
    lanes = wk_ref.shape[1]
    cosine, sine = widen(cos_ref[...], lanes), widen(sin_ref[...], lanes)
    query = project_own(normed, inner, place, 0, wq_ref, b_ref)
    q_raw_ref[...] = query.astype(jnp.bfloat16)
    q_ref[...] = turned_heads(query, gains_ref[2:3, :lanes], cosine, sine, width)
    key = project_own(normed, inner, place, 1, wk_ref, b_ref)
    k_raw_ref[...] = key.astype(jnp.bfloat16)
    k_ref[...] = turned_heads(key, gains_ref[3:4, :lanes], cosine, sine, width)
    v_ref[...] = project_own(normed, inner, place, 2, wv_ref, b_ref).astype(jnp.bfloat16)


def project_heads(
    kept,
    arrived,
    later,
    gains,
    weights,
    a_qkv,
    b_qkv,
    meta,
    cos_table,
    sin_table,
    width,
):
    rows, features = kept.shape
    tile = 512
    grid = (features // tile,)

    def tiled(height):
        return pl.BlockSpec((height, tile), lambda step: (0, step))

    def shape(dtype):
        return jax.ShapeDtypeStruct((rows, features), dtype)

    full, few = whole_block((rows, features)), whole_block((rows, LANES))
    low = shape(jnp.bfloat16)
    anywhere = pl.BlockSpec(memory_space=pl.ANY)
    results = pl.pallas_call(
        functools.partial(project_heads_kernel, width),
        grid=grid,
        in_specs=[full, whole_block(arrived.shape), whole_block(gains.shape)]
        + [tiled(features)] * 3
        + [whole_block((features, LANES)), tiled(LANES), few, few, few]
        + [anywhere],
        out_specs=[full, full, few] + [tiled(rows)] * 5 + [anywhere],
        input_output_aliases={11: 8},
        out_shape=[
            low,
            low,
            jax.ShapeDtypeStruct((rows, LANES), jnp.bfloat16),
            low,
            low,
            low,
            low,
            low,
            jax.ShapeDtypeStruct(later.shape, later.dtype),
        ],
        compiler_params=pltpu.CompilerParams(vmem_limit_bytes=VMEM_LIMIT),
        cost_estimate=pl.CostEstimate(
            flops=9 * rows * features * features,
            bytes_accessed=4 * features * features + 14 * rows * features,
            transcendentals=0,
        ),
        name="project_heads",
    )(
        kept,
        arrived,
        gains,
        *weights,
        a_qkv,
        b_qkv,
        meta,
        cos_table,
        sin_table,
        later,
    )
    return results


def project_heads_back_kernel(
    count,
    width,
    devices,
    gq_ref,
    *refs,
):
    gk_refs, gv_refs, refs = refs[:count], refs[count : 2 * count], refs[2 * count :]
    (
        q_raw_ref,
        k_raw_ref,
        normed_any,
        inner_ref,
        x_any,
        residual_any,
        gains_ref,
        wq_ref,
        wk_ref,
        wv_ref,
        a_ref,
        b_ref,
        meta_ref,
        cos_ref,
        sin_ref,
    ) = refs[:15]
    if devices:
        out_ref, tail_ref, spread_ref = refs[-9:-6]
    else:
        out_ref, tail_ref, grad_a_ref, grad_b_ref = refs[-10:-6]
    total_ref, few_ref, tall_ref, square_ref, held_ref, sems = refs[-6:]
    step = pl.program_id(0)
    lanes = wq_ref.shape[1]
    mask, place = turn_mask(meta_ref)
    cosine, sine = widen(cos_ref[...], lanes), widen(sin_ref[...], lanes)

    def turned_back(grad, raw, head_gain):
        raw = raw.astype(jnp.float32)
        grad = grad * cosine - swap_halves(grad, width) * sine
        scale = lax.rsqrt(head_mean(raw * raw, width) + NORM_EPS)
        unit = raw * scale
        grad = grad * head_gain
        return (scale * (grad - unit * head_mean(grad * unit, width))).astype(jnp.bfloat16)

    def summed(term_refs):
        total = term_refs[0][...].astype(jnp.float32)
        for ref in term_refs[1:]:
            total = total + ref[...].astype(jnp.float32)
        return total

    copies = [
        pltpu.make_async_copy(source, held_ref.at[index], sems.at[index])
        for index, source in enumerate((normed_any, x_any, residual_any))
    ]

    @pl.when(step == 0)
    def _():
        for copy in copies:
            copy.start()
        total_ref[...] = jnp.zeros(total_ref.shape, jnp.float32)
        few_ref[...] = jnp.zeros(few_ref.shape, jnp.float32)

    inner_turned = jnp.transpose(inner_ref[...].astype(jnp.float32) * ADAPTER_SCALE).astype(
        jnp.bfloat16
    )
    errors = [
        turned_back(gq_ref[...].astype(jnp.float32), q_raw_ref[...], gains_ref[2:3, :lanes]),
        turned_back(summed(gk_refs), k_raw_ref[...], gains_ref[3:4, :lanes]),
        summed(gv_refs).astype(jnp.bfloat16),
    ]
    total_ref[...] += contract_last(
        beside(*errors), beside(wq_ref[...], wk_ref[...], wv_ref[...])
    )
    few = few_ref[...]
    wide = 2 * RANK
    for index, error in enumerate(errors):
        few = few + jnp.where(place == index, contract_last(error, b_ref[...]), 0.0)
        here = slice(index * wide, (index + 1) * wide)
        grad_b = dot(inner_turned[here], error)
        for part in range(lanes // LANES):
            square_ref[part, here, :] = grad_b[:, part * LANES : (part + 1) * LANES]
    square_ref[:, 3 * wide :, :] = jnp.zeros(
        (lanes // LANES, LANES - 3 * wide, LANES), jnp.float32
    )
    if devices:
        chunks = held_ref.shape[2] // LANES
        for index in range(lanes // LANES):
            for first, starts in ((wide, (0, wide)), (wide + RANK, (2 * wide, 3 * wide))):
                spread_square_to(
                    spread_ref,
                    first,
                    square_ref,
                    starts,
                    step * (lanes // LANES) + index,
                    chunks,
                    index,
                )
    else:
        for part in range(lanes // LANES):
            grad_b_ref[:, part * LANES : (part + 1) * LANES] = square_ref[part].astype(
                jnp.bfloat16
            )
    few_ref[...] = few

    @pl.when(step == pl.num_programs(0) - 1)
    def _():
        low = (ADAPTER_SCALE * few_ref[...] * mask).astype(jnp.bfloat16)
        low_turned = jnp.transpose(low.astype(jnp.float32)).astype(jnp.bfloat16)
        for copy in copies:
            copy.wait()
        tall_ref[...] = jnp.transpose(dot(low_turned, held_ref[0]))
        if devices:
            spread_wide_to(spread_ref, 0, tall_ref)
        else:
            grad_a_ref[...] = tall_ref[...].astype(jnp.bfloat16)
        grad = total_ref[...] + contract_last(low, a_ref[...])
        out = held_ref[2].astype(jnp.float32) + row_norm_back(
            held_ref[1].astype(jnp.float32), gains_ref[0:1, :], grad
        )
        out_ref[...] = out.astype(jnp.bfloat16)
        tail_ref[...] = out[out.shape[0] - tail_ref.shape[0] :].astype(jnp.bfloat16)


def project_heads_back(
    devices,
    after,
    grad_query,
    key_terms,
    value_terms,
    query_raw,
    key_raw,
    normed,
    inner,
    rows_in,
    grad_residual,
    gains,
    weights,
    a_qkv,
    b_qkv,
    meta,
    cos_table,
    sin_table,
    width,
):
    rows, features = rows_in.shape
    count = len(key_terms)
    tile = 256

    def tiled(height):
        return pl.BlockSpec((height, tile), lambda step: (0, step))

    full = whole_block((rows, features))
    anywhere = pl.BlockSpec(memory_space=pl.ANY)
    if devices:
        spread = (devices, 4 * RANK, LANES)
        grad_specs = [whole_block(spread)]
        grad_shapes = [jax.ShapeDtypeStruct(spread, jnp.bfloat16)]
    else:
        grad_specs = [whole_block((features, LANES)), tiled(LANES)]
        grad_shapes = [
            jax.ShapeDtypeStruct((features, LANES), jnp.bfloat16),
            jax.ShapeDtypeStruct((LANES, features), jnp.bfloat16),
        ]
    return pl.pallas_call(
        functools.partial(project_heads_back_kernel, count, width, devices),
        grid=(features // tile,),
        in_specs=[tiled(rows)] * (3 + 2 * count)
        + [anywhere, whole_block((rows, LANES)), anywhere, anywhere, whole_block(gains.shape)]
        + [tiled(features)] * 3
        + [whole_block((features, LANES)), tiled(LANES), whole_block(meta.shape)]
        + [whole_block((rows, LANES))] * 2
        + [anywhere] * len(after),
        out_specs=[full, whole_block((rows // 2, features)), *grad_specs],
        out_shape=[
            jax.ShapeDtypeStruct((rows, features), jnp.bfloat16),
            jax.ShapeDtypeStruct((rows // 2, features), jnp.bfloat16),
            *grad_shapes,
        ],
        scratch_shapes=[
            pltpu.VMEM((rows, features), jnp.float32),
            pltpu.VMEM((rows, LANES), jnp.float32),
            pltpu.VMEM((features, LANES), jnp.float32),
            pltpu.VMEM((tile // LANES, LANES, LANES), jnp.float32),
            pltpu.VMEM((3, rows, features), jnp.bfloat16),
            pltpu.SemaphoreType.DMA((3,)),
        ],
        compiler_params=pltpu.CompilerParams(vmem_limit_bytes=VMEM_LIMIT),
        cost_estimate=pl.CostEstimate(
            flops=8 * rows * features * features,
            bytes_accessed=6 * features * features + 30 * rows * features,
            transcendentals=0,
        ),
        name="project_heads_back",
    )(
        grad_query,
        *key_terms,
        *value_terms,
        query_raw,
        key_raw,
        normed,
        inner,
        rows_in,
        grad_residual,
        gains,
        *weights,
        a_qkv,
        b_qkv,
        meta,
        cos_table,
        sin_table,
        *after,
    )


def spread_wide_to(spread_ref, first, held_ref):
    devices = spread_ref.shape[0]
    count = held_ref.shape[0] // devices
    for device in range(devices):
        spread_ref[device, first : first + count, :] = held_ref[
            pl.ds(device, count, stride=devices), :
        ].astype(jnp.bfloat16)


def spread_square_to(spread_ref, first, held_ref, starts, chunk, chunks, index):
    classes = spread_ref.shape[0] // chunks
    count = 2 * RANK // classes
    for part in range(classes):
        rows = [
            held_ref[index, pl.ds(start + part, count, stride=classes), :]
            for start in starts
        ]
        spread_ref[part * chunks + chunk, first : first + 2 * count, :] = jnp.concatenate(
            rows, axis=0
        ).astype(jnp.bfloat16)


def feed_forward_kernel(
    devices,
    turn_ref,
    att_ref,
    x_any,
    kept_any,
    arrived_any,
    gains_ref,
    wo_ref,
    wg_any,
    wu_any,
    wd_any,
    a_guo_ref,
    a_down_ref,
    b_gu_ref,
    b_do_ref,
    meta_ref,
    out_any,
    tail_any,
    grad_res_any,
    grad_att_ref,
    *refs,
):
    if devices:
        spread_ref, refs = refs[0], refs[1:]
    else:
        (grad_a_ref, grad_ad_ref, grad_bgu_ref, grad_bdo_ref), refs = refs[:4], refs[4:]
    (
        res_ref,
        hidden_ref,
        inner_ref,
        inner_turned_ref,
        sum_ref,
        grad_hidden_ref,
        inner_down_ref,
        few_ref,
        few_down_ref,
        few_down_turned_ref,
        down_ref,
        tall_ref,
        square_ref,
        e_ref,
        x_ref,
        arrived_ref,
        wg_ref,
        wu_ref,
        wd_ref,
        out_ref,
        grad_res_ref,
        rows_sems,
        tile_sems,
        out_sems,
    ) = refs
    step = pl.program_id(0)
    steps = pl.num_programs(0)
    mask, place = turn_mask(meta_ref)
    tile = wg_ref.shape[2]
    swap_rows = arrived_ref.shape[0]
    row_copies = [
        pltpu.make_async_copy(source, target, rows_sems.at[index])
        for index, (source, target) in enumerate(
            ((x_any, x_ref), (kept_any, e_ref), (arrived_any, arrived_ref))
        )
    ]

    def tile_copies(number):
        slot = number % 2
        here = pl.ds(pl.multiple_of(number * tile, tile), tile)
        pairs = (
            (wg_any.at[:, here], wg_ref.at[slot]),
            (wu_any.at[:, here], wu_ref.at[slot]),
            (wd_any.at[here, :], wd_ref.at[slot]),
        )
        return [
            pltpu.make_async_copy(source, target, tile_sems.at[slot, index])
            for index, (source, target) in enumerate(pairs)
        ]

    features = wo_ref.shape[0]
    wide = 2 * RANK

    def only(values, index):
        return jnp.where(place == index, values, 0.0).astype(jnp.bfloat16)

    def turn(values):
        return jnp.transpose(values.astype(jnp.float32)).astype(jnp.bfloat16)

    @pl.when(step == 0)
    def _():
        for copy in row_copies:
            copy.start()
        for copy in tile_copies(0):
            copy.start()
        att = att_ref[...]
        inner_out = dot(att, a_guo_ref[...]) * mask
        attention_out = dot(
            beside(att, only(ADAPTER_SCALE * inner_out, 2)), above(wo_ref[...], b_do_ref[...])
        )
        row_copies[0].wait()
        res = x_ref[...].astype(jnp.float32) + attention_out
        res_ref[...] = res
        hidden = (res * row_norm(res) * gains_ref[1:2, :]).astype(jnp.bfloat16)
        hidden_ref[...] = hidden
        inner = dot(hidden, a_guo_ref[...]) * mask
        inner = jnp.where(place == 2, inner_out, inner).astype(jnp.bfloat16)
        inner_ref[...] = inner
        inner_turned_ref[...] = turn(inner.astype(jnp.float32) * ADAPTER_SCALE)
        for copy in row_copies[1:]:
            copy.wait()
        e_ref[e_ref.shape[0] - swap_rows :, :] += arrived_ref[...]
        few_down = only(ADAPTER_SCALE * contract_last(e_ref[...], b_do_ref[...]) * mask, 0)
        few_down_ref[...] = few_down
        few_down_turned_ref[...] = turn(few_down)[:wide]
        sum_ref[...] = jnp.zeros(sum_ref.shape, jnp.float32)
        grad_hidden_ref[...] = jnp.zeros(grad_hidden_ref.shape, jnp.float32)
        inner_down_ref[...] = jnp.zeros(inner_down_ref.shape, jnp.float32)
        few_ref[...] = jnp.zeros(few_ref.shape, jnp.float32)

    @pl.when(step + 1 < steps)
    def _():
        for copy in tile_copies(step + 1):
            copy.start()

    for copy in tile_copies(step):
        copy.wait()
    slot = step % 2
    hidden = hidden_ref[...]
    inner = ADAPTER_SCALE * inner_ref[...].astype(jnp.float32)
    gate_weight, up_weight, down_weight = wg_ref[slot], wu_ref[slot], wd_ref[slot]
    b_tile = b_gu_ref[...]
    gate = dot(beside(hidden, only(inner, 0)), above(gate_weight, b_tile))
    up = dot(beside(hidden, only(inner, 1)), above(up_weight, b_tile))
    grad_act = contract_last(
        beside(e_ref[...], few_down_ref[...]), beside(down_weight, a_down_ref[...])
    )
    sigmoid = 1.0 / (1.0 + jnp.exp(-gate))
    silu = gate * sigmoid
    act = (silu * up).astype(jnp.bfloat16)
    grad_up = (grad_act * silu).astype(jnp.bfloat16)
    grad_gate = (grad_act * up * (sigmoid * (1.0 + gate * (1.0 - sigmoid)))).astype(jnp.bfloat16)
    sum_ref[...] += dot(act, down_weight)
    inner_down_ref[...] += dot(act, a_down_ref[...])
    grad_hidden_ref[...] += contract_last(
        beside(grad_gate, grad_up), beside(gate_weight, up_weight)
    )
    few_ref[...] += jnp.where(
        place == 0, contract_last(grad_gate, b_tile), contract_last(grad_up, b_tile)
    )
    grad_b_gate = dot(inner_turned_ref[:wide, :], grad_gate).astype(jnp.bfloat16)
    grad_b_up = dot(inner_turned_ref[wide : 2 * wide, :], grad_up).astype(jnp.bfloat16)
    if devices:
        for index in range(tile // LANES):
            device = step * (tile // LANES) + index
            chunk = slice(index * LANES, (index + 1) * LANES)
            spread_ref[device, 2 * wide : 3 * wide, :] = grad_b_gate[:, chunk]
            spread_ref[device, 3 * wide : 4 * wide, :] = grad_b_up[:, chunk]
    else:
        grad_bgu_ref[:wide, :] = grad_b_gate
        grad_bgu_ref[wide:, :] = grad_b_up
    per_quarter = features // tile
    down_ref[
        pl.ds(pl.multiple_of((step // per_quarter) * wide, wide), wide),
        pl.ds(pl.multiple_of((step % per_quarter) * tile, tile), tile),
    ] = dot(few_down_turned_ref[...], act)

    out_copies = [
        pltpu.make_async_copy(source, target, out_sems.at[index])
        for index, (source, target) in enumerate(
            (
                (out_ref, out_any),
                (out_ref.at[out_ref.shape[0] - swap_rows :, :], tail_any),
                (grad_res_ref, grad_res_any),
            )
        )
    ]

    @pl.when(step == steps - 1)
    def _():
        grads_out = e_ref[...]
        inner_down = only(inner_down_ref[...] * mask, 0)
        res = res_ref[...]
        out_ref[...] = (
            res + sum_ref[...] + ADAPTER_SCALE * dot(inner_down, b_do_ref[...])
        ).astype(jnp.bfloat16)
        for copy in out_copies[:2]:
            copy.start()
        few = jnp.where(place < 2, ADAPTER_SCALE * few_ref[...] * mask, 0.0).astype(jnp.bfloat16)
        grad_hidden = grad_hidden_ref[...] + contract_last(few, a_guo_ref[...])
        grad_res = grads_out.astype(jnp.float32) + row_norm_back(
            res, gains_ref[1:2, :], grad_hidden
        )
        low = grad_res.astype(jnp.bfloat16)
        grad_res_ref[...] = low
        out_copies[2].start()
        few_out = only(ADAPTER_SCALE * contract_last(low, b_do_ref[...]) * mask, 2)
        grad_att_ref[...] = contract_last(
            beside(low, few_out), beside(wo_ref[...], a_guo_ref[...])
        ).astype(jnp.bfloat16)
        grad_a = dot(turn(few), hidden_ref[...]) + dot(turn(few_out), att_ref[...])
        inner_out = only(inner_ref[...].astype(jnp.float32), 2)
        grad_b = ADAPTER_SCALE * (
            dot(turn(inner_down), grads_out) + dot(turn(inner_out), low)
        )
        if devices:
            lane = lax.broadcasted_iota(jnp.int32, (features, LANES), 1)
            told = jnp.where(
                lane == 3 * wide, turn_ref[0], jnp.where(lane == 3 * wide + 1, turn_ref[1], 0)
            )
            tall_ref[...] = jnp.transpose(grad_a) + told.astype(jnp.float32)
            spread_wide_to(spread_ref, 0, tall_ref)
            tall_ref[...] = jnp.transpose(down_ref[...])
            spread_wide_to(spread_ref, wide, tall_ref)
            chunks = features // LANES
            for chunk in range(chunks):
                square_ref[chunk] = grad_b[:, chunk * LANES : (chunk + 1) * LANES]
                spread_square_to(
                    spread_ref, 4 * wide, square_ref, (0, 2 * wide), chunk, chunks, chunk
                )
        else:
            grad_a_ref[...] = jnp.transpose(grad_a).astype(jnp.bfloat16)
            grad_ad_ref[...] = jnp.transpose(down_ref[...]).astype(jnp.bfloat16)
            grad_bdo_ref[...] = grad_b.astype(jnp.bfloat16)
        for copy in out_copies:
            copy.wait()


def feed_forward(
    devices,
    turn_adapter,
    attended,
    rows_in,
    kept,
    arrived,
    gains,
    weights,
    selected,
    meta,
):
    rows, features = rows_in.shape
    hidden = weights[1].shape[1]
    tile = 1024
    full = whole_block((rows, features))
    square = whole_block((features, features))
    anywhere = pl.BlockSpec(memory_space=pl.ANY)

    def shape(height, length, dtype):
        return jax.ShapeDtypeStruct((height, length), dtype)

    if devices:
        spread = (devices, 9 * RANK, LANES)
        grad_specs = [whole_block(spread)]
        grad_shapes = [jax.ShapeDtypeStruct(spread, jnp.bfloat16)]
    else:
        grad_specs = [
            whole_block((features, LANES)),
            whole_block((features, LANES)),
            pl.BlockSpec((4 * RANK, tile), lambda step: (0, step)),
            whole_block((LANES, features)),
        ]
        grad_shapes = [
            shape(features, LANES, jnp.bfloat16),
            shape(features, LANES, jnp.bfloat16),
            shape(4 * RANK, hidden, jnp.bfloat16),
            shape(LANES, features, jnp.bfloat16),
        ]
    return pl.pallas_call(
        functools.partial(feed_forward_kernel, devices),
        grid=(hidden // tile,),
        in_specs=[
            pl.BlockSpec(memory_space=pltpu.SMEM),
            full,
            anywhere,
            anywhere,
            anywhere,
            whole_block(gains.shape),
            square,
            anywhere,
            anywhere,
            anywhere,
            whole_block((features, LANES)),
            pl.BlockSpec((tile, LANES), lambda step: (step, 0)),
            pl.BlockSpec((LANES, tile), lambda step: (0, step)),
            whole_block((LANES, features)),
            whole_block(meta.shape),
        ],
        out_specs=[anywhere, anywhere, anywhere, full, *grad_specs],
        out_shape=[
            shape(rows, features, jnp.bfloat16),
            shape(*arrived.shape, jnp.bfloat16),
            shape(rows, features, jnp.bfloat16),
            shape(rows, features, jnp.bfloat16),
            *grad_shapes,
        ],
        scratch_shapes=[
            pltpu.VMEM((rows, features), jnp.float32),
            pltpu.VMEM((rows, features), jnp.bfloat16),
            pltpu.VMEM((rows, LANES), jnp.bfloat16),
            pltpu.VMEM((LANES, rows), jnp.bfloat16),
            pltpu.VMEM((rows, features), jnp.float32),
            pltpu.VMEM((rows, features), jnp.float32),
            pltpu.VMEM((rows, LANES), jnp.float32),
            pltpu.VMEM((rows, LANES), jnp.float32),
            pltpu.VMEM((rows, LANES), jnp.bfloat16),
            pltpu.VMEM((2 * RANK, rows), jnp.bfloat16),
            pltpu.VMEM((LANES, features), jnp.float32),
            pltpu.VMEM((features, LANES), jnp.float32),
            pltpu.VMEM((features // LANES, LANES, LANES), jnp.float32),
            pltpu.VMEM((rows, features), jnp.bfloat16),
            pltpu.VMEM((rows, features), jnp.bfloat16),
            pltpu.VMEM(arrived.shape, jnp.bfloat16),
            pltpu.VMEM((2, features, tile), jnp.bfloat16),
            pltpu.VMEM((2, features, tile), jnp.bfloat16),
            pltpu.VMEM((2, tile, features), jnp.bfloat16),
            pltpu.VMEM((rows, features), jnp.bfloat16),
            pltpu.VMEM((rows, features), jnp.bfloat16),
            pltpu.SemaphoreType.DMA((3,)),
            pltpu.SemaphoreType.DMA((2, 3)),
            pltpu.SemaphoreType.DMA((3,)),
        ],
        compiler_params=pltpu.CompilerParams(vmem_limit_bytes=VMEM_LIMIT),
        cost_estimate=pl.CostEstimate(
            flops=14 * rows * features * hidden,
            bytes_accessed=8 * features * hidden + 16 * rows * features,
            transcendentals=0,
        ),
        name="feed_forward",
    )(
        turn_adapter,
        attended,
        rows_in,
        kept,
        arrived,
        gains,
        *weights,
        *selected,
        meta,
    )


def settle_owned(grads, moment1, moment2, devices):
    grads = lax.all_to_all(grads, ALL, 0, 0, tiled=True)
    grads = grads[:, : moment1.shape[0] // (LANES * devices)]
    grad_shard = jnp.transpose(grads, (1, 0, 2)).reshape(-1).astype(jnp.float32)
    current = jnp.zeros((), jnp.float32)
    first_moment, second_moment, _ = adam(current, moment1, moment2, grad_shard)
    return grad_shard, first_moment, second_moment


def per_device(
    tokens,
    cotangent,
    variate,
    seq_len,
    seq_adapter,
    block_order,
    attn_gain,
    ffn_gain,
    q_gain,
    k_gain,
    attn_bias,
    query_weight,
    key_weight,
    value_weight,
    output_weight,
    gate_weight,
    up_weight,
    down_weight,
    adapters,
    moment1,
    moment2,
):
    groups = axis_count(GROUP)
    member = lax.axis_index(GROUP)
    row_count, feature_width = tokens.shape
    hidden_width = gate_weight.shape[1]
    head_width = q_gain.shape[0]
    half_devices = groups // 2
    segments = seq_len.shape[1]
    chosen, back, turn_adapter, cos_table, sin_table, key_metas = plan(
        groups, row_count, head_width, member[None], seq_len, seq_adapter, block_order, variate
    )
    meta = key_metas[0]
    axes = ALL
    devices = axis_count(PACKS) * groups
    even = spreads_evenly(devices, groups, feature_width, hidden_width, adapters.shape[0])
    spread = devices if even else 0
    gains = gain_rows(attn_gain, ffn_gain, q_gain, k_gain)


    held = (gather_half(tokens, groups), gather_half(cotangent, groups))
    sent_tokens, sent_grads = pick(chosen, row_count, row_count // 2, *held)
    arrived_tokens = to_other_half(sent_tokens, groups)
    a_qkv, a_guo, a_down, b_qkv, b_gu, b_do, *spread_state = select(
        spread,
        turn_adapter,
        lax.axis_index(axes)[None],
        adapters,
        (moment1.reshape(-1, LANES), moment2.reshape(-1, LANES)),
        feature_width,
        hidden_width,
        sent_tokens,
    )
    if even:
        params, moments = spread_state
        moments = lax.all_to_all(moments, axes, 0, 0, tiled=True)
    kept_tokens, kept_grads = pick(chosen, 0, row_count, *held)
    (
        my_tokens,
        normed,
        inner,
        query_raw,
        key_raw,
        query_low,
        key_low,
        value_low,
        sent_grads,
    ) = project_heads(
        kept_tokens,
        arrived_tokens,
        sent_grads,
        gains,
        (query_weight, key_weight, value_weight),
        a_qkv,
        b_qkv,
        meta,
        cos_table,
        sin_table,
        head_width,
    )
    arrived_grads = to_other_half(sent_grads, groups)
    keys = gather_half(key_low, groups)
    values = gather_half(value_low, groups)
    attended_low, log_total = attend(
        attn_bias, query_low, meta, keys, values, key_metas, segments, head_width
    )
    layer_rows, layer_tail, grad_residual, grad_attended, *forward_grads = feed_forward(
        spread,
        turn_adapter,
        attended_low,
        my_tokens,
        kept_grads,
        arrived_grads,
        gains,
        (output_weight, gate_weight, up_weight, down_weight),
        (a_guo, a_down, b_gu, b_do),
        meta,
    )
    layer_back = to_other_half(layer_tail, groups)

    results = attend_back(
        attn_bias,
        query_low,
        meta,
        log_total,
        attended_low,
        grad_attended,
        keys,
        values,
        key_metas,
        segments,
        head_width,
    )
    after = []
    if even:
        total_rows = adapters.shape[0] // LANES
        late_rows = 6 * feature_width // devices
        early = lax.all_to_all(forward_grads[0], axes, 0, 0, tiled=True)
    grad_query = results[0]
    grad_keys = results[1 : 1 + half_devices]
    grad_values = results[1 + half_devices :]
    key_terms, value_terms = [grad_keys[0]], [grad_values[0]]
    for shift in range(1, half_devices):
        back_shift = half_devices - shift
        key_terms.append(within_half(grad_keys[shift], back_shift, groups))
        value_terms.append(within_half(grad_values[shift], back_shift, groups))
    grad_rows, grad_tail, *back_grads = project_heads_back(
        spread,
        after,
        grad_query,
        key_terms,
        value_terms,
        query_raw,
        key_raw,
        normed,
        inner,
        my_tokens,
        grad_residual,
        gains,
        (query_weight, key_weight, value_weight),
        a_qkv,
        b_qkv,
        meta,
        cos_table,
        sin_table,
        head_width,
    )
    def bring_back(tail):
        return gather_half(grad_rows, groups) + gather_half(to_other_half(tail, groups), groups)

    if not even:
        grads = (*back_grads, *forward_grads)
        column = jnp.arange(2 * RANK, dtype=jnp.int32)
        few_choice = one_hot(
            jnp.arange(LANES, dtype=jnp.int32)[:, None]
            == (jnp.repeat(turn_adapter, RANK) * RANK + column % RANK)[None, :]
        )
        settled = settle_shards(grads, few_choice, adapters, moment1, moment2, groups)
        layer_held = gather_half(layer_rows, groups) + gather_half(layer_back, groups)
        layer_out = pick(back, 0, row_count, layer_held)[0]
        input_grad = pick(back, 0, row_count, bring_back(grad_tail))[0]
        return (layer_out, input_grad) + settled
    late = lax.all_to_all(back_grads[0], axes, 0, 0, tiled=True)
    early_grad, early_new, late_m1, late_m2, tall, square = settle_early(
        early, moments, params, late_rows, [grad_rows]
    )
    swap = [(0, 1), (1, 0)]
    far_count = lax.axis_size("far")
    bit = 1
    early_outer = early_new
    while bit < far_count:
        pairs = [(i, i ^ bit) for i in range(far_count)]
        early_outer = jnp.concatenate([early_outer, lax.ppermute(early_outer, "far", pairs)])
        bit *= 2
    early_near = lax.ppermute(early_outer, "near", swap)
    early_half = lax.ppermute(early_outer, "half", swap)
    early_far = lax.ppermute(early_half, "near", swap)
    own_grads, late_new, grad_tail, layer_back = settle_late(
        tall, square, late, params, late_m1, late_m2, early_grad, [grad_tail, layer_back], []
    )
    layer_held = gather_half(layer_rows, groups) + gather_half(layer_back, groups)
    layer_out = pick(back, 0, row_count, layer_held)[0]
    late_outer = lax.all_to_all(late_new, PACKS, 0, 0, tiled=True)
    late_pieces = gather_inner(late_outer, groups)
    own_grads = hand_on([late_outer, layer_out], own_grads)[0]
    input_grad = pick(back, 0, row_count, bring_back(grad_tail))[0]
    early_pieces = [[early_outer], [early_near], [early_half], [early_far]]
    early_pieces += [
        [lax.ppermute(part, "core", swap) for part in piece] for piece in early_pieces
    ]
    far = lax.axis_index("far") ^ jnp.arange(far_count, dtype=jnp.int32)
    near, half, core = [lax.axis_index(name) for name in ALL[1:]]
    early_device = jnp.concatenate(
        [
            ((far * 2 + (near ^ flip_near)) * 2 + (half ^ flip_half)) * 2 + (core ^ flip_core)
            for flip_core in (0, 1)
            for flip_near, flip_half in ((0, 0), (1, 0), (0, 1), (1, 1))
        ]
    )
    late_pieces = [[piece] for piece in late_pieces]
    order = placing_order(piece_devices(groups, devices), 16)
    adapters_new = assemble(order, late_pieces, total_rows, 0, None, [input_grad])
    adapters_new = assemble(
        placing_order(early_device, 16), early_pieces, total_rows, late_rows, adapters_new, []
    )
    owned = settle_owned(own_grads, moment1, moment2, devices)
    return (layer_out, input_grad, *owned, adapters_new.reshape(-1))


def solution(mesh):
    packs, groups = mesh.shape["dp"], mesh.shape["group"]
    cut = jax.sharding.Mesh(mesh.devices.reshape(packs // 2, 2, groups // 2, 2), ALL)
    in_specs = (
        P(ALL, None),
        P(ALL, None),
        P(PACKS),
        P(PACKS, None),
        P(PACKS, None),
        P(PACKS, None),
        P(),
        P(),
        P(),
        P(),
        P(),
        P(),
        P(),
        P(),
        P(),
        P(),
        P(),
        P(),
        P(),
        P(ALL),
        P(ALL),
    )
    out_specs = (
        P(ALL, None),
        P(ALL, None),
        P(ALL),
        P(ALL),
        P(ALL),
        P(),
    )
    return jax.shard_map(
        per_device, mesh=cut, in_specs=in_specs, out_specs=out_specs, check_vma=False
    )
```
